32 devices in a mesh: wide: 8 (over y, x, core), narrow: 4 (over z).
Axes of the slice: x: 2, y: 2, z: 4, core: 2. Of those that a mesh axis runs over, the one named last changes fastest.
Arguments:
- tokens: bfloat16 [8192, 1536], P(('wide', 'narrow')), may hold values from -6 to 6
- gain_one: float32 [1536], replicated, may hold values from 0.5 to 1.5
- in_weight: bfloat16 [1536, 6216], P(('wide', 'narrow')), may hold values from -0.15625 to 0.15625
- forget_bias: float32 [24], replicated, may hold values from 1 to 7
- out_weight: bfloat16 [1536, 1536], P(('wide', 'narrow')), may hold values from -0.625 to 0.625
- gain_two: float32 [1536], replicated, may hold values from 0.5 to 1.5
- gate_up_weight: bfloat16 [1536, 8192], P(('wide', 'narrow')), may hold values from -0.15625 to 0.15625
- down_weight: bfloat16 [4096, 1536], P(('wide', 'narrow')), may hold values from -0.09375 to 0.09375
- segment_ids: int32 [8, 1024], P('wide'), may hold values from 0 to 2, as said below
- cotangent: bfloat16 [8192, 1536], P(('wide', 'narrow')), may hold values from -6 to 6
Outputs:
- output: bfloat16 [8192, 1536], P(('wide', 'narrow'))
- grad_tokens: float32 [8192, 1536], P(('wide', 'narrow'))
- grad_gain_one: float32 [1536], replicated
- grad_in_weight: float32 [1536, 6216], P('wide', 'narrow')
- grad_forget_bias: float32 [24], replicated
- grad_out_weight: float32 [1536, 1536], P('wide', 'narrow')
- grad_gain_two: float32 [1536], replicated
- grad_gate_up: float32 [1536, 8192], P('wide', 'narrow')
- grad_down: float32 [4096, 1536], P('wide', 'narrow')
The draws below stay inside these ranges and needn't reach their ends.
Inputs may be any that keep to these rules, and one draw needn't show every extreme that they name: `segment_ids`: each slot holds three runs of rows with ids 0, 1, 2 in order: a first run (id 0), one whole sequence longer than 768 rows (id 1), and a last run (id 2); each run is attended as a sequence of its own, rows never attend across slots, and the first and last runs have at least one row each.
All inputs are finite; a program needn't handle non-finite values.
Results may differ from the reference program's by a relative error of at most 0.017.
Values may be sent and summed in bfloat16 or wider, within the bound.
A program may use at most 256 MiB of HBM per device.

```python
import jax
import jax.numpy as jnp
from jax import lax

D = 1536
H = 24
HD = 64
FF = 4096
TOK_DEV = 256
SLOT = 1024
SLOTS = 8
TOKENS = 8192


def draw_segment_ids(key, part):
    key = jax.random.fold_in(key, 11)
    length_key, second = jax.random.split(key)
    long_length = SLOT - TOK_DEV + 1 + jax.random.randint(length_key, (SLOTS, 1), 0, TOK_DEV - 2)
    remaining = SLOT - long_length
    leading = jax.random.randint(second, (SLOTS, 1), 1, remaining)
    position = jnp.arange(SLOT, dtype=jnp.int32)[None, :]
    first_edge = (position >= leading).astype(jnp.int32)
    second_edge = (position >= leading + long_length).astype(jnp.int32)
    return (first_edge + second_edge).astype(jnp.int32)


def block_levels(key, dims, cuts, smallest, high):
    def one(dim, shards_of):
        heights = jax.random.uniform(jax.random.fold_in(jax.random.fold_in(key, 6), dim), (shards_of,), jnp.float32, smallest / len(cuts), high / len(cuts))
        return jnp.repeat(jnp.exp(heights), dims[dim] // shards_of).reshape((-1,) + (1,) * (len(dims) - dim - 1))

    loudness = one(*cuts[0])
    for cut in cuts[1:]:
        loudness = loudness * one(*cut)
    return loudness


def centred(stream_key, extent, spread, reach, cuts=(), kind=jnp.bfloat16):
    entries = jax.random.normal(stream_key, extent, jnp.float32) * spread
    if len(cuts) > 0:
        entries = block_levels(stream_key, extent, cuts, -0.22, 0.18) * entries
    return jnp.clip(entries, min=-reach, max=reach).astype(kind)


def setup_inputs(seed: int = 0) -> dict:
    key_of = jax.random.split(jax.random.key(seed), 11)
    tokens = centred(key_of[0], (TOKENS, D), 1.0, 6.0, ((0, 32),))
    gain_one = jnp.clip(1.0 + 0.1 * jax.random.normal(key_of[1], (D,), jnp.float32), 0.5, 1.5)
    in_weight = centred(key_of[2], (D, 4 * D + 3 * H), D ** -0.5, 0.15625, ((0, 32),))
    forget_bias = jnp.clip(jax.random.uniform(key_of[3], (H,), jnp.float32, 1.0, 7.0), 1.0, 7.0)
    out_weight = centred(key_of[4], (D, D), (D // 16) ** -0.5, 0.625, ((0, 32),))
    gain_two = jnp.clip(1.0 + 0.1 * jax.random.normal(key_of[5], (D,), jnp.float32), 0.5, 1.5)
    gate_up_weight = centred(key_of[6], (D, 2 * FF), D ** -0.5, 0.15625, ((0, 32),))
    down_weight = centred(key_of[7], (FF, D), FF ** -0.5, 0.09375, ((0, 32),))
    segment_ids = draw_segment_ids(jax.random.fold_in(key_of[10], 71), 0)
    cotangent = centred(key_of[9], (TOKENS, D), 1.0, 6.0, ((0, 32),))
    return {"tokens": tokens, "gain_one": gain_one, "in_weight": in_weight, "forget_bias": forget_bias, "out_weight": out_weight, "gain_two": gain_two, "gate_up_weight": gate_up_weight, "down_weight": down_weight, "segment_ids": segment_ids, "cotangent": cotangent}


EPSILON = 1e-06
MASKED_SCORE = -1e+30
PRECISE = lax.Precision.HIGHEST

@jax.custom_vjp
def low(v):
    return lax.optimization_barrier(v.astype(jnp.bfloat16)).astype(jnp.float32)

@jax.custom_vjp
def low_back(v):
    return v

def low_keep(v):
    return (low(v), None)

def low_pass(kept, grad):
    return (grad,)

def back_keep(v):
    return (v, None)

def back_low(kept, grad):
    return (low(grad),)
low.defvjp(low_keep, low_pass)
low_back.defvjp(back_keep, back_low)

def matmul(left, right):
    return jnp.dot(left, right, precision=PRECISE, preferred_element_type=jnp.float32)

def rms_norm(values, gain_vector):
    factor = lax.rsqrt(lax.optimization_barrier(jnp.mean(values * values, axis=-1, keepdims=True)) + EPSILON)
    return values * factor * gain_vector

def prepare(queries, keys_in, values_in, forget, key_shift, value_shift, continued):
    key_prev = jnp.concatenate([jnp.zeros_like(keys_in[:1]), keys_in[:-1]], axis=0) * continued[:, None, None]
    value_prev = jnp.concatenate([jnp.zeros_like(values_in[:1]), values_in[:-1]], axis=0) * continued[:, None, None]
    key_mix = jax.nn.sigmoid(key_shift)[:, :, None]
    value_mix = jax.nn.sigmoid(value_shift)[:, :, None]
    shifted_keys = keys_in + key_mix * (key_prev - keys_in)
    shifted_values = values_in + value_mix * (value_prev - values_in)
    query_norm = queries * lax.rsqrt(lax.optimization_barrier(jnp.mean(queries * queries, axis=-1, keepdims=True)) + EPSILON)
    key_norm = shifted_keys * lax.rsqrt(lax.optimization_barrier(jnp.mean(shifted_keys * shifted_keys, axis=-1, keepdims=True)) + EPSILON)
    decay = jnp.cumsum(jax.nn.log_sigmoid(forget), axis=0)
    return (query_norm, key_norm, shifted_values, decay)

def continuation(segments, dtype_like):
    joined = (segments[1:] == segments[:-1]).astype(dtype_like.dtype)
    return jnp.concatenate([jnp.zeros((1,), dtype_like.dtype), joined])

def slot_attention(packed):
    queries, keys_in, values_in, forget, key_shift, value_shift, segments = packed
    continued = continuation(segments, queries)
    query_norm, key_norm, shifted_values, decay = prepare(queries, keys_in, values_in, forget, key_shift, value_shift, continued)
    query_low = low(query_norm)
    key_low = low(key_norm)
    value_low = low(shifted_values)
    block_rows = min(512, SLOT)
    score_scale = HD ** (-0.5)
    offsets = jnp.arange(SLOT // block_rows, dtype=jnp.int32) * block_rows
    col_index = jnp.arange(SLOT, dtype=jnp.int32)

    def attend_block(offset):
        row_index = offset + jnp.arange(block_rows, dtype=jnp.int32)
        query_block = lax.dynamic_slice_in_dim(query_low, offset, block_rows, 0)
        decay_block = lax.dynamic_slice_in_dim(decay, offset, block_rows, 0)
        segment_block = lax.dynamic_slice_in_dim(segments, offset, block_rows, 0)
        scores = jnp.einsum('qhd,khd->hqk', query_block, key_low, precision=PRECISE) * score_scale
        scores = low_back(scores + decay_block.T[:, :, None] - decay.T[:, None, :])
        visible = (col_index[None, :] <= row_index[:, None]) & (segment_block[:, None] == segments[None, :])
        scores = jnp.where(visible[None], scores, MASKED_SCORE)
        largest = lax.optimization_barrier(jnp.max(scores, axis=-1, keepdims=True))
        exponent_terms = jnp.exp(scores - largest)
        weights_low = low(exponent_terms / lax.optimization_barrier(jnp.sum(exponent_terms, axis=-1, keepdims=True)))
        return jnp.einsum('hqk,khd->qhd', weights_low, value_low, precision=PRECISE)
    outputs = lax.map(jax.checkpoint(attend_block), offsets)
    return outputs.reshape(SLOT, H, HD)

def layer(inputs, gain_one, in_weight, forget_bias, out_weight, gain_two, gate_up_weight, down_weight, segment_ids):
    normed_one = low(rms_norm(inputs, gain_one))
    projected = low_back(matmul(normed_one, in_weight))
    base = 4 * D
    queries = low(projected[:, :D]).reshape(SLOTS, SLOT, H, HD)
    keys_in = low(projected[:, D:2 * D]).reshape(SLOTS, SLOT, H, HD)
    values_in = low(projected[:, 2 * D:3 * D]).reshape(SLOTS, SLOT, H, HD)
    gate_logit = projected[:, 3 * D:4 * D]
    forget = low(projected[:, base:base + H] + forget_bias).reshape(SLOTS, SLOT, H)
    key_shift = low(projected[:, base + H:base + 2 * H]).reshape(SLOTS, SLOT, H)
    value_shift = low(projected[:, base + 2 * H:base + 3 * H]).reshape(SLOTS, SLOT, H)
    attended = lax.map(jax.checkpoint(slot_attention), (queries, keys_in, values_in, forget, key_shift, value_shift, segment_ids))
    attended = low(low_back(attended.reshape(TOKENS, D)))
    mixed = low(attended * jax.nn.sigmoid(gate_logit))
    branch_one = low_back(matmul(mixed, out_weight))
    middle = inputs + branch_one
    normed_two = low(rms_norm(middle, gain_two))
    gate_up = low_back(matmul(normed_two, gate_up_weight))
    hidden = low(jax.nn.silu(gate_up[:, :FF]) * gate_up[:, FF:])
    branch_two = low_back(matmul(hidden, down_weight))
    return middle + branch_two

def reference(tokens, gain_one, in_weight, forget_bias, out_weight, gain_two, gate_up_weight, down_weight, segment_ids, cotangent):

    def wrapped(inputs, gain_a, weight_in, bias_vector, weight_out, gain_b, weight_gate_up, weight_down):
        return layer(inputs, gain_a, weight_in, bias_vector, weight_out, gain_b, weight_gate_up, weight_down, segment_ids)
    floats = (tokens.astype(jnp.float32), gain_one.astype(jnp.float32), in_weight.astype(jnp.float32), forget_bias.astype(jnp.float32), out_weight.astype(jnp.float32), gain_two.astype(jnp.float32), gate_up_weight.astype(jnp.float32), down_weight.astype(jnp.float32))
    output, pullback = jax.vjp(wrapped, *floats)
    grads = pullback(cotangent.astype(jnp.float32))
    return (output.astype(jnp.bfloat16), grads[0], grads[1], grads[2], grads[3], grads[4], grads[5], grads[6], grads[7])
```

```python
import functools

import jax
import jax.numpy as jnp
from jax import lax
from jax.experimental import pallas as pl
from jax.experimental.pallas import tpu as pltpu
from jax.sharding import PartitionSpec as P

EPSILON = 1e-06
SEPARATE = 128.0
F32 = jnp.float32
BF16 = jnp.bfloat16
LANES = 128
EXACT = lax.Precision.HIGHEST
ANY = pl.BlockSpec(memory_space=pl.ANY)


def dot_f32(left, right, dims=((1,), (0,))):
    return lax.dot_general(left, right, (dims, ((), ())), preferred_element_type=F32)


def along_narrow(block, step, narrow):
    pairs = [(i, (i + step) % narrow) for i in range(narrow)]
    return lax.ppermute(block, "narrow", pairs)


def along_wide(block, flip, wide):
    return lax.ppermute(block, "wide", [(i, i ^ flip) for i in range(wide)])


def gather_narrow(block, narrow, slot, shape):
    me = lambda: lax.axis_index("narrow")
    if narrow != 4:
        pieces = [block] + [along_narrow(block, k, narrow) for k in range(1, narrow)]
        return assemble(pieces, lambda k, t: slot(lax.rem(me() + narrow - k, narrow), t), shape)
    two = lax.ppermute(block, "narrow", [(0, 2), (2, 0), (1, 3), (3, 1)])
    one = lax.ppermute(block, "narrow", [(0, 1), (1, 0), (2, 3), (3, 2)])
    middle = lax.ppermute(block, "narrow", [(1, 2), (2, 1)])
    end = lax.ppermute(two, "narrow", [(2, 3), (1, 0)])
    is_middle = lambda: (me() == 1) | (me() == 2)

    def plan(sources, targets):
        t = targets[0]
        far = slot(flipped(me(), 3), t)
        return [
            (sources[0], slot(me(), t)),
            (sources[1], slot(flipped(me(), 1), t)),
            (sources[2], slot(flipped(me(), 2), t)),
            (sources[3], far, is_middle()),
            (sources[4], far, jnp.logical_not(is_middle())),
        ]

    whole = jax.ShapeDtypeStruct(shape, block.dtype)
    return local_copies(plan, 5, [block, one, two, middle, end], [whole], True)[0]


def from_wide(block, wide):
    even = [block] + [along_wide(block, k, wide) for k in range(2, wide, 2)]
    pieces = []
    for piece in even:
        pieces += [piece, along_wide(piece, 1, wide)]
    return pieces


def copy_kernel(plan, count, *refs):
    sources, targets, sems = refs[:count], refs[count:-1], refs[-1]
    copies = plan(sources, targets)

    def each(act):
        for n, (src, dst, *when) in enumerate(copies):
            copy = pltpu.make_async_copy(src, dst, sems.at[n])
            if when:
                pl.when(when[0])(functools.partial(act, copy))
            else:
                act(copy)

    each(lambda copy: copy.start())
    each(lambda copy: copy.wait())


def local_copies(plan, copies, sources, shapes, gather):
    moved = sum(s.size * s.dtype.itemsize for s in shapes)
    inside = pl.BlockSpec(memory_space=pltpu.VMEM)
    out = pl.pallas_call(
        functools.partial(copy_kernel, plan, len(sources)),
        out_shape=shapes,
        in_specs=[ANY if gather else inside] * len(sources),
        out_specs=[inside if gather else ANY] * len(shapes),
        compiler_params=pltpu.CompilerParams(vmem_limit_bytes=16 * 2**20),
        scratch_shapes=[pltpu.SemaphoreType.DMA((copies,))],
        cost_estimate=pl.CostEstimate(flops=0, bytes_accessed=2 * moved, transcendentals=0),
    )(*sources)
    return out


def assemble(pieces, place, shape):
    def plan(sources, targets):
        return [(src, place(k, targets[0])) for k, src in enumerate(sources)]

    whole = jax.ShapeDtypeStruct(shape, pieces[0].dtype)
    return local_copies(plan, len(pieces), pieces, [whole], True)[0]


def narrow_order(k, narrow):
    return lax.rem(lax.axis_index("narrow") + narrow - k, narrow)


def narrow_target(k, narrow):
    return lax.rem(lax.axis_index("narrow") + k, narrow)


def flipped(me, k):
    out = me
    bit = 1
    while bit <= k:
        if k & bit:
            out = out + bit - 2 * bit * lax.rem(lax.div(out, bit), 2)
        bit *= 2
    return out


def wide_order(k):
    return flipped(lax.axis_index("wide"), k)


def nothing_kernel(*refs):
    pass


def follow(array, *earlier):
    return pl.pallas_call(
        nothing_kernel,
        out_shape=jax.ShapeDtypeStruct(array.shape, array.dtype),
        in_specs=[ANY] * (1 + len(earlier)),
        out_specs=ANY,
        input_output_aliases={0: 0},
    )(array, *earlier)


def rms_factor(values):
    return lax.rsqrt(jnp.mean(values * values, axis=-1, keepdims=True) + EPSILON)


def rms_back(values, gain, grad):
    factor = rms_factor(values)
    normed = values * factor
    grad_gain = jnp.sum(grad * normed, axis=0)
    scaled = grad * gain
    inner = jnp.mean(scaled * normed, axis=-1, keepdims=True)
    return (factor * (scaled - normed * inner), grad_gain)


def log_sigmoid(v):
    return jnp.minimum(v, 0.0) - jnp.log1p(jnp.exp(-jnp.abs(v)))


def iota(shape, dim):
    return lax.broadcasted_iota(jnp.int32, shape, dim)


def running_sum(v, reverse):
    rows = v.shape[0]
    index = iota(v.shape, 0)
    step = 1
    while step < rows:
        if reverse:
            v = v + jnp.where(index < rows - step, pltpu.roll(v, rows - step, 0), 0.0)
        else:
            v = v + jnp.where(index >= step, pltpu.roll(v, step, 0), 0.0)
        step *= 2
    return v


def half_of(lane, head_size):
    return (lane >= head_size).astype(jnp.int32)


def spread(first, head_size):
    row, lane = iota((LANES, LANES), 0), iota((LANES, LANES), 1)
    return row == first + half_of(lane, head_size)


def collect(first, head_size):
    row, lane = iota((LANES, LANES), 0), iota((LANES, LANES), 1)
    return lane == first + half_of(row, head_size)


def same_head(head_size):
    row, lane = iota((LANES, LANES), 0), iota((LANES, LANES), 1)
    return (half_of(row, head_size) == half_of(lane, head_size)).astype(F32)


def exact_dot(left, right):
    return lax.dot_general(
        left, right, (((1,), (0,)), ((), ())), precision=EXACT, preferred_element_type=F32
    )


def head_mean(v, head_size):
    return exact_dot(v, same_head(head_size)) * (1.0 / head_size)


def prologue(pair, heads, head_size, q_ref, k_ref, v_ref, small_low, cont):
    spot = lambda group: spread(group * heads + 2 * pair, head_size).astype(BF16)
    key_mix = jax.nn.sigmoid(dot_f32(small_low, spot(1)))
    value_mix = jax.nn.sigmoid(dot_f32(small_low, spot(2)))
    queries = q_ref[...].astype(BF16).astype(F32)
    keys = k_ref[...].astype(BF16).astype(F32)
    values = v_ref[...].astype(BF16).astype(F32)
    key_step = pltpu.roll(keys, 1, 0) * cont - keys
    value_step = pltpu.roll(values, 1, 0) * cont - values
    shifted = keys + key_mix * key_step
    value_low = (values + value_mix * value_step).astype(BF16)
    query_factor = lax.rsqrt(head_mean(queries * queries, head_size) + EPSILON)
    key_factor = lax.rsqrt(head_mean(shifted * shifted, head_size) + EPSILON)
    return (
        queries * query_factor,
        shifted * key_factor,
        value_low,
        query_factor,
        key_factor,
        key_mix,
        value_mix,
        key_step,
        value_step,
    )


def small_columns(small_ref, bias_ref):
    return (small_ref[...] + bias_ref[0:1, :]).astype(BF16)


def decay_of(small_low, cont):
    return running_sum(log_sigmoid(small_low.astype(F32)) - SEPARATE * (1.0 - cont), False)


def forward_kernel(
    heads, head_size, block, q_ref, k_ref, v_ref, gate_ref, small_ref, bias_ref, cont_ref,
    mixed_ref, att_ref, log_ref, decay_scr,
):
    pair = pl.program_id(0)
    cont = cont_ref[...]
    small_low = small_columns(small_ref, bias_ref)

    @pl.when(pair == 0)
    def _():
        decay_scr[...] = decay_of(small_low, cont)

    query, key, value_low, *unused = prologue(
        pair, heads, head_size, q_ref, k_ref, v_ref, small_low, cont
    )
    rows = query.shape[0]
    query = query.astype(BF16) * BF16(head_size**-0.5)
    key = key.astype(BF16)
    decay = exact_dot(decay_scr[...], spread(2 * pair, head_size).astype(F32))
    decay_rows = decay.T
    lane = iota((1, LANES), 1)
    ones = jnp.ones((rows, LANES), BF16)
    value_wide = jnp.concatenate([value_low, ones], axis=1)
    for i in range(rows // block):
        lo, hi = i * block, (i + 1) * block
        row_index = iota((block, hi), 0) + lo
        visible = iota((block, hi), 1) <= row_index
        outs, sums = [], []
        for head in range(2):
            mine = (lane >= head_size) if head else (lane < head_size)
            at = head * head_size
            left = jnp.where(mine, query[lo:hi], BF16(0.0))
            scores = dot_f32(left, key[:hi], ((1,), (1,)))
            scores = scores + decay[lo:hi, at : at + 1] - decay_rows[at : at + 1, :hi]
            weights = jnp.where(visible, jnp.exp(scores), 0.0).astype(BF16)
            both = dot_f32(weights, value_wide[:hi])
            outs.append(both[:, :LANES])
            sums.append(both[:, LANES:])
        first = lane < head_size
        total = jnp.where(first, sums[0], sums[1])
        attended = (jnp.where(first, outs[0], outs[1]) / total).astype(BF16)
        att_ref[lo:hi, :] = attended
        log_ref[lo:hi, :] = jnp.log(total)
        opened = jax.nn.sigmoid(gate_ref[lo:hi, :])
        mixed_ref[lo:hi, :] = (attended.astype(F32) * opened).astype(BF16)


def backward_kernel(
    heads, head_size, block, q_ref, k_ref, v_ref, gate_ref, small_ref, bias_ref, cont_ref,
    att_ref, log_ref, grad_ref, out_ref, bias_grad_ref, decay_scr, small_scr, dq_scr,
):
    pair = pl.program_id(0)
    cont = cont_ref[...]
    small_low = small_columns(small_ref, bias_ref)
    rows = cont.shape[0]
    width = heads * head_size

    @pl.when(pair == 0)
    def _():
        decay_scr[...] = decay_of(small_low, cont)
        small_scr[...] = jnp.zeros_like(small_scr)

    (
        query_norm, key_norm, value_low, query_factor, key_factor, key_mix, value_mix, key_step,
        value_step,
    ) = prologue(pair, heads, head_size, q_ref, k_ref, v_ref, small_low, cont)
    query = query_norm.astype(BF16) * BF16(head_size**-0.5)
    key = key_norm.astype(BF16)
    opened = jax.nn.sigmoid(gate_ref[...])
    attended = att_ref[...].astype(F32)
    grad_mixed = grad_ref[...].astype(F32)
    grad_low = (grad_mixed * opened).astype(BF16)
    grad_gate = grad_mixed * attended * opened * (1.0 - opened)

    def columns(group):
        at = group * width + pair * LANES
        return pl.ds(pl.multiple_of(at, LANES), LANES)

    out_ref[:, columns(3)] = grad_gate.astype(BF16)
    inner = exact_dot(grad_low.astype(F32) * attended, same_head(head_size))
    decay = exact_dot(decay_scr[...], spread(2 * pair, head_size).astype(F32))
    level_rows = (decay - log_ref[...]).T
    inner_rows = inner.T
    lane = iota((1, LANES), 1)
    ones = jnp.ones((rows, LANES), BF16)
    query_wide = jnp.concatenate([query, ones], axis=1)
    key_wide = jnp.concatenate([key, ones], axis=1)
    key_parts, value_parts, query_parts = [], [], []
    for head in range(2):
        mine = (lane >= head_size) if head else (lane < head_size)
        at = head * head_size
        keys_out, values_out = [], []
        for j in range(rows // block):
            lo, hi = j * block, (j + 1) * block
            span = rows - lo
            visible = iota((block, span), 0) <= iota((block, span), 1)
            scores = dot_f32(
                jnp.where(mine, key[lo:hi], BF16(0.0)), query[lo:], ((1,), (1,))
            )
            scores = scores + level_rows[at : at + 1, lo:] - decay[lo:hi, at : at + 1]
            probs = jnp.where(visible, jnp.exp(scores), 0.0)
            grad_probs = dot_f32(
                jnp.where(mine, value_low[lo:hi], BF16(0.0)), grad_low[lo:], ((1,), (1,))
            )
            grad_scores = (probs * (grad_probs - inner_rows[at : at + 1, lo:])).astype(BF16)
            values_out.append(dot_f32(probs.astype(BF16), grad_low[lo:]))
            keys_out.append(dot_f32(grad_scores, query_wide[lo:]))
            part = dot_f32(grad_scores, key_wide[lo:hi], ((0,), (0,)))
            if j == 0:
                dq_scr[...] = part
            else:
                dq_scr[lo:, :] += part
        key_parts.append(jnp.concatenate(keys_out, axis=0))
        value_parts.append(jnp.concatenate(values_out, axis=0))
        query_parts.append(dq_scr[...])
    first = lane < head_size

    def join(parts):
        return jnp.where(first, parts[0], parts[1])

    grad_query = join([p[:, :LANES] for p in query_parts]) * head_size**-0.5
    grad_key = join([p[:, :LANES] for p in key_parts])
    grad_value = join(value_parts)
    grad_decay = join([p[:, LANES:] for p in query_parts]) - join([p[:, LANES:] for p in key_parts])

    def norm_back(grad, normed, factor):
        return factor * (grad - normed * head_mean(grad * normed, head_size))

    def shift_back(grad, mix):
        return grad * (1.0 - mix) + pltpu.roll(grad * mix * cont, rows - 1, 0)

    grad_query = norm_back(grad_query, query_norm, query_factor)
    grad_shifted = norm_back(grad_key, key_norm, key_factor)
    out_ref[:, columns(0)] = grad_query.astype(BF16)
    out_ref[:, columns(1)] = shift_back(grad_shifted, key_mix).astype(BF16)
    out_ref[:, columns(2)] = shift_back(grad_value, value_mix).astype(BF16)
    key_logit = grad_shifted * key_step * key_mix * (1.0 - key_mix)
    value_logit = grad_value * value_step * value_mix * (1.0 - value_mix)
    single = (lax.rem(lane, head_size) == 0).astype(F32)
    small_scr[...] += (
        exact_dot(grad_decay * single, collect(2 * pair, head_size).astype(F32))
        + exact_dot(key_logit, collect(heads + 2 * pair, head_size).astype(F32))
        + exact_dot(value_logit, collect(2 * heads + 2 * pair, head_size).astype(F32))
    )

    @pl.when(pair == pl.num_programs(0) - 1)
    def _():
        grads = small_scr[...]
        forget = running_sum(grads, True) * jax.nn.sigmoid(-small_low.astype(F32))
        result = jnp.where(lane < heads, forget, grads)
        out_ref[:, 4 * width :] = result.astype(BF16)
        bias_grad_ref[...] = jnp.broadcast_to(
            jnp.sum(result, axis=0, keepdims=True), bias_grad_ref.shape
        )


def attention_specs(rows, pairs):
    def block_at(group):
        return pl.BlockSpec((rows, LANES), lambda p: (0, group * pairs + p))

    def fixed(height, column=0):
        return pl.BlockSpec((height, LANES), lambda p: (0, column))

    base = [block_at(0), block_at(1), block_at(2), block_at(3), fixed(rows, 4 * pairs), fixed(8), fixed(rows)]
    return base, pl.BlockSpec((rows, LANES), lambda p: (0, p))


def attention_forward(projected, bias, cont, heads, head_size, block):
    rows = projected.shape[0]
    pairs = heads * head_size // LANES
    base, own = attention_specs(rows, pairs)
    wide = jax.ShapeDtypeStruct((rows, heads * head_size), BF16)
    return pl.pallas_call(
        functools.partial(forward_kernel, heads, head_size, block),
        grid=(pairs,),
        in_specs=base,
        out_specs=[own] * 3,
        out_shape=[wide, wide, jax.ShapeDtypeStruct(wide.shape, F32)],
        scratch_shapes=[pltpu.VMEM((rows, LANES), F32)],
        compiler_params=pltpu.CompilerParams(vmem_limit_bytes=48 * 2**20),
        cost_estimate=pl.CostEstimate(
            flops=heads * rows * rows * 400, bytes_accessed=rows * 1664 * 6, transcendentals=heads * rows * rows // 2
        ),
    )(*([projected] * 5), bias, cont)


def attention_backward(projected, bias, cont, attended, logs, grad, heads, head_size, block):
    rows = projected.shape[0]
    pairs = heads * head_size // LANES
    base, own = attention_specs(rows, pairs)
    columns = 4 * heads * head_size + LANES
    return pl.pallas_call(
        functools.partial(backward_kernel, heads, head_size, block),
        grid=(pairs,),
        in_specs=base + [own] * 3,
        out_specs=[
            pl.BlockSpec((rows, columns), lambda p: (0, 0)),
            pl.BlockSpec((8, LANES), lambda p: (0, 0)),
        ],
        out_shape=[
            jax.ShapeDtypeStruct((rows, columns), BF16),
            jax.ShapeDtypeStruct((8, LANES), F32),
        ],
        scratch_shapes=[
            pltpu.VMEM((rows, LANES), F32),
            pltpu.VMEM((rows, LANES), F32),
            pltpu.VMEM((rows, 2 * LANES), F32),
        ],
        compiler_params=pltpu.CompilerParams(vmem_limit_bytes=56 * 2**20),
        cost_estimate=pl.CostEstimate(
            flops=heads * rows * rows * 1000, bytes_accessed=rows * 1664 * 8, transcendentals=heads * rows * rows // 2
        ),
    )(*([projected] * 5), bias, cont, attended, logs, grad)


def reduce_wide(pieces, wide):
    received = along_wide(jnp.stack(pieces[1::2]), 1, wide)
    summed = [
        (pieces[2 * n].astype(F32) + received[n].astype(F32)).astype(BF16) for n in range(wide // 2)
    ]
    total = summed[0].astype(F32)
    for n in range(1, wide // 2):
        total = total + along_wide(summed[n], 2 * n, wide).astype(F32)
    return total


def reduce_narrow(share, narrow):
    me = lax.axis_index("narrow")
    if narrow != 4:
        total = share(me).astype(F32)
        for k in range(1, narrow):
            total = total + along_narrow(share(lax.rem(me + k, narrow)), k, narrow).astype(F32)
        return total
    far = share(flipped(me, 3))
    joined = lax.ppermute(far, "narrow", [(0, 1), (3, 2)])
    middle = lax.ppermute(far, "narrow", [(1, 2), (2, 1)])
    one = lax.ppermute(share(flipped(me, 1)), "narrow", [(0, 1), (1, 0), (2, 3), (3, 2)])
    two = (share(flipped(me, 2)).astype(F32) + joined.astype(F32)).astype(BF16)
    two = lax.ppermute(two, "narrow", [(0, 2), (2, 0), (1, 3), (3, 1)])
    total = share(me).astype(F32) + one.astype(F32)
    return total + middle.astype(F32) + two.astype(F32)


def total_of(values, wide, narrow):
    bit = 1
    while bit < wide:
        values = values + along_wide(values, bit, wide)
        bit *= 2
    bit = 1
    while bit < narrow:
        values = values + lax.ppermute(values, "narrow", [(i, i ^ bit) for i in range(narrow)])
        bit *= 2
    return values


def on_device(
    tokens, gain_one, in_weight, forget_bias, out_weight, gain_two, gate_up_weight, down_weight,
    segment_ids, cotangent,
):
    wide, narrow = lax.axis_size("wide"), lax.axis_size("narrow")
    w, z = lax.axis_index("wide"), lax.axis_index("narrow")
    rows, width = tokens.shape
    slot = rows * narrow
    heads = forget_bias.shape[0]
    head_size = width // heads
    own_heads = heads // narrow
    own_width = own_heads * head_size
    part_rows = in_weight.shape[0]
    hidden_all = down_weight.shape[0] * wide * narrow
    unit = hidden_all // (2 * wide)
    columns = 4 * own_width + LANES
    base = 4 * width

    small = in_weight[:, base:].reshape(part_rows, 3, narrow, own_heads)
    small = jnp.moveaxis(small, 2, 0).reshape(narrow, part_rows, 3 * own_heads)
    small = jnp.pad(small, ((0, 0), (0, 0), (0, LANES - 3 * own_heads)))

    def split_in(sources, targets):
        copies = []
        for k, target in enumerate(targets):
            to = narrow_target(k, narrow)
            for group in range(4):
                at = pl.multiple_of(group * width + to * own_width, LANES)
                copies.append(
                    (
                        sources[0].at[:, pl.ds(at, own_width)],
                        target.at[:, pl.ds(group * own_width, own_width)],
                    )
                )
            copies.append((sources[1].at[to], target.at[:, pl.ds(4 * own_width, LANES)]))
        return copies

    in_parts = local_copies(
        split_in, 5 * narrow, [in_weight, small],
        [jax.ShapeDtypeStruct((part_rows, columns), BF16)] * narrow, False,
    )
    in_pieces = [in_parts[0]] + [along_narrow(in_parts[k], k, narrow) for k in range(1, narrow)]
    in_block = assemble(
        in_pieces, lambda k, t: t.at[narrow_order(k, narrow)], (narrow, part_rows, columns)
    )

    slot_tokens = gather_narrow(
        tokens, narrow, lambda n, t: t.at[n], (narrow, rows, width)
    ).reshape(slot, width)
    in_full = assemble(
        from_wide(in_block, wide), lambda k, t: t.at[wide_order(k)],
        (wide, narrow, part_rows, columns),
    ).reshape(width, columns)
    slot_floats = slot_tokens.astype(F32)
    normed_one = (slot_floats * rms_factor(slot_floats) * gain_one).astype(BF16)
    projected = dot_f32(normed_one, in_full)

    out_block = gather_narrow(
        follow(out_weight, slot_tokens), narrow, lambda n, t: t.at[n], (narrow,) + out_weight.shape
    )
    out_full = assemble(
        from_wide(out_block, wide), lambda k, t: t.at[wide_order(k)], (wide,) + out_block.shape
    ).reshape(width, width)

    def split_up(sources, targets):
        copies = []
        for k, target in enumerate(targets):
            to = wide_order(k)
            for group in range(4):
                at = pl.multiple_of((group * wide + to) * unit, 64)
                copies.append(
                    (
                        sources[0].at[:, pl.ds(at, unit)],
                        target.at[:, pl.ds(group * unit, unit)],
                    )
                )
        return copies

    if unit % LANES == 0:
        up_parts = local_copies(
            split_up, 4 * wide, [gate_up_weight],
            [jax.ShapeDtypeStruct((part_rows, 4 * unit), BF16)] * wide, False,
        )
    else:
        grouped = jnp.moveaxis(gate_up_weight.reshape(part_rows, 4, wide, unit), 2, 0)
        grouped = grouped.reshape(wide, part_rows, 4 * unit)
        up_parts = [
            lax.dynamic_index_in_dim(grouped, wide_order(k), 0, False) for k in range(wide)
        ]
    up_pieces = [up_parts[0]] + [along_wide(up_parts[k], k, wide) for k in range(1, wide)]
    up_block = assemble(up_pieces, lambda k, t: t.at[wide_order(k)], (wide, part_rows, 4 * unit))
    up_full = gather_narrow(
        follow(up_block, out_block), narrow, lambda n, t: t.at[:, n],
        (wide, narrow, part_rows, 4 * unit),
    ).reshape(width, 4 * unit)
    down_rows = down_weight.shape[0]
    pairs = []
    for i in range(wide * narrow):
        to_wide = (i % (2 * wide)) // 2
        to_narrow = i % 2 + 2 * (i // (2 * wide))
        pairs.append((i, to_wide * narrow + to_narrow))
    down_block = lax.ppermute(follow(down_weight, slot_tokens), ("wide", "narrow"), pairs)
    down_full = gather_narrow(
        follow(down_block, up_full), narrow, lambda n, t: t.at[n], (narrow, down_rows, width)
    ).reshape(2 * unit, width)

    segments = segment_ids[0]
    joined = (segments[1:] == segments[:-1]).astype(F32)
    cont = jnp.concatenate([jnp.zeros((1,), F32), joined])
    cont = jnp.broadcast_to(cont[:, None], (slot, LANES))
    own_bias = lax.dynamic_slice_in_dim(forget_bias, z * own_heads, own_heads)
    bias = jnp.broadcast_to(jnp.pad(own_bias, (0, LANES - own_heads))[None], (8, LANES))
    block = min(256, slot)
    mixed, attended, logs = attention_forward(
        projected, bias, cont, own_heads, head_size, block
    )

    def rows_of(k, array):
        return lax.dynamic_slice_in_dim(array, lax.rem(z + k, narrow) * rows, rows, 0)

    def columns_of(k, array, size):
        return lax.dynamic_slice_in_dim(array, lax.rem(z + k, narrow) * size, size, 1)

    def share_columns(array, size):
        return lambda n: lax.dynamic_slice_in_dim(array, n * size, size, 1)

    mixed_pieces = [rows_of(0, mixed)] + [
        along_narrow(rows_of(k, mixed), k, narrow) for k in range(1, narrow)
    ]

    def at_columns(k, target):
        at = pl.multiple_of(narrow_order(k, narrow) * own_width, LANES)
        return target.at[:, pl.ds(at, own_width)]

    mixed_rows = assemble(mixed_pieces, at_columns, (rows, width))
    inputs = tokens.astype(F32)
    middle = inputs + dot_f32(mixed_rows, out_full)
    normed_two = (middle * rms_factor(middle) * gain_two).astype(BF16)

    plane_normed = jnp.concatenate(from_wide(normed_two, wide), axis=0)
    plane_grad = jnp.concatenate(from_wide(follow(cotangent, in_full), wide), axis=0)
    gate_up = dot_f32(plane_normed, up_full)
    gate, up = gate_up[:, : 2 * unit], gate_up[:, 2 * unit :]
    opened = jax.nn.sigmoid(gate)
    hidden = (gate * opened * up).astype(BF16)
    grad_hidden = dot_f32(plane_grad, down_full, ((1,), (1,)))
    gate_up_grad = jnp.concatenate(
        [
            grad_hidden * up * (opened * (1.0 + gate * (1.0 - opened))),
            grad_hidden * gate * opened,
        ],
        axis=1,
    ).astype(BF16)
    grad_normed_two = dot_f32(gate_up_grad, up_full, ((1,), (1,))).astype(BF16)
    grad_up_full = dot_f32(plane_normed, gate_up_grad, ((0,), (0,))).astype(BF16)
    grad_down_full = dot_f32(hidden, plane_grad, ((0,), (0,))).astype(BF16)

    def row_pieces(array):
        return [array[k * rows : (k + 1) * rows] for k in range(wide)]

    grad_normed_two = reduce_wide(row_pieces(grad_normed_two), wide)
    upstream = cotangent.astype(F32)
    grad_middle_norm, grad_gain_two = rms_back(middle, gain_two, grad_normed_two)
    grad_middle = upstream + grad_middle_norm
    branch_one_grad = grad_middle.astype(BF16)
    grad_mixed = dot_f32(branch_one_grad, out_full, ((1,), (1,))).astype(BF16)
    grad_pieces = [columns_of(0, grad_mixed, own_width)] + [
        along_narrow(columns_of(k, grad_mixed, own_width), k, narrow) for k in range(1, narrow)
    ]
    slot_grad = assemble(
        grad_pieces, lambda k, t: t.at[narrow_order(k, narrow)], (narrow, rows, own_width)
    ).reshape(slot, own_width)
    branch_two = dot_f32(follow(hidden, grad_normed_two), down_full).astype(BF16)
    output = (middle + reduce_wide(row_pieces(branch_two), wide)).astype(BF16)

    projected_grad, bias_grad = attention_backward(
        projected, bias, cont, attended, logs, slot_grad, own_heads, head_size, block
    )
    grad_normed_one_part = dot_f32(projected_grad, in_full, ((1,), (1,))).astype(BF16)
    grad_normed_one = reduce_narrow(
        lambda n: lax.dynamic_slice_in_dim(grad_normed_one_part, n * rows, rows, 0), narrow
    )
    grad_inputs, grad_gain_one = rms_back(inputs, gain_one, grad_normed_one)
    grad_tokens = grad_middle + grad_inputs

    grad_up = reduce_narrow(share_columns(grad_up_full, unit), narrow)
    grad_up = grad_up.astype(BF16)
    wide_rows = width // wide
    grad_up_pieces = []
    for k in range(wide):
        piece = lax.dynamic_slice_in_dim(grad_up, wide_order(k) * wide_rows, wide_rows, 0)
        grad_up_pieces.append(along_wide(piece, k, wide) if k else piece)
    if unit % LANES == 0:
        grad_up = assemble(
            grad_up_pieces,
            lambda k, t: t.at[:, pl.ds(pl.multiple_of(wide_order(k) * unit, LANES), unit)],
            (wide_rows, wide * unit),
        )
    else:
        grad_up = assemble(
            grad_up_pieces, lambda k, t: t.at[wide_order(k)], (wide, wide_rows, unit)
        )
        grad_up = jnp.moveaxis(grad_up, 0, 1).reshape(wide_rows, wide * unit)
    grad_up = grad_up.astype(F32)

    narrow_width = width // narrow
    grad_down = reduce_narrow(share_columns(grad_down_full, narrow_width), narrow).astype(BF16)
    low_half, high_half = grad_down[:unit], grad_down[unit:]
    is_odd = lax.rem(w, 2) == 1
    first_send = jnp.where(is_odd, high_half, low_half)
    second_send = jnp.where(is_odd, low_half, high_half)
    half = wide // 2
    first_got = lax.ppermute(
        first_send, "wide", [(i, i // 2 + (half if i % 2 else 0)) for i in range(wide)]
    )
    second_got = lax.ppermute(
        second_send, "wide", [(i, i // 2 + (0 if i % 2 else half)) for i in range(wide)]
    )
    in_low = w < half
    grad_down = jnp.concatenate(
        [
            jnp.where(in_low, first_got, second_got),
            jnp.where(in_low, second_got, first_got),
        ],
        axis=0,
    ).astype(F32)

    grad_out_full = dot_f32(mixed_rows, branch_one_grad, ((0,), (0,))).astype(BF16)

    def wide_pieces(array):
        return [
            lax.dynamic_slice_in_dim(array, wide_order(k) * wide_rows, wide_rows, 0)
            for k in range(wide)
        ]

    grad_out = reduce_wide(wide_pieces(grad_out_full), wide).astype(BF16)
    grad_out = reduce_narrow(share_columns(grad_out, narrow_width), narrow)
    grad_in_full = dot_f32(normed_one, projected_grad, ((0,), (0,))).astype(BF16)
    grad_in = reduce_wide(wide_pieces(grad_in_full), wide).astype(BF16)
    grad_small = grad_in[:, 4 * own_width :]
    sections = []
    for j in range(4):
        own = grad_in[:, j * own_width : (j + 1) * own_width]
        after = grad_in[:, (j + 1) * own_width : (j + 1) * own_width + LANES]
        sections.append(jnp.concatenate([own, after], axis=1))
    sections = jnp.stack(sections)
    got = []
    for k in range(narrow):
        piece = lax.dynamic_index_in_dim(sections, lax.rem(z + k, narrow), 0, False)
        got.append(along_narrow(piece, k, narrow) if k else piece)
    got = assemble(
        got, lambda k, t: t.at[narrow_order(k, narrow)],
        (narrow, wide_rows, own_width + LANES),
    )
    extra = 3 * heads
    section = jnp.concatenate([got[n, :, :own_width] for n in range(narrow)], axis=1)
    small_all = jnp.stack([got[n, :, own_width : own_width + 3 * own_heads] for n in range(narrow)])
    small_all = small_all.reshape(narrow, wide_rows, 3, own_heads)
    small_all = jnp.transpose(small_all, (1, 2, 0, 3)).reshape(wide_rows, extra)
    next_first = got[0, :, own_width : own_width + extra]
    tail = jnp.where(z == narrow - 1, small_all, next_first)
    joined_columns = jnp.concatenate([section, tail], axis=1)
    shard = (base + extra) // narrow
    grad_in = lax.dynamic_slice_in_dim(joined_columns, z * (shard - width), shard, 1).astype(F32)

    all_bias = lax.dynamic_update_slice(
        jnp.zeros((heads,), F32), bias_grad[0, :own_heads], (z * own_heads,)
    )
    packed = jnp.concatenate([grad_gain_one, grad_gain_two, all_bias])
    packed = total_of(packed, wide, narrow)
    return (
        output,
        grad_tokens,
        packed[:width],
        grad_in,
        packed[2 * width :],
        grad_out,
        packed[width : 2 * width],
        grad_up,
        grad_down,
    )


def solution(mesh):
    both = ("wide", "narrow")
    in_specs = (
        P(both, None), P(), P(both, None), P(), P(both, None), P(), P(both, None), P(both, None),
        P("wide", None), P(both, None),
    )
    out_specs = (
        P(both, None), P(both, None), P(), P("wide", "narrow"), P(), P("wide", "narrow"), P(),
        P("wide", "narrow"), P("wide", "narrow"),
    )
    return jax.shard_map(
        on_device, mesh=mesh, in_specs=in_specs, out_specs=out_specs, check_vma=False
    )
```

```python
import functools

import jax
import jax.numpy as jnp
from jax import lax
from jax.experimental import pallas as pl
from jax.experimental.pallas import tpu as pltpu
from jax.sharding import PartitionSpec as P

EPSILON = 1e-06
SEPARATE = 128.0
F32 = jnp.float32
BF16 = jnp.bfloat16
LANES = 128
EXACT = lax.Precision.HIGHEST
ANY = pl.BlockSpec(memory_space=pl.ANY)


def dot_f32(left, right, dims=((1,), (0,))):
    return lax.dot_general(left, right, (dims, ((), ())), preferred_element_type=F32)


def along_wide(block, flip, wide):
    return lax.ppermute(block, "wide", [(i, i ^ flip) for i in range(wide)])


def copy_kernel(plan, count, *refs):
    sources, targets, sems = refs[:count], refs[count:-1], refs[-1]
    copies = plan(sources, targets)

    def each(act):
        for n, (src, dst, *when) in enumerate(copies):
            copy = pltpu.make_async_copy(src, dst, sems.at[n])
            if when:
                pl.when(when[0])(functools.partial(act, copy))
            else:
                act(copy)

    each(lambda copy: copy.start())
    each(lambda copy: copy.wait())


def local_copies(plan, copies, sources, shapes, gather):
    moved = sum(s.size * s.dtype.itemsize for s in shapes)
    inside = pl.BlockSpec(memory_space=pltpu.VMEM)
    return pl.pallas_call(
        functools.partial(copy_kernel, plan, len(sources)),
        out_shape=shapes,
        in_specs=[ANY if gather else inside] * len(sources),
        out_specs=[inside if gather else ANY] * len(shapes),
        compiler_params=pltpu.CompilerParams(vmem_limit_bytes=16 * 2**20),
        scratch_shapes=[pltpu.SemaphoreType.DMA((copies,))],
        cost_estimate=pl.CostEstimate(flops=0, bytes_accessed=2 * moved, transcendentals=0),
    )(*sources)


def flipped(me, k):
    out = me
    bit = 1
    while bit <= k:
        if k & bit:
            out = out + bit - 2 * bit * lax.rem(lax.div(out, bit), 2)
        bit *= 2
    return out


LINE_TWO = [(0, 2), (2, 0), (1, 3), (3, 1)]
LINE_ONE = [(0, 1), (1, 0), (2, 3), (3, 2)]
LINE_MIDDLE = [(1, 2), (2, 1)]
LINE_OUT = [(2, 3), (1, 0)]
LINE_IN = [(0, 1), (3, 2)]


def on_line(block, pairs):
    return lax.ppermute(block, "narrow", pairs)


def follow(array, *earlier):
    return lax.optimization_barrier((array, *earlier))[0]


MESH = pl.DeviceIdType.MESH
VMEM = pl.BlockSpec(memory_space=pltpu.VMEM)
DMA = pltpu.SemaphoreType.DMA


def greet(devices):
    barrier = pltpu.get_barrier_semaphore()
    for device in devices:
        pl.semaphore_signal(barrier, inc=1, device_id=device, device_id_type=MESH)
    pl.semaphore_wait(barrier, len(devices))


class Sender:
    def __init__(self, send, recv):
        self.send, self.recv, self.used = send, recv, 0

    def plan(self, src, dst, device):
        n = self.used
        self.used += 1
        return pltpu.make_async_remote_copy(
            src_ref=src, dst_ref=dst, send_sem=self.send.at[n], recv_sem=self.recv.at[n],
            device_id=device, device_id_type=MESH,
        )


def narrow_device(n):
    return {"narrow": n}


def wide_device(n):
    return {"wide": n}


def wide_steps(wide):
    return [1] + list(range(2, wide, 2))


def by_device(ref, w):
    return (lambda k: ref.at[flipped(w, k)]), (lambda k, to: ref.at[flipped(w, k)])


class WideGather:
    def __init__(self, sender, w, wide, part, target):
        self.far = list(range(2, wide, 2))
        self.first = {
            k: sender.plan(part(0), target(0, k), wide_device(flipped(w, k)))
            for k in wide_steps(wide)
        }
        sibling = wide_device(flipped(w, 1))
        self.second = {k: sender.plan(part(k), target(k, 1), sibling) for k in self.far}

    def start(self):
        for k in self.far + [1]:
            self.first[k].start()

    def pass_on(self):
        for k in self.far:
            self.first[k].wait_recv()
            self.second[k].start()

    def finish(self):
        self.first[1].wait_recv()
        for k in self.far:
            self.second[k].wait_recv()
        for copy in list(self.first.values()) + list(self.second.values()):
            copy.wait_send()


def gather_kernel(
    wide, x_ref, in_ref, out_ref, up_ref, slot_ref, in_full, out_full, up_block, send, recv, local
):
    w, z = lax.axis_index("wide"), lax.axis_index("narrow")
    line = [flipped(z, k) for k in range(4)]
    sender = Sender(send, recv)
    own = [
        pltpu.make_async_copy(in_ref.at[z], in_full.at[w, z], local.at[0]),
        pltpu.make_async_copy(out_ref, out_full.at[w, z], local.at[1]),
        pltpu.make_async_copy(x_ref, slot_ref.at[z], local.at[2]),
        pltpu.make_async_copy(up_ref.at[w], up_block.at[w], local.at[3]),
    ]
    for copy in own:
        copy.start()
    greet(
        [narrow_device(line[k]) for k in (1, 2, 3)]
        + [wide_device(flipped(w, k)) for k in range(1, wide)]
    )
    ups = [
        sender.plan(up_ref.at[flipped(w, k)], up_block.at[w], wide_device(flipped(w, k)))
        for k in range(1, wide)
    ]
    is_middle = (z == 1) | (z == 2)
    is_end = (z == 0) | (z == 3)
    ins = [
        sender.plan(in_ref.at[line[k]], in_full.at[w, z], narrow_device(line[k])) for k in (2, 3, 1)
    ]
    outs = [sender.plan(out_ref, out_full.at[w, z], narrow_device(line[k])) for k in (2, 3, 1)]
    two = sender.plan(x_ref, slot_ref.at[z], narrow_device(line[2]))
    one = sender.plan(x_ref, slot_ref.at[z], narrow_device(line[1]))
    middle = sender.plan(x_ref, slot_ref.at[z], narrow_device(line[3]))
    relay = sender.plan(slot_ref.at[line[2]], slot_ref.at[line[2]], narrow_device(line[1]))
    in_wide = WideGather(sender, w, wide, *by_device(in_full, w))
    out_wide = WideGather(sender, w, wide, *by_device(out_full, w))
    for copy in ins + outs + ups:
        copy.start()
    own[0].wait()
    for copy in ins:
        copy.wait_recv()
    in_wide.start()
    two.start()
    one.start()
    own[1].wait()
    for copy in outs:
        copy.wait_recv()
    out_wide.start()
    in_wide.pass_on()
    two.wait_recv()

    @pl.when(is_middle)
    def _():
        relay.start()
        middle.start()

    out_wide.pass_on()
    one.wait_recv()
    own[2].wait()
    own[3].wait()
    for copy in ups:
        copy.wait()

    @pl.when(is_middle)
    def _():
        middle.wait_recv()
        middle.wait_send()
        relay.wait_send()

    @pl.when(is_end)
    def _():
        relay.wait_recv()

    for copy in ins + outs + [two, one]:
        copy.wait_send()
    in_wide.finish()
    out_wide.finish()


def gather_all(tokens, in_parts, out_weight, up_parts):
    narrow, wide = in_parts.shape[0], up_parts.shape[0]
    steps = 10 + 4 * wide
    shapes = [
        (narrow,) + tokens.shape, (wide,) + in_parts.shape, (wide, narrow) + out_weight.shape,
        up_parts.shape,
    ]
    return pl.pallas_call(
        functools.partial(gather_kernel, wide),
        out_shape=[jax.ShapeDtypeStruct(shape, BF16) for shape in shapes],
        in_specs=[ANY] * 4,
        out_specs=[VMEM] * 4,
        scratch_shapes=[DMA((steps,)), DMA((steps,)), DMA((4,))],
        compiler_params=pltpu.CompilerParams(
            collective_id=0, has_side_effects=True, vmem_limit_bytes=32 * 2**20
        ),
    )(tokens, in_parts, out_weight, up_parts)


def exchange_kernel(source, target, src_ref, dst_ref, send, recv, local):
    z = lax.axis_index("narrow")
    line = [flipped(z, k) for k in range(4)]
    sender = Sender(send, recv)
    own = pltpu.make_async_copy(source(src_ref, z), target(dst_ref, z), local.at[0])
    own.start()
    greet([narrow_device(line[k]) for k in (1, 2, 3)])
    copies = [
        sender.plan(source(src_ref, line[k]), target(dst_ref, z), narrow_device(line[k]))
        for k in (2, 3, 1)
    ]
    for copy in copies:
        copy.start()
    own.wait()
    for copy in copies:
        copy.wait()


def exchange(array, source, target, shape, collective_id):
    return pl.pallas_call(
        functools.partial(exchange_kernel, source, target),
        out_shape=jax.ShapeDtypeStruct(shape, array.dtype),
        in_specs=[ANY],
        out_specs=VMEM,
        scratch_shapes=[DMA((3,)), DMA((3,)), DMA((1,))],
        compiler_params=pltpu.CompilerParams(
            collective_id=collective_id, has_side_effects=True, vmem_limit_bytes=16 * 2**20
        ),
    )(array)


def place_of(k, wide):
    return k // 2 + (k % 2) * (wide // 2)


def rows_kernel(wide, *refs):
    half = wide // 2
    grads = refs[:half]
    (
        src_ref, up_ref, up_two, up_one, down_ref, dst_ref, grad_ref, up_full, down_full, send,
        recv, local,
    ) = refs[half:]
    w, z = lax.axis_index("wide"), lax.axis_index("narrow")
    line = [flipped(z, k) for k in range(4)]
    is_middle = (z == 1) | (z == 2)
    is_end = (z == 0) | (z == 3)
    sender = Sender(send, recv)
    up_at = lambda n: up_full.at[:, n]
    down_at = lambda n: down_full.at[n]
    moves = [
        (src_ref, dst_ref.at[0]), (down_ref, down_at(z)),
        (up_ref, up_at(z)), (up_two, up_at(line[2])), (up_one, up_at(line[1])),
    ] + [(grads[n], grad_ref.at[n]) for n in range(half)]
    own = [pltpu.make_async_copy(src, dst, local.at[n]) for n, (src, dst) in enumerate(moves)]
    for copy in own:
        copy.start()
    greet(
        [wide_device(flipped(w, k)) for k in wide_steps(wide)]
        + [narrow_device(line[k]) for k in (1, 2, 3)]
    )
    gather = WideGather(
        sender, w, wide, lambda k: src_ref if k == 0 else dst_ref.at[place_of(k, wide)],
        lambda k, to: dst_ref.at[place_of(k ^ to, wide)],
    )
    middle = sender.plan(up_ref, up_at(z), narrow_device(line[3]))
    relay = sender.plan(up_two, up_at(line[2]), narrow_device(line[1]))
    down_two = sender.plan(down_ref, down_at(z), narrow_device(line[2]))
    down_one = sender.plan(down_ref, down_at(z), narrow_device(line[1]))
    down_middle = sender.plan(down_ref, down_at(z), narrow_device(line[3]))
    down_relay = sender.plan(down_at(line[2]), down_at(line[2]), narrow_device(line[1]))
    gather.start()
    down_two.start()

    @pl.when(is_middle)
    def _():
        relay.start()

    down_two.wait_recv()

    @pl.when(is_middle)
    def _():
        down_relay.start()
        middle.start()
        down_middle.start()

    down_one.start()
    sibling = wide_device(flipped(w, 1))
    copies = [sender.plan(grads[n], grad_ref.at[half + n], sibling) for n in range(half)]
    for copy in copies:
        copy.start()
    gather.pass_on()

    @pl.when(is_middle)
    def _():
        middle.wait()
        down_middle.wait()
        relay.wait_send()
        down_relay.wait_send()

    @pl.when(is_end)
    def _():
        relay.wait_recv()
        down_relay.wait_recv()

    down_two.wait_send()
    for copy in own + copies + [down_one]:
        copy.wait()
    gather.finish()


def gather_rows(array, grads, ups, down, collective_id):
    half = len(grads)
    wide = 2 * half
    whole = jax.ShapeDtypeStruct((wide,) + array.shape, array.dtype)
    up_shape = ups[0].shape
    full = jax.ShapeDtypeStruct((up_shape[0], 4) + up_shape[1:], BF16)
    return pl.pallas_call(
        functools.partial(rows_kernel, wide),
        out_shape=[whole, whole, full, jax.ShapeDtypeStruct((4,) + down.shape, BF16)],
        in_specs=[ANY] * (half + 5),
        out_specs=[VMEM, ANY if wide > 8 else VMEM, VMEM, VMEM],
        scratch_shapes=[DMA((2 * wide + 6,)), DMA((2 * wide + 6,)), DMA((half + 5,))],
        compiler_params=pltpu.CompilerParams(
            collective_id=collective_id, has_side_effects=True, vmem_limit_bytes=48 * 2**20
        ),
    )(*grads, array, *ups, down)


def hidden_kernel(
    half, normed_ref, grad_ref, up_ref, down_ref, hidden_ref, mid_ref, even_ref, odd_ref, branch_ref
):
    size = down_ref.shape[0]
    gate_up = dot_f32(normed_ref[...], up_ref[...])
    grad_hidden = dot_f32(grad_ref[...], down_ref[...], ((1,), (1,)))
    gate, up = gate_up[:, :size], gate_up[:, size:]
    opened = jax.nn.sigmoid(gate)
    acted = gate * opened
    hidden_ref[...] = (acted * up).astype(BF16)
    mid_ref[:, :size] = (grad_hidden * up * (opened * (1.0 + gate * (1.0 - opened)))).astype(BF16)
    mid_ref[:, size:] = (grad_hidden * acted).astype(BF16)
    grad_normed = dot_f32(mid_ref[...], up_ref[...], ((1,), (1,))).astype(BF16)
    branch_ref[...] = dot_f32(hidden_ref[...], down_ref[...]).astype(BF16)
    step = pl.program_id(0)

    @pl.when(step < half)
    def _():
        even_ref[...] = grad_normed

    @pl.when(step >= half)
    def _():
        odd_ref[...] = grad_normed


def feed_forward(normed, grad, up_full, down_full, rows):
    total, width = normed.shape
    blocks = total // rows
    half = blocks // 2
    size = down_full.shape[0]
    row_block = lambda columns: pl.BlockSpec((rows, columns), lambda i: (i, 0))
    fixed = lambda array: pl.BlockSpec(array.shape, lambda i: (0, 0))
    return pl.pallas_call(
        functools.partial(hidden_kernel, half),
        grid=(blocks,),
        in_specs=[row_block(width), row_block(width), fixed(up_full), fixed(down_full)],
        out_specs=[
            row_block(size), row_block(2 * size),
            pl.BlockSpec((rows, width), lambda i: (jnp.minimum(i, half - 1), 0)),
            pl.BlockSpec((rows, width), lambda i: (jnp.maximum(i - half, 0), 0)),
            row_block(width),
        ],
        out_shape=[
            jax.ShapeDtypeStruct((total, size), BF16),
            jax.ShapeDtypeStruct((total, 2 * size), BF16),
            jax.ShapeDtypeStruct((total // 2, width), BF16),
            jax.ShapeDtypeStruct((total // 2, width), BF16),
            jax.ShapeDtypeStruct((total, width), BF16),
        ],
        compiler_params=pltpu.CompilerParams(vmem_limit_bytes=48 * 2**20),
    )(normed, grad, up_full, down_full)


def middle_kernel(
    wide, even_ref, odd_ref, branch_ref, up_ref, down_ref, norm_sum, branch_sum, up_src, down_src,
    up_acc, down_acc, core_buf, own_buf, far_buf, branch_buf, up_join, up_one, up_mid, down_join,
    down_one, down_mid, up_own, down_own, send, recv, local,
):
    w, z = lax.axis_index("wide"), lax.axis_index("narrow")
    line = [flipped(z, k) for k in range(4)]
    half = wide // 2
    unit = up_src.shape[1]
    part = down_src.shape[1]
    sender = Sender(send, recv)
    is_middle = (z == 1) | (z == 2)
    is_end = (z == 0) | (z == 3)

    def up_share(n):
        return up_ref.at[:, pl.ds(pl.multiple_of(n * unit, unit), unit)]

    def down_share(n):
        return down_ref.at[:, pl.ds(pl.multiple_of(n * part, part), part)]

    moves = [
        (up_share(line[2]), up_src), (down_share(line[2]), down_src),
        (up_share(z), up_own), (down_share(z), down_own),
    ]
    moves += [(even_ref.at[n], own_buf.at[n]) for n in range(half)]
    pairs = branch_sum.shape[0]
    moves += [(branch_ref.at[n], branch_sum.at[n]) for n in range(pairs)]
    own = [pltpu.make_async_copy(src, dst, local.at[n]) for n, (src, dst) in enumerate(moves)]
    for copy in own:
        copy.start()
    greet(
        [wide_device(flipped(w, k)) for k in wide_steps(wide)]
        + [narrow_device(line[k]) for k in (1, 3)]
    )
    sibling = wide_device(flipped(w, 1))
    core = [sender.plan(odd_ref.at[n], core_buf.at[n], sibling) for n in range(half)]
    far = [
        sender.plan(own_buf.at[n], far_buf.at[n - 1], wide_device(flipped(w, 2 * n)))
        for n in range(1, half)
    ]
    branch_core = [
        sender.plan(branch_ref.at[pairs + n], branch_buf.at[n], sibling) for n in range(pairs)
    ]
    joins = [
        sender.plan(up_share(line[3]), up_join, narrow_device(line[1])),
        sender.plan(down_share(line[3]), down_join, narrow_device(line[1])),
    ]
    mids = [
        sender.plan(up_share(line[3]), up_mid, narrow_device(line[3])),
        sender.plan(down_share(line[3]), down_mid, narrow_device(line[3])),
    ]
    ones = [
        sender.plan(up_share(line[1]), up_one, narrow_device(line[1])),
        sender.plan(down_share(line[1]), down_one, narrow_device(line[1])),
    ]
    order = list(range(1, half)) + [0]
    for n in order:
        core[n].start()

    @pl.when(is_end)
    def _():
        for copy in joins:
            copy.start()

    @pl.when(is_middle)
    def _():
        for copy in mids:
            copy.start()

    for copy in ones:
        copy.start()
    for n in order:
        core[n].wait_recv()
        own[4 + n].wait()
        total = own_buf[n].astype(F32) + core_buf[n].astype(F32)
        own_buf[n] = total.astype(BF16)
        if n > 0:
            far[n - 1].start()
    for copy in branch_core:
        copy.start()
    for n in range(pairs):
        branch_core[n].wait_recv()
        own[4 + half + n].wait()
        total = branch_sum[n].astype(F32) + branch_buf[n].astype(F32)
        branch_sum[n] = total.astype(BF16)
    for n in range(4):
        own[n].wait()

    @pl.when(is_middle)
    def _():
        for copy in joins:
            copy.wait_recv()
        up_src[...] = (up_src[...].astype(F32) + up_join[...].astype(F32)).astype(BF16)
        down_src[...] = (down_src[...].astype(F32) + down_join[...].astype(F32)).astype(BF16)

    total = own_buf[0].astype(F32)
    for n in range(1, half):
        far[n - 1].wait_recv()
        total = total + far_buf[n - 1].astype(F32)
    norm_sum[...] = total
    for copy in ones:
        copy.wait_recv()
    up_acc[...] = up_own[...].astype(F32) + up_one[...].astype(F32)
    down_acc[...] = down_own[...].astype(F32) + down_one[...].astype(F32)

    @pl.when(is_middle)
    def _():
        for copy in mids:
            copy.wait()
        up_acc[...] += up_mid[...].astype(F32)
        down_acc[...] += down_mid[...].astype(F32)

    @pl.when(is_end)
    def _():
        for copy in joins:
            copy.wait_send()

    for copy in core + far + branch_core + ones:
        copy.wait_send()


def middle_sums(even, odd, branch, grad_up, grad_down, collective_id):
    half, rows, width = even.shape
    wide = 2 * half
    unit, part = grad_up.shape[1] // 4, grad_down.shape[1] // 4
    up_shape, down_shape = (grad_up.shape[0], unit), (grad_down.shape[0], part)
    steps = 4 * half + 6
    rows_buf = pltpu.VMEM((half, rows, width), BF16)
    pairs = branch.shape[0] // 2
    return pl.pallas_call(
        functools.partial(middle_kernel, wide),
        out_shape=[
            jax.ShapeDtypeStruct((rows, width), F32),
            jax.ShapeDtypeStruct((pairs,) + branch.shape[1:], BF16),
            jax.ShapeDtypeStruct(up_shape, BF16),
            jax.ShapeDtypeStruct(down_shape, BF16),
            jax.ShapeDtypeStruct(up_shape, F32),
            jax.ShapeDtypeStruct(down_shape, F32),
        ],
        in_specs=[ANY] * 5,
        out_specs=[VMEM] * 6,
        scratch_shapes=[
            rows_buf, rows_buf, pltpu.VMEM((half - 1, rows, width), BF16),
            pltpu.VMEM((pairs,) + branch.shape[1:], BF16),
            *[pltpu.VMEM(up_shape, BF16)] * 3, *[pltpu.VMEM(down_shape, BF16)] * 3,
            pltpu.VMEM(up_shape, BF16), pltpu.VMEM(down_shape, BF16),
            DMA((steps,)), DMA((steps,)), DMA((4 + 2 * half,)),
        ],
        compiler_params=pltpu.CompilerParams(
            collective_id=collective_id, has_side_effects=True, vmem_limit_bytes=56 * 2**20
        ),
    )(even, odd, branch, grad_up, grad_down)


def last_kernel(
    wide, rows, own_width, norm_ref, in_ref, out_ref, up_ref, norm_sum, in_got, out_sum, up_got,
    join_buf, one_buf, mid_buf, two_buf, two_src, own_norm, in_core, in_own, in_far, in_sum,
    out_core, out_own, out_far, out_low, out_buf, send, recv, local,
):
    w, z = lax.axis_index("wide"), lax.axis_index("narrow")
    line = [flipped(z, k) for k in range(4)]
    half = wide // 2
    unit = up_ref.shape[1]
    wide_rows = up_got.shape[0]
    sender = Sender(send, recv)
    is_middle = (z == 1) | (z == 2)
    is_end = (z == 0) | (z == 3)

    def norm_block(n):
        return norm_ref.at[pl.ds(pl.multiple_of(n * rows, rows), rows), :]

    def out_columns(n):
        return pl.ds(pl.multiple_of(n * own_width, LANES), own_width)

    def up_rows(n):
        return up_ref.at[pl.ds(pl.multiple_of(n * wide_rows, 16), wide_rows), :]

    def up_columns(n):
        return up_got.at[:, pl.ds(pl.multiple_of(n * unit, LANES), unit)]

    def section(n):
        return in_sum.at[:, pl.ds(pl.multiple_of(n * own_width, LANES), own_width + LANES)]

    moves = [
        (norm_block(line[2]), two_src), (norm_block(z), own_norm), (up_rows(w), up_columns(w)),
    ]
    moves += [(in_ref.at[flipped(w, 2 * n)], in_own.at[n]) for n in range(half)]
    moves += [(out_ref.at[flipped(w, 2 * n)], out_own.at[n]) for n in range(half)]
    own = [pltpu.make_async_copy(src, dst, local.at[n]) for n, (src, dst) in enumerate(moves)]
    for copy in own:
        copy.start()
    greet(
        [narrow_device(line[k]) for k in (1, 2, 3)]
        + [wide_device(flipped(w, k)) for k in range(1, wide)]
    )
    sibling = wide_device(flipped(w, 1))

    def over_wide(ref, core_buf, own_buf, far_buf):
        core = [
            sender.plan(ref.at[flipped(w, 2 * n + 1)], core_buf.at[n], sibling)
            for n in range(half)
        ]
        far = [
            sender.plan(own_buf.at[n], far_buf.at[n - 1], wide_device(flipped(w, 2 * n)))
            for n in range(1, half)
        ]
        return core, far

    joined = sender.plan(norm_block(line[3]), join_buf, narrow_device(line[1]))
    one = sender.plan(norm_block(line[1]), one_buf, narrow_device(line[1]))
    middle = sender.plan(norm_block(line[3]), mid_buf, narrow_device(line[3]))
    two = sender.plan(two_src, two_buf, narrow_device(line[2]))
    in_steps = over_wide(in_ref, in_core, in_own, in_far)
    out_steps = over_wide(out_ref, out_core, out_own, out_far)
    sections = [
        sender.plan(section(line[k]), in_got.at[z], narrow_device(line[k])) for k in (2, 3, 1)
    ]
    outs = [
        sender.plan(out_low.at[:, out_columns(line[k])], out_buf.at[k - 1], narrow_device(line[k]))
        for k in (1, 2, 3)
    ]
    ups = [
        sender.plan(up_rows(flipped(w, k)), up_columns(w), wide_device(flipped(w, k)))
        for k in range(1, wide)
    ]
    order = list(range(1, half)) + [0]
    for core in (in_steps[0], out_steps[0]):
        for n in order:
            core[n].start()

    @pl.when(is_end)
    def _():
        joined.start()

    def between_cores(steps, core_buf, own_buf, first):
        core, far = steps
        for n in order:
            core[n].wait_recv()
            own[first + n].wait()
            total = own_buf[n].astype(F32) + core_buf[n].astype(F32)
            own_buf[n] = total.astype(BF16)
            if n > 0:
                far[n - 1].start()

    def between_chips(steps, own_buf, far_buf):
        total = own_buf[0].astype(F32)
        for n in range(1, half):
            steps[1][n - 1].wait_recv()
            total = total + far_buf[n - 1].astype(F32)
        return total.astype(BF16)

    between_cores(in_steps, in_core, in_own, 3)
    own[0].wait()

    @pl.when(is_middle)
    def _():
        joined.wait_recv()
        two_src[...] = (two_src[...].astype(F32) + join_buf[...].astype(F32)).astype(BF16)
        middle.start()

    two.start()
    one.start()
    between_cores(out_steps, out_core, out_own, 3 + half)
    in_sum[...] = between_chips(in_steps, in_own, in_far)
    mine = pltpu.make_async_copy(section(z), in_got.at[z], local.at[3 + 2 * half])
    mine.start()
    for copy in sections:
        copy.start()
    out_low[...] = between_chips(out_steps, out_own, out_far)
    for copy in outs + ups:
        copy.start()
    own[1].wait()
    own[2].wait()
    one.wait_recv()
    norm_sum[...] = own_norm[...].astype(F32) + one_buf[...].astype(F32)

    @pl.when(is_middle)
    def _():
        middle.wait()
        norm_sum[...] += mid_buf[...].astype(F32)

    two.wait_recv()
    norm_sum[...] += two_buf[...].astype(F32)
    total = out_low[:, out_columns(z)].astype(F32)
    for n in range(3):
        outs[n].wait_recv()
        total = total + out_buf[n].astype(F32)
    out_sum[...] = total
    for copy in sections + ups:
        copy.wait_recv()
    mine.wait()

    @pl.when(is_end)
    def _():
        joined.wait_send()

    sent = [one, two] + in_steps[0] + in_steps[1] + out_steps[0] + out_steps[1]
    for copy in sent + sections + outs + ups:
        copy.wait_send()


def last_transfers(norm_part, in_part, out_part, up_part, rows, own_width, collective_id):
    wide, wide_rows, columns = in_part.shape
    half = wide // 2
    width = norm_part.shape[1]
    unit = up_part.shape[1]
    steps = 4 + 4 * half + 6 + wide
    block = pltpu.VMEM((rows, width), BF16)
    sums = lambda size: [
        pltpu.VMEM((half, wide_rows, size), BF16), pltpu.VMEM((half, wide_rows, size), BF16),
        pltpu.VMEM((half - 1, wide_rows, size), BF16), pltpu.VMEM((wide_rows, size), BF16),
    ]
    return pl.pallas_call(
        functools.partial(last_kernel, wide, rows, own_width),
        out_shape=[
            jax.ShapeDtypeStruct((rows, width), F32),
            jax.ShapeDtypeStruct((4, wide_rows, own_width + LANES), BF16),
            jax.ShapeDtypeStruct((wide_rows, own_width), F32),
            jax.ShapeDtypeStruct((wide_rows, wide * unit), BF16),
        ],
        in_specs=[ANY] * 4,
        out_specs=[VMEM] * 4,
        scratch_shapes=[
            *[block] * 6, *sums(columns), *sums(width),
            pltpu.VMEM((3, wide_rows, own_width), BF16),
            DMA((steps,)), DMA((steps,)), DMA((4 + 2 * half,)),
        ],
        compiler_params=pltpu.CompilerParams(
            collective_id=collective_id, has_side_effects=True, vmem_limit_bytes=48 * 2**20
        ),
    )(norm_part, in_part, out_part, up_part)


def total_kernel(wide, v_ref, out_ref, narrow_buf, wide_buf, sum_buf, send, recv):
    w, z = lax.axis_index("wide"), lax.axis_index("narrow")
    greet(
        [narrow_device(flipped(z, k)) for k in (1, 2, 3)]
        + [wide_device(flipped(w, k)) for k in range(1, wide)]
    )
    sender = Sender(send, recv)
    first = [
        sender.plan(v_ref, narrow_buf.at[z], narrow_device(flipped(z, k))) for k in (1, 2, 3)
    ]
    second = [
        sender.plan(sum_buf, wide_buf.at[w], wide_device(flipped(w, k))) for k in range(1, wide)
    ]
    for copy in first:
        copy.start()
    narrow_buf[z] = v_ref[...]
    for copy in first:
        copy.wait()
    sum_buf[...] = narrow_buf[0] + narrow_buf[1] + narrow_buf[2] + narrow_buf[3]
    for copy in second:
        copy.start()
    wide_buf[w] = sum_buf[...]
    for copy in second:
        copy.wait()
    total = wide_buf[0]
    for n in range(1, wide):
        total = total + wide_buf[n]
    out_ref[...] = total


def total_of(values, wide, collective_id):
    size = values.shape[0]
    height = -(-size // (8 * LANES)) * 8
    padded = jnp.pad(values, (0, height * LANES - size)).reshape(height, LANES)
    total = pl.pallas_call(
        functools.partial(total_kernel, wide),
        out_shape=jax.ShapeDtypeStruct(padded.shape, F32),
        in_specs=[VMEM],
        out_specs=VMEM,
        scratch_shapes=[
            pltpu.VMEM((4,) + padded.shape, F32),
            pltpu.VMEM((wide,) + padded.shape, F32),
            pltpu.VMEM(padded.shape, F32),
            DMA((wide + 2,)), DMA((wide + 2,)),
        ],
        compiler_params=pltpu.CompilerParams(collective_id=collective_id, has_side_effects=True),
    )(padded)
    return total.reshape(-1)[:size]


def rms_factor(values):
    return lax.rsqrt(jnp.mean(values * values, axis=-1, keepdims=True) + EPSILON)


def rms_back(values, gain, grad):
    factor = rms_factor(values)
    normed = values * factor
    grad_gain = jnp.sum(grad * normed, axis=0)
    scaled = grad * gain
    inner = jnp.mean(scaled * normed, axis=-1, keepdims=True)
    return (factor * (scaled - normed * inner), grad_gain)


def log_sigmoid(v):
    return jnp.minimum(v, 0.0) - jnp.log1p(jnp.exp(-jnp.abs(v)))


def iota(shape, dim):
    return lax.broadcasted_iota(jnp.int32, shape, dim)


def running_sum(v, reverse):
    rows = v.shape[0]
    index = iota(v.shape, 0)
    step = 1
    while step < rows:
        if reverse:
            v = v + jnp.where(index < rows - step, pltpu.roll(v, rows - step, 0), 0.0)
        else:
            v = v + jnp.where(index >= step, pltpu.roll(v, step, 0), 0.0)
        step *= 2
    return v


def half_of(lane, head_size):
    return (lane >= head_size).astype(jnp.int32)


def spread(first, head_size):
    row, lane = iota((LANES, LANES), 0), iota((LANES, LANES), 1)
    return row == first + half_of(lane, head_size)


def collect(first, head_size):
    row, lane = iota((LANES, LANES), 0), iota((LANES, LANES), 1)
    return lane == first + half_of(row, head_size)


def same_head(head_size):
    row, lane = iota((LANES, LANES), 0), iota((LANES, LANES), 1)
    return (half_of(row, head_size) == half_of(lane, head_size)).astype(F32)


def exact_dot(left, right):
    return lax.dot_general(
        left, right, (((1,), (0,)), ((), ())), precision=EXACT, preferred_element_type=F32
    )


def head_mean(v, head_size):
    return exact_dot(v, same_head(head_size)) * (1.0 / head_size)


def prologue(pair, heads, head_size, q_ref, k_ref, v_ref, small_low, cont):
    spot = lambda group: spread(group * heads + 2 * pair, head_size).astype(BF16)
    key_mix = jax.nn.sigmoid(dot_f32(small_low, spot(1)))
    value_mix = jax.nn.sigmoid(dot_f32(small_low, spot(2)))
    queries = q_ref[...].astype(BF16).astype(F32)
    keys = k_ref[...].astype(BF16).astype(F32)
    values = v_ref[...].astype(BF16).astype(F32)
    key_step = pltpu.roll(keys, 1, 0) * cont - keys
    value_step = pltpu.roll(values, 1, 0) * cont - values
    shifted = keys + key_mix * key_step
    value_low = (values + value_mix * value_step).astype(BF16)
    query_factor = lax.rsqrt(head_mean(queries * queries, head_size) + EPSILON)
    key_factor = lax.rsqrt(head_mean(shifted * shifted, head_size) + EPSILON)
    return (
        queries * query_factor,
        shifted * key_factor,
        value_low,
        query_factor,
        key_factor,
        key_mix,
        value_mix,
        key_step,
        value_step,
    )


def small_columns(small_ref, bias_ref):
    return (small_ref[...] + bias_ref[0:1, :]).astype(BF16)


def decay_of(small_low, cont):
    return running_sum(log_sigmoid(small_low.astype(F32)) - SEPARATE * (1.0 - cont), False)


def forward_kernel(
    heads, head_size, block, q_ref, k_ref, v_ref, gate_ref, small_ref, bias_ref, cont_ref,
    mixed_ref, att_ref, log_ref, decay_scr,
):
    pair = pl.program_id(0)
    cont = cont_ref[...]
    small_low = small_columns(small_ref, bias_ref)

    @pl.when(pair == 0)
    def _():
        decay_scr[...] = decay_of(small_low, cont)

    query, key, value_low, *unused = prologue(
        pair, heads, head_size, q_ref, k_ref, v_ref, small_low, cont
    )
    rows = query.shape[0]
    query = query.astype(BF16) * BF16(head_size**-0.5)
    key = key.astype(BF16)
    decay = exact_dot(decay_scr[...], spread(2 * pair, head_size).astype(F32))
    decay_rows = decay.T
    lane = iota((1, LANES), 1)
    ones = jnp.ones((rows, LANES), BF16)
    value_wide = jnp.concatenate([value_low, ones], axis=1)
    for i in range(rows // block):
        lo, hi = i * block, (i + 1) * block
        row_index = iota((block, hi), 0) + lo
        visible = iota((block, hi), 1) <= row_index
        outs, sums = [], []
        for head in range(2):
            mine = (lane >= head_size) if head else (lane < head_size)
            at = head * head_size
            left = jnp.where(mine, query[lo:hi], BF16(0.0))
            scores = dot_f32(left, key[:hi], ((1,), (1,)))
            scores = scores + decay[lo:hi, at : at + 1] - decay_rows[at : at + 1, :hi]
            weights = jnp.where(visible, jnp.exp(scores), 0.0).astype(BF16)
            both = dot_f32(weights, value_wide[:hi])
            outs.append(both[:, :LANES])
            sums.append(both[:, LANES:])
        first = lane < head_size
        total = jnp.where(first, sums[0], sums[1])
        attended = (jnp.where(first, outs[0], outs[1]) / total).astype(BF16)
        att_ref[lo:hi, :] = attended
        log_ref[lo:hi, :] = jnp.log(total)
        opened = jax.nn.sigmoid(gate_ref[lo:hi, :])
        mixed_ref[lo:hi, :] = (attended.astype(F32) * opened).astype(BF16)


def backward_kernel(
    heads, head_size, block, q_ref, k_ref, v_ref, gate_ref, small_ref, bias_ref, cont_ref,
    att_ref, log_ref, grad_ref, out_ref, bias_grad_ref, decay_scr, small_scr, dq_scr,
):
    pair = pl.program_id(0)
    cont = cont_ref[...]
    small_low = small_columns(small_ref, bias_ref)
    rows = cont.shape[0]
    width = heads * head_size

    @pl.when(pair == 0)
    def _():
        decay_scr[...] = decay_of(small_low, cont)
        small_scr[...] = jnp.zeros_like(small_scr)

    (
        query_norm, key_norm, value_low, query_factor, key_factor, key_mix, value_mix, key_step,
        value_step,
    ) = prologue(pair, heads, head_size, q_ref, k_ref, v_ref, small_low, cont)
    query = query_norm.astype(BF16) * BF16(head_size**-0.5)
    key = key_norm.astype(BF16)
    opened = jax.nn.sigmoid(gate_ref[...])
    attended = att_ref[...].astype(F32)
    grad_mixed = grad_ref[...].astype(F32)
    grad_low = (grad_mixed * opened).astype(BF16)
    grad_gate = grad_mixed * attended * opened * (1.0 - opened)

    def columns(group):
        at = group * width + pair * LANES
        return pl.ds(pl.multiple_of(at, LANES), LANES)

    out_ref[:, columns(3)] = grad_gate.astype(BF16)
    inner = exact_dot(grad_low.astype(F32) * attended, same_head(head_size))
    decay = exact_dot(decay_scr[...], spread(2 * pair, head_size).astype(F32))
    level_rows = (decay - log_ref[...]).T
    inner_rows = inner.T
    lane = iota((1, LANES), 1)
    ones = jnp.ones((rows, LANES), BF16)
    query_wide = jnp.concatenate([query, ones], axis=1)
    key_wide = jnp.concatenate([key, ones], axis=1)
    key_parts, value_parts, query_parts = [], [], []
    for head in range(2):
        mine = (lane >= head_size) if head else (lane < head_size)
        at = head * head_size
        keys_out, values_out = [], []
        for j in range(rows // block):
            lo, hi = j * block, (j + 1) * block
            span = rows - lo
            visible = iota((block, span), 0) <= iota((block, span), 1)
            scores = dot_f32(
                jnp.where(mine, key[lo:hi], BF16(0.0)), query[lo:], ((1,), (1,))
            )
            scores = scores + level_rows[at : at + 1, lo:] - decay[lo:hi, at : at + 1]
            probs = jnp.where(visible, jnp.exp(scores), 0.0)
            grad_probs = dot_f32(
                jnp.where(mine, value_low[lo:hi], BF16(0.0)), grad_low[lo:], ((1,), (1,))
            )
            grad_scores = (probs * (grad_probs - inner_rows[at : at + 1, lo:])).astype(BF16)
            values_out.append(dot_f32(probs.astype(BF16), grad_low[lo:]))
            keys_out.append(dot_f32(grad_scores, query_wide[lo:]))
            part = dot_f32(grad_scores, key_wide[lo:hi], ((0,), (0,)))
            if j == 0:
                dq_scr[...] = part
            else:
                dq_scr[lo:, :] += part
        key_parts.append(jnp.concatenate(keys_out, axis=0))
        value_parts.append(jnp.concatenate(values_out, axis=0))
        query_parts.append(dq_scr[...])
    first = lane < head_size

    def join(parts):
        return jnp.where(first, parts[0], parts[1])

    grad_query = join([p[:, :LANES] for p in query_parts]) * head_size**-0.5
    grad_key = join([p[:, :LANES] for p in key_parts])
    grad_value = join(value_parts)
    grad_decay = join([p[:, LANES:] for p in query_parts]) - join([p[:, LANES:] for p in key_parts])

    def norm_back(grad, normed, factor):
        return factor * (grad - normed * head_mean(grad * normed, head_size))

    def shift_back(grad, mix):
        return grad * (1.0 - mix) + pltpu.roll(grad * mix * cont, rows - 1, 0)

    grad_query = norm_back(grad_query, query_norm, query_factor)
    grad_shifted = norm_back(grad_key, key_norm, key_factor)
    out_ref[:, columns(0)] = grad_query.astype(BF16)
    out_ref[:, columns(1)] = shift_back(grad_shifted, key_mix).astype(BF16)
    out_ref[:, columns(2)] = shift_back(grad_value, value_mix).astype(BF16)
    key_logit = grad_shifted * key_step * key_mix * (1.0 - key_mix)
    value_logit = grad_value * value_step * value_mix * (1.0 - value_mix)
    single = (lax.rem(lane, head_size) == 0).astype(F32)
    small_scr[...] += (
        exact_dot(grad_decay * single, collect(2 * pair, head_size).astype(F32))
        + exact_dot(key_logit, collect(heads + 2 * pair, head_size).astype(F32))
        + exact_dot(value_logit, collect(2 * heads + 2 * pair, head_size).astype(F32))
    )

    @pl.when(pair == pl.num_programs(0) - 1)
    def _():
        grads = small_scr[...]
        forget = running_sum(grads, True) * jax.nn.sigmoid(-small_low.astype(F32))
        result = jnp.where(lane < heads, forget, grads)
        out_ref[:, 4 * width :] = result.astype(BF16)
        bias_grad_ref[...] = jnp.broadcast_to(
            jnp.sum(result, axis=0, keepdims=True), bias_grad_ref.shape
        )


def attention_specs(rows, pairs):
    def block_at(group):
        return pl.BlockSpec((rows, LANES), lambda p: (0, group * pairs + p))

    def fixed(height, column=0):
        return pl.BlockSpec((height, LANES), lambda p: (0, column))

    base = [block_at(0), block_at(1), block_at(2), block_at(3), fixed(rows, 4 * pairs), fixed(8), fixed(rows)]
    return base, pl.BlockSpec((rows, LANES), lambda p: (0, p))


def attention_forward(projected, bias, cont, heads, head_size, block):
    rows = projected.shape[0]
    pairs = heads * head_size // LANES
    base, own = attention_specs(rows, pairs)
    wide = jax.ShapeDtypeStruct((rows, heads * head_size), BF16)
    return pl.pallas_call(
        functools.partial(forward_kernel, heads, head_size, block),
        grid=(pairs,),
        in_specs=base,
        out_specs=[own] * 3,
        out_shape=[wide, wide, jax.ShapeDtypeStruct(wide.shape, F32)],
        scratch_shapes=[pltpu.VMEM((rows, LANES), F32)],
        compiler_params=pltpu.CompilerParams(vmem_limit_bytes=48 * 2**20),
    )(*([projected] * 5), bias, cont)


def attention_backward(projected, bias, cont, attended, logs, grad, heads, head_size, block):
    rows = projected.shape[0]
    pairs = heads * head_size // LANES
    base, own = attention_specs(rows, pairs)
    columns = 4 * heads * head_size + LANES
    return pl.pallas_call(
        functools.partial(backward_kernel, heads, head_size, block),
        grid=(pairs,),
        in_specs=base + [own] * 3,
        out_specs=[
            pl.BlockSpec((rows, columns), lambda p: (0, 0)),
            pl.BlockSpec((8, LANES), lambda p: (0, 0)),
        ],
        out_shape=[
            jax.ShapeDtypeStruct((rows, columns), BF16),
            jax.ShapeDtypeStruct((8, LANES), F32),
        ],
        scratch_shapes=[
            pltpu.VMEM((rows, LANES), F32),
            pltpu.VMEM((rows, LANES), F32),
            pltpu.VMEM((rows, 2 * LANES), F32),
        ],
        compiler_params=pltpu.CompilerParams(vmem_limit_bytes=56 * 2**20),
    )(*([projected] * 5), bias, cont, attended, logs, grad)


def add_up(parts):
    total = parts[0].astype(F32)
    for part in parts[1:]:
        total = total + part.astype(F32)
    return total


def on_device(
    tokens, gain_one, in_weight, forget_bias, out_weight, gain_two, gate_up_weight, down_weight,
    segment_ids, cotangent,
):
    wide, narrow = lax.axis_size("wide"), lax.axis_size("narrow")
    w, z = lax.axis_index("wide"), lax.axis_index("narrow")
    rows, width = tokens.shape
    slot = rows * narrow
    heads = forget_bias.shape[0]
    head_size = width // heads
    own_heads = heads // narrow
    own_width = own_heads * head_size
    part_rows = in_weight.shape[0]
    hidden_all = down_weight.shape[0] * wide * narrow
    unit = hidden_all // (2 * wide)
    columns = 4 * own_width + LANES
    base = 4 * width

    small = in_weight[:, base:].reshape(part_rows, 3, narrow, own_heads)
    small = jnp.moveaxis(small, 2, 0).reshape(narrow, part_rows, 3 * own_heads)
    small = jnp.pad(small, ((0, 0), (0, 0), (0, LANES - 3 * own_heads)))
    aligned = unit % LANES == 0

    def split_weights(sources, targets):
        copies = [(sources[1], targets[0].at[:, :, pl.ds(4 * own_width, LANES)])]
        for n in range(narrow):
            for group in range(4):
                copies.append(
                    (
                        sources[0].at[:, pl.ds(group * width + n * own_width, own_width)],
                        targets[0].at[n, :, pl.ds(group * own_width, own_width)],
                    )
                )
        if aligned:
            for n in range(wide):
                for group in range(4):
                    copies.append(
                        (
                            sources[2].at[:, pl.ds((group * wide + n) * unit, unit)],
                            targets[1].at[n, :, pl.ds(group * unit, unit)],
                        )
                    )
        return copies

    shapes = [
        jax.ShapeDtypeStruct((narrow, part_rows, columns), BF16),
        jax.ShapeDtypeStruct((wide, part_rows, 4 * unit), BF16),
    ]
    copies = 4 * narrow + 1
    if aligned:
        in_parts, up_parts = local_copies(
            split_weights, copies + 4 * wide, [in_weight, small, gate_up_weight], shapes, False
        )
    else:
        in_parts = local_copies(split_weights, copies, [in_weight, small], shapes[:1], False)[0]
        up_parts = jnp.moveaxis(gate_up_weight.reshape(part_rows, 4, wide, unit), 2, 0)
        up_parts = up_parts.reshape(wide, part_rows, 4 * unit)

    grads = [cotangent] + [along_wide(cotangent, k, wide) for k in range(2, wide, 2)]
    down_rows = down_weight.shape[0]
    pairs = []
    for i in range(wide * narrow):
        to_wide = (i % (2 * wide)) // 2
        to_narrow = i % 2 + 2 * (i // (2 * wide))
        pairs.append((i, to_wide * narrow + to_narrow))
    down_block = lax.ppermute(down_weight, ("wide", "narrow"), pairs)

    slot_tokens, in_full, out_full, up_block = gather_all(tokens, in_parts, out_weight, up_parts)
    slot_tokens = slot_tokens.reshape(slot, width)
    in_full = in_full.reshape(width, columns)
    out_full = out_full.reshape(width, width)
    grads = [cotangent] + [follow(piece, slot_tokens) for piece in grads[1:]]

    up_two = on_line(up_block, LINE_TWO)
    up_one = on_line(up_block, LINE_ONE)

    slot_floats = slot_tokens.astype(F32)
    normed_one = (slot_floats * rms_factor(slot_floats) * gain_one).astype(BF16)
    projected = dot_f32(normed_one, in_full)

    segments = segment_ids[0]
    joined = (segments[1:] == segments[:-1]).astype(F32)
    cont = jnp.concatenate([jnp.zeros((1,), F32), joined])
    cont = jnp.broadcast_to(cont[:, None], (slot, LANES))
    own_bias = lax.dynamic_slice_in_dim(forget_bias, z * own_heads, own_heads)
    bias = jnp.broadcast_to(jnp.pad(own_bias, (0, LANES - own_heads))[None], (8, LANES))
    block = min(256, slot)
    mixed, attended, logs = attention_forward(
        projected, bias, cont, own_heads, head_size, block
    )

    def row_block(ref, n):
        return ref.at[pl.ds(pl.multiple_of(n * rows, rows), rows), :]

    def column_block(ref, n):
        return ref.at[:, pl.ds(pl.multiple_of(n * own_width, LANES), own_width)]

    mixed_rows = exchange(mixed, row_block, column_block, (rows, width), 1)
    inputs = tokens.astype(F32)
    middle = inputs + dot_f32(mixed_rows, out_full)
    normed_two = (middle * rms_factor(middle) * gain_two).astype(BF16)

    half = wide // 2
    ups = [up_block] + [follow(piece, normed_two) for piece in (up_two, up_one)]
    plane_normed, plane_grad, up_full, down_full = gather_rows(
        normed_two, grads, ups, follow(down_block, normed_two), 2
    )
    plane_normed = plane_normed.reshape(wide * rows, width)
    plane_grad = plane_grad.reshape(wide * rows, width)
    up_full = up_full.reshape(width, 4 * unit)
    down_full = down_full.reshape(2 * unit, width)
    hidden, gate_up_grad, norm_even, norm_odd, branch = feed_forward(
        plane_normed, plane_grad, up_full, down_full, rows
    )
    grad_up_full = dot_f32(plane_normed, gate_up_grad, ((0,), (0,))).astype(BF16)
    grad_down_full = dot_f32(hidden, plane_grad, ((0,), (0,))).astype(BF16)
    if unit % LANES:
        grouped = grad_up_full.reshape(width, 4, unit)
        grad_up_full = jnp.pad(grouped, ((0, 0), (0, 0), (0, LANES - unit))).reshape(width, -1)
    branch = branch.reshape(wide, rows, width)
    fits = wide <= 8
    grad_normed_two, branch_sum, up_src, down_src, up_acc, down_acc = middle_sums(
        norm_even.reshape(half, rows, width), norm_odd.reshape(half, rows, width),
        branch if fits else branch[:2, :16], grad_up_full, grad_down_full, 6,
    )
    if not fits:
        received = along_wide(branch[half:], 1, wide)
        branch_sum = (branch[:half].astype(F32) + received.astype(F32)).astype(BF16)
    branch_parts = [branch_sum[0]] + [
        along_wide(branch_sum[n], 2 * n, wide) for n in range(1, half)
    ]
    upstream = cotangent.astype(F32)
    grad_middle_norm, grad_gain_two = rms_back(middle, gain_two, grad_normed_two)
    grad_middle = upstream + grad_middle_norm
    branch_one_grad = grad_middle.astype(BF16)
    grad_mixed = dot_f32(branch_one_grad, out_full, ((1,), (1,))).astype(BF16)
    slot_grad = exchange(grad_mixed, column_block, row_block, (slot, own_width), 3)
    up_two = on_line(follow(up_src, slot_grad), LINE_TWO)
    down_two = on_line(follow(down_src, slot_grad), LINE_TWO)

    projected_grad, bias_grad = attention_backward(
        projected, bias, cont, attended, logs, slot_grad, own_heads, head_size, block
    )
    norm_part = dot_f32(projected_grad, in_full, ((1,), (1,))).astype(BF16)
    in_part = dot_f32(normed_one, projected_grad, ((0,), (0,))).astype(BF16)

    wide_rows = width // wide
    out_part = dot_f32(mixed_rows, branch_one_grad, ((0,), (0,))).astype(BF16)
    branch_parts = [follow(part, in_part, norm_part) for part in branch_parts]
    output = (middle + add_up(branch_parts)).astype(BF16)
    up_part = (up_acc + follow(up_two, in_part, norm_part).astype(F32)).astype(BF16)
    grad_down = (down_acc + follow(down_two, in_part, norm_part).astype(F32)).astype(BF16)
    low_half, high_half = grad_down[:unit], grad_down[unit:]
    is_odd = lax.rem(w, 2) == 1
    first_send = jnp.where(is_odd, high_half, low_half)
    second_send = jnp.where(is_odd, low_half, high_half)
    first_got = lax.ppermute(
        first_send, "wide", [(i, i // 2 + (half if i % 2 else 0)) for i in range(wide)]
    )
    second_got = lax.ppermute(
        second_send, "wide", [(i, i // 2 + (0 if i % 2 else half)) for i in range(wide)]
    )
    norm_sum, got, grad_out, grad_up = last_transfers(
        norm_part, in_part.reshape(wide, wide_rows, columns),
        out_part.reshape(wide, wide_rows, width), up_part, rows, own_width, 4,
    )
    if not aligned:
        grad_up = grad_up.reshape(wide_rows, wide, LANES)[:, :, :unit]
        grad_up = grad_up.reshape(wide_rows, wide * unit)
    first_got, second_got = follow(first_got, norm_sum), follow(second_got, norm_sum)
    grad_up = grad_up.astype(F32)
    grad_inputs, grad_gain_one = rms_back(inputs, gain_one, norm_sum)
    grad_tokens = grad_middle + grad_inputs
    in_low = w < half
    grad_down = jnp.concatenate(
        [
            jnp.where(in_low, first_got, second_got),
            jnp.where(in_low, second_got, first_got),
        ],
        axis=0,
    ).astype(F32)

    extra = 3 * heads
    section = jnp.concatenate([got[n, :, :own_width] for n in range(narrow)], axis=1)
    small_all = jnp.stack([got[n, :, own_width : own_width + 3 * own_heads] for n in range(narrow)])
    small_all = small_all.reshape(narrow, wide_rows, 3, own_heads)
    small_all = jnp.transpose(small_all, (1, 2, 0, 3)).reshape(wide_rows, extra)
    next_first = got[0, :, own_width : own_width + extra]
    tail = jnp.where(z == narrow - 1, small_all, next_first)
    joined_columns = jnp.concatenate([section, tail], axis=1)
    shard = (base + extra) // narrow
    grad_in = lax.dynamic_slice_in_dim(joined_columns, z * (shard - width), shard, 1).astype(F32)

    all_bias = lax.dynamic_update_slice(
        jnp.zeros((heads,), F32), bias_grad[0, :own_heads], (z * own_heads,)
    )
    packed = jnp.concatenate([grad_gain_one, grad_gain_two, all_bias])
    packed = total_of(packed, wide, 5)
    return (
        output,
        grad_tokens,
        packed[:width],
        grad_in,
        packed[2 * width :],
        grad_out,
        packed[width : 2 * width],
        grad_up,
        grad_down,
    )


def solution(mesh):
    both = ("wide", "narrow")
    in_specs = (
        P(both, None), P(), P(both, None), P(), P(both, None), P(), P(both, None), P(both, None),
        P("wide", None), P(both, None),
    )
    out_specs = (
        P(both, None), P(both, None), P(), P("wide", "narrow"), P(), P("wide", "narrow"), P(),
        P("wide", "narrow"), P("wide", "narrow"),
    )
    return jax.shard_map(
        on_device, mesh=mesh, in_specs=in_specs, out_specs=out_specs, check_vma=False
    )
```

```python
import functools

import jax
import jax.numpy as jnp
from jax import lax
from jax.experimental import pallas as pl
from jax.experimental.pallas import tpu as pltpu
from jax.sharding import PartitionSpec as P

EPSILON = 1e-06
SEPARATE = 128.0
F32 = jnp.float32
BF16 = jnp.bfloat16
LANES = 128
EXACT = lax.Precision.HIGHEST
ANY = pl.BlockSpec(memory_space=pl.ANY)


def dot_f32(left, right, dims=((1,), (0,))):
    return lax.dot_general(left, right, (dims, ((), ())), preferred_element_type=F32)


def along_wide(block, flip, wide):
    return lax.ppermute(block, "wide", [(i, i ^ flip) for i in range(wide)])


def copy_kernel(plan, count, *refs):
    sources, targets, sems = refs[:count], refs[count:-1], refs[-1]
    copies = plan(sources, targets)

    def each(act):
        for n, (src, dst, *when) in enumerate(copies):
            copy = pltpu.make_async_copy(src, dst, sems.at[n])
            if when:
                pl.when(when[0])(functools.partial(act, copy))
            else:
                act(copy)

    each(lambda copy: copy.start())
    each(lambda copy: copy.wait())


def local_copies(plan, copies, sources, shapes, gather):
    moved = sum(s.size * s.dtype.itemsize for s in shapes)
    inside = pl.BlockSpec(memory_space=pltpu.VMEM)
    return pl.pallas_call(
        functools.partial(copy_kernel, plan, len(sources)),
        out_shape=shapes,
        in_specs=[ANY if gather else inside] * len(sources),
        out_specs=[inside if gather else ANY] * len(shapes),
        compiler_params=pltpu.CompilerParams(vmem_limit_bytes=16 * 2**20),
        scratch_shapes=[pltpu.SemaphoreType.DMA((copies,))],
        cost_estimate=pl.CostEstimate(flops=0, bytes_accessed=2 * moved, transcendentals=0),
    )(*sources)


def flipped(me, k):
    out = me
    bit = 1
    while bit <= k:
        if k & bit:
            out = out + bit - 2 * bit * lax.rem(lax.div(out, bit), 2)
        bit *= 2
    return out


LINE_TWO = [(0, 2), (2, 0), (1, 3), (3, 1)]
LINE_ONE = [(0, 1), (1, 0), (2, 3), (3, 2)]
LINE_MIDDLE = [(1, 2), (2, 1)]
LINE_OUT = [(2, 3), (1, 0)]
LINE_IN = [(0, 1), (3, 2)]


def on_line(block, pairs):
    return lax.ppermute(block, "narrow", pairs)


def follow(array, *earlier):
    return lax.optimization_barrier((array, *earlier))[0]


MESH = pl.DeviceIdType.MESH
VMEM = pl.BlockSpec(memory_space=pltpu.VMEM)
DMA = pltpu.SemaphoreType.DMA


def greet(devices):
    barrier = pltpu.get_barrier_semaphore()
    for device in devices:
        pl.semaphore_signal(barrier, inc=1, device_id=device, device_id_type=MESH)
    pl.semaphore_wait(barrier, len(devices))


class Sender:
    def __init__(self, send, recv):
        self.send, self.recv, self.used = send, recv, 0

    def plan(self, src, dst, device):
        n = self.used
        self.used += 1
        return pltpu.make_async_remote_copy(
            src_ref=src, dst_ref=dst, send_sem=self.send.at[n], recv_sem=self.recv.at[n],
            device_id=device, device_id_type=MESH,
        )


def narrow_device(n):
    return {"narrow": n}


def wide_device(n):
    return {"wide": n}


def wide_steps(wide):
    return [1] + list(range(2, wide, 2))


def straight_steps(wide):
    return [k for k in range(2, wide, 2) if k & (k - 1) == 0]


def diagonal_steps(wide):
    return [k for k in range(2, wide, 2) if k & (k - 1)]


def by_device(ref, w):
    return (lambda k: ref.at[flipped(w, k)]), (lambda k, to: ref.at[flipped(w, k)])


class WideGather:
    def __init__(self, sender, w, wide, part, target):
        self.far = list(range(2, wide, 2))
        self.first = {
            k: sender.plan(part(0), target(0, k), wide_device(flipped(w, k)))
            for k in wide_steps(wide)
        }
        sibling = wide_device(flipped(w, 1))
        self.second = {k: sender.plan(part(k), target(k, 1), sibling) for k in self.far}

    def start(self):
        for k in self.far + [1]:
            self.first[k].start()

    def pass_on(self):
        for k in self.far:
            self.first[k].wait_recv()
            self.second[k].start()

    def finish(self):
        self.first[1].wait_recv()
        for k in self.far:
            self.second[k].wait_recv()
        for copy in list(self.first.values()) + list(self.second.values()):
            copy.wait_send()


def gather_kernel(
    wide, x_ref, in_ref, out_ref, up_ref, grad_ref, slot_ref, in_full, out_full, up_block, grad_far,
    send, recv, local,
):
    w, z = lax.axis_index("wide"), lax.axis_index("narrow")
    line = [flipped(z, k) for k in range(4)]
    sender = Sender(send, recv)
    own = [
        pltpu.make_async_copy(in_ref.at[z], in_full.at[w, z], local.at[0]),
        pltpu.make_async_copy(out_ref, out_full.at[w, z], local.at[1]),
        pltpu.make_async_copy(x_ref, slot_ref.at[z], local.at[2]),
        pltpu.make_async_copy(up_ref.at[w], up_block.at[w], local.at[3]),
    ]
    for copy in own:
        copy.start()
    greet(
        [narrow_device(line[k]) for k in (1, 2, 3)]
        + [wide_device(flipped(w, k)) for k in range(1, wide)]
    )
    ups = [
        sender.plan(up_ref.at[flipped(w, k)], up_block.at[w], wide_device(flipped(w, k)))
        for k in range(1, wide)
    ]
    grads = [
        sender.plan(grad_ref, grad_far.at[n], wide_device(flipped(w, k)))
        for n, k in enumerate(diagonal_steps(wide))
    ]
    is_middle = (z == 1) | (z == 2)
    is_end = (z == 0) | (z == 3)
    ins = [
        sender.plan(in_ref.at[line[k]], in_full.at[w, z], narrow_device(line[k])) for k in (2, 3, 1)
    ]
    outs = [sender.plan(out_ref, out_full.at[w, z], narrow_device(line[k])) for k in (2, 3, 1)]
    two = sender.plan(x_ref, slot_ref.at[z], narrow_device(line[2]))
    one = sender.plan(x_ref, slot_ref.at[z], narrow_device(line[1]))
    middle = sender.plan(x_ref, slot_ref.at[z], narrow_device(line[3]))
    relay = sender.plan(slot_ref.at[line[2]], slot_ref.at[line[2]], narrow_device(line[1]))
    in_wide = WideGather(sender, w, wide, *by_device(in_full, w))
    out_wide = WideGather(sender, w, wide, *by_device(out_full, w))
    for copy in ins + outs + ups:
        copy.start()
    own[0].wait()
    for copy in ins:
        copy.wait_recv()
    in_wide.start()
    two.start()
    one.start()
    own[1].wait()
    for copy in outs:
        copy.wait_recv()
    out_wide.start()
    in_wide.pass_on()
    for copy in grads:
        copy.start()
    two.wait_recv()

    @pl.when(is_middle)
    def _():
        relay.start()
        middle.start()

    out_wide.pass_on()
    one.wait_recv()
    own[2].wait()
    own[3].wait()
    for copy in ups + grads:
        copy.wait()

    @pl.when(is_middle)
    def _():
        middle.wait_recv()
        middle.wait_send()
        relay.wait_send()

    @pl.when(is_end)
    def _():
        relay.wait_recv()

    for copy in ins + outs + [two, one]:
        copy.wait_send()
    in_wide.finish()
    out_wide.finish()


def gather_all(tokens, in_parts, out_weight, up_parts, cotangent):
    narrow, wide = in_parts.shape[0], up_parts.shape[0]
    steps = 10 + 4 * wide
    shapes = [
        (narrow,) + tokens.shape, (wide,) + in_parts.shape, (wide, narrow) + out_weight.shape,
        up_parts.shape, (len(diagonal_steps(wide)),) + cotangent.shape,
    ]
    return pl.pallas_call(
        functools.partial(gather_kernel, wide),
        out_shape=[jax.ShapeDtypeStruct(shape, BF16) for shape in shapes],
        in_specs=[ANY] * 5,
        out_specs=[VMEM] * 5,
        scratch_shapes=[DMA((steps,)), DMA((steps,)), DMA((4,))],
        compiler_params=pltpu.CompilerParams(
            collective_id=0, has_side_effects=True, vmem_limit_bytes=40 * 2**20
        ),
    )(tokens, in_parts, out_weight, up_parts, cotangent)


def exchange_kernel(source, target, steps, *refs):
    count = len(steps)
    src_ref, sides, dst_ref = refs[0], refs[1 : 1 + count], refs[1 + count]
    got = refs[2 + count : 2 + 2 * count]
    send, recv, local = refs[2 + 2 * count :]
    w, z = lax.axis_index("wide"), lax.axis_index("narrow")
    line = [flipped(z, k) for k in range(4)]
    sender = Sender(send, recv)
    own = pltpu.make_async_copy(source(src_ref, z), target(dst_ref, z), local.at[0])
    own.start()
    greet(
        [narrow_device(line[k]) for k in (1, 2, 3)] + [wide_device(flipped(w, k)) for k in steps]
    )
    copies = [
        sender.plan(source(src_ref, line[k]), target(dst_ref, z), narrow_device(line[k]))
        for k in (2, 3, 1)
    ]
    copies += [
        sender.plan(sides[n], got[n], wide_device(flipped(w, k))) for n, k in enumerate(steps)
    ]
    for copy in copies:
        copy.start()
    own.wait()
    for copy in copies:
        copy.wait()


def exchange(array, source, target, shape, steps, sides, collective_id):
    count = len(steps) + 4
    return pl.pallas_call(
        functools.partial(exchange_kernel, source, target, steps),
        out_shape=[jax.ShapeDtypeStruct(shape, array.dtype)]
        + [jax.ShapeDtypeStruct(side.shape, side.dtype) for side in sides],
        in_specs=[ANY] * (1 + len(sides)),
        out_specs=[VMEM] * (1 + len(sides)),
        scratch_shapes=[DMA((count,)), DMA((count,)), DMA((1,))],
        compiler_params=pltpu.CompilerParams(
            collective_id=collective_id, has_side_effects=True, vmem_limit_bytes=16 * 2**20
        ),
    )(array, *sides)


def place_of(k, wide):
    return k // 2 + (k % 2) * (wide // 2)


def rows_kernel(wide, *refs):
    half = wide // 2
    grads = refs[:half]
    (
        src_ref, up_ref, up_two, up_one, down_ref, down_two, down_one, dst_ref, grad_ref, up_full,
        down_full, send, recv, local,
    ) = refs[half:]
    w, z = lax.axis_index("wide"), lax.axis_index("narrow")
    line = [flipped(z, k) for k in range(4)]
    is_middle = (z == 1) | (z == 2)
    is_end = (z == 0) | (z == 3)
    sender = Sender(send, recv)
    up_at = lambda n: up_full.at[:, n]
    down_at = lambda n: down_full.at[n]
    moves = [
        (src_ref, dst_ref.at[0]),
        (down_ref, down_at(z)), (down_two, down_at(line[2])), (down_one, down_at(line[1])),
        (up_ref, up_at(z)), (up_two, up_at(line[2])), (up_one, up_at(line[1])),
    ] + [(grads[n], grad_ref.at[n]) for n in range(half)]
    own = [pltpu.make_async_copy(src, dst, local.at[n]) for n, (src, dst) in enumerate(moves)]
    for copy in own:
        copy.start()
    greet(
        [wide_device(flipped(w, k)) for k in wide_steps(wide)]
        + [narrow_device(line[k]) for k in (1, 3)]
    )
    gather = WideGather(
        sender, w, wide, lambda k: src_ref if k == 0 else dst_ref.at[place_of(k, wide)],
        lambda k, to: dst_ref.at[place_of(k ^ to, wide)],
    )
    middles = [
        sender.plan(up_ref, up_at(z), narrow_device(line[3])),
        sender.plan(down_ref, down_at(z), narrow_device(line[3])),
    ]
    relays = [
        sender.plan(up_two, up_at(line[2]), narrow_device(line[1])),
        sender.plan(down_two, down_at(line[2]), narrow_device(line[1])),
    ]
    gather.start()

    @pl.when(is_middle)
    def _():
        for copy in middles + relays:
            copy.start()

    sibling = wide_device(flipped(w, 1))
    copies = [sender.plan(grads[n], grad_ref.at[half + n], sibling) for n in range(half)]
    for copy in copies:
        copy.start()
    gather.pass_on()

    @pl.when(is_middle)
    def _():
        for copy in middles:
            copy.wait()
        for copy in relays:
            copy.wait_send()

    @pl.when(is_end)
    def _():
        for copy in relays:
            copy.wait_recv()

    for copy in own + copies:
        copy.wait()
    gather.finish()


def gather_rows(array, grads, ups, downs, collective_id):
    half = len(grads)
    wide = 2 * half
    whole = jax.ShapeDtypeStruct((wide,) + array.shape, array.dtype)
    up_shape = ups[0].shape
    full = jax.ShapeDtypeStruct((up_shape[0], 4) + up_shape[1:], BF16)
    return pl.pallas_call(
        functools.partial(rows_kernel, wide),
        out_shape=[whole, whole, full, jax.ShapeDtypeStruct((4,) + downs[0].shape, BF16)],
        in_specs=[ANY] * (half + 7),
        out_specs=[VMEM, ANY if wide > 8 else VMEM, VMEM, VMEM],
        scratch_shapes=[DMA((2 * wide + 4,)), DMA((2 * wide + 4,)), DMA((half + 7,))],
        compiler_params=pltpu.CompilerParams(
            collective_id=collective_id, has_side_effects=True, vmem_limit_bytes=48 * 2**20
        ),
    )(*grads, array, *ups, *downs)


def hidden_kernel(
    half, normed_ref, grad_ref, up_ref, down_ref, hidden_ref, mid_ref, even_ref, odd_ref, branch_ref
):
    size = down_ref.shape[0]
    gate_up = dot_f32(normed_ref[...], up_ref[...])
    grad_hidden = dot_f32(grad_ref[...], down_ref[...], ((1,), (1,)))
    gate, up = gate_up[:, :size], gate_up[:, size:]
    opened = jax.nn.sigmoid(gate)
    acted = gate * opened
    hidden_ref[...] = (acted * up).astype(BF16)
    mid_ref[:, :size] = (grad_hidden * up * (opened * (1.0 + gate * (1.0 - opened)))).astype(BF16)
    mid_ref[:, size:] = (grad_hidden * acted).astype(BF16)
    grad_normed = dot_f32(mid_ref[...], up_ref[...], ((1,), (1,))).astype(BF16)
    branch_ref[...] = dot_f32(hidden_ref[...], down_ref[...]).astype(BF16)
    step = pl.program_id(0)

    @pl.when(step < half)
    def _():
        even_ref[...] = grad_normed

    @pl.when(step >= half)
    def _():
        odd_ref[...] = grad_normed


def feed_forward(normed, grad, up_full, down_full, rows):
    total, width = normed.shape
    blocks = total // rows
    half = blocks // 2
    size = down_full.shape[0]
    row_block = lambda columns: pl.BlockSpec((rows, columns), lambda i: (i, 0))
    fixed = lambda array: pl.BlockSpec(array.shape, lambda i: (0, 0))
    return pl.pallas_call(
        functools.partial(hidden_kernel, half),
        grid=(blocks,),
        in_specs=[row_block(width), row_block(width), fixed(up_full), fixed(down_full)],
        out_specs=[
            row_block(size), row_block(2 * size),
            pl.BlockSpec((rows, width), lambda i: (jnp.minimum(i, half - 1), 0)),
            pl.BlockSpec((rows, width), lambda i: (jnp.maximum(i - half, 0), 0)),
            row_block(width),
        ],
        out_shape=[
            jax.ShapeDtypeStruct((total, size), BF16),
            jax.ShapeDtypeStruct((total, 2 * size), BF16),
            jax.ShapeDtypeStruct((total // 2, width), BF16),
            jax.ShapeDtypeStruct((total // 2, width), BF16),
            jax.ShapeDtypeStruct((total, width), BF16),
        ],
        compiler_params=pltpu.CompilerParams(vmem_limit_bytes=48 * 2**20),
    )(normed, grad, up_full, down_full)


def middle_kernel(
    wide, even_ref, got_ref, branch_ref, up_ref, down_ref, norm_sum, branch_sum, up_src, down_src,
    up_one, down_one, up_acc, down_acc, core_buf, own_buf, far_buf, branch_buf, up_join, up_mid,
    down_join, down_mid, up_own, down_own, send, recv, local,
):
    w, z = lax.axis_index("wide"), lax.axis_index("narrow")
    line = [flipped(z, k) for k in range(4)]
    half = wide // 2
    unit = up_src.shape[1]
    part = down_src.shape[1]
    sender = Sender(send, recv)
    is_middle = (z == 1) | (z == 2)
    is_end = (z == 0) | (z == 3)

    def up_share(n):
        return up_ref.at[:, pl.ds(pl.multiple_of(n * unit, unit), unit)]

    def down_share(n):
        return down_ref.at[:, pl.ds(pl.multiple_of(n * part, part), part)]

    moves = [
        (up_share(line[2]), up_src), (down_share(line[2]), down_src),
        (up_share(z), up_own), (down_share(z), down_own),
        (up_share(line[1]), up_one), (down_share(line[1]), down_one),
    ]
    moves += [(got_ref.at[n], core_buf.at[n]) for n in range(half)]
    moves += [(even_ref.at[n], own_buf.at[n]) for n in range(half)]
    pairs = branch_sum.shape[0]
    moves += [(branch_ref.at[n], branch_sum.at[n]) for n in range(pairs)]
    own = [pltpu.make_async_copy(src, dst, local.at[n]) for n, (src, dst) in enumerate(moves)]
    for copy in own:
        copy.start()
    greet(
        [wide_device(flipped(w, k)) for k in wide_steps(wide)]
        + [narrow_device(line[k]) for k in (1, 3)]
    )
    sibling = wide_device(flipped(w, 1))
    far = [
        sender.plan(own_buf.at[n], far_buf.at[n - 1], wide_device(flipped(w, 2 * n)))
        for n in range(1, half)
    ]
    branch_core = [
        sender.plan(branch_ref.at[pairs + n], branch_buf.at[n], sibling) for n in range(pairs)
    ]
    joins = [
        sender.plan(up_share(line[3]), up_join, narrow_device(line[1])),
        sender.plan(down_share(line[3]), down_join, narrow_device(line[1])),
    ]
    mids = [
        sender.plan(up_share(line[3]), up_mid, narrow_device(line[3])),
        sender.plan(down_share(line[3]), down_mid, narrow_device(line[3])),
    ]
    order = list(range(1, half)) + [0]

    @pl.when(is_end)
    def _():
        for copy in joins:
            copy.start()

    @pl.when(is_middle)
    def _():
        for copy in mids:
            copy.start()

    for n in order:
        own[6 + n].wait()
        own[6 + half + n].wait()
        total = own_buf[n].astype(F32) + core_buf[n].astype(F32)
        own_buf[n] = total.astype(BF16)
        if n > 0:
            far[n - 1].start()
    for copy in branch_core:
        copy.start()
    for n in range(pairs):
        branch_core[n].wait_recv()
        own[6 + 2 * half + n].wait()
        total = branch_sum[n].astype(F32) + branch_buf[n].astype(F32)
        branch_sum[n] = total.astype(BF16)
    for n in range(6):
        own[n].wait()

    @pl.when(is_middle)
    def _():
        for copy in joins:
            copy.wait_recv()
        up_src[...] = (up_src[...].astype(F32) + up_join[...].astype(F32)).astype(BF16)
        down_src[...] = (down_src[...].astype(F32) + down_join[...].astype(F32)).astype(BF16)

    total = own_buf[0].astype(F32)
    for n in range(1, half):
        far[n - 1].wait_recv()
        total = total + far_buf[n - 1].astype(F32)
    norm_sum[...] = total
    up_acc[...] = up_own[...].astype(F32)
    down_acc[...] = down_own[...].astype(F32)

    @pl.when(is_middle)
    def _():
        for copy in mids:
            copy.wait()
        up_acc[...] += up_mid[...].astype(F32)
        down_acc[...] += down_mid[...].astype(F32)

    @pl.when(is_end)
    def _():
        for copy in joins:
            copy.wait_send()

    for copy in far + branch_core:
        copy.wait_send()


def middle_sums(even, got, branch, grad_up, grad_down, collective_id):
    half, rows, width = even.shape
    wide = 2 * half
    unit, part = grad_up.shape[1] // 4, grad_down.shape[1] // 4
    up_shape, down_shape = (grad_up.shape[0], unit), (grad_down.shape[0], part)
    steps = 4 * half + 6
    rows_buf = pltpu.VMEM((half, rows, width), BF16)
    pairs = branch.shape[0] // 2
    return pl.pallas_call(
        functools.partial(middle_kernel, wide),
        out_shape=[
            jax.ShapeDtypeStruct((rows, width), F32),
            jax.ShapeDtypeStruct((pairs,) + branch.shape[1:], BF16),
            *[jax.ShapeDtypeStruct(up_shape, BF16), jax.ShapeDtypeStruct(down_shape, BF16)] * 2,
            jax.ShapeDtypeStruct(up_shape, F32),
            jax.ShapeDtypeStruct(down_shape, F32),
        ],
        in_specs=[ANY] * 5,
        out_specs=[VMEM] * 8,
        scratch_shapes=[
            rows_buf, rows_buf, pltpu.VMEM((half - 1, rows, width), BF16),
            pltpu.VMEM((pairs,) + branch.shape[1:], BF16),
            *[pltpu.VMEM(up_shape, BF16)] * 2, *[pltpu.VMEM(down_shape, BF16)] * 2,
            pltpu.VMEM(up_shape, BF16), pltpu.VMEM(down_shape, BF16),
            DMA((steps,)), DMA((steps,)), DMA((6 + 3 * half,)),
        ],
        compiler_params=pltpu.CompilerParams(
            collective_id=collective_id, has_side_effects=True, vmem_limit_bytes=58 * 2**20
        ),
    )(even, got, branch, grad_up, grad_down)


def last_kernel(
    wide, rows, own_width, norm_ref, in_ref, out_ref, up_ref, branch_ref, norm_sum, in_got, out_sum,
    up_got, branch_got,
    join_buf, one_buf, mid_buf, two_buf, two_src, own_norm, in_core, in_own, in_far, in_sum,
    out_core, out_own, out_far, out_low, out_buf, send, recv, local,
):
    w, z = lax.axis_index("wide"), lax.axis_index("narrow")
    line = [flipped(z, k) for k in range(4)]
    half = wide // 2
    unit = up_ref.shape[1]
    wide_rows = up_got.shape[0]
    sender = Sender(send, recv)
    is_middle = (z == 1) | (z == 2)
    is_end = (z == 0) | (z == 3)

    def norm_block(n):
        return norm_ref.at[pl.ds(pl.multiple_of(n * rows, rows), rows), :]

    def out_columns(n):
        return pl.ds(pl.multiple_of(n * own_width, LANES), own_width)

    def up_rows(n):
        return up_ref.at[pl.ds(pl.multiple_of(n * wide_rows, 16), wide_rows), :]

    def up_columns(n):
        return up_got.at[:, pl.ds(pl.multiple_of(n * unit, LANES), unit)]

    def section(n):
        return in_sum.at[:, pl.ds(pl.multiple_of(n * own_width, LANES), own_width + LANES)]

    moves = [
        (norm_block(line[2]), two_src), (norm_block(z), own_norm), (up_rows(w), up_columns(w)),
    ]
    moves += [(in_ref.at[flipped(w, 2 * n)], in_own.at[n]) for n in range(half)]
    moves += [(out_ref.at[flipped(w, 2 * n)], out_own.at[n]) for n in range(half)]
    own = [pltpu.make_async_copy(src, dst, local.at[n]) for n, (src, dst) in enumerate(moves)]
    for copy in own:
        copy.start()
    greet(
        [narrow_device(line[k]) for k in (1, 2, 3)]
        + [wide_device(flipped(w, k)) for k in range(1, wide)]
    )
    sibling = wide_device(flipped(w, 1))

    def over_wide(ref, core_buf, own_buf, far_buf):
        core = [
            sender.plan(ref.at[flipped(w, 2 * n + 1)], core_buf.at[n], sibling)
            for n in range(half)
        ]
        far = [
            sender.plan(own_buf.at[n], far_buf.at[n - 1], wide_device(flipped(w, 2 * n)))
            for n in range(1, half)
        ]
        return core, far

    joined = sender.plan(norm_block(line[3]), join_buf, narrow_device(line[1]))
    one = sender.plan(norm_block(line[1]), one_buf, narrow_device(line[1]))
    middle = sender.plan(norm_block(line[3]), mid_buf, narrow_device(line[3]))
    two = sender.plan(two_src, two_buf, narrow_device(line[2]))
    in_steps = over_wide(in_ref, in_core, in_own, in_far)
    out_steps = over_wide(out_ref, out_core, out_own, out_far)
    sections = [
        sender.plan(section(line[k]), in_got.at[z], narrow_device(line[k])) for k in (2, 3, 1)
    ]
    outs = [
        sender.plan(out_low.at[:, out_columns(line[k])], out_buf.at[k - 1], narrow_device(line[k]))
        for k in (1, 2, 3)
    ]
    ups = [
        sender.plan(up_rows(flipped(w, k)), up_columns(w), wide_device(flipped(w, k)))
        for k in range(1, wide)
    ]
    branches = [
        sender.plan(branch_ref.at[n], branch_got.at[n], wide_device(flipped(w, k)))
        for n, k in enumerate(diagonal_steps(wide))
    ]
    order = list(range(1, half)) + [0]
    for core in (in_steps[0], out_steps[0]):
        for n in order:
            core[n].start()

    @pl.when(is_end)
    def _():
        joined.start()

    @pl.when(is_middle)
    def _():
        middle.start()

    def between_cores(steps, core_buf, own_buf, first):
        core, far = steps
        for n in order:
            core[n].wait_recv()
            own[first + n].wait()
            total = own_buf[n].astype(F32) + core_buf[n].astype(F32)
            own_buf[n] = total.astype(BF16)
            if n > 0:
                far[n - 1].start()

    def between_chips(steps, own_buf, far_buf):
        total = own_buf[0].astype(F32)
        for n in range(1, half):
            steps[1][n - 1].wait_recv()
            total = total + far_buf[n - 1].astype(F32)
        return total.astype(BF16)

    between_cores(in_steps, in_core, in_own, 3)
    own[0].wait()

    @pl.when(is_middle)
    def _():
        joined.wait_recv()
        two_src[...] = (two_src[...].astype(F32) + join_buf[...].astype(F32)).astype(BF16)

    two.start()
    one.start()
    between_cores(out_steps, out_core, out_own, 3 + half)
    for copy in branches:
        copy.start()
    in_sum[...] = between_chips(in_steps, in_own, in_far)
    mine = pltpu.make_async_copy(section(z), in_got.at[z], local.at[3 + 2 * half])
    mine.start()
    for copy in sections:
        copy.start()
    out_low[...] = between_chips(out_steps, out_own, out_far)
    for copy in outs + ups:
        copy.start()
    own[1].wait()
    own[2].wait()
    one.wait_recv()
    norm_sum[...] = own_norm[...].astype(F32) + one_buf[...].astype(F32)

    @pl.when(is_middle)
    def _():
        middle.wait()
        norm_sum[...] += mid_buf[...].astype(F32)

    two.wait_recv()
    norm_sum[...] += two_buf[...].astype(F32)
    total = out_low[:, out_columns(z)].astype(F32)
    for n in range(3):
        outs[n].wait_recv()
        total = total + out_buf[n].astype(F32)
    out_sum[...] = total
    for copy in sections + ups + branches:
        copy.wait_recv()
    mine.wait()

    @pl.when(is_end)
    def _():
        joined.wait_send()

    sent = [one, two] + in_steps[0] + in_steps[1] + out_steps[0] + out_steps[1]
    for copy in sent + sections + outs + ups + branches:
        copy.wait_send()


def last_transfers(norm_part, in_part, out_part, up_part, branches, rows, own_width, collective_id):
    wide, wide_rows, columns = in_part.shape
    half = wide // 2
    width = norm_part.shape[1]
    unit = up_part.shape[1]
    steps = 4 + 4 * half + 6 + 2 * wide
    block = pltpu.VMEM((rows, width), BF16)
    sums = lambda size: [
        pltpu.VMEM((half, wide_rows, size), BF16), pltpu.VMEM((half, wide_rows, size), BF16),
        pltpu.VMEM((half - 1, wide_rows, size), BF16), pltpu.VMEM((wide_rows, size), BF16),
    ]
    return pl.pallas_call(
        functools.partial(last_kernel, wide, rows, own_width),
        out_shape=[
            jax.ShapeDtypeStruct((rows, width), F32),
            jax.ShapeDtypeStruct((4, wide_rows, own_width + LANES), BF16),
            jax.ShapeDtypeStruct((wide_rows, own_width), F32),
            jax.ShapeDtypeStruct((wide_rows, wide * unit), BF16),
            jax.ShapeDtypeStruct(branches.shape, BF16),
        ],
        in_specs=[ANY] * 5,
        out_specs=[VMEM] * 5,
        scratch_shapes=[
            *[block] * 6, *sums(columns), *sums(width),
            pltpu.VMEM((3, wide_rows, own_width), BF16),
            DMA((steps,)), DMA((steps,)), DMA((4 + 2 * half,)),
        ],
        compiler_params=pltpu.CompilerParams(
            collective_id=collective_id, has_side_effects=True, vmem_limit_bytes=48 * 2**20
        ),
    )(norm_part, in_part, out_part, up_part, branches)


def total_kernel(wide, v_ref, out_ref, narrow_buf, wide_buf, sum_buf, send, recv):
    w, z = lax.axis_index("wide"), lax.axis_index("narrow")
    greet(
        [narrow_device(flipped(z, k)) for k in (1, 2, 3)]
        + [wide_device(flipped(w, k)) for k in range(1, wide)]
    )
    sender = Sender(send, recv)
    first = [
        sender.plan(v_ref, narrow_buf.at[z], narrow_device(flipped(z, k))) for k in (1, 2, 3)
    ]
    second = [
        sender.plan(sum_buf, wide_buf.at[w], wide_device(flipped(w, k))) for k in range(1, wide)
    ]
    for copy in first:
        copy.start()
    narrow_buf[z] = v_ref[...]
    for copy in first:
        copy.wait()
    sum_buf[...] = narrow_buf[0] + narrow_buf[1] + narrow_buf[2] + narrow_buf[3]
    for copy in second:
        copy.start()
    wide_buf[w] = sum_buf[...]
    for copy in second:
        copy.wait()
    total = wide_buf[0]
    for n in range(1, wide):
        total = total + wide_buf[n]
    out_ref[...] = total


def total_of(values, wide, collective_id):
    size = values.shape[0]
    height = -(-size // (8 * LANES)) * 8
    padded = jnp.pad(values, (0, height * LANES - size)).reshape(height, LANES)
    total = pl.pallas_call(
        functools.partial(total_kernel, wide),
        out_shape=jax.ShapeDtypeStruct(padded.shape, F32),
        in_specs=[VMEM],
        out_specs=VMEM,
        scratch_shapes=[
            pltpu.VMEM((4,) + padded.shape, F32),
            pltpu.VMEM((wide,) + padded.shape, F32),
            pltpu.VMEM(padded.shape, F32),
            DMA((wide + 2,)), DMA((wide + 2,)),
        ],
        compiler_params=pltpu.CompilerParams(collective_id=collective_id, has_side_effects=True),
    )(padded)
    return total.reshape(-1)[:size]


def rms_factor(values):
    return lax.rsqrt(jnp.mean(values * values, axis=-1, keepdims=True) + EPSILON)


def rms_back(values, gain, grad):
    factor = rms_factor(values)
    normed = values * factor
    grad_gain = jnp.sum(grad * normed, axis=0)
    scaled = grad * gain
    inner = jnp.mean(scaled * normed, axis=-1, keepdims=True)
    return (factor * (scaled - normed * inner), grad_gain)


def log_sigmoid(v):
    return jnp.minimum(v, 0.0) - jnp.log1p(jnp.exp(-jnp.abs(v)))


def iota(shape, dim):
    return lax.broadcasted_iota(jnp.int32, shape, dim)


def running_sum(v, reverse):
    rows = v.shape[0]
    index = iota(v.shape, 0)
    step = 1
    while step < rows:
        if reverse:
            v = v + jnp.where(index < rows - step, pltpu.roll(v, rows - step, 0), 0.0)
        else:
            v = v + jnp.where(index >= step, pltpu.roll(v, step, 0), 0.0)
        step *= 2
    return v


def half_of(lane, head_size):
    return (lane >= head_size).astype(jnp.int32)


def spread(first, head_size):
    row, lane = iota((LANES, LANES), 0), iota((LANES, LANES), 1)
    return row == first + half_of(lane, head_size)


def collect(first, head_size):
    row, lane = iota((LANES, LANES), 0), iota((LANES, LANES), 1)
    return lane == first + half_of(row, head_size)


def same_head(head_size):
    row, lane = iota((LANES, LANES), 0), iota((LANES, LANES), 1)
    return (half_of(row, head_size) == half_of(lane, head_size)).astype(F32)


def exact_dot(left, right):
    return lax.dot_general(
        left, right, (((1,), (0,)), ((), ())), precision=EXACT, preferred_element_type=F32
    )


def head_mean(v, head_size):
    return exact_dot(v, same_head(head_size)) * (1.0 / head_size)


def prologue(pair, heads, head_size, q_ref, k_ref, v_ref, small_low, cont):
    spot = lambda group: spread(group * heads + 2 * pair, head_size).astype(BF16)
    key_mix = jax.nn.sigmoid(dot_f32(small_low, spot(1)))
    value_mix = jax.nn.sigmoid(dot_f32(small_low, spot(2)))
    queries = q_ref[...].astype(BF16).astype(F32)
    keys = k_ref[...].astype(BF16).astype(F32)
    values = v_ref[...].astype(BF16).astype(F32)
    key_step = pltpu.roll(keys, 1, 0) * cont - keys
    value_step = pltpu.roll(values, 1, 0) * cont - values
    shifted = keys + key_mix * key_step
    value_low = (values + value_mix * value_step).astype(BF16)
    query_factor = lax.rsqrt(head_mean(queries * queries, head_size) + EPSILON)
    key_factor = lax.rsqrt(head_mean(shifted * shifted, head_size) + EPSILON)
    return (
        queries * query_factor,
        shifted * key_factor,
        value_low,
        query_factor,
        key_factor,
        key_mix,
        value_mix,
        key_step,
        value_step,
    )


def small_columns(small_ref, bias_ref):
    return (small_ref[...] + bias_ref[0:1, :]).astype(BF16)


def decay_of(small_low, cont):
    return running_sum(log_sigmoid(small_low.astype(F32)) - SEPARATE * (1.0 - cont), False)


def forward_kernel(
    heads, head_size, block, q_ref, k_ref, v_ref, gate_ref, small_ref, bias_ref, cont_ref,
    mixed_ref, att_ref, log_ref, decay_scr,
):
    pair = pl.program_id(0)
    cont = cont_ref[...]
    small_low = small_columns(small_ref, bias_ref)

    @pl.when(pair == 0)
    def _():
        decay_scr[...] = decay_of(small_low, cont)

    query, key, value_low, *unused = prologue(
        pair, heads, head_size, q_ref, k_ref, v_ref, small_low, cont
    )
    rows = query.shape[0]
    query = query.astype(BF16) * BF16(head_size**-0.5)
    key = key.astype(BF16)
    decay = exact_dot(decay_scr[...], spread(2 * pair, head_size).astype(F32))
    decay_rows = decay.T
    lane = iota((1, LANES), 1)
    ones = jnp.ones((rows, LANES), BF16)
    value_wide = jnp.concatenate([value_low, ones], axis=1)
    for i in range(rows // block):
        lo, hi = i * block, (i + 1) * block
        row_index = iota((block, hi), 0) + lo
        visible = iota((block, hi), 1) <= row_index
        outs, sums = [], []
        for head in range(2):
            mine = (lane >= head_size) if head else (lane < head_size)
            at = head * head_size
            left = jnp.where(mine, query[lo:hi], BF16(0.0))
            scores = dot_f32(left, key[:hi], ((1,), (1,)))
            scores = scores + decay[lo:hi, at : at + 1] - decay_rows[at : at + 1, :hi]
            weights = jnp.where(visible, jnp.exp(scores), 0.0).astype(BF16)
            both = dot_f32(weights, value_wide[:hi])
            outs.append(both[:, :LANES])
            sums.append(both[:, LANES:])
        first = lane < head_size
        total = jnp.where(first, sums[0], sums[1])
        attended = (jnp.where(first, outs[0], outs[1]) / total).astype(BF16)
        att_ref[lo:hi, :] = attended
        log_ref[lo:hi, :] = jnp.log(total)
        opened = jax.nn.sigmoid(gate_ref[lo:hi, :])
        mixed_ref[lo:hi, :] = (attended.astype(F32) * opened).astype(BF16)


def backward_kernel(
    heads, head_size, block, q_ref, k_ref, v_ref, gate_ref, small_ref, bias_ref, cont_ref,
    att_ref, log_ref, grad_ref, up_src, down_src, up_one, down_one, out_ref, bias_grad_ref,
    up_two_got, down_two_got, up_one_got, down_one_got, decay_scr, small_scr, dq_scr, send, recv,
):
    pair = pl.program_id(0)
    z = lax.axis_index("narrow")
    sender = Sender(send, recv)
    copies = [
        sender.plan(up_src, up_two_got, narrow_device(flipped(z, 2))),
        sender.plan(down_src, down_two_got, narrow_device(flipped(z, 2))),
        sender.plan(up_one, up_one_got, narrow_device(flipped(z, 1))),
        sender.plan(down_one, down_one_got, narrow_device(flipped(z, 1))),
    ]

    @pl.when(pair == 0)
    def _():
        greet([narrow_device(flipped(z, 1)), narrow_device(flipped(z, 2))])
        for copy in copies:
            copy.start()

    cont = cont_ref[...]
    small_low = small_columns(small_ref, bias_ref)
    rows = cont.shape[0]
    width = heads * head_size

    @pl.when(pair == 0)
    def _():
        decay_scr[...] = decay_of(small_low, cont)
        small_scr[...] = jnp.zeros_like(small_scr)

    (
        query_norm, key_norm, value_low, query_factor, key_factor, key_mix, value_mix, key_step,
        value_step,
    ) = prologue(pair, heads, head_size, q_ref, k_ref, v_ref, small_low, cont)
    query = query_norm.astype(BF16) * BF16(head_size**-0.5)
    key = key_norm.astype(BF16)
    opened = jax.nn.sigmoid(gate_ref[...])
    attended = att_ref[...].astype(F32)
    grad_mixed = grad_ref[...].astype(F32)
    grad_low = (grad_mixed * opened).astype(BF16)
    grad_gate = grad_mixed * attended * opened * (1.0 - opened)

    def columns(group):
        at = group * width + pair * LANES
        return pl.ds(pl.multiple_of(at, LANES), LANES)

    out_ref[:, columns(3)] = grad_gate.astype(BF16)
    inner = exact_dot(grad_low.astype(F32) * attended, same_head(head_size))
    decay = exact_dot(decay_scr[...], spread(2 * pair, head_size).astype(F32))
    level_rows = (decay - log_ref[...]).T
    inner_rows = inner.T
    lane = iota((1, LANES), 1)
    ones = jnp.ones((rows, LANES), BF16)
    query_wide = jnp.concatenate([query, ones], axis=1)
    key_wide = jnp.concatenate([key, ones], axis=1)
    key_parts, value_parts, query_parts = [], [], []
    for head in range(2):
        mine = (lane >= head_size) if head else (lane < head_size)
        at = head * head_size
        keys_out, values_out = [], []
        for j in range(rows // block):
            lo, hi = j * block, (j + 1) * block
            span = rows - lo
            visible = iota((block, span), 0) <= iota((block, span), 1)
            scores = dot_f32(
                jnp.where(mine, key[lo:hi], BF16(0.0)), query[lo:], ((1,), (1,))
            )
            scores = scores + level_rows[at : at + 1, lo:] - decay[lo:hi, at : at + 1]
            probs = jnp.where(visible, jnp.exp(scores), 0.0)
            grad_probs = dot_f32(
                jnp.where(mine, value_low[lo:hi], BF16(0.0)), grad_low[lo:], ((1,), (1,))
            )
            grad_scores = (probs * (grad_probs - inner_rows[at : at + 1, lo:])).astype(BF16)
            values_out.append(dot_f32(probs.astype(BF16), grad_low[lo:]))
            keys_out.append(dot_f32(grad_scores, query_wide[lo:]))
            part = dot_f32(grad_scores, key_wide[lo:hi], ((0,), (0,)))
            if j == 0:
                dq_scr[...] = part
            else:
                dq_scr[lo:, :] += part
        key_parts.append(jnp.concatenate(keys_out, axis=0))
        value_parts.append(jnp.concatenate(values_out, axis=0))
        query_parts.append(dq_scr[...])
    first = lane < head_size

    def join(parts):
        return jnp.where(first, parts[0], parts[1])

    grad_query = join([p[:, :LANES] for p in query_parts]) * head_size**-0.5
    grad_key = join([p[:, :LANES] for p in key_parts])
    grad_value = join(value_parts)
    grad_decay = join([p[:, LANES:] for p in query_parts]) - join([p[:, LANES:] for p in key_parts])

    def norm_back(grad, normed, factor):
        return factor * (grad - normed * head_mean(grad * normed, head_size))

    def shift_back(grad, mix):
        return grad * (1.0 - mix) + pltpu.roll(grad * mix * cont, rows - 1, 0)

    grad_query = norm_back(grad_query, query_norm, query_factor)
    grad_shifted = norm_back(grad_key, key_norm, key_factor)
    out_ref[:, columns(0)] = grad_query.astype(BF16)
    out_ref[:, columns(1)] = shift_back(grad_shifted, key_mix).astype(BF16)
    out_ref[:, columns(2)] = shift_back(grad_value, value_mix).astype(BF16)
    key_logit = grad_shifted * key_step * key_mix * (1.0 - key_mix)
    value_logit = grad_value * value_step * value_mix * (1.0 - value_mix)
    single = (lax.rem(lane, head_size) == 0).astype(F32)
    small_scr[...] += (
        exact_dot(grad_decay * single, collect(2 * pair, head_size).astype(F32))
        + exact_dot(key_logit, collect(heads + 2 * pair, head_size).astype(F32))
        + exact_dot(value_logit, collect(2 * heads + 2 * pair, head_size).astype(F32))
    )

    @pl.when(pair == pl.num_programs(0) - 1)
    def _():
        grads = small_scr[...]
        forget = running_sum(grads, True) * jax.nn.sigmoid(-small_low.astype(F32))
        result = jnp.where(lane < heads, forget, grads)
        out_ref[:, 4 * width :] = result.astype(BF16)
        bias_grad_ref[...] = jnp.broadcast_to(
            jnp.sum(result, axis=0, keepdims=True), bias_grad_ref.shape
        )
        for copy in copies:
            copy.wait()


def attention_specs(rows, pairs):
    def block_at(group):
        return pl.BlockSpec((rows, LANES), lambda p: (0, group * pairs + p))

    def fixed(height, column=0):
        return pl.BlockSpec((height, LANES), lambda p: (0, column))

    base = [block_at(0), block_at(1), block_at(2), block_at(3), fixed(rows, 4 * pairs), fixed(8), fixed(rows)]
    return base, pl.BlockSpec((rows, LANES), lambda p: (0, p))


def attention_forward(projected, bias, cont, heads, head_size, block):
    rows = projected.shape[0]
    pairs = heads * head_size // LANES
    base, own = attention_specs(rows, pairs)
    wide = jax.ShapeDtypeStruct((rows, heads * head_size), BF16)
    return pl.pallas_call(
        functools.partial(forward_kernel, heads, head_size, block),
        grid=(pairs,),
        in_specs=base,
        out_specs=[own] * 3,
        out_shape=[wide, wide, jax.ShapeDtypeStruct(wide.shape, F32)],
        scratch_shapes=[pltpu.VMEM((rows, LANES), F32)],
        compiler_params=pltpu.CompilerParams(vmem_limit_bytes=48 * 2**20),
    )(*([projected] * 5), bias, cont)


def attention_backward(
    projected, bias, cont, attended, logs, grad, shares, heads, head_size, block, collective_id
):
    rows = projected.shape[0]
    pairs = heads * head_size // LANES
    base, own = attention_specs(rows, pairs)
    columns = 4 * heads * head_size + LANES
    return pl.pallas_call(
        functools.partial(backward_kernel, heads, head_size, block),
        grid=(pairs,),
        in_specs=base + [own] * 3 + [ANY] * 4,
        out_specs=[
            pl.BlockSpec((rows, columns), lambda p: (0, 0)),
            pl.BlockSpec((8, LANES), lambda p: (0, 0)),
        ]
        + [ANY] * 4,
        out_shape=[
            jax.ShapeDtypeStruct((rows, columns), BF16),
            jax.ShapeDtypeStruct((8, LANES), F32),
        ]
        + [jax.ShapeDtypeStruct(share.shape, BF16) for share in shares],
        scratch_shapes=[
            pltpu.VMEM((rows, LANES), F32),
            pltpu.VMEM((rows, LANES), F32),
            pltpu.VMEM((rows, 2 * LANES), F32),
            DMA((4,)),
            DMA((4,)),
        ],
        compiler_params=pltpu.CompilerParams(
            collective_id=collective_id, has_side_effects=True, vmem_limit_bytes=56 * 2**20
        ),
    )(*([projected] * 5), bias, cont, attended, logs, grad, *shares)


def add_up(parts):
    total = parts[0].astype(F32)
    for part in parts[1:]:
        total = total + part.astype(F32)
    return total


def on_device(
    tokens, gain_one, in_weight, forget_bias, out_weight, gain_two, gate_up_weight, down_weight,
    segment_ids, cotangent,
):
    wide, narrow = lax.axis_size("wide"), lax.axis_size("narrow")
    w, z = lax.axis_index("wide"), lax.axis_index("narrow")
    rows, width = tokens.shape
    slot = rows * narrow
    heads = forget_bias.shape[0]
    head_size = width // heads
    own_heads = heads // narrow
    own_width = own_heads * head_size
    part_rows = in_weight.shape[0]
    hidden_all = down_weight.shape[0] * wide * narrow
    unit = hidden_all // (2 * wide)
    columns = 4 * own_width + LANES
    base = 4 * width

    small = in_weight[:, base:].reshape(part_rows, 3, narrow, own_heads)
    small = jnp.moveaxis(small, 2, 0).reshape(narrow, part_rows, 3 * own_heads)
    small = jnp.pad(small, ((0, 0), (0, 0), (0, LANES - 3 * own_heads)))
    aligned = unit % LANES == 0

    def split_weights(sources, targets):
        copies = [(sources[1], targets[0].at[:, :, pl.ds(4 * own_width, LANES)])]
        for n in range(narrow):
            for group in range(4):
                copies.append(
                    (
                        sources[0].at[:, pl.ds(group * width + n * own_width, own_width)],
                        targets[0].at[n, :, pl.ds(group * own_width, own_width)],
                    )
                )
        if aligned:
            for n in range(wide):
                for group in range(4):
                    copies.append(
                        (
                            sources[2].at[:, pl.ds((group * wide + n) * unit, unit)],
                            targets[1].at[n, :, pl.ds(group * unit, unit)],
                        )
                    )
        return copies

    shapes = [
        jax.ShapeDtypeStruct((narrow, part_rows, columns), BF16),
        jax.ShapeDtypeStruct((wide, part_rows, 4 * unit), BF16),
    ]
    copies = 4 * narrow + 1
    if aligned:
        in_parts, up_parts = local_copies(
            split_weights, copies + 4 * wide, [in_weight, small, gate_up_weight], shapes, False
        )
    else:
        in_parts = local_copies(split_weights, copies, [in_weight, small], shapes[:1], False)[0]
        up_parts = jnp.moveaxis(gate_up_weight.reshape(part_rows, 4, wide, unit), 2, 0)
        up_parts = up_parts.reshape(wide, part_rows, 4 * unit)

    down_rows = down_weight.shape[0]
    pairs = []
    for i in range(wide * narrow):
        to_wide = (i % (2 * wide)) // 2
        to_narrow = i % 2 + 2 * (i // (2 * wide))
        pairs.append((i, to_wide * narrow + to_narrow))
    down_block = lax.ppermute(down_weight, ("wide", "narrow"), pairs)

    slot_tokens, in_full, out_full, up_block, grad_far = gather_all(
        tokens, in_parts, out_weight, up_parts, cotangent
    )
    slot_tokens = slot_tokens.reshape(slot, width)
    in_full = in_full.reshape(width, columns)
    out_full = out_full.reshape(width, width)

    up_two = on_line(up_block, LINE_TWO)
    up_one = on_line(up_block, LINE_ONE)

    slot_floats = slot_tokens.astype(F32)
    normed_one = (slot_floats * rms_factor(slot_floats) * gain_one).astype(BF16)
    projected = dot_f32(normed_one, in_full)

    segments = segment_ids[0]
    joined = (segments[1:] == segments[:-1]).astype(F32)
    cont = jnp.concatenate([jnp.zeros((1,), F32), joined])
    cont = jnp.broadcast_to(cont[:, None], (slot, LANES))
    own_bias = lax.dynamic_slice_in_dim(forget_bias, z * own_heads, own_heads)
    bias = jnp.broadcast_to(jnp.pad(own_bias, (0, LANES - own_heads))[None], (8, LANES))
    block = min(256, slot)
    mixed, attended, logs = attention_forward(
        projected, bias, cont, own_heads, head_size, block
    )

    def row_block(ref, n):
        return ref.at[pl.ds(pl.multiple_of(n * rows, rows), rows), :]

    def column_block(ref, n):
        return ref.at[:, pl.ds(pl.multiple_of(n * own_width, LANES), own_width)]

    straight, diagonal = straight_steps(wide), diagonal_steps(wide)
    mixed_rows, *grad_near = exchange(
        mixed, row_block, column_block, (rows, width), straight, [cotangent] * len(straight), 1
    )
    grads = {0: cotangent}
    grads.update({k: grad_near[n] for n, k in enumerate(straight)})
    grads.update({k: grad_far[n] for n, k in enumerate(diagonal)})
    grads = [grads[k] for k in range(0, wide, 2)]
    down_block = follow(down_block, mixed_rows)
    down_two = on_line(down_block, LINE_TWO)
    down_one = on_line(down_block, LINE_ONE)
    inputs = tokens.astype(F32)
    middle = inputs + dot_f32(mixed_rows, out_full)
    normed_two = (middle * rms_factor(middle) * gain_two).astype(BF16)

    half = wide // 2
    ups = [up_block] + [follow(piece, normed_two) for piece in (up_two, up_one)]
    plane_normed, plane_grad, up_full, down_full = gather_rows(
        normed_two, grads, ups, [down_block, down_two, down_one], 2
    )
    plane_normed = plane_normed.reshape(wide * rows, width)
    plane_grad = plane_grad.reshape(wide * rows, width)
    up_full = up_full.reshape(width, 4 * unit)
    down_full = down_full.reshape(2 * unit, width)
    hidden, gate_up_grad, norm_even, norm_odd, branch = feed_forward(
        plane_normed, plane_grad, up_full, down_full, rows
    )
    grad_up_full = dot_f32(plane_normed, gate_up_grad, ((0,), (0,))).astype(BF16)
    grad_down_full = dot_f32(hidden, plane_grad, ((0,), (0,))).astype(BF16)
    if unit % LANES:
        grouped = grad_up_full.reshape(width, 4, unit)
        grad_up_full = jnp.pad(grouped, ((0, 0), (0, 0), (0, LANES - unit))).reshape(width, -1)
    branch = branch.reshape(wide, rows, width)
    fits = wide <= 8
    norm_got = along_wide(norm_odd.reshape(half, rows, width), 1, wide)
    (
        grad_normed_two, branch_sum, up_src, down_src, up_one, down_one, up_acc, down_acc,
    ) = middle_sums(
        norm_even.reshape(half, rows, width), norm_got,
        branch if fits else branch[:2, :16], grad_up_full, grad_down_full, 6,
    )
    if not fits:
        received = along_wide(branch[half:], 1, wide)
        branch_sum = (branch[:half].astype(F32) + received.astype(F32)).astype(BF16)
    upstream = cotangent.astype(F32)
    grad_middle_norm, grad_gain_two = rms_back(middle, gain_two, grad_normed_two)
    grad_middle = upstream + grad_middle_norm
    branch_one_grad = grad_middle.astype(BF16)
    grad_mixed = dot_f32(branch_one_grad, out_full, ((1,), (1,))).astype(BF16)
    slot_grad, *branch_near = exchange(
        grad_mixed, column_block, row_block, (slot, own_width), straight,
        [branch_sum[k // 2] for k in straight], 3,
    )

    projected_grad, bias_grad, up_two, down_two, up_one, down_one = attention_backward(
        projected, bias, cont, attended, logs, slot_grad, [up_src, down_src, up_one, down_one],
        own_heads, head_size, block, 7,
    )
    norm_part = dot_f32(projected_grad, in_full, ((1,), (1,))).astype(BF16)
    in_part = dot_f32(normed_one, projected_grad, ((0,), (0,))).astype(BF16)

    wide_rows = width // wide
    out_part = dot_f32(mixed_rows, branch_one_grad, ((0,), (0,))).astype(BF16)
    late = lambda part: part.astype(F32)
    up_part = (up_acc + late(up_one) + late(up_two)).astype(BF16)
    grad_down = (down_acc + late(down_one) + late(down_two)).astype(BF16)
    low_half, high_half = grad_down[:unit], grad_down[unit:]
    is_odd = lax.rem(w, 2) == 1
    first_send = jnp.where(is_odd, high_half, low_half)
    second_send = jnp.where(is_odd, low_half, high_half)
    first_got = lax.ppermute(
        first_send, "wide", [(i, i // 2 + (half if i % 2 else 0)) for i in range(wide)]
    )
    second_got = lax.ppermute(
        second_send, "wide", [(i, i // 2 + (0 if i % 2 else half)) for i in range(wide)]
    )
    norm_sum, got, grad_out, grad_up, branch_far = last_transfers(
        norm_part, in_part.reshape(wide, wide_rows, columns),
        out_part.reshape(wide, wide_rows, width), up_part,
        jnp.stack([branch_sum[k // 2] for k in diagonal]), rows, own_width, 4,
    )
    branch_far = [branch_far[n] for n in range(len(diagonal))]
    output = (middle + add_up([branch_sum[0]] + branch_near + branch_far)).astype(BF16)
    if not aligned:
        grad_up = grad_up.reshape(wide_rows, wide, LANES)[:, :, :unit]
        grad_up = grad_up.reshape(wide_rows, wide * unit)
    first_got, second_got = follow(first_got, norm_sum), follow(second_got, norm_sum)
    grad_up = grad_up.astype(F32)
    grad_inputs, grad_gain_one = rms_back(inputs, gain_one, norm_sum)
    grad_tokens = grad_middle + grad_inputs
    in_low = w < half
    grad_down = jnp.concatenate(
        [
            jnp.where(in_low, first_got, second_got),
            jnp.where(in_low, second_got, first_got),
        ],
        axis=0,
    ).astype(F32)

    extra = 3 * heads
    section = jnp.concatenate([got[n, :, :own_width] for n in range(narrow)], axis=1)
    small_all = jnp.stack([got[n, :, own_width : own_width + 3 * own_heads] for n in range(narrow)])
    small_all = small_all.reshape(narrow, wide_rows, 3, own_heads)
    small_all = jnp.transpose(small_all, (1, 2, 0, 3)).reshape(wide_rows, extra)
    next_first = got[0, :, own_width : own_width + extra]
    tail = jnp.where(z == narrow - 1, small_all, next_first)
    joined_columns = jnp.concatenate([section, tail], axis=1)
    shard = (base + extra) // narrow
    grad_in = lax.dynamic_slice_in_dim(joined_columns, z * (shard - width), shard, 1).astype(F32)

    all_bias = lax.dynamic_update_slice(
        jnp.zeros((heads,), F32), bias_grad[0, :own_heads], (z * own_heads,)
    )
    packed = jnp.concatenate([grad_gain_one, grad_gain_two, all_bias])
    packed = total_of(packed, wide, 5)
    return (
        output,
        grad_tokens,
        packed[:width],
        grad_in,
        packed[2 * width :],
        grad_out,
        packed[width : 2 * width],
        grad_up,
        grad_down,
    )


def solution(mesh):
    both = ("wide", "narrow")
    in_specs = (
        P(both, None), P(), P(both, None), P(), P(both, None), P(), P(both, None), P(both, None),
        P("wide", None), P(both, None),
    )
    out_specs = (
        P(both, None), P(both, None), P(), P("wide", "narrow"), P(), P("wide", "narrow"), P(),
        P("wide", "narrow"), P("wide", "narrow"),
    )
    return jax.shard_map(
        on_device, mesh=mesh, in_specs=in_specs, out_specs=out_specs, check_vma=False
    )
```

```python
import functools

import jax
import jax.numpy as jnp
from jax import lax
from jax.experimental import pallas as pl
from jax.experimental.pallas import tpu as pltpu
from jax.sharding import PartitionSpec as P

EPSILON = 1e-06
SEPARATE = 128.0
F32 = jnp.float32
BF16 = jnp.bfloat16
LANES = 128
EXACT = lax.Precision.HIGHEST
ANY = pl.BlockSpec(memory_space=pl.ANY)


def dot_f32(left, right, dims=((1,), (0,))):
    return lax.dot_general(left, right, (dims, ((), ())), preferred_element_type=F32)


def along_wide(block, flip, wide):
    return lax.ppermute(block, "wide", [(i, i ^ flip) for i in range(wide)])


def copy_kernel(plan, count, *refs):
    sources, targets, sems = refs[:count], refs[count:-1], refs[-1]
    copies = plan(sources, targets)

    def each(act):
        for n, (src, dst, *when) in enumerate(copies):
            copy = pltpu.make_async_copy(src, dst, sems.at[n])
            if when:
                pl.when(when[0])(functools.partial(act, copy))
            else:
                act(copy)

    each(lambda copy: copy.start())
    each(lambda copy: copy.wait())


def local_copies(plan, copies, sources, shapes, gather):
    moved = sum(s.size * s.dtype.itemsize for s in shapes)
    inside = pl.BlockSpec(memory_space=pltpu.VMEM)
    return pl.pallas_call(
        functools.partial(copy_kernel, plan, len(sources)),
        out_shape=shapes,
        in_specs=[ANY if gather else inside] * len(sources),
        out_specs=[inside if gather else ANY] * len(shapes),
        compiler_params=pltpu.CompilerParams(vmem_limit_bytes=16 * 2**20),
        scratch_shapes=[pltpu.SemaphoreType.DMA((copies,))],
        cost_estimate=pl.CostEstimate(flops=0, bytes_accessed=2 * moved, transcendentals=0),
    )(*sources)


def flipped(me, k):
    out = me
    bit = 1
    while bit <= k:
        if k & bit:
            out = out + bit - 2 * bit * lax.rem(lax.div(out, bit), 2)
        bit *= 2
    return out


LINE_TWO = [(0, 2), (2, 0), (1, 3), (3, 1)]
LINE_ONE = [(0, 1), (1, 0), (2, 3), (3, 2)]
LINE_MIDDLE = [(1, 2), (2, 1)]
LINE_OUT = [(2, 3), (1, 0)]
LINE_IN = [(0, 1), (3, 2)]


def on_line(block, pairs):
    return lax.ppermute(block, "narrow", pairs)


def follow(array, *earlier):
    return lax.optimization_barrier((array, *earlier))[0]


MESH = pl.DeviceIdType.MESH
VMEM = pl.BlockSpec(memory_space=pltpu.VMEM)
DMA = pltpu.SemaphoreType.DMA


def greet(devices):
    barrier = pltpu.get_barrier_semaphore()
    for device in devices:
        pl.semaphore_signal(barrier, inc=1, device_id=device, device_id_type=MESH)
    pl.semaphore_wait(barrier, len(devices))


class Sender:
    def __init__(self, send, recv):
        self.send, self.recv, self.used = send, recv, 0

    def plan(self, src, dst, device):
        n = self.used
        self.used += 1
        return pltpu.make_async_remote_copy(
            src_ref=src, dst_ref=dst, send_sem=self.send.at[n], recv_sem=self.recv.at[n],
            device_id=device, device_id_type=MESH,
        )


def narrow_device(n):
    return {"narrow": n}


def wide_device(n):
    return {"wide": n}


def wide_steps(wide):
    return [1] + list(range(2, wide, 2))


def straight_steps(wide):
    return [k for k in range(2, wide, 2) if k & (k - 1) == 0]


def diagonal_steps(wide):
    return [k for k in range(2, wide, 2) if k & (k - 1)]


def by_device(ref, w):
    return (lambda k: ref.at[flipped(w, k)]), (lambda k, to: ref.at[flipped(w, k)])


class WideGather:
    def __init__(self, sender, w, wide, part, target):
        self.far = list(range(2, wide, 2))
        self.first = {
            k: sender.plan(part(0), target(0, k), wide_device(flipped(w, k)))
            for k in wide_steps(wide)
        }
        sibling = wide_device(flipped(w, 1))
        self.second = {k: sender.plan(part(k), target(k, 1), sibling) for k in self.far}

    def start(self):
        for k in self.far + [1]:
            self.first[k].start()

    def pass_on(self):
        for k in self.far:
            self.first[k].wait_recv()
            self.second[k].start()

    def received(self):
        self.first[1].wait_recv()
        for k in self.far:
            self.second[k].wait_recv()

    def sent(self):
        for copy in list(self.first.values()) + list(self.second.values()):
            copy.wait_send()

    def finish(self):
        self.received()
        self.sent()


def gather_kernel(
    wide, x_ref, in_ref, out_ref, up_ref, grad_ref, slot_ref, in_full, out_full, up_block, grad_far,
    send, recv, local,
):
    w, z = lax.axis_index("wide"), lax.axis_index("narrow")
    line = [flipped(z, k) for k in range(4)]
    sender = Sender(send, recv)
    own = [
        pltpu.make_async_copy(in_ref.at[z], in_full.at[w, z], local.at[0]),
        pltpu.make_async_copy(out_ref, out_full.at[w, z], local.at[1]),
        pltpu.make_async_copy(x_ref, slot_ref.at[z], local.at[2]),
        pltpu.make_async_copy(up_ref.at[w], up_block.at[w], local.at[3]),
    ]
    for copy in own:
        copy.start()
    greet(
        [narrow_device(line[k]) for k in (1, 2, 3)]
        + [wide_device(flipped(w, k)) for k in range(1, wide)]
    )
    ups = [
        sender.plan(up_ref.at[flipped(w, k)], up_block.at[w], wide_device(flipped(w, k)))
        for k in range(1, wide)
    ]
    grads = [
        sender.plan(grad_ref, grad_far.at[n], wide_device(flipped(w, k)))
        for n, k in enumerate(diagonal_steps(wide))
    ]
    is_middle = (z == 1) | (z == 2)
    is_end = (z == 0) | (z == 3)
    ins = [
        sender.plan(in_ref.at[line[k]], in_full.at[w, z], narrow_device(line[k])) for k in (2, 3, 1)
    ]
    outs = [sender.plan(out_ref, out_full.at[w, z], narrow_device(line[k])) for k in (2, 3, 1)]
    two = sender.plan(x_ref, slot_ref.at[z], narrow_device(line[2]))
    one = sender.plan(x_ref, slot_ref.at[z], narrow_device(line[1]))
    middle = sender.plan(x_ref, slot_ref.at[z], narrow_device(line[3]))
    relay = sender.plan(slot_ref.at[line[2]], slot_ref.at[line[2]], narrow_device(line[1]))
    in_wide = WideGather(sender, w, wide, *by_device(in_full, w))
    out_wide = WideGather(sender, w, wide, *by_device(out_full, w))
    for copy in ins + outs + ups:
        copy.start()
    own[0].wait()
    for copy in ins:
        copy.wait_recv()
    in_wide.start()
    two.start()
    one.start()
    own[1].wait()
    for copy in outs:
        copy.wait_recv()
    out_wide.start()
    in_wide.pass_on()
    for copy in grads:
        copy.start()
    two.wait_recv()

    @pl.when(is_middle)
    def _():
        relay.start()
        middle.start()

    out_wide.pass_on()
    one.wait_recv()
    own[2].wait()
    own[3].wait()
    for copy in ups + grads:
        copy.wait()

    @pl.when(is_middle)
    def _():
        middle.wait_recv()
        middle.wait_send()
        relay.wait_send()

    @pl.when(is_end)
    def _():
        relay.wait_recv()

    for copy in ins + outs + [two, one]:
        copy.wait_send()
    in_wide.finish()
    out_wide.finish()


def gather_all(tokens, in_parts, out_weight, up_parts, cotangent):
    narrow, wide = in_parts.shape[0], up_parts.shape[0]
    steps = 10 + 4 * wide
    shapes = [
        (narrow,) + tokens.shape, (wide,) + in_parts.shape, (wide, narrow) + out_weight.shape,
        up_parts.shape, (len(diagonal_steps(wide)),) + cotangent.shape,
    ]
    return pl.pallas_call(
        functools.partial(gather_kernel, wide),
        out_shape=[jax.ShapeDtypeStruct(shape, BF16) for shape in shapes],
        in_specs=[ANY] * 5,
        out_specs=[VMEM] * 5,
        scratch_shapes=[DMA((steps,)), DMA((steps,)), DMA((4,))],
        compiler_params=pltpu.CompilerParams(
            collective_id=0, has_side_effects=True, vmem_limit_bytes=40 * 2**20
        ),
    )(tokens, in_parts, out_weight, up_parts, cotangent)


def exchange_kernel(source, target, steps, *refs):
    count = len(steps)
    src_ref, sides, dst_ref = refs[0], refs[1 : 1 + count], refs[1 + count]
    got = refs[2 + count : 2 + 2 * count]
    send, recv, local = refs[2 + 2 * count :]
    w, z = lax.axis_index("wide"), lax.axis_index("narrow")
    line = [flipped(z, k) for k in range(4)]
    sender = Sender(send, recv)
    own = pltpu.make_async_copy(source(src_ref, z), target(dst_ref, z), local.at[0])
    own.start()
    greet(
        [narrow_device(line[k]) for k in (1, 2, 3)] + [wide_device(flipped(w, k)) for k in steps]
    )
    copies = [
        sender.plan(source(src_ref, line[k]), target(dst_ref, z), narrow_device(line[k]))
        for k in (2, 3, 1)
    ]
    copies += [
        sender.plan(sides[n], got[n], wide_device(flipped(w, k))) for n, k in enumerate(steps)
    ]
    for copy in copies:
        copy.start()
    own.wait()
    for copy in copies:
        copy.wait()


def exchange(array, source, target, shape, steps, sides, collective_id):
    count = len(steps) + 4
    return pl.pallas_call(
        functools.partial(exchange_kernel, source, target, steps),
        out_shape=[jax.ShapeDtypeStruct(shape, array.dtype)]
        + [jax.ShapeDtypeStruct(side.shape, side.dtype) for side in sides],
        in_specs=[ANY] * (1 + len(sides)),
        out_specs=[VMEM] * (1 + len(sides)),
        scratch_shapes=[DMA((count,)), DMA((count,)), DMA((1,))],
        compiler_params=pltpu.CompilerParams(
            collective_id=collective_id, has_side_effects=True, vmem_limit_bytes=16 * 2**20
        ),
    )(array, *sides)


def place_of(k, wide):
    return k // 2 + (k % 2) * (wide // 2)


def rows_kernel(wide, *refs):
    half = wide // 2
    grads = refs[:half]
    (
        src_ref, up_ref, up_two, up_one, down_ref, down_two, down_one, dst_ref, grad_ref, up_full,
        down_full, send, recv, local,
    ) = refs[half:]
    w, z = lax.axis_index("wide"), lax.axis_index("narrow")
    line = [flipped(z, k) for k in range(4)]
    is_middle = (z == 1) | (z == 2)
    is_end = (z == 0) | (z == 3)
    sender = Sender(send, recv)
    up_at = lambda n: up_full.at[:, n]
    down_at = lambda n: down_full.at[n]
    moves = [
        (src_ref, dst_ref.at[0]),
        (down_ref, down_at(z)), (down_two, down_at(line[2])), (down_one, down_at(line[1])),
        (up_ref, up_at(z)), (up_two, up_at(line[2])), (up_one, up_at(line[1])),
    ] + [(grads[n], grad_ref.at[n]) for n in range(half)]
    own = [pltpu.make_async_copy(src, dst, local.at[n]) for n, (src, dst) in enumerate(moves)]
    for copy in own:
        copy.start()
    greet(
        [wide_device(flipped(w, k)) for k in wide_steps(wide)]
        + [narrow_device(line[k]) for k in (1, 3)]
    )
    gather = WideGather(
        sender, w, wide, lambda k: src_ref if k == 0 else dst_ref.at[place_of(k, wide)],
        lambda k, to: dst_ref.at[place_of(k ^ to, wide)],
    )
    middles = [
        sender.plan(up_ref, up_at(z), narrow_device(line[3])),
        sender.plan(down_ref, down_at(z), narrow_device(line[3])),
    ]
    relays = [
        sender.plan(up_two, up_at(line[2]), narrow_device(line[1])),
        sender.plan(down_two, down_at(line[2]), narrow_device(line[1])),
    ]
    gather.start()

    @pl.when(is_middle)
    def _():
        for copy in middles + relays:
            copy.start()

    sibling = wide_device(flipped(w, 1))
    copies = [sender.plan(grads[n], grad_ref.at[half + n], sibling) for n in range(half)]
    for copy in copies:
        copy.start()
    gather.pass_on()

    @pl.when(is_middle)
    def _():
        for copy in middles:
            copy.wait()
        for copy in relays:
            copy.wait_send()

    @pl.when(is_end)
    def _():
        for copy in relays:
            copy.wait_recv()

    for copy in own + copies:
        copy.wait()
    gather.finish()


def gather_rows(array, grads, ups, downs, collective_id):
    half = len(grads)
    wide = 2 * half
    whole = jax.ShapeDtypeStruct((wide,) + array.shape, array.dtype)
    up_shape = ups[0].shape
    full = jax.ShapeDtypeStruct((up_shape[0], 4) + up_shape[1:], BF16)
    return pl.pallas_call(
        functools.partial(rows_kernel, wide),
        out_shape=[whole, whole, full, jax.ShapeDtypeStruct((4,) + downs[0].shape, BF16)],
        in_specs=[ANY] * (half + 7),
        out_specs=[VMEM, ANY if wide > 8 else VMEM, VMEM, VMEM],
        scratch_shapes=[DMA((2 * wide + 4,)), DMA((2 * wide + 4,)), DMA((half + 7,))],
        compiler_params=pltpu.CompilerParams(
            collective_id=collective_id, has_side_effects=True, vmem_limit_bytes=48 * 2**20
        ),
    )(*grads, array, *ups, *downs)


def hidden_kernel(
    half, normed_ref, grad_ref, up_ref, down_ref, hidden_ref, mid_ref, even_ref, odd_ref, branch_ref
):
    size = down_ref.shape[0]
    gate_up = dot_f32(normed_ref[...], up_ref[...])
    grad_hidden = dot_f32(grad_ref[...], down_ref[...], ((1,), (1,)))
    gate, up = gate_up[:, :size], gate_up[:, size:]
    opened = jax.nn.sigmoid(gate)
    acted = gate * opened
    hidden_ref[...] = (acted * up).astype(BF16)
    mid_ref[:, :size] = (grad_hidden * up * (opened * (1.0 + gate * (1.0 - opened)))).astype(BF16)
    mid_ref[:, size:] = (grad_hidden * acted).astype(BF16)
    grad_normed = dot_f32(mid_ref[...], up_ref[...], ((1,), (1,))).astype(BF16)
    branch_ref[...] = dot_f32(hidden_ref[...], down_ref[...]).astype(BF16)
    step = pl.program_id(0)

    @pl.when(step < half)
    def _():
        even_ref[...] = grad_normed

    @pl.when(step >= half)
    def _():
        odd_ref[...] = grad_normed


def feed_forward(normed, grad, up_full, down_full, rows):
    total, width = normed.shape
    blocks = total // rows
    half = blocks // 2
    size = down_full.shape[0]
    row_block = lambda columns: pl.BlockSpec((rows, columns), lambda i: (i, 0))
    fixed = lambda array: pl.BlockSpec(array.shape, lambda i: (0, 0))
    return pl.pallas_call(
        functools.partial(hidden_kernel, half),
        grid=(blocks,),
        in_specs=[row_block(width), row_block(width), fixed(up_full), fixed(down_full)],
        out_specs=[
            row_block(size), row_block(2 * size),
            pl.BlockSpec((rows, width), lambda i: (jnp.minimum(i, half - 1), 0)),
            pl.BlockSpec((rows, width), lambda i: (jnp.maximum(i - half, 0), 0)),
            row_block(width),
        ],
        out_shape=[
            jax.ShapeDtypeStruct((total, size), BF16),
            jax.ShapeDtypeStruct((total, 2 * size), BF16),
            jax.ShapeDtypeStruct((total // 2, width), BF16),
            jax.ShapeDtypeStruct((total // 2, width), BF16),
            jax.ShapeDtypeStruct((total, width), BF16),
        ],
        compiler_params=pltpu.CompilerParams(vmem_limit_bytes=48 * 2**20),
    )(normed, grad, up_full, down_full)


def middle_kernel(
    wide, even_ref, got_ref, branch_ref, up_ref, down_ref, norm_sum, branch_sum, up_src, down_src,
    up_one, down_one, up_acc, down_acc, core_buf, own_buf, far_buf, branch_buf, up_join, up_mid,
    down_join, down_mid, up_own, down_own, send, recv, local,
):
    w, z = lax.axis_index("wide"), lax.axis_index("narrow")
    line = [flipped(z, k) for k in range(4)]
    half = wide // 2
    unit = up_src.shape[1]
    part = down_src.shape[1]
    sender = Sender(send, recv)
    is_middle = (z == 1) | (z == 2)
    is_end = (z == 0) | (z == 3)

    def up_share(n):
        return up_ref.at[:, pl.ds(pl.multiple_of(n * unit, unit), unit)]

    def down_share(n):
        return down_ref.at[:, pl.ds(pl.multiple_of(n * part, part), part)]

    moves = [
        (up_share(line[2]), up_src), (down_share(line[2]), down_src),
        (up_share(z), up_own), (down_share(z), down_own),
        (up_share(line[1]), up_one), (down_share(line[1]), down_one),
    ]
    moves += [(got_ref.at[n], core_buf.at[n]) for n in range(half)]
    moves += [(even_ref.at[n], own_buf.at[n]) for n in range(half)]
    pairs = branch_sum.shape[0]
    moves += [(branch_ref.at[n], branch_sum.at[n]) for n in range(pairs)]
    own = [pltpu.make_async_copy(src, dst, local.at[n]) for n, (src, dst) in enumerate(moves)]
    for copy in own:
        copy.start()
    greet(
        [wide_device(flipped(w, k)) for k in wide_steps(wide)]
        + [narrow_device(line[k]) for k in (1, 3)]
    )
    sibling = wide_device(flipped(w, 1))
    far = [
        sender.plan(own_buf.at[n], far_buf.at[n - 1], wide_device(flipped(w, 2 * n)))
        for n in range(1, half)
    ]
    branch_core = [
        sender.plan(branch_ref.at[pairs + n], branch_buf.at[n], sibling) for n in range(pairs)
    ]
    joins = [
        sender.plan(up_share(line[3]), up_join, narrow_device(line[1])),
        sender.plan(down_share(line[3]), down_join, narrow_device(line[1])),
    ]
    mids = [
        sender.plan(up_share(line[3]), up_mid, narrow_device(line[3])),
        sender.plan(down_share(line[3]), down_mid, narrow_device(line[3])),
    ]
    order = list(range(1, half)) + [0]

    @pl.when(is_end)
    def _():
        for copy in joins:
            copy.start()

    @pl.when(is_middle)
    def _():
        for copy in mids:
            copy.start()

    for n in order:
        own[6 + n].wait()
        own[6 + half + n].wait()
        total = own_buf[n].astype(F32) + core_buf[n].astype(F32)
        own_buf[n] = total.astype(BF16)
        if n > 0:
            far[n - 1].start()
    for copy in branch_core:
        copy.start()
    for n in range(pairs):
        branch_core[n].wait_recv()
        own[6 + 2 * half + n].wait()
        total = branch_sum[n].astype(F32) + branch_buf[n].astype(F32)
        branch_sum[n] = total.astype(BF16)
    for n in range(6):
        own[n].wait()

    @pl.when(is_middle)
    def _():
        for copy in joins:
            copy.wait_recv()
        up_src[...] = (up_src[...].astype(F32) + up_join[...].astype(F32)).astype(BF16)
        down_src[...] = (down_src[...].astype(F32) + down_join[...].astype(F32)).astype(BF16)

    total = own_buf[0].astype(F32)
    for n in range(1, half):
        far[n - 1].wait_recv()
        total = total + far_buf[n - 1].astype(F32)
    norm_sum[...] = total
    up_acc[...] = up_own[...].astype(F32)
    down_acc[...] = down_own[...].astype(F32)

    @pl.when(is_middle)
    def _():
        for copy in mids:
            copy.wait()
        up_acc[...] += up_mid[...].astype(F32)
        down_acc[...] += down_mid[...].astype(F32)

    @pl.when(is_end)
    def _():
        for copy in joins:
            copy.wait_send()

    for copy in far + branch_core:
        copy.wait_send()


def middle_sums(even, got, branch, grad_up, grad_down, collective_id):
    half, rows, width = even.shape
    wide = 2 * half
    unit, part = grad_up.shape[1] // 4, grad_down.shape[1] // 4
    up_shape, down_shape = (grad_up.shape[0], unit), (grad_down.shape[0], part)
    steps = 4 * half + 6
    rows_buf = pltpu.VMEM((half, rows, width), BF16)
    pairs = branch.shape[0] // 2
    return pl.pallas_call(
        functools.partial(middle_kernel, wide),
        out_shape=[
            jax.ShapeDtypeStruct((rows, width), F32),
            jax.ShapeDtypeStruct((pairs,) + branch.shape[1:], BF16),
            *[jax.ShapeDtypeStruct(up_shape, BF16), jax.ShapeDtypeStruct(down_shape, BF16)] * 2,
            jax.ShapeDtypeStruct(up_shape, F32),
            jax.ShapeDtypeStruct(down_shape, F32),
        ],
        in_specs=[ANY] * 5,
        out_specs=[VMEM] * 8,
        scratch_shapes=[
            rows_buf, rows_buf, pltpu.VMEM((half - 1, rows, width), BF16),
            pltpu.VMEM((pairs,) + branch.shape[1:], BF16),
            *[pltpu.VMEM(up_shape, BF16)] * 2, *[pltpu.VMEM(down_shape, BF16)] * 2,
            pltpu.VMEM(up_shape, BF16), pltpu.VMEM(down_shape, BF16),
            DMA((steps,)), DMA((steps,)), DMA((6 + 3 * half,)),
        ],
        compiler_params=pltpu.CompilerParams(
            collective_id=collective_id, has_side_effects=True, vmem_limit_bytes=58 * 2**20
        ),
    )(even, got, branch, grad_up, grad_down)


def last_kernel(
    wide, rows, own_width, norm_ref, in_ref, out_ref, up_ref, branch_ref, norm_sum, in_got, out_sum,
    up_got, branch_got,
    join_buf, one_buf, mid_buf, two_buf, two_src, own_norm, in_core, in_own, in_far, in_sum,
    out_core, out_own, out_far, out_low, out_buf, send, recv, local,
):
    w, z = lax.axis_index("wide"), lax.axis_index("narrow")
    line = [flipped(z, k) for k in range(4)]
    half = wide // 2
    unit = up_ref.shape[1]
    wide_rows = up_got.shape[0]
    sender = Sender(send, recv)
    is_middle = (z == 1) | (z == 2)
    is_end = (z == 0) | (z == 3)

    def norm_block(n):
        return norm_ref.at[pl.ds(pl.multiple_of(n * rows, rows), rows), :]

    def out_columns(n):
        return pl.ds(pl.multiple_of(n * own_width, LANES), own_width)

    def up_rows(n):
        return up_ref.at[pl.ds(pl.multiple_of(n * wide_rows, 16), wide_rows), :]

    def up_columns(n):
        return up_got.at[:, pl.ds(pl.multiple_of(n * unit, LANES), unit)]

    def section(n):
        return in_sum.at[:, pl.ds(pl.multiple_of(n * own_width, LANES), own_width + LANES)]

    moves = [
        (norm_block(line[2]), two_src), (norm_block(z), own_norm), (up_rows(w), up_columns(w)),
    ]
    moves += [(in_ref.at[flipped(w, 2 * n)], in_own.at[n]) for n in range(half)]
    moves += [(out_ref.at[flipped(w, 2 * n)], out_own.at[n]) for n in range(half)]
    own = [pltpu.make_async_copy(src, dst, local.at[n]) for n, (src, dst) in enumerate(moves)]
    for copy in own:
        copy.start()
    greet(
        [narrow_device(line[k]) for k in (1, 2, 3)]
        + [wide_device(flipped(w, k)) for k in range(1, wide)]
    )
    sibling = wide_device(flipped(w, 1))

    def over_wide(ref, core_buf, own_buf, far_buf):
        core = [
            sender.plan(ref.at[flipped(w, 2 * n + 1)], core_buf.at[n], sibling)
            for n in range(half)
        ]
        far = [
            sender.plan(own_buf.at[n], far_buf.at[n - 1], wide_device(flipped(w, 2 * n)))
            for n in range(1, half)
        ]
        return core, far

    joined = sender.plan(norm_block(line[3]), join_buf, narrow_device(line[1]))
    one = sender.plan(norm_block(line[1]), one_buf, narrow_device(line[1]))
    middle = sender.plan(norm_block(line[3]), mid_buf, narrow_device(line[3]))
    two = sender.plan(two_src, two_buf, narrow_device(line[2]))
    in_steps = over_wide(in_ref, in_core, in_own, in_far)
    out_steps = over_wide(out_ref, out_core, out_own, out_far)
    sections = [
        sender.plan(section(line[k]), in_got.at[z], narrow_device(line[k])) for k in (2, 3, 1)
    ]
    outs = [
        sender.plan(out_low.at[:, out_columns(line[k])], out_buf.at[k - 1], narrow_device(line[k]))
        for k in (1, 2, 3)
    ]
    ups = [
        sender.plan(up_rows(flipped(w, k)), up_columns(w), wide_device(flipped(w, k)))
        for k in range(1, wide)
    ]
    branches = [
        sender.plan(branch_ref.at[n], branch_got.at[n], wide_device(flipped(w, k)))
        for n, k in enumerate(diagonal_steps(wide))
    ]
    order = list(range(1, half)) + [0]
    for core in (in_steps[0], out_steps[0]):
        for n in order:
            core[n].start()

    @pl.when(is_end)
    def _():
        joined.start()

    @pl.when(is_middle)
    def _():
        middle.start()

    def between_cores(steps, core_buf, own_buf, first):
        core, far = steps
        for n in order:
            core[n].wait_recv()
            own[first + n].wait()
            total = own_buf[n].astype(F32) + core_buf[n].astype(F32)
            own_buf[n] = total.astype(BF16)
            if n > 0:
                far[n - 1].start()

    def between_chips(steps, own_buf, far_buf):
        total = own_buf[0].astype(F32)
        for n in range(1, half):
            steps[1][n - 1].wait_recv()
            total = total + far_buf[n - 1].astype(F32)
        return total.astype(BF16)

    between_cores(in_steps, in_core, in_own, 3)
    own[0].wait()

    @pl.when(is_middle)
    def _():
        joined.wait_recv()
        two_src[...] = (two_src[...].astype(F32) + join_buf[...].astype(F32)).astype(BF16)

    two.start()
    one.start()
    between_cores(out_steps, out_core, out_own, 3 + half)
    for copy in branches:
        copy.start()
    in_sum[...] = between_chips(in_steps, in_own, in_far)
    mine = pltpu.make_async_copy(section(z), in_got.at[z], local.at[3 + 2 * half])
    mine.start()
    for copy in sections:
        copy.start()
    out_low[...] = between_chips(out_steps, out_own, out_far)
    for copy in outs + ups:
        copy.start()
    own[1].wait()
    own[2].wait()
    one.wait_recv()
    norm_sum[...] = own_norm[...].astype(F32) + one_buf[...].astype(F32)

    @pl.when(is_middle)
    def _():
        middle.wait()
        norm_sum[...] += mid_buf[...].astype(F32)

    two.wait_recv()
    norm_sum[...] += two_buf[...].astype(F32)
    total = out_low[:, out_columns(z)].astype(F32)
    for n in range(3):
        outs[n].wait_recv()
        total = total + out_buf[n].astype(F32)
    out_sum[...] = total
    for copy in sections + ups + branches:
        copy.wait_recv()
    mine.wait()

    @pl.when(is_end)
    def _():
        joined.wait_send()

    sent = [one, two] + in_steps[0] + in_steps[1] + out_steps[0] + out_steps[1]
    for copy in sent + sections + outs + ups + branches:
        copy.wait_send()


def last_transfers(norm_part, in_part, out_part, up_part, branches, rows, own_width, collective_id):
    wide, wide_rows, columns = in_part.shape
    half = wide // 2
    width = norm_part.shape[1]
    unit = up_part.shape[1]
    steps = 4 + 4 * half + 6 + 2 * wide
    block = pltpu.VMEM((rows, width), BF16)
    sums = lambda size: [
        pltpu.VMEM((half, wide_rows, size), BF16), pltpu.VMEM((half, wide_rows, size), BF16),
        pltpu.VMEM((half - 1, wide_rows, size), BF16), pltpu.VMEM((wide_rows, size), BF16),
    ]
    return pl.pallas_call(
        functools.partial(last_kernel, wide, rows, own_width),
        out_shape=[
            jax.ShapeDtypeStruct((rows, width), F32),
            jax.ShapeDtypeStruct((4, wide_rows, own_width + LANES), BF16),
            jax.ShapeDtypeStruct((wide_rows, own_width), F32),
            jax.ShapeDtypeStruct((wide_rows, wide * unit), BF16),
            jax.ShapeDtypeStruct(branches.shape, BF16),
        ],
        in_specs=[ANY] * 5,
        out_specs=[VMEM] * 5,
        scratch_shapes=[
            *[block] * 6, *sums(columns), *sums(width),
            pltpu.VMEM((3, wide_rows, own_width), BF16),
            DMA((steps,)), DMA((steps,)), DMA((4 + 2 * half,)),
        ],
        compiler_params=pltpu.CompilerParams(
            collective_id=collective_id, has_side_effects=True, vmem_limit_bytes=48 * 2**20
        ),
    )(norm_part, in_part, out_part, up_part, branches)


def total_kernel(wide, v_ref, out_ref, narrow_buf, wide_buf, sum_buf, send, recv):
    w, z = lax.axis_index("wide"), lax.axis_index("narrow")
    greet(
        [narrow_device(flipped(z, k)) for k in (1, 2, 3)]
        + [wide_device(flipped(w, k)) for k in range(1, wide)]
    )
    sender = Sender(send, recv)
    first = [
        sender.plan(v_ref, narrow_buf.at[z], narrow_device(flipped(z, k))) for k in (1, 2, 3)
    ]
    second = [
        sender.plan(sum_buf, wide_buf.at[w], wide_device(flipped(w, k))) for k in range(1, wide)
    ]
    for copy in first:
        copy.start()
    narrow_buf[z] = v_ref[...]
    for copy in first:
        copy.wait()
    sum_buf[...] = narrow_buf[0] + narrow_buf[1] + narrow_buf[2] + narrow_buf[3]
    for copy in second:
        copy.start()
    wide_buf[w] = sum_buf[...]
    for copy in second:
        copy.wait()
    total = wide_buf[0]
    for n in range(1, wide):
        total = total + wide_buf[n]
    out_ref[...] = total


def total_of(values, wide, collective_id):
    size = values.shape[0]
    height = -(-size // (8 * LANES)) * 8
    padded = jnp.pad(values, (0, height * LANES - size)).reshape(height, LANES)
    total = pl.pallas_call(
        functools.partial(total_kernel, wide),
        out_shape=jax.ShapeDtypeStruct(padded.shape, F32),
        in_specs=[VMEM],
        out_specs=VMEM,
        scratch_shapes=[
            pltpu.VMEM((4,) + padded.shape, F32),
            pltpu.VMEM((wide,) + padded.shape, F32),
            pltpu.VMEM(padded.shape, F32),
            DMA((wide + 2,)), DMA((wide + 2,)),
        ],
        compiler_params=pltpu.CompilerParams(collective_id=collective_id, has_side_effects=True),
    )(padded)
    return total.reshape(-1)[:size]


def rms_factor(values):
    return lax.rsqrt(jnp.mean(values * values, axis=-1, keepdims=True) + EPSILON)


def rms_back(values, gain, grad):
    factor = rms_factor(values)
    normed = values * factor
    grad_gain = jnp.sum(grad * normed, axis=0)
    scaled = grad * gain
    inner = jnp.mean(scaled * normed, axis=-1, keepdims=True)
    return (factor * (scaled - normed * inner), grad_gain)


def log_sigmoid(v):
    return jnp.minimum(v, 0.0) - jnp.log1p(jnp.exp(-jnp.abs(v)))


def iota(shape, dim):
    return lax.broadcasted_iota(jnp.int32, shape, dim)


def running_sum(v, reverse):
    rows = v.shape[0]
    index = iota(v.shape, 0)
    step = 1
    while step < rows:
        if reverse:
            v = v + jnp.where(index < rows - step, pltpu.roll(v, rows - step, 0), 0.0)
        else:
            v = v + jnp.where(index >= step, pltpu.roll(v, step, 0), 0.0)
        step *= 2
    return v


def half_of(lane, head_size):
    return (lane >= head_size).astype(jnp.int32)


def spread(first, head_size):
    row, lane = iota((LANES, LANES), 0), iota((LANES, LANES), 1)
    return row == first + half_of(lane, head_size)


def collect(first, head_size):
    row, lane = iota((LANES, LANES), 0), iota((LANES, LANES), 1)
    return lane == first + half_of(row, head_size)


def same_head(head_size):
    row, lane = iota((LANES, LANES), 0), iota((LANES, LANES), 1)
    return (half_of(row, head_size) == half_of(lane, head_size)).astype(F32)


def exact_dot(left, right):
    return lax.dot_general(
        left, right, (((1,), (0,)), ((), ())), precision=EXACT, preferred_element_type=F32
    )


def head_mean(v, head_size):
    return exact_dot(v, same_head(head_size)) * (1.0 / head_size)


def prologue(pair, heads, head_size, q_ref, k_ref, v_ref, small_low, cont):
    spot = lambda group: spread(group * heads + 2 * pair, head_size).astype(BF16)
    key_mix = jax.nn.sigmoid(dot_f32(small_low, spot(1)))
    value_mix = jax.nn.sigmoid(dot_f32(small_low, spot(2)))
    queries = q_ref[...].astype(BF16).astype(F32)
    keys = k_ref[...].astype(BF16).astype(F32)
    values = v_ref[...].astype(BF16).astype(F32)
    key_step = pltpu.roll(keys, 1, 0) * cont - keys
    value_step = pltpu.roll(values, 1, 0) * cont - values
    shifted = keys + key_mix * key_step
    value_low = (values + value_mix * value_step).astype(BF16)
    query_factor = lax.rsqrt(head_mean(queries * queries, head_size) + EPSILON)
    key_factor = lax.rsqrt(head_mean(shifted * shifted, head_size) + EPSILON)
    return (
        queries * query_factor,
        shifted * key_factor,
        value_low,
        query_factor,
        key_factor,
        key_mix,
        value_mix,
        key_step,
        value_step,
    )


def small_columns(small_ref, bias_ref):
    return (small_ref[...] + bias_ref[0:1, :]).astype(BF16)


def decay_of(small_low, cont):
    return running_sum(log_sigmoid(small_low.astype(F32)) - SEPARATE * (1.0 - cont), False)


def forward_pair(
    pair, heads, head_size, block, q_ref, k_ref, v_ref, gate_ref, small_low, cont, decay_all,
    mixed_ref, att_ref, log_ref,
):
    query, key, value_low, *unused = prologue(
        pair, heads, head_size, q_ref, k_ref, v_ref, small_low, cont
    )
    rows = query.shape[0]
    query = query.astype(BF16) * BF16(head_size**-0.5)
    key = key.astype(BF16)
    decay = exact_dot(decay_all, spread(2 * pair, head_size).astype(F32))
    decay_rows = decay.T
    lane = iota((1, LANES), 1)
    ones = jnp.ones((rows, LANES), BF16)
    value_wide = jnp.concatenate([value_low, ones], axis=1)
    for i in range(rows // block):
        lo, hi = i * block, (i + 1) * block
        row_index = iota((block, hi), 0) + lo
        visible = iota((block, hi), 1) <= row_index
        outs, sums = [], []
        for head in range(2):
            mine = (lane >= head_size) if head else (lane < head_size)
            at = head * head_size
            left = jnp.where(mine, query[lo:hi], BF16(0.0))
            scores = dot_f32(left, key[:hi], ((1,), (1,)))
            scores = scores + decay[lo:hi, at : at + 1] - decay_rows[at : at + 1, :hi]
            weights = jnp.where(visible, jnp.exp(scores), 0.0).astype(BF16)
            both = dot_f32(weights, value_wide[:hi])
            outs.append(both[:, :LANES])
            sums.append(both[:, LANES:])
        first = lane < head_size
        total = jnp.where(first, sums[0], sums[1])
        attended = (jnp.where(first, outs[0], outs[1]) / total).astype(BF16)
        att_ref[lo:hi, :] = attended
        log_ref[lo:hi, :] = jnp.log(total)
        opened = jax.nn.sigmoid(gate_ref[lo:hi, :])
        mixed_ref[lo:hi, :] = (attended.astype(F32) * opened).astype(BF16)


def forward_kernel(
    heads, head_size, block, q_ref, k_ref, v_ref, gate_ref, small_ref, bias_ref, cont_ref,
    mixed_ref, att_ref, log_ref, decay_scr,
):
    pair = pl.program_id(0)
    cont = cont_ref[...]
    small_low = small_columns(small_ref, bias_ref)

    @pl.when(pair == 0)
    def _():
        decay_scr[...] = decay_of(small_low, cont)

    forward_pair(
        pair, heads, head_size, block, q_ref, k_ref, v_ref, gate_ref, small_low, cont,
        decay_scr[...], mixed_ref, att_ref, log_ref,
    )


def share_of(ref, like, n):
    size = like.shape[1]
    if ref.shape[1] == size:
        return ref
    return ref.at[:, pl.ds(pl.multiple_of(n * size, size), size)]


def backward_kernel(
    heads, head_size, block, q_ref, k_ref, v_ref, gate_ref, small_ref, bias_ref, cont_ref,
    att_ref, log_ref, grad_ref, up_src, down_src, up_one, down_one, out_ref, bias_grad_ref,
    up_two_got, down_two_got, up_one_got, down_one_got, decay_scr, small_scr, dq_scr, send, recv,
):
    pair = pl.program_id(0)
    z = lax.axis_index("narrow")
    sender = Sender(send, recv)
    copies = [
        sender.plan(up_src, up_two_got, narrow_device(flipped(z, 2))),
        sender.plan(down_src, down_two_got, narrow_device(flipped(z, 2))),
        sender.plan(share_of(up_one, up_src, flipped(z, 1)), up_one_got, narrow_device(flipped(z, 1))),
        sender.plan(
            share_of(down_one, down_src, flipped(z, 1)), down_one_got, narrow_device(flipped(z, 1))
        ),
    ]

    @pl.when(pair == 0)
    def _():
        greet([narrow_device(flipped(z, 1)), narrow_device(flipped(z, 2))])
        for copy in copies:
            copy.start()

    cont = cont_ref[...]
    small_low = small_columns(small_ref, bias_ref)
    rows = cont.shape[0]
    width = heads * head_size

    @pl.when(pair == 0)
    def _():
        decay_scr[...] = decay_of(small_low, cont)
        small_scr[...] = jnp.zeros_like(small_scr)

    (
        query_norm, key_norm, value_low, query_factor, key_factor, key_mix, value_mix, key_step,
        value_step,
    ) = prologue(pair, heads, head_size, q_ref, k_ref, v_ref, small_low, cont)
    query = query_norm.astype(BF16) * BF16(head_size**-0.5)
    key = key_norm.astype(BF16)
    opened = jax.nn.sigmoid(gate_ref[...])
    attended = att_ref[...].astype(F32)
    grad_mixed = grad_ref[...].astype(F32)
    grad_low = (grad_mixed * opened).astype(BF16)
    grad_gate = grad_mixed * attended * opened * (1.0 - opened)

    def columns(group):
        at = group * width + pair * LANES
        return pl.ds(pl.multiple_of(at, LANES), LANES)

    out_ref[:, columns(3)] = grad_gate.astype(BF16)
    inner = exact_dot(grad_low.astype(F32) * attended, same_head(head_size))
    decay = exact_dot(decay_scr[...], spread(2 * pair, head_size).astype(F32))
    level_rows = (decay - log_ref[...]).T
    inner_rows = inner.T
    lane = iota((1, LANES), 1)
    ones = jnp.ones((rows, LANES), BF16)
    query_wide = jnp.concatenate([query, ones], axis=1)
    key_wide = jnp.concatenate([key, ones], axis=1)
    key_parts, value_parts, query_parts = [], [], []
    for head in range(2):
        mine = (lane >= head_size) if head else (lane < head_size)
        at = head * head_size
        keys_out, values_out = [], []
        for j in range(rows // block):
            lo, hi = j * block, (j + 1) * block
            span = rows - lo
            visible = iota((block, span), 0) <= iota((block, span), 1)
            scores = dot_f32(
                jnp.where(mine, key[lo:hi], BF16(0.0)), query[lo:], ((1,), (1,))
            )
            scores = scores + level_rows[at : at + 1, lo:] - decay[lo:hi, at : at + 1]
            probs = jnp.where(visible, jnp.exp(scores), 0.0)
            grad_probs = dot_f32(
                jnp.where(mine, value_low[lo:hi], BF16(0.0)), grad_low[lo:], ((1,), (1,))
            )
            grad_scores = (probs * (grad_probs - inner_rows[at : at + 1, lo:])).astype(BF16)
            values_out.append(dot_f32(probs.astype(BF16), grad_low[lo:]))
            keys_out.append(dot_f32(grad_scores, query_wide[lo:]))
            part = dot_f32(grad_scores, key_wide[lo:hi], ((0,), (0,)))
            if j == 0:
                dq_scr[...] = part
            else:
                dq_scr[lo:, :] += part
        key_parts.append(jnp.concatenate(keys_out, axis=0))
        value_parts.append(jnp.concatenate(values_out, axis=0))
        query_parts.append(dq_scr[...])
    first = lane < head_size

    def join(parts):
        return jnp.where(first, parts[0], parts[1])

    grad_query = join([p[:, :LANES] for p in query_parts]) * head_size**-0.5
    grad_key = join([p[:, :LANES] for p in key_parts])
    grad_value = join(value_parts)
    grad_decay = join([p[:, LANES:] for p in query_parts]) - join([p[:, LANES:] for p in key_parts])

    def norm_back(grad, normed, factor):
        return factor * (grad - normed * head_mean(grad * normed, head_size))

    def shift_back(grad, mix):
        return grad * (1.0 - mix) + pltpu.roll(grad * mix * cont, rows - 1, 0)

    grad_query = norm_back(grad_query, query_norm, query_factor)
    grad_shifted = norm_back(grad_key, key_norm, key_factor)
    out_ref[:, columns(0)] = grad_query.astype(BF16)
    out_ref[:, columns(1)] = shift_back(grad_shifted, key_mix).astype(BF16)
    out_ref[:, columns(2)] = shift_back(grad_value, value_mix).astype(BF16)
    key_logit = grad_shifted * key_step * key_mix * (1.0 - key_mix)
    value_logit = grad_value * value_step * value_mix * (1.0 - value_mix)
    single = (lax.rem(lane, head_size) == 0).astype(F32)
    small_scr[...] += (
        exact_dot(grad_decay * single, collect(2 * pair, head_size).astype(F32))
        + exact_dot(key_logit, collect(heads + 2 * pair, head_size).astype(F32))
        + exact_dot(value_logit, collect(2 * heads + 2 * pair, head_size).astype(F32))
    )

    @pl.when(pair == pl.num_programs(0) - 1)
    def _():
        grads = small_scr[...]
        forget = running_sum(grads, True) * jax.nn.sigmoid(-small_low.astype(F32))
        result = jnp.where(lane < heads, forget, grads)
        out_ref[:, 4 * width :] = result.astype(BF16)
        bias_grad_ref[...] = jnp.broadcast_to(
            jnp.sum(result, axis=0, keepdims=True), bias_grad_ref.shape
        )
        for copy in copies:
            copy.wait()


def attention_specs(rows, pairs):
    def block_at(group):
        return pl.BlockSpec((rows, LANES), lambda p: (0, group * pairs + p))

    def fixed(height, column=0):
        return pl.BlockSpec((height, LANES), lambda p: (0, column))

    base = [block_at(0), block_at(1), block_at(2), block_at(3), fixed(rows, 4 * pairs), fixed(8), fixed(rows)]
    return base, pl.BlockSpec((rows, LANES), lambda p: (0, p))


def attention_forward(projected, bias, cont, heads, head_size, block):
    rows = projected.shape[0]
    pairs = heads * head_size // LANES
    base, own = attention_specs(rows, pairs)
    wide = jax.ShapeDtypeStruct((rows, heads * head_size), BF16)
    return pl.pallas_call(
        functools.partial(forward_kernel, heads, head_size, block),
        grid=(pairs,),
        in_specs=base,
        out_specs=[own] * 3,
        out_shape=[wide, wide, jax.ShapeDtypeStruct(wide.shape, F32)],
        scratch_shapes=[pltpu.VMEM((rows, LANES), F32)],
        compiler_params=pltpu.CompilerParams(vmem_limit_bytes=48 * 2**20),
    )(*([projected] * 5), bias, cont)


def attention_backward(
    projected, bias, cont, attended, logs, grad, shares, heads, head_size, block, collective_id
):
    rows = projected.shape[0]
    pairs = heads * head_size // LANES
    base, own = attention_specs(rows, pairs)
    columns = 4 * heads * head_size + LANES
    return pl.pallas_call(
        functools.partial(backward_kernel, heads, head_size, block),
        grid=(pairs,),
        in_specs=base + [own] * 3 + [ANY] * 4,
        out_specs=[
            pl.BlockSpec((rows, columns), lambda p: (0, 0)),
            pl.BlockSpec((8, LANES), lambda p: (0, 0)),
        ]
        + [ANY] * 4,
        out_shape=[
            jax.ShapeDtypeStruct((rows, columns), BF16),
            jax.ShapeDtypeStruct((8, LANES), F32),
        ]
        + [jax.ShapeDtypeStruct(share.shape, BF16) for share in shares[:2] * 2],
        scratch_shapes=[
            pltpu.VMEM((rows, LANES), F32),
            pltpu.VMEM((rows, LANES), F32),
            pltpu.VMEM((rows, 2 * LANES), F32),
            DMA((4,)),
            DMA((4,)),
        ],
        compiler_params=pltpu.CompilerParams(
            collective_id=collective_id, has_side_effects=True, vmem_limit_bytes=56 * 2**20
        ),
    )(*([projected] * 5), bias, cont, attended, logs, grad, *shares)


def first_kernel(
    wide, heads, head_size, block, x_ref, in_ref, out_ref, up_ref, grad_ref, down_ref, gain_one_ref,
    gain_two_ref, bias_ref, cont_ref, normed_out, in_out, out_out, proj_out, att_ref, log_ref,
    mixed_rows, middle_ref, normed_two_ref, up_out, up_two, up_one, down_got, grad_got, slot, in_buf,
    out_buf, up_buf, normed, proj, mixed, decay_scr, send, recv, local,
):
    w, z = lax.axis_index("wide"), lax.axis_index("narrow")
    line = [flipped(z, k) for k in range(4)]
    rows, width = x_ref.shape
    own_width = heads * head_size
    part_rows = out_ref.shape[0]
    is_middle = (z == 1) | (z == 2)
    is_end = (z == 0) | (z == 3)
    sender = Sender(send, recv)
    used = []

    def local_copy(src, dst):
        copy = pltpu.make_async_copy(src, dst, local.at[len(used)])
        used.append(copy)
        return copy

    def slot_rows(n):
        return slot.at[pl.ds(pl.multiple_of(n * rows, rows), rows), :]

    def weight_rows(ref, w_of, z_of):
        at = (w_of * 4 + z_of) * part_rows
        return ref.at[pl.ds(pl.multiple_of(at, 16), part_rows), :]

    def wide_rows(ref, w_of):
        at = w_of * 4 * part_rows
        return ref.at[pl.ds(pl.multiple_of(at, 16), 4 * part_rows), :]

    def by_rows(ref):
        return (
            (lambda k: wide_rows(ref, flipped(w, k))),
            (lambda k, to: wide_rows(ref, flipped(w, k))),
        )

    own_in = local_copy(in_ref.at[z], weight_rows(in_buf, w, z))
    own_out = local_copy(out_ref, weight_rows(out_buf, w, z))
    own_x = local_copy(x_ref, slot_rows(z))
    own_up = local_copy(up_ref.at[w], up_buf.at[w])
    for copy in used:
        copy.start()

    index = w * 4 + z
    down_wide = lax.div(lax.rem(index, 2 * wide), 2)
    down_narrow = lax.rem(index, 2) + 2 * lax.div(index, 2 * wide)
    from_index = 2 * wide * lax.div(z, 2) + 2 * w + lax.rem(z, 2)
    from_wide_index, from_narrow_index = lax.div(from_index, 4), lax.rem(from_index, 4)
    moves = jnp.logical_not((down_wide == w) & (down_narrow == z))
    down_push = sender.plan(
        down_ref, down_got, {"wide": down_wide, "narrow": down_narrow}
    )
    down_stay = local_copy(down_ref, down_got)

    barrier = pltpu.get_barrier_semaphore()
    partners = [narrow_device(line[k]) for k in (1, 2, 3)]
    partners += [wide_device(flipped(w, k)) for k in range(1, wide)]
    for device in partners:
        pl.semaphore_signal(barrier, inc=1, device_id=device, device_id_type=MESH)

    @pl.when(moves)
    def _():
        for device in (
            {"wide": from_wide_index, "narrow": from_narrow_index},
            {"wide": down_wide, "narrow": down_narrow},
        ):
            pl.semaphore_signal(barrier, inc=1, device_id=device, device_id_type=MESH)
        pl.semaphore_wait(barrier, len(partners) + 2)

    @pl.when(jnp.logical_not(moves))
    def _():
        pl.semaphore_wait(barrier, len(partners))

    ins = [
        sender.plan(in_ref.at[line[k]], weight_rows(in_buf, w, z), narrow_device(line[k]))
        for k in (2, 3, 1)
    ]
    outs = [
        sender.plan(out_ref, weight_rows(out_buf, w, z), narrow_device(line[k])) for k in (2, 3, 1)
    ]
    ups = [
        sender.plan(up_ref.at[flipped(w, k)], up_buf.at[w], wide_device(flipped(w, k)))
        for k in range(1, wide)
    ]
    grads = {
        k: sender.plan(grad_ref, grad_got.at[k // 2 - 1], wide_device(flipped(w, k)))
        for k in range(2, wide, 2)
    }
    two = sender.plan(x_ref, slot_rows(z), narrow_device(line[2]))
    one = sender.plan(x_ref, slot_rows(z), narrow_device(line[1]))
    middle = sender.plan(x_ref, slot_rows(z), narrow_device(line[3]))
    relay = sender.plan(slot_rows(line[2]), slot_rows(line[2]), narrow_device(line[1]))
    in_wide = WideGather(sender, w, wide, *by_rows(in_buf))
    out_wide = WideGather(sender, w, wide, *by_rows(out_buf))
    up_steps = [
        sender.plan(up_buf, up_two, narrow_device(line[2])),
        sender.plan(up_buf, up_one, narrow_device(line[1])),
    ]
    mixes = [
        sender.plan(
            mixed.at[pl.ds(pl.multiple_of(line[k] * rows, rows), rows), :],
            mixed_rows.at[:, pl.ds(pl.multiple_of(z * own_width, LANES), own_width)],
            narrow_device(line[k]),
        )
        for k in (2, 3, 1)
    ]

    for copy in ins + outs + ups:
        copy.start()
    own_in.wait()
    for copy in ins:
        copy.wait_recv()
    in_wide.start()
    two.start()
    one.start()
    own_out.wait()
    for copy in outs:
        copy.wait_recv()
    out_wide.start()
    in_wide.pass_on()
    for k in diagonal_steps(wide):
        grads[k].start()
    two.wait_recv()

    @pl.when(is_middle)
    def _():
        relay.start()
        middle.start()

    own_up.wait()
    for copy in ups:
        copy.wait_recv()
    up_back = local_copy(up_buf, up_out)
    up_back.start()
    out_wide.pass_on()
    in_wide.received()
    in_back = local_copy(in_buf, in_out)
    in_back.start()
    one.wait_recv()
    own_x.wait()

    @pl.when(is_middle)
    def _():
        middle.wait_recv()

    @pl.when(is_end)
    def _():
        relay.wait_recv()

    for copy in up_steps:
        copy.start()

    @pl.when(moves)
    def _():
        down_push.start()

    @pl.when(jnp.logical_not(moves))
    def _():
        down_stay.start()

    for k in straight_steps(wide):
        grads[k].start()

    def project(n, carry):
        at = pl.ds(pl.multiple_of(n * rows, rows), rows)
        values = slot[at, :].astype(F32)
        low = (values * rms_factor(values) * gain_one_ref[0:1, :]).astype(BF16)
        normed[at, :] = low
        proj[at, :] = dot_f32(low, in_buf[...])
        return carry

    lax.fori_loop(0, slot.shape[0] // rows, project, 0)
    normed_back = local_copy(normed, normed_out)
    proj_back = local_copy(proj, proj_out)
    normed_back.start()
    proj_back.start()

    cont = cont_ref[...]
    groups = own_width // LANES
    small_low = small_columns(proj.at[:, pl.ds(4 * own_width, LANES)], bias_ref)
    decay_scr[...] = decay_of(small_low, cont)

    def attend(pair, carry):
        def at(group):
            return pl.ds(pl.multiple_of((group * groups + pair) * LANES, LANES), LANES)

        forward_pair(
            pair, heads, head_size, block, proj.at[:, at(0)], proj.at[:, at(1)], proj.at[:, at(2)],
            proj.at[:, at(3)], small_low, cont, decay_scr[...], mixed.at[:, at(0)],
            att_ref.at[:, at(0)], log_ref.at[:, at(0)],
        )
        return carry

    lax.fori_loop(0, groups, attend, 0)
    for copy in mixes:
        copy.start()
    mixed_rows[:, pl.ds(pl.multiple_of(z * own_width, LANES), own_width)] = mixed[
        pl.ds(pl.multiple_of(z * rows, rows), rows), :
    ]
    out_wide.received()
    out_back = local_copy(out_buf, out_out)
    out_back.start()
    for copy in mixes:
        copy.wait_recv()
    inputs = slot[pl.ds(pl.multiple_of(z * rows, rows), rows), :].astype(F32)
    values = inputs + dot_f32(mixed_rows[...], out_buf[...])
    middle_ref[...] = values
    normed_two_ref[...] = (values * rms_factor(values) * gain_two_ref[0:1, :]).astype(BF16)

    for copy in up_steps:
        copy.wait()
    for copy in grads.values():
        copy.wait()

    @pl.when(moves)
    def _():
        down_push.wait()

    @pl.when(jnp.logical_not(moves))
    def _():
        down_stay.wait()

    @pl.when(is_middle)
    def _():
        relay.wait_send()
        middle.wait_send()

    for copy in ins + outs + ups + [two, one] + mixes:
        copy.wait_send()
    in_wide.sent()
    out_wide.sent()
    for copy in (up_back, in_back, normed_back, proj_back, out_back):
        copy.wait()


def first_part(
    tokens, in_parts, out_weight, up_parts, cotangent, down_weight, gain_one, gain_two, bias, cont,
    heads, head_size, block, collective_id,
):
    wide = up_parts.shape[0]
    rows, width = tokens.shape
    slot, own_width, columns = 4 * rows, heads * head_size, in_parts.shape[2]
    steps = 3 * wide + 2 * wide + 24
    shape = jax.ShapeDtypeStruct
    return pl.pallas_call(
        functools.partial(first_kernel, wide, heads, head_size, block),
        out_shape=[
            shape((slot, width), BF16), shape((width, columns), BF16), shape((width, width), BF16),
            shape((slot, columns), F32), shape((slot, own_width), BF16),
            shape((slot, own_width), F32), shape((rows, width), BF16), shape((rows, width), F32),
            shape((rows, width), BF16), shape(up_parts.shape, BF16), shape(up_parts.shape, BF16),
            shape(up_parts.shape, BF16), shape(down_weight.shape, BF16),
            shape((wide // 2 - 1, rows, width), BF16),
        ],
        in_specs=[ANY] * 6 + [VMEM] * 4,
        out_specs=[ANY] * 4 + [VMEM] * 5 + [ANY] * 5,
        scratch_shapes=[
            pltpu.VMEM((slot, width), BF16), pltpu.VMEM((width, columns), BF16),
            pltpu.VMEM((width, width), BF16), pltpu.VMEM(up_parts.shape, BF16),
            pltpu.VMEM((slot, width), BF16), pltpu.VMEM((slot, columns), F32),
            pltpu.VMEM((slot, own_width), BF16), pltpu.VMEM((slot, LANES), F32),
            DMA((steps,)), DMA((steps,)), DMA((10,)),
        ],
        compiler_params=pltpu.CompilerParams(
            collective_id=collective_id, has_side_effects=True, vmem_limit_bytes=60 * 2**20
        ),
    )(
        tokens, in_parts, out_weight, up_parts, cotangent, down_weight,
        jnp.broadcast_to(gain_one[None], (8, width)), jnp.broadcast_to(gain_two[None], (8, width)),
        bias, cont,
    )


def second_kernel(
    wide, src_ref, grad_ref, far_grads, up_ref, up_two, up_one, down_ref, norm_sum, branch_sum,
    up_src, down_src, up_acc, down_acc, up_grad_out, down_grad_out, normed, grads, up_full,
    down_full, hidden, mid, rows_buf, core_buf, far_buf, branch_buf, up_join, up_mid, down_join,
    down_mid, up_grad, down_grad, send, recv, local,
):
    w, z = lax.axis_index("wide"), lax.axis_index("narrow")
    line = [flipped(z, k) for k in range(4)]
    rows, width = src_ref.shape
    half = wide // 2
    size = hidden.shape[1]
    unit, part = up_src.shape[1], down_src.shape[1]
    is_middle = (z == 1) | (z == 2)
    is_end = (z == 0) | (z == 3)
    sender = Sender(send, recv)
    sibling = wide_device(flipped(w, 1))

    def at_place(ref, place):
        return ref.at[pl.ds(pl.multiple_of(place * rows, rows), rows), :]

    up_at = lambda n: up_full.at[:, n]
    down_at = lambda n: down_full.at[n]
    moves = [
        (src_ref, at_place(normed, 0)), (up_ref, up_at(z)), (up_two, up_at(line[2])),
        (up_one, up_at(line[1])), (down_ref, down_at(z)), (grad_ref, at_place(grads, 0)),
    ] + [(far_grads.at[n - 1], at_place(grads, n)) for n in range(1, half)]
    own = [pltpu.make_async_copy(src, dst, local.at[n]) for n, (src, dst) in enumerate(moves)]
    for copy in own:
        copy.start()
    greet(
        [wide_device(flipped(w, k)) for k in wide_steps(wide)]
        + [narrow_device(line[k]) for k in (1, 2, 3)]
    )
    gather = WideGather(
        sender, w, wide, lambda k: src_ref if k == 0 else at_place(normed, place_of(k, wide)),
        lambda k, to: at_place(normed, place_of(k ^ to, wide)),
    )
    middle = sender.plan(up_ref, up_at(z), narrow_device(line[3]))
    relay = sender.plan(up_two, up_at(line[2]), narrow_device(line[1]))
    down_two = sender.plan(down_ref, down_at(z), narrow_device(line[2]))
    down_one = sender.plan(down_ref, down_at(z), narrow_device(line[1]))
    down_middle = sender.plan(down_ref, down_at(z), narrow_device(line[3]))
    down_relay = sender.plan(down_at(line[2]), down_at(line[2]), narrow_device(line[1]))
    passed = [
        sender.plan(
            grad_ref if n == 0 else far_grads.at[n - 1], at_place(grads, half + n), sibling
        )
        for n in range(half)
    ]
    core = [
        sender.plan(at_place(rows_buf, half + n), core_buf.at[n], sibling) for n in range(half)
    ]
    far = [
        sender.plan(at_place(rows_buf, n), far_buf.at[n - 1], wide_device(flipped(w, 2 * n)))
        for n in range(1, half)
    ]
    branch_core = [
        sender.plan(at_place(normed, half + n), branch_buf.at[n], sibling) for n in range(half)
    ]

    def up_share(n):
        return up_grad.at[:, pl.ds(pl.multiple_of(n * unit, unit), unit)]

    def down_share(n):
        return down_grad.at[:, pl.ds(pl.multiple_of(n * part, part), part)]

    down_joined = sender.plan(down_share(line[3]), down_join, narrow_device(line[1]))
    down_direct = sender.plan(down_share(line[3]), down_mid, narrow_device(line[3]))
    up_joined = sender.plan(up_share(line[3]), up_join, narrow_device(line[1]))
    up_direct = sender.plan(up_share(line[3]), up_mid, narrow_device(line[3]))

    gather.start()
    down_two.start()

    @pl.when(is_middle)
    def _():
        relay.start()

    down_two.wait_recv()

    @pl.when(is_middle)
    def _():
        down_relay.start()
        middle.start()
        down_middle.start()

    down_one.start()
    for copy in passed:
        copy.start()
    gather.pass_on()
    gather.received()
    for copy in own:
        copy.wait()
    for copy in passed + [down_one]:
        copy.wait_recv()

    @pl.when(is_middle)
    def _():
        middle.wait_recv()
        down_middle.wait_recv()

    @pl.when(is_end)
    def _():
        relay.wait_recv()
        down_relay.wait_recv()

    up_shape = (width, 4 * unit)
    down_shape = (size, width)

    def block(t, carry):
        place = lax.rem(t + half, wide) + jnp.where(t < half, 0, 1)
        place = jnp.where(place == half, jnp.where(t < half, half, 0), place)
        at = pl.ds(pl.multiple_of(place * rows, rows), rows)
        gate_up = dot_f32(normed[at, :], up_full[...].reshape(up_shape))
        grad_hidden = dot_f32(grads[at, :], down_full[...].reshape(down_shape), ((1,), (1,)))
        gate, up = gate_up[:, :size], gate_up[:, size:]
        opened = jax.nn.sigmoid(gate)
        acted = gate * opened
        hidden[at, :] = (acted * up).astype(BF16)
        mid[at, :size] = (grad_hidden * up * (opened * (1.0 + gate * (1.0 - opened)))).astype(BF16)
        mid[at, size:] = (grad_hidden * acted).astype(BF16)
        rows_buf[at, :] = dot_f32(mid[at, :], up_full[...].reshape(up_shape), ((1,), (1,))).astype(
            BF16
        )
        for n in range(half):

            @pl.when(t == n)
            def _():
                core[n].start()

        for n in range(half):

            @pl.when(t == half + lax.rem(n + half - 1, half))
            def _():
                core[n].wait_recv()
                total = rows_buf[n * rows : (n + 1) * rows, :].astype(F32) + core_buf[n].astype(F32)
                rows_buf[n * rows : (n + 1) * rows, :] = total.astype(BF16)
                if n > 0:
                    far[n - 1].start()

        return carry

    lax.fori_loop(0, wide, block, 0)

    step = min(256, size)
    for n in range(size // step):
        cut = slice(n * step, (n + 1) * step)
        down_grad[cut, :] = dot_f32(hidden[:, cut], grads[...], ((0,), (0,))).astype(BF16)

    @pl.when(is_end)
    def _():
        down_joined.start()

    @pl.when(is_middle)
    def _():
        down_direct.start()

    def up_rows(n, carry):
        at = pl.ds(pl.multiple_of(n * 256, 256), 256)
        up_grad[at, :] = dot_f32(normed[:, at], mid[...], ((0,), (0,))).astype(BF16)
        return carry

    lax.fori_loop(0, width // 256, up_rows, 0)

    @pl.when(is_end)
    def _():
        up_joined.start()

    @pl.when(is_middle)
    def _():
        up_direct.start()

    backs = [
        pltpu.make_async_copy(up_grad, up_grad_out, local.at[5 + half]),
        pltpu.make_async_copy(down_grad, down_grad_out, local.at[6 + half]),
        pltpu.make_async_copy(up_share(line[2]), up_src, local.at[7 + half]),
        pltpu.make_async_copy(down_share(line[2]), down_src, local.at[8 + half]),
    ]
    for copy in backs:
        copy.start()
    gather.sent()

    def branch(t, carry):
        place = lax.rem(t + half, wide)
        at = pl.ds(pl.multiple_of(place * rows, rows), rows)
        normed[at, :] = dot_f32(hidden[at, :], down_full[...].reshape(down_shape)).astype(BF16)
        for n in range(half):

            @pl.when(t == n)
            def _():
                branch_core[n].start()

        return carry

    lax.fori_loop(0, wide, branch, 0)
    for n in range(half):
        branch_core[n].wait_recv()
        total = normed[n * rows : (n + 1) * rows, :].astype(F32) + branch_buf[n].astype(F32)
        branch_sum[n] = total.astype(BF16)

    total = rows_buf[:rows, :].astype(F32)
    for n in range(1, half):
        far[n - 1].wait_recv()
        total = total + far_buf[n - 1].astype(F32)
    norm_sum[...] = total
    for copy in backs:
        copy.wait()
    up_acc[...] = up_grad[:, pl.ds(pl.multiple_of(z * unit, unit), unit)]
    down_acc[...] = down_grad[:, pl.ds(pl.multiple_of(z * part, part), part)]

    @pl.when(is_middle)
    def _():
        down_joined.wait_recv()
        down_src[...] = (down_src[...].astype(F32) + down_join[...].astype(F32)).astype(BF16)
        up_joined.wait_recv()
        up_src[...] = (up_src[...].astype(F32) + up_join[...].astype(F32)).astype(BF16)
        down_direct.wait()
        down_acc[...] = (down_acc[...].astype(F32) + down_mid[...].astype(F32)).astype(BF16)
        up_direct.wait()
        up_acc[...] = (up_acc[...].astype(F32) + up_mid[...].astype(F32)).astype(BF16)
        for copy in (relay, middle, down_relay, down_middle):
            copy.wait_send()

    @pl.when(is_end)
    def _():
        down_joined.wait_send()
        up_joined.wait_send()

    for copy in passed + core + far + branch_core + [down_two, down_one]:
        copy.wait_send()


def second_part(normed, grad, far_grads, ups, down, collective_id):
    rows, width = normed.shape
    half = far_grads.shape[0] + 1
    wide = 2 * half
    wide_of_up, part_rows, mid_size = ups[0].shape
    down_rows = down.shape[0]
    size, unit, part = mid_size // 2, mid_size // 4, width // 4
    steps = 6 + wide + 4 * half + 8
    total = wide * rows
    shape = jax.ShapeDtypeStruct
    vmem = lambda *dims: pltpu.VMEM(dims, BF16)
    return pl.pallas_call(
        functools.partial(second_kernel, wide),
        out_shape=[
            shape((rows, width), F32), shape((half, rows, width), BF16),
            shape((width, unit), BF16), shape((size, part), BF16),
            shape((width, unit), BF16), shape((size, part), BF16),
            shape((width, mid_size), BF16), shape((size, width), BF16),
        ],
        in_specs=[ANY] * 7,
        out_specs=[VMEM] * 6 + [ANY] * 2,
        scratch_shapes=[
            vmem(total, width), vmem(total, width), vmem(wide, 4, part_rows, mid_size),
            vmem(4, down_rows, width), vmem(total, size), vmem(total, mid_size), vmem(total, width),
            vmem(half, rows, width), vmem(half - 1, rows, width), vmem(half, rows, width),
            vmem(width, unit), vmem(width, unit), vmem(size, part), vmem(size, part),
            vmem(width, mid_size), vmem(size, width),
            DMA((steps,)), DMA((steps,)), DMA((9 + half,)),
        ],
        compiler_params=pltpu.CompilerParams(
            collective_id=collective_id, has_side_effects=True, vmem_limit_bytes=63 * 2**20
        ),
    )(normed, grad, far_grads, *ups, down)


def add_up(parts):
    total = parts[0].astype(F32)
    for part in parts[1:]:
        total = total + part.astype(F32)
    return total


def on_device(
    tokens, gain_one, in_weight, forget_bias, out_weight, gain_two, gate_up_weight, down_weight,
    segment_ids, cotangent,
):
    wide, narrow = lax.axis_size("wide"), lax.axis_size("narrow")
    w, z = lax.axis_index("wide"), lax.axis_index("narrow")
    rows, width = tokens.shape
    slot = rows * narrow
    heads = forget_bias.shape[0]
    head_size = width // heads
    own_heads = heads // narrow
    own_width = own_heads * head_size
    part_rows = in_weight.shape[0]
    hidden_all = down_weight.shape[0] * wide * narrow
    unit = hidden_all // (2 * wide)
    columns = 4 * own_width + LANES
    base = 4 * width

    small = in_weight[:, base:].reshape(part_rows, 3, narrow, own_heads)
    small = jnp.moveaxis(small, 2, 0).reshape(narrow, part_rows, 3 * own_heads)
    small = jnp.pad(small, ((0, 0), (0, 0), (0, LANES - 3 * own_heads)))
    aligned = unit % LANES == 0

    def split_weights(sources, targets):
        copies = [(sources[1], targets[0].at[:, :, pl.ds(4 * own_width, LANES)])]
        for n in range(narrow):
            for group in range(4):
                copies.append(
                    (
                        sources[0].at[:, pl.ds(group * width + n * own_width, own_width)],
                        targets[0].at[n, :, pl.ds(group * own_width, own_width)],
                    )
                )
        if aligned:
            for n in range(wide):
                for group in range(4):
                    copies.append(
                        (
                            sources[2].at[:, pl.ds((group * wide + n) * unit, unit)],
                            targets[1].at[n, :, pl.ds(group * unit, unit)],
                        )
                    )
        return copies

    shapes = [
        jax.ShapeDtypeStruct((narrow, part_rows, columns), BF16),
        jax.ShapeDtypeStruct((wide, part_rows, 4 * unit), BF16),
    ]
    copies = 4 * narrow + 1
    if aligned:
        in_parts, up_parts = local_copies(
            split_weights, copies + 4 * wide, [in_weight, small, gate_up_weight], shapes, False
        )
    else:
        in_parts = local_copies(split_weights, copies, [in_weight, small], shapes[:1], False)[0]
        up_parts = jnp.moveaxis(gate_up_weight.reshape(part_rows, 4, wide, unit), 2, 0)
        up_parts = up_parts.reshape(wide, part_rows, 4 * unit)

    segments = segment_ids[0]
    joined = (segments[1:] == segments[:-1]).astype(F32)
    cont = jnp.concatenate([jnp.zeros((1,), F32), joined])
    cont = jnp.broadcast_to(cont[:, None], (slot, LANES))
    own_bias = lax.dynamic_slice_in_dim(forget_bias, z * own_heads, own_heads)
    bias = jnp.broadcast_to(jnp.pad(own_bias, (0, LANES - own_heads))[None], (8, LANES))
    block = min(256, slot)
    def row_block(ref, n):
        return ref.at[pl.ds(pl.multiple_of(n * rows, rows), rows), :]

    def column_block(ref, n):
        return ref.at[:, pl.ds(pl.multiple_of(n * own_width, LANES), own_width)]

    straight, diagonal = straight_steps(wide), diagonal_steps(wide)
    inputs = tokens.astype(F32)
    half = wide // 2
    if aligned and part_rows % 16 == 0:
        (
            normed_one, in_full, out_full, projected, attended, logs, mixed_rows, middle, normed_two,
            up_block, up_two, up_one, down_block, grad_got,
        ) = first_part(
            tokens, in_parts, out_weight, up_parts, cotangent, down_weight, gain_one, gain_two,
            bias, cont, own_heads, head_size, block, 0,
        )
    else:
        pairs = []
        for i in range(wide * narrow):
            to_wide = (i % (2 * wide)) // 2
            to_narrow = i % 2 + 2 * (i // (2 * wide))
            pairs.append((i, to_wide * narrow + to_narrow))
        down_block = lax.ppermute(down_weight, ("wide", "narrow"), pairs)

        slot_tokens, in_full, out_full, up_block, grad_far = gather_all(
            tokens, in_parts, out_weight, up_parts, cotangent
        )
        slot_tokens = slot_tokens.reshape(slot, width)
        in_full = in_full.reshape(width, columns)
        out_full = out_full.reshape(width, width)

        up_two = on_line(up_block, LINE_TWO)
        up_one = on_line(up_block, LINE_ONE)

        slot_floats = slot_tokens.astype(F32)
        normed_one = (slot_floats * rms_factor(slot_floats) * gain_one).astype(BF16)
        projected = dot_f32(normed_one, in_full)

        mixed, attended, logs = attention_forward(
            projected, bias, cont, own_heads, head_size, block
        )

        mixed_rows, *grad_near = exchange(
            mixed, row_block, column_block, (rows, width), straight, [cotangent] * len(straight), 1
        )
        grads = {0: cotangent}
        grads.update({k: grad_near[n] for n, k in enumerate(straight)})
        grads.update({k: grad_far[n] for n, k in enumerate(diagonal)})
        grads = [grads[k] for k in range(0, wide, 2)]
        down_block = follow(down_block, mixed_rows)
        down_two = on_line(down_block, LINE_TWO)
        down_one = on_line(down_block, LINE_ONE)
        middle = inputs + dot_f32(mixed_rows, out_full)
        normed_two = (middle * rms_factor(middle) * gain_two).astype(BF16)

    if aligned and part_rows % 16 == 0:
        (
            grad_normed_two, branch_sum, up_src, down_src, up_acc, down_acc, up_one, down_one,
        ) = second_part(
            normed_two, cotangent, grad_got, [up_block, up_two, up_one], down_block, 2
        )
    else:
        ups = [up_block] + [follow(piece, normed_two) for piece in (up_two, up_one)]
        plane_normed, plane_grad, up_full, down_full = gather_rows(
            normed_two, grads, ups, [down_block, down_two, down_one], 2
        )
        plane_normed = plane_normed.reshape(wide * rows, width)
        plane_grad = plane_grad.reshape(wide * rows, width)
        up_full = up_full.reshape(width, 4 * unit)
        down_full = down_full.reshape(2 * unit, width)
        hidden, gate_up_grad, norm_even, norm_odd, branch = feed_forward(
            plane_normed, plane_grad, up_full, down_full, rows
        )
        grad_up_full = dot_f32(plane_normed, gate_up_grad, ((0,), (0,))).astype(BF16)
        grad_down_full = dot_f32(hidden, plane_grad, ((0,), (0,))).astype(BF16)
        if unit % LANES:
            grouped = grad_up_full.reshape(width, 4, unit)
            grad_up_full = jnp.pad(grouped, ((0, 0), (0, 0), (0, LANES - unit))).reshape(width, -1)
        branch = branch.reshape(wide, rows, width)
        fits = wide <= 8
        norm_got = along_wide(norm_odd.reshape(half, rows, width), 1, wide)
        (
            grad_normed_two, branch_sum, up_src, down_src, up_one, down_one, up_acc, down_acc,
        ) = middle_sums(
            norm_even.reshape(half, rows, width), norm_got,
            branch if fits else branch[:2, :16], grad_up_full, grad_down_full, 6,
        )
        if not fits:
            received = along_wide(branch[half:], 1, wide)
            branch_sum = (branch[:half].astype(F32) + received.astype(F32)).astype(BF16)
    upstream = cotangent.astype(F32)
    grad_middle_norm, grad_gain_two = rms_back(middle, gain_two, grad_normed_two)
    grad_middle = upstream + grad_middle_norm
    branch_one_grad = grad_middle.astype(BF16)
    grad_mixed = dot_f32(branch_one_grad, out_full, ((1,), (1,))).astype(BF16)
    slot_grad, *branch_near = exchange(
        grad_mixed, column_block, row_block, (slot, own_width), straight,
        [branch_sum[k // 2] for k in straight], 3,
    )

    projected_grad, bias_grad, up_two, down_two, up_one, down_one = attention_backward(
        projected, bias, cont, attended, logs, slot_grad, [up_src, down_src, up_one, down_one],
        own_heads, head_size, block, 7,
    )
    norm_part = dot_f32(projected_grad, in_full, ((1,), (1,))).astype(BF16)
    in_part = dot_f32(normed_one, projected_grad, ((0,), (0,))).astype(BF16)

    wide_rows = width // wide
    out_part = dot_f32(mixed_rows, branch_one_grad, ((0,), (0,))).astype(BF16)
    late = lambda part: part.astype(F32)
    up_part = (late(up_acc) + late(up_one) + late(up_two)).astype(BF16)
    grad_down = (late(down_acc) + late(down_one) + late(down_two)).astype(BF16)
    low_half, high_half = grad_down[:unit], grad_down[unit:]
    is_odd = lax.rem(w, 2) == 1
    first_send = jnp.where(is_odd, high_half, low_half)
    second_send = jnp.where(is_odd, low_half, high_half)
    first_got = lax.ppermute(
        first_send, "wide", [(i, i // 2 + (half if i % 2 else 0)) for i in range(wide)]
    )
    second_got = lax.ppermute(
        second_send, "wide", [(i, i // 2 + (0 if i % 2 else half)) for i in range(wide)]
    )
    norm_sum, got, grad_out, grad_up, branch_far = last_transfers(
        norm_part, in_part.reshape(wide, wide_rows, columns),
        out_part.reshape(wide, wide_rows, width), up_part,
        jnp.stack([branch_sum[k // 2] for k in diagonal]), rows, own_width, 4,
    )
    branch_far = [branch_far[n] for n in range(len(diagonal))]
    output = (middle + add_up([branch_sum[0]] + branch_near + branch_far)).astype(BF16)
    if not aligned:
        grad_up = grad_up.reshape(wide_rows, wide, LANES)[:, :, :unit]
        grad_up = grad_up.reshape(wide_rows, wide * unit)
    first_got, second_got = follow(first_got, norm_sum), follow(second_got, norm_sum)
    grad_up = grad_up.astype(F32)
    grad_inputs, grad_gain_one = rms_back(inputs, gain_one, norm_sum)
    grad_tokens = grad_middle + grad_inputs
    in_low = w < half
    grad_down = jnp.concatenate(
        [
            jnp.where(in_low, first_got, second_got),
            jnp.where(in_low, second_got, first_got),
        ],
        axis=0,
    ).astype(F32)

    extra = 3 * heads
    section = jnp.concatenate([got[n, :, :own_width] for n in range(narrow)], axis=1)
    small_all = jnp.stack([got[n, :, own_width : own_width + 3 * own_heads] for n in range(narrow)])
    small_all = small_all.reshape(narrow, wide_rows, 3, own_heads)
    small_all = jnp.transpose(small_all, (1, 2, 0, 3)).reshape(wide_rows, extra)
    next_first = got[0, :, own_width : own_width + extra]
    tail = jnp.where(z == narrow - 1, small_all, next_first)
    joined_columns = jnp.concatenate([section, tail], axis=1)
    shard = (base + extra) // narrow
    grad_in = lax.dynamic_slice_in_dim(joined_columns, z * (shard - width), shard, 1).astype(F32)

    all_bias = lax.dynamic_update_slice(
        jnp.zeros((heads,), F32), bias_grad[0, :own_heads], (z * own_heads,)
    )
    packed = jnp.concatenate([grad_gain_one, grad_gain_two, all_bias])
    packed = total_of(packed, wide, 5)
    return (
        output,
        grad_tokens,
        packed[:width],
        grad_in,
        packed[2 * width :],
        grad_out,
        packed[width : 2 * width],
        grad_up,
        grad_down,
    )


def solution(mesh):
    both = ("wide", "narrow")
    in_specs = (
        P(both, None), P(), P(both, None), P(), P(both, None), P(), P(both, None), P(both, None),
        P("wide", None), P(both, None),
    )
    out_specs = (
        P(both, None), P(both, None), P(), P("wide", "narrow"), P(), P("wide", "narrow"), P(),
        P("wide", "narrow"), P("wide", "narrow"),
    )
    return jax.shard_map(
        on_device, mesh=mesh, in_specs=in_specs, out_specs=out_specs, check_vma=False
    )
```

```python
import functools

import jax
import jax.numpy as jnp
from jax import lax
from jax.experimental import pallas as pl
from jax.experimental.pallas import tpu as pltpu
from jax.sharding import PartitionSpec as P

EPSILON = 1e-06
SEPARATE = 128.0
F32 = jnp.float32
BF16 = jnp.bfloat16
LANES = 128
EXACT = lax.Precision.HIGHEST
ANY = pl.BlockSpec(memory_space=pl.ANY)


def dot_f32(left, right, dims=((1,), (0,))):
    return lax.dot_general(left, right, (dims, ((), ())), preferred_element_type=F32)


def along_wide(block, flip, wide):
    return lax.ppermute(block, "wide", [(i, i ^ flip) for i in range(wide)])


def copy_kernel(plan, count, *refs):
    sources, targets, sems = refs[:count], refs[count:-1], refs[-1]
    copies = plan(sources, targets)

    def each(act):
        for n, (src, dst, *when) in enumerate(copies):
            copy = pltpu.make_async_copy(src, dst, sems.at[n])
            if when:
                pl.when(when[0])(functools.partial(act, copy))
            else:
                act(copy)

    each(lambda copy: copy.start())
    each(lambda copy: copy.wait())


def local_copies(plan, copies, sources, shapes, gather):
    moved = sum(s.size * s.dtype.itemsize for s in shapes)
    inside = pl.BlockSpec(memory_space=pltpu.VMEM)
    return pl.pallas_call(
        functools.partial(copy_kernel, plan, len(sources)),
        out_shape=shapes,
        in_specs=[ANY if gather else inside] * len(sources),
        out_specs=[inside if gather else ANY] * len(shapes),
        compiler_params=pltpu.CompilerParams(vmem_limit_bytes=16 * 2**20),
        scratch_shapes=[pltpu.SemaphoreType.DMA((copies,))],
        cost_estimate=pl.CostEstimate(flops=0, bytes_accessed=2 * moved, transcendentals=0),
    )(*sources)


def flipped(me, k):
    out = me
    bit = 1
    while bit <= k:
        if k & bit:
            out = out + bit - 2 * bit * lax.rem(lax.div(out, bit), 2)
        bit *= 2
    return out


LINE_TWO = [(0, 2), (2, 0), (1, 3), (3, 1)]
LINE_ONE = [(0, 1), (1, 0), (2, 3), (3, 2)]
LINE_MIDDLE = [(1, 2), (2, 1)]
LINE_OUT = [(2, 3), (1, 0)]
LINE_IN = [(0, 1), (3, 2)]


def on_line(block, pairs):
    return lax.ppermute(block, "narrow", pairs)


def follow(array, *earlier):
    return lax.optimization_barrier((array, *earlier))[0]


MESH = pl.DeviceIdType.MESH
VMEM = pl.BlockSpec(memory_space=pltpu.VMEM)
DMA = pltpu.SemaphoreType.DMA


def greet(devices):
    barrier = pltpu.get_barrier_semaphore()
    for device in devices:
        pl.semaphore_signal(barrier, inc=1, device_id=device, device_id_type=MESH)
    pl.semaphore_wait(barrier, len(devices))


class Sender:
    def __init__(self, send, recv):
        self.send, self.recv, self.used = send, recv, 0

    def plan(self, src, dst, device):
        n = self.used
        self.used += 1
        return pltpu.make_async_remote_copy(
            src_ref=src, dst_ref=dst, send_sem=self.send.at[n], recv_sem=self.recv.at[n],
            device_id=device, device_id_type=MESH,
        )


def narrow_device(n):
    return {"narrow": n}


def wide_device(n):
    return {"wide": n}


def wide_steps(wide):
    return [1] + list(range(2, wide, 2))


def straight_steps(wide):
    return [k for k in range(2, wide, 2) if k & (k - 1) == 0]


def diagonal_steps(wide):
    return [k for k in range(2, wide, 2) if k & (k - 1)]


def by_device(ref, w):
    return (lambda k: ref.at[flipped(w, k)]), (lambda k, to: ref.at[flipped(w, k)])


class WideGather:
    def __init__(self, sender, w, wide, part, target):
        self.far = list(range(2, wide, 2))
        self.first = {
            k: sender.plan(part(0), target(0, k), wide_device(flipped(w, k)))
            for k in wide_steps(wide)
        }
        sibling = wide_device(flipped(w, 1))
        self.second = {k: sender.plan(part(k), target(k, 1), sibling) for k in self.far}

    def start(self):
        for k in self.far + [1]:
            self.first[k].start()

    def pass_on(self):
        for k in self.far:
            self.first[k].wait_recv()
            self.second[k].start()

    def received(self):
        self.first[1].wait_recv()
        for k in self.far:
            self.second[k].wait_recv()

    def sent(self):
        for copy in list(self.first.values()) + list(self.second.values()):
            copy.wait_send()

    def finish(self):
        self.received()
        self.sent()


def gather_kernel(
    wide, x_ref, in_ref, out_ref, up_ref, grad_ref, slot_ref, in_full, out_full, up_block, grad_far,
    send, recv, local,
):
    w, z = lax.axis_index("wide"), lax.axis_index("narrow")
    line = [flipped(z, k) for k in range(4)]
    sender = Sender(send, recv)
    own = [
        pltpu.make_async_copy(in_ref.at[z], in_full.at[w, z], local.at[0]),
        pltpu.make_async_copy(out_ref, out_full.at[w, z], local.at[1]),
        pltpu.make_async_copy(x_ref, slot_ref.at[z], local.at[2]),
        pltpu.make_async_copy(up_ref.at[w], up_block.at[w], local.at[3]),
    ]
    for copy in own:
        copy.start()
    greet(
        [narrow_device(line[k]) for k in (1, 2, 3)]
        + [wide_device(flipped(w, k)) for k in range(1, wide)]
    )
    ups = [
        sender.plan(up_ref.at[flipped(w, k)], up_block.at[w], wide_device(flipped(w, k)))
        for k in range(1, wide)
    ]
    grads = [
        sender.plan(grad_ref, grad_far.at[n], wide_device(flipped(w, k)))
        for n, k in enumerate(diagonal_steps(wide))
    ]
    is_middle = (z == 1) | (z == 2)
    is_end = (z == 0) | (z == 3)
    ins = [
        sender.plan(in_ref.at[line[k]], in_full.at[w, z], narrow_device(line[k])) for k in (2, 3, 1)
    ]
    outs = [sender.plan(out_ref, out_full.at[w, z], narrow_device(line[k])) for k in (2, 3, 1)]
    two = sender.plan(x_ref, slot_ref.at[z], narrow_device(line[2]))
    one = sender.plan(x_ref, slot_ref.at[z], narrow_device(line[1]))
    middle = sender.plan(x_ref, slot_ref.at[z], narrow_device(line[3]))
    relay = sender.plan(slot_ref.at[line[2]], slot_ref.at[line[2]], narrow_device(line[1]))
    in_wide = WideGather(sender, w, wide, *by_device(in_full, w))
    out_wide = WideGather(sender, w, wide, *by_device(out_full, w))
    for copy in ins + outs + ups:
        copy.start()
    own[0].wait()
    for copy in ins:
        copy.wait_recv()
    in_wide.start()
    two.start()
    one.start()
    own[1].wait()
    for copy in outs:
        copy.wait_recv()
    out_wide.start()
    in_wide.pass_on()
    for copy in grads:
        copy.start()
    two.wait_recv()

    @pl.when(is_middle)
    def _():
        relay.start()
        middle.start()

    out_wide.pass_on()
    one.wait_recv()
    own[2].wait()
    own[3].wait()
    for copy in ups + grads:
        copy.wait()

    @pl.when(is_middle)
    def _():
        middle.wait_recv()
        middle.wait_send()
        relay.wait_send()

    @pl.when(is_end)
    def _():
        relay.wait_recv()

    for copy in ins + outs + [two, one]:
        copy.wait_send()
    in_wide.finish()
    out_wide.finish()


def gather_all(tokens, in_parts, out_weight, up_parts, cotangent):
    narrow, wide = in_parts.shape[0], up_parts.shape[0]
    steps = 10 + 4 * wide
    shapes = [
        (narrow,) + tokens.shape, (wide,) + in_parts.shape, (wide, narrow) + out_weight.shape,
        up_parts.shape, (len(diagonal_steps(wide)),) + cotangent.shape,
    ]
    return pl.pallas_call(
        functools.partial(gather_kernel, wide),
        out_shape=[jax.ShapeDtypeStruct(shape, BF16) for shape in shapes],
        in_specs=[ANY] * 5,
        out_specs=[VMEM] * 5,
        scratch_shapes=[DMA((steps,)), DMA((steps,)), DMA((4,))],
        compiler_params=pltpu.CompilerParams(
            collective_id=0, has_side_effects=True, vmem_limit_bytes=40 * 2**20
        ),
    )(tokens, in_parts, out_weight, up_parts, cotangent)


def exchange_kernel(source, target, steps, *refs):
    count = len(steps)
    src_ref, sides, dst_ref = refs[0], refs[1 : 1 + count], refs[1 + count]
    got = refs[2 + count : 2 + 2 * count]
    send, recv, local = refs[2 + 2 * count :]
    w, z = lax.axis_index("wide"), lax.axis_index("narrow")
    line = [flipped(z, k) for k in range(4)]
    sender = Sender(send, recv)
    own = pltpu.make_async_copy(source(src_ref, z), target(dst_ref, z), local.at[0])
    own.start()
    greet(
        [narrow_device(line[k]) for k in (1, 2, 3)] + [wide_device(flipped(w, k)) for k in steps]
    )
    copies = [
        sender.plan(source(src_ref, line[k]), target(dst_ref, z), narrow_device(line[k]))
        for k in (2, 3, 1)
    ]
    copies += [
        sender.plan(sides[n], got[n], wide_device(flipped(w, k))) for n, k in enumerate(steps)
    ]
    for copy in copies:
        copy.start()
    own.wait()
    for copy in copies:
        copy.wait()


def exchange(array, source, target, shape, steps, sides, collective_id):
    count = len(steps) + 4
    return pl.pallas_call(
        functools.partial(exchange_kernel, source, target, steps),
        out_shape=[jax.ShapeDtypeStruct(shape, array.dtype)]
        + [jax.ShapeDtypeStruct(side.shape, side.dtype) for side in sides],
        in_specs=[ANY] * (1 + len(sides)),
        out_specs=[VMEM] * (1 + len(sides)),
        scratch_shapes=[DMA((count,)), DMA((count,)), DMA((1,))],
        compiler_params=pltpu.CompilerParams(
            collective_id=collective_id, has_side_effects=True, vmem_limit_bytes=16 * 2**20
        ),
    )(array, *sides)


def place_of(k, wide):
    return k // 2 + (k % 2) * (wide // 2)


def rows_kernel(wide, *refs):
    half = wide // 2
    grads = refs[:half]
    (
        src_ref, up_ref, up_two, up_one, down_ref, down_two, down_one, dst_ref, grad_ref, up_full,
        down_full, send, recv, local,
    ) = refs[half:]
    w, z = lax.axis_index("wide"), lax.axis_index("narrow")
    line = [flipped(z, k) for k in range(4)]
    is_middle = (z == 1) | (z == 2)
    is_end = (z == 0) | (z == 3)
    sender = Sender(send, recv)
    up_at = lambda n: up_full.at[:, n]
    down_at = lambda n: down_full.at[n]
    moves = [
        (src_ref, dst_ref.at[0]),
        (down_ref, down_at(z)), (down_two, down_at(line[2])), (down_one, down_at(line[1])),
        (up_ref, up_at(z)), (up_two, up_at(line[2])), (up_one, up_at(line[1])),
    ] + [(grads[n], grad_ref.at[n]) for n in range(half)]
    own = [pltpu.make_async_copy(src, dst, local.at[n]) for n, (src, dst) in enumerate(moves)]
    for copy in own:
        copy.start()
    greet(
        [wide_device(flipped(w, k)) for k in wide_steps(wide)]
        + [narrow_device(line[k]) for k in (1, 3)]
    )
    gather = WideGather(
        sender, w, wide, lambda k: src_ref if k == 0 else dst_ref.at[place_of(k, wide)],
        lambda k, to: dst_ref.at[place_of(k ^ to, wide)],
    )
    middles = [
        sender.plan(up_ref, up_at(z), narrow_device(line[3])),
        sender.plan(down_ref, down_at(z), narrow_device(line[3])),
    ]
    relays = [
        sender.plan(up_two, up_at(line[2]), narrow_device(line[1])),
        sender.plan(down_two, down_at(line[2]), narrow_device(line[1])),
    ]
    gather.start()

    @pl.when(is_middle)
    def _():
        for copy in middles + relays:
            copy.start()

    sibling = wide_device(flipped(w, 1))
    copies = [sender.plan(grads[n], grad_ref.at[half + n], sibling) for n in range(half)]
    for copy in copies:
        copy.start()
    gather.pass_on()

    @pl.when(is_middle)
    def _():
        for copy in middles:
            copy.wait()
        for copy in relays:
            copy.wait_send()

    @pl.when(is_end)
    def _():
        for copy in relays:
            copy.wait_recv()

    for copy in own + copies:
        copy.wait()
    gather.finish()


def gather_rows(array, grads, ups, downs, collective_id):
    half = len(grads)
    wide = 2 * half
    whole = jax.ShapeDtypeStruct((wide,) + array.shape, array.dtype)
    up_shape = ups[0].shape
    full = jax.ShapeDtypeStruct((up_shape[0], 4) + up_shape[1:], BF16)
    return pl.pallas_call(
        functools.partial(rows_kernel, wide),
        out_shape=[whole, whole, full, jax.ShapeDtypeStruct((4,) + downs[0].shape, BF16)],
        in_specs=[ANY] * (half + 7),
        out_specs=[VMEM, ANY if wide > 8 else VMEM, VMEM, VMEM],
        scratch_shapes=[DMA((2 * wide + 4,)), DMA((2 * wide + 4,)), DMA((half + 7,))],
        compiler_params=pltpu.CompilerParams(
            collective_id=collective_id, has_side_effects=True, vmem_limit_bytes=48 * 2**20
        ),
    )(*grads, array, *ups, *downs)


def hidden_kernel(
    half, normed_ref, grad_ref, up_ref, down_ref, hidden_ref, mid_ref, even_ref, odd_ref, branch_ref
):
    size = down_ref.shape[0]
    gate_up = dot_f32(normed_ref[...], up_ref[...])
    grad_hidden = dot_f32(grad_ref[...], down_ref[...], ((1,), (1,)))
    gate, up = gate_up[:, :size], gate_up[:, size:]
    opened = jax.nn.sigmoid(gate)
    acted = gate * opened
    hidden_ref[...] = (acted * up).astype(BF16)
    mid_ref[:, :size] = (grad_hidden * up * (opened * (1.0 + gate * (1.0 - opened)))).astype(BF16)
    mid_ref[:, size:] = (grad_hidden * acted).astype(BF16)
    grad_normed = dot_f32(mid_ref[...], up_ref[...], ((1,), (1,))).astype(BF16)
    branch_ref[...] = dot_f32(hidden_ref[...], down_ref[...]).astype(BF16)
    step = pl.program_id(0)

    @pl.when(step < half)
    def _():
        even_ref[...] = grad_normed

    @pl.when(step >= half)
    def _():
        odd_ref[...] = grad_normed


def feed_forward(normed, grad, up_full, down_full, rows):
    total, width = normed.shape
    blocks = total // rows
    half = blocks // 2
    size = down_full.shape[0]
    row_block = lambda columns: pl.BlockSpec((rows, columns), lambda i: (i, 0))
    fixed = lambda array: pl.BlockSpec(array.shape, lambda i: (0, 0))
    return pl.pallas_call(
        functools.partial(hidden_kernel, half),
        grid=(blocks,),
        in_specs=[row_block(width), row_block(width), fixed(up_full), fixed(down_full)],
        out_specs=[
            row_block(size), row_block(2 * size),
            pl.BlockSpec((rows, width), lambda i: (jnp.minimum(i, half - 1), 0)),
            pl.BlockSpec((rows, width), lambda i: (jnp.maximum(i - half, 0), 0)),
            row_block(width),
        ],
        out_shape=[
            jax.ShapeDtypeStruct((total, size), BF16),
            jax.ShapeDtypeStruct((total, 2 * size), BF16),
            jax.ShapeDtypeStruct((total // 2, width), BF16),
            jax.ShapeDtypeStruct((total // 2, width), BF16),
            jax.ShapeDtypeStruct((total, width), BF16),
        ],
        compiler_params=pltpu.CompilerParams(vmem_limit_bytes=48 * 2**20),
    )(normed, grad, up_full, down_full)


def middle_kernel(
    wide, even_ref, got_ref, branch_ref, up_ref, down_ref, norm_sum, branch_sum, up_src, down_src,
    up_one, down_one, up_acc, down_acc, core_buf, own_buf, far_buf, branch_buf, up_join, up_mid,
    down_join, down_mid, up_own, down_own, send, recv, local,
):
    w, z = lax.axis_index("wide"), lax.axis_index("narrow")
    line = [flipped(z, k) for k in range(4)]
    half = wide // 2
    unit = up_src.shape[1]
    part = down_src.shape[1]
    sender = Sender(send, recv)
    is_middle = (z == 1) | (z == 2)
    is_end = (z == 0) | (z == 3)

    def up_share(n):
        return up_ref.at[:, pl.ds(pl.multiple_of(n * unit, unit), unit)]

    def down_share(n):
        return down_ref.at[:, pl.ds(pl.multiple_of(n * part, part), part)]

    moves = [
        (up_share(line[2]), up_src), (down_share(line[2]), down_src),
        (up_share(z), up_own), (down_share(z), down_own),
        (up_share(line[1]), up_one), (down_share(line[1]), down_one),
    ]
    moves += [(got_ref.at[n], core_buf.at[n]) for n in range(half)]
    moves += [(even_ref.at[n], own_buf.at[n]) for n in range(half)]
    pairs = branch_sum.shape[0]
    moves += [(branch_ref.at[n], branch_sum.at[n]) for n in range(pairs)]
    own = [pltpu.make_async_copy(src, dst, local.at[n]) for n, (src, dst) in enumerate(moves)]
    for copy in own:
        copy.start()
    greet(
        [wide_device(flipped(w, k)) for k in wide_steps(wide)]
        + [narrow_device(line[k]) for k in (1, 3)]
    )
    sibling = wide_device(flipped(w, 1))
    far = [
        sender.plan(own_buf.at[n], far_buf.at[n - 1], wide_device(flipped(w, 2 * n)))
        for n in range(1, half)
    ]
    branch_core = [
        sender.plan(branch_ref.at[pairs + n], branch_buf.at[n], sibling) for n in range(pairs)
    ]
    joins = [
        sender.plan(up_share(line[3]), up_join, narrow_device(line[1])),
        sender.plan(down_share(line[3]), down_join, narrow_device(line[1])),
    ]
    mids = [
        sender.plan(up_share(line[3]), up_mid, narrow_device(line[3])),
        sender.plan(down_share(line[3]), down_mid, narrow_device(line[3])),
    ]
    order = list(range(1, half)) + [0]

    @pl.when(is_end)
    def _():
        for copy in joins:
            copy.start()

    @pl.when(is_middle)
    def _():
        for copy in mids:
            copy.start()

    for n in order:
        own[6 + n].wait()
        own[6 + half + n].wait()
        total = own_buf[n].astype(F32) + core_buf[n].astype(F32)
        own_buf[n] = total.astype(BF16)
        if n > 0:
            far[n - 1].start()
    for copy in branch_core:
        copy.start()
    for n in range(pairs):
        branch_core[n].wait_recv()
        own[6 + 2 * half + n].wait()
        total = branch_sum[n].astype(F32) + branch_buf[n].astype(F32)
        branch_sum[n] = total.astype(BF16)
    for n in range(6):
        own[n].wait()

    @pl.when(is_middle)
    def _():
        for copy in joins:
            copy.wait_recv()
        up_src[...] = (up_src[...].astype(F32) + up_join[...].astype(F32)).astype(BF16)
        down_src[...] = (down_src[...].astype(F32) + down_join[...].astype(F32)).astype(BF16)

    total = own_buf[0].astype(F32)
    for n in range(1, half):
        far[n - 1].wait_recv()
        total = total + far_buf[n - 1].astype(F32)
    norm_sum[...] = total
    up_acc[...] = up_own[...].astype(F32)
    down_acc[...] = down_own[...].astype(F32)

    @pl.when(is_middle)
    def _():
        for copy in mids:
            copy.wait()
        up_acc[...] += up_mid[...].astype(F32)
        down_acc[...] += down_mid[...].astype(F32)

    @pl.when(is_end)
    def _():
        for copy in joins:
            copy.wait_send()

    for copy in far + branch_core:
        copy.wait_send()


def middle_sums(even, got, branch, grad_up, grad_down, collective_id):
    half, rows, width = even.shape
    wide = 2 * half
    unit, part = grad_up.shape[1] // 4, grad_down.shape[1] // 4
    up_shape, down_shape = (grad_up.shape[0], unit), (grad_down.shape[0], part)
    steps = 4 * half + 6
    rows_buf = pltpu.VMEM((half, rows, width), BF16)
    pairs = branch.shape[0] // 2
    return pl.pallas_call(
        functools.partial(middle_kernel, wide),
        out_shape=[
            jax.ShapeDtypeStruct((rows, width), F32),
            jax.ShapeDtypeStruct((pairs,) + branch.shape[1:], BF16),
            *[jax.ShapeDtypeStruct(up_shape, BF16), jax.ShapeDtypeStruct(down_shape, BF16)] * 2,
            jax.ShapeDtypeStruct(up_shape, F32),
            jax.ShapeDtypeStruct(down_shape, F32),
        ],
        in_specs=[ANY] * 5,
        out_specs=[VMEM] * 8,
        scratch_shapes=[
            rows_buf, rows_buf, pltpu.VMEM((half - 1, rows, width), BF16),
            pltpu.VMEM((pairs,) + branch.shape[1:], BF16),
            *[pltpu.VMEM(up_shape, BF16)] * 2, *[pltpu.VMEM(down_shape, BF16)] * 2,
            pltpu.VMEM(up_shape, BF16), pltpu.VMEM(down_shape, BF16),
            DMA((steps,)), DMA((steps,)), DMA((6 + 3 * half,)),
        ],
        compiler_params=pltpu.CompilerParams(
            collective_id=collective_id, has_side_effects=True, vmem_limit_bytes=58 * 2**20
        ),
    )(even, got, branch, grad_up, grad_down)


def last_kernel(
    wide, rows, own_width, own_heads, norm_ref, in_ref, out_ref, up_parts, down_parts, branch_refs,
    token_ref, middle_ref, grad_ref, gain_ref, small_ref, output, grad_tokens, grad_in, grad_out,
    grad_up, grad_down, totals, join_buf, one_buf, mid_buf, two_buf, two_src, own_norm, norm_sum,
    in_core, in_own, in_far, in_sum, in_got, out_own, out_buf, up_low, up_bufs, up_got, down_low,
    down_bufs, down_got, branch_bufs, narrow_buf, wide_buf, sum_buf, send, recv, down_send, down_recv,
    local,
):
    w, z = lax.axis_index("wide"), lax.axis_index("narrow")
    line = [flipped(z, k) for k in range(4)]
    half = wide // 2
    unit = up_low.shape[1]
    wide_rows, width = grad_in.shape[0], token_ref.shape[1]
    sender = Sender(send, recv)
    is_middle = (z == 1) | (z == 2)
    is_end = (z == 0) | (z == 3)

    def norm_block(n):
        return norm_ref.at[pl.ds(pl.multiple_of(n * rows, rows), rows), :]

    def out_columns(n):
        return out_ref.at[:, pl.ds(pl.multiple_of(n * own_width, LANES), own_width)]

    def up_rows(n):
        return up_low.at[pl.ds(pl.multiple_of(n * wide_rows, 16), wide_rows), :]

    def up_columns(n):
        return up_got.at[:, pl.ds(pl.multiple_of(n * unit, LANES), unit)]

    def section(n):
        return in_sum.at[:, pl.ds(pl.multiple_of(n * own_width, LANES), own_width + LANES)]

    moves = [
        (norm_block(line[2]), two_src), (norm_block(z), own_norm), (out_columns(z), out_own),
    ]
    moves += [(in_ref.at[flipped(w, 2 * n)], in_own.at[n]) for n in range(half)]
    ffn_at = len(moves)
    moves += [(ref, up_bufs.at[n]) for n, ref in enumerate(up_parts)]
    moves += [(ref, down_bufs.at[n]) for n, ref in enumerate(down_parts)]
    branch_at = len(moves)
    moves += [(ref, branch_bufs.at[n]) for n, ref in enumerate(branch_refs)]
    own = [pltpu.make_async_copy(src, dst, local.at[n]) for n, (src, dst) in enumerate(moves)]
    for copy in own:
        copy.start()
    greet(
        [narrow_device(line[k]) for k in (1, 2, 3)]
        + [wide_device(flipped(w, k)) for k in range(1, wide)]
    )
    sibling = wide_device(flipped(w, 1))
    joined = sender.plan(norm_block(line[3]), join_buf, narrow_device(line[1]))
    one = sender.plan(norm_block(line[1]), one_buf, narrow_device(line[1]))
    middle = sender.plan(norm_block(line[3]), mid_buf, narrow_device(line[3]))
    two = sender.plan(two_src, two_buf, narrow_device(line[2]))
    core = [
        sender.plan(in_ref.at[flipped(w, 2 * n + 1)], in_core.at[n], sibling) for n in range(half)
    ]
    far = [
        sender.plan(in_own.at[n], in_far.at[n - 1], wide_device(flipped(w, 2 * n)))
        for n in range(1, half)
    ]
    sections = [
        sender.plan(section(line[k]), in_got.at[z], narrow_device(line[k])) for k in (2, 3, 1)
    ]
    outs = [
        sender.plan(out_columns(line[k]), out_buf.at[k - 1], narrow_device(line[k]))
        for k in (1, 2, 3)
    ]
    ups = [
        sender.plan(up_rows(flipped(w, k)), up_columns(w), wide_device(flipped(w, k)))
        for k in range(1, wide)
    ]
    first = [
        sender.plan(sum_buf, narrow_buf.at[z], narrow_device(line[k])) for k in (1, 2, 3)
    ]
    second = [
        sender.plan(sum_buf, wide_buf.at[w], wide_device(flipped(w, k))) for k in range(1, wide)
    ]
    parity, target = lax.rem(w, 2), lax.div(w, 2)
    depth = down_low.shape[0] // 2
    down_at = pl.ds(pl.multiple_of(parity * depth, 16), depth)
    downs = []
    for n in range(2):
        owner = target + n * half
        src, dst = down_low.at[pl.ds(n * depth, depth), :], down_got.at[down_at, :]
        push = pltpu.make_async_remote_copy(
            src_ref=src, dst_ref=dst, send_sem=down_send.at[n], recv_sem=down_recv.at[parity],
            device_id=wide_device(owner), device_id_type=MESH,
        )
        stay = pltpu.make_async_copy(src, dst, local.at[len(moves) + 1 + n])
        downs.append((owner == w, push, stay))

    order = list(range(1, half)) + [0]
    for n in order:
        core[n].start()

    @pl.when(is_end)
    def _():
        joined.start()

    @pl.when(is_middle)
    def _():
        middle.start()

    for n in order:
        core[n].wait_recv()
        own[3 + n].wait()
        total = in_own[n].astype(F32) + in_core[n].astype(F32)
        in_own[n] = total.astype(BF16)
        if n > 0:
            far[n - 1].start()
    own[0].wait()

    @pl.when(is_middle)
    def _():
        joined.wait_recv()
        two_src[...] = (two_src[...].astype(F32) + join_buf[...].astype(F32)).astype(BF16)

    two.start()
    one.start()
    for n in range(6):
        own[ffn_at + n].wait()
    up_low[...] = add_up([up_bufs[n] for n in range(3)]).astype(BF16)
    down_low[...] = add_up([down_bufs[n] for n in range(3)]).astype(BF16)
    for copy in ups:
        copy.start()
    for stays, push, stay in downs:
        pl.when(stays)(stay.start)
        pl.when(jnp.logical_not(stays))(push.start)
    up_got[:, pl.ds(pl.multiple_of(w * unit, LANES), unit)] = up_low[
        pl.ds(pl.multiple_of(w * wide_rows, 16), wide_rows), :
    ]
    total = middle_ref[...]
    for n in range(half):
        own[branch_at + n].wait()
        total = total + branch_bufs[n].astype(F32)
    output[...] = total.astype(BF16)

    total = in_own[0].astype(F32)
    for n in range(1, half):
        far[n - 1].wait_recv()
        total = total + in_far[n - 1].astype(F32)
    in_sum[...] = total.astype(BF16)
    mine = pltpu.make_async_copy(section(z), in_got.at[z], local.at[len(moves)])
    mine.start()
    for copy in sections + outs:
        copy.start()
    own[1].wait()
    own[2].wait()
    one.wait_recv()
    norm_sum[...] = own_norm[...].astype(F32) + one_buf[...].astype(F32)

    @pl.when(is_middle)
    def _():
        middle.wait()
        norm_sum[...] += mid_buf[...].astype(F32)

    two.wait_recv()
    grads = norm_sum[...] + two_buf[...].astype(F32)
    values = token_ref[...].astype(F32)
    factor = rms_factor(values)
    normed = values * factor
    scaled = grads * gain_ref[0:1, :]
    inner = jnp.mean(scaled * normed, axis=-1, keepdims=True)
    grad_tokens[...] = grad_ref[...] + factor * (scaled - normed * inner)
    narrow_buf[z] = small_ref[...]
    narrow_buf[z, 0:1, :] = jnp.sum(grads * normed, axis=0, keepdims=True)
    sum_buf[...] = narrow_buf[z]
    for copy in first:
        copy.start()

    for copy in ups:
        copy.wait_recv()
    grad_up[...] = up_got[...].astype(F32)
    for n, (stays, push, stay) in enumerate(downs):
        pl.when(stays)(stay.wait)
        pl.when(jnp.logical_not(stays))(push.wait_send)
    for n in range(2):
        source = lax.rem(2 * w + n, wide)
        arrived = pltpu.make_async_remote_copy(
            src_ref=down_low.at[pl.ds(0, depth), :], dst_ref=down_got.at[pl.ds(n * depth, depth), :],
            send_sem=down_send.at[n], recv_sem=down_recv.at[n], device_id=sibling,
            device_id_type=MESH,
        )
        pl.when(source != w)(arrived.wait_recv)
    grad_down[...] = down_got[...].astype(F32)

    for copy in first:
        copy.wait()
    sum_buf[...] = narrow_buf[0] + narrow_buf[1] + narrow_buf[2] + narrow_buf[3]
    for copy in second:
        copy.start()
    wide_buf[w] = sum_buf[...]

    total = out_own[...].astype(F32)
    for n in range(3):
        outs[n].wait_recv()
        total = total + out_buf[n].astype(F32)
    grad_out[...] = total
    for copy in sections:
        copy.wait_recv()
    mine.wait()
    row, lane = iota((LANES, LANES), 0), iota((LANES, LANES), 1)
    last = jnp.zeros((wide_rows, LANES), F32)
    for n in range(4):
        group = lax.div(row, own_heads)
        place = group * (4 * own_heads) + n * own_heads + row - group * own_heads
        spot = ((lane == place) & (row < 3 * own_heads)).astype(BF16)
        last = last + dot_f32(in_got[n, :, own_width:], spot)
    after = jnp.where(z == 3, last, in_got[0, :, own_width:].astype(F32))
    whole = jnp.concatenate(
        [in_got[n, :, :own_width].astype(F32) for n in range(4)] + [after], axis=1
    )
    move = whole.shape[1] - (grad_in.shape[1] - width) * z
    grad_in[...] = pltpu.roll(whole, lax.rem(move, whole.shape[1]), 1)[:, : grad_in.shape[1]]

    for copy in second:
        copy.wait()
    total = wide_buf[0]
    for n in range(1, wide):
        total = total + wide_buf[n]
    totals[...] = total

    @pl.when(is_end)
    def _():
        joined.wait_send()

    for copy in [one, two] + core + far + sections + outs + ups:
        copy.wait_send()


def grouped_last_kernel(wide, rows, own_width, own_heads, *refs):
    half = wide // 2
    last_kernel(
        wide, rows, own_width, own_heads, *refs[:3], refs[3:6], refs[6:9], refs[9 : 9 + half],
        *refs[9 + half :],
    )


def last_part(
    norm_part, in_part, out_low, ups, downs, branches, tokens, middle, grad_middle, gain, small, own_width,
    own_heads, shard, collective_id,
):
    wide, wide_rows, columns = in_part.shape
    half = wide // 2
    rows, width = tokens.shape
    unit = ups[0].shape[1]
    steps = 4 + 2 * half + 9 + 2 * wide
    shape = jax.ShapeDtypeStruct
    vmem = lambda *dims: pltpu.VMEM(dims, BF16)
    return pl.pallas_call(
        functools.partial(grouped_last_kernel, wide, rows, own_width, own_heads),
        out_shape=[
            shape((rows, width), BF16), shape((rows, width), F32), shape((wide_rows, shard), F32),
            shape((wide_rows, own_width), F32), shape((wide_rows, wide * unit), F32),
            shape(downs[0].shape, F32), shape(small.shape, F32),
        ],
        in_specs=[ANY] * (9 + half) + [VMEM] * 5,
        out_specs=[VMEM] * 7,
        scratch_shapes=[
            *[vmem(rows, width)] * 6, pltpu.VMEM((rows, width), F32),
            vmem(half, wide_rows, columns), vmem(half, wide_rows, columns),
            vmem(half - 1, wide_rows, columns), vmem(wide_rows, columns),
            vmem(4, wide_rows, own_width + LANES), vmem(wide_rows, own_width),
            vmem(3, wide_rows, own_width), vmem(*ups[0].shape), vmem(3, *ups[0].shape),
            vmem(wide_rows, wide * unit), vmem(*downs[0].shape), vmem(3, *downs[0].shape),
            vmem(*downs[0].shape), vmem(half, rows, width),
            pltpu.VMEM((4,) + small.shape, F32), pltpu.VMEM((wide,) + small.shape, F32),
            pltpu.VMEM(small.shape, F32),
            DMA((steps,)), DMA((steps,)), DMA((2,)), DMA((2,)), DMA((12 + 2 * half,)),
        ],
        compiler_params=pltpu.CompilerParams(
            collective_id=collective_id, has_side_effects=True, vmem_limit_bytes=60 * 2**20
        ),
    )(
        norm_part, in_part, out_low, *ups, *downs, *branches, tokens, middle, grad_middle,
        jnp.broadcast_to(gain[None], (8, width)), small,
    )


def rms_factor(values):
    return lax.rsqrt(jnp.mean(values * values, axis=-1, keepdims=True) + EPSILON)


def rms_back(values, gain, grad):
    factor = rms_factor(values)
    normed = values * factor
    grad_gain = jnp.sum(grad * normed, axis=0)
    scaled = grad * gain
    inner = jnp.mean(scaled * normed, axis=-1, keepdims=True)
    return (factor * (scaled - normed * inner), grad_gain)


def log_sigmoid(v):
    return jnp.minimum(v, 0.0) - jnp.log1p(jnp.exp(-jnp.abs(v)))


def iota(shape, dim):
    return lax.broadcasted_iota(jnp.int32, shape, dim)


def running_sum(v, reverse):
    rows = v.shape[0]
    index = iota(v.shape, 0)
    step = 1
    while step < rows:
        if reverse:
            v = v + jnp.where(index < rows - step, pltpu.roll(v, rows - step, 0), 0.0)
        else:
            v = v + jnp.where(index >= step, pltpu.roll(v, step, 0), 0.0)
        step *= 2
    return v


def half_of(lane, head_size):
    return (lane >= head_size).astype(jnp.int32)


def spread(first, head_size):
    row, lane = iota((LANES, LANES), 0), iota((LANES, LANES), 1)
    return row == first + half_of(lane, head_size)


def collect(first, head_size):
    row, lane = iota((LANES, LANES), 0), iota((LANES, LANES), 1)
    return lane == first + half_of(row, head_size)


def same_head(head_size):
    row, lane = iota((LANES, LANES), 0), iota((LANES, LANES), 1)
    return (half_of(row, head_size) == half_of(lane, head_size)).astype(F32)


def exact_dot(left, right):
    return lax.dot_general(
        left, right, (((1,), (0,)), ((), ())), precision=EXACT, preferred_element_type=F32
    )


def head_mean(v, head_size):
    return exact_dot(v, same_head(head_size)) * (1.0 / head_size)


def prologue(pair, heads, head_size, q_ref, k_ref, v_ref, small_low, cont):
    spot = lambda group: spread(group * heads + 2 * pair, head_size).astype(BF16)
    key_mix = jax.nn.sigmoid(dot_f32(small_low, spot(1)))
    value_mix = jax.nn.sigmoid(dot_f32(small_low, spot(2)))
    queries = q_ref[...].astype(BF16).astype(F32)
    keys = k_ref[...].astype(BF16).astype(F32)
    values = v_ref[...].astype(BF16).astype(F32)
    key_step = pltpu.roll(keys, 1, 0) * cont - keys
    value_step = pltpu.roll(values, 1, 0) * cont - values
    shifted = keys + key_mix * key_step
    value_low = (values + value_mix * value_step).astype(BF16)
    query_factor = lax.rsqrt(head_mean(queries * queries, head_size) + EPSILON)
    key_factor = lax.rsqrt(head_mean(shifted * shifted, head_size) + EPSILON)
    return (
        queries * query_factor,
        shifted * key_factor,
        value_low,
        query_factor,
        key_factor,
        key_mix,
        value_mix,
        key_step,
        value_step,
    )


def small_columns(small_ref, bias_ref):
    return (small_ref[...] + bias_ref[0:1, :]).astype(BF16)


def decay_of(small_low, cont):
    return running_sum(log_sigmoid(small_low.astype(F32)) - SEPARATE * (1.0 - cont), False)


def forward_pair(
    pair, heads, head_size, block, q_ref, k_ref, v_ref, gate_ref, small_low, cont, decay_all,
    mixed_ref, att_ref, log_ref,
):
    query, key, value_low, *unused = prologue(
        pair, heads, head_size, q_ref, k_ref, v_ref, small_low, cont
    )
    rows = query.shape[0]
    query = query.astype(BF16) * BF16(head_size**-0.5)
    key = key.astype(BF16)
    decay = exact_dot(decay_all, spread(2 * pair, head_size).astype(F32))
    decay_rows = decay.T
    lane = iota((1, LANES), 1)
    ones = jnp.ones((rows, LANES), BF16)
    value_wide = jnp.concatenate([value_low, ones], axis=1)
    for i in range(rows // block):
        lo, hi = i * block, (i + 1) * block
        row_index = iota((block, hi), 0) + lo
        visible = iota((block, hi), 1) <= row_index
        outs, sums = [], []
        for head in range(2):
            mine = (lane >= head_size) if head else (lane < head_size)
            at = head * head_size
            left = jnp.where(mine, query[lo:hi], BF16(0.0))
            scores = dot_f32(left, key[:hi], ((1,), (1,)))
            scores = scores + decay[lo:hi, at : at + 1] - decay_rows[at : at + 1, :hi]
            weights = jnp.where(visible, jnp.exp(scores), 0.0).astype(BF16)
            both = dot_f32(weights, value_wide[:hi])
            outs.append(both[:, :LANES])
            sums.append(both[:, LANES:])
        first = lane < head_size
        total = jnp.where(first, sums[0], sums[1])
        attended = (jnp.where(first, outs[0], outs[1]) / total).astype(BF16)
        att_ref[lo:hi, :] = attended
        log_ref[lo:hi, :] = jnp.log(total)
        opened = jax.nn.sigmoid(gate_ref[lo:hi, :])
        mixed_ref[lo:hi, :] = (attended.astype(F32) * opened).astype(BF16)


def forward_kernel(
    heads, head_size, block, q_ref, k_ref, v_ref, gate_ref, small_ref, bias_ref, cont_ref,
    mixed_ref, att_ref, log_ref, decay_scr,
):
    pair = pl.program_id(0)
    cont = cont_ref[...]
    small_low = small_columns(small_ref, bias_ref)

    @pl.when(pair == 0)
    def _():
        decay_scr[...] = decay_of(small_low, cont)

    forward_pair(
        pair, heads, head_size, block, q_ref, k_ref, v_ref, gate_ref, small_low, cont,
        decay_scr[...], mixed_ref, att_ref, log_ref,
    )


def share_of(ref, like, n):
    size = like.shape[1]
    if ref.shape[1] == size:
        return ref
    return ref.at[:, pl.ds(pl.multiple_of(n * size, size), size)]


def backward_kernel(
    heads, head_size, block, wide, *refs
):
    q_ref, k_ref, v_ref, gate_ref, small_ref, bias_ref, cont_ref, att_ref, log_ref, grad_ref = refs[:10]
    in_ref, normed_ref, up_src, down_src, up_one, down_one, part_ref, branch_ref = refs[10:18]
    out_ref, bias_grad_ref, norm_ref, in_part_ref, part_sum = refs[18:23]
    up_two_got, down_two_got, up_one_got, down_one_got, branch_got = refs[23:28]
    decay_scr, small_scr, dq_scr, part_core, part_own, part_far, send, recv, local = refs[28:]
    pair = pl.program_id(0)
    pairs = heads * head_size // LANES
    half = wide // 2
    row_steps = out_ref.shape[0] // norm_ref.shape[0]
    w, z = lax.axis_index("wide"), lax.axis_index("narrow")
    sender = Sender(send, recv)
    one, two = flipped(z, 1), flipped(z, 2)
    copies = [
        sender.plan(up_src, up_two_got, narrow_device(two)),
        sender.plan(down_src, down_two_got, narrow_device(two)),
        sender.plan(share_of(up_one, up_src, one), up_one_got, narrow_device(one)),
        sender.plan(share_of(down_one, down_src, one), down_one_got, narrow_device(one)),
    ]
    core = [
        sender.plan(part_ref.at[flipped(w, 2 * n + 1)], part_core.at[n], wide_device(flipped(w, 1)))
        for n in range(half)
    ]
    far = [
        sender.plan(part_own.at[n], part_far.at[n - 1], wide_device(flipped(w, 2 * n)))
        for n in range(1, half)
    ]
    branches = [
        sender.plan(branch_ref.at[k // 2], branch_got.at[n], wide_device(flipped(w, k)))
        for n, k in enumerate(diagonal_steps(wide))
    ]
    own = [
        pltpu.make_async_copy(part_ref.at[flipped(w, 2 * n)], part_own.at[n], local.at[n])
        for n in range(half)
    ]

    @pl.when(pair == 0)
    def _():
        greet(
            [narrow_device(one), narrow_device(two)]
            + [wide_device(flipped(w, k)) for k in wide_steps(wide)]
        )
        for copy in copies + core + own + branches:
            copy.start()

    @pl.when(pair == 1)
    def _():
        for n in range(half):
            core[n].wait_recv()
            own[n].wait()
            part_own[n] = (part_own[n].astype(F32) + part_core[n].astype(F32)).astype(BF16)
            if n > 0:
                far[n - 1].start()

    @pl.when(pair < pairs)
    def _():
        backward_pair(
            pair, pairs, heads, head_size, block, q_ref, k_ref, v_ref, gate_ref, small_ref,
            bias_ref, cont_ref, att_ref, log_ref, grad_ref, out_ref, bias_grad_ref, decay_scr,
            small_scr, dq_scr,
        )

    @pl.when((pair >= pairs) & (pair < pairs + row_steps))
    def _():
        size = norm_ref.shape[0]
        at = pl.ds(pl.multiple_of((pair - pairs) * size, size), size)
        norm_ref[...] = dot_f32(out_ref[at, :], in_ref[...], ((1,), (1,))).astype(BF16)

    @pl.when(pair >= pairs + row_steps)
    def _():
        in_part_ref[...] = dot_f32(normed_ref[...], out_ref[...], ((0,), (0,))).astype(BF16)

    @pl.when(pair == pl.num_programs(0) - 1)
    def _():
        total = part_own[0].astype(F32)
        for n in range(1, half):
            far[n - 1].wait_recv()
            total = total + part_far[n - 1].astype(F32)
        part_sum[...] = total.astype(BF16)
        for copy in copies + branches:
            copy.wait()
        for copy in core + far:
            copy.wait_send()


def backward_pair(
    pair, pairs, heads, head_size, block, q_ref, k_ref, v_ref, gate_ref, small_ref, bias_ref, cont_ref,
    att_ref, log_ref, grad_ref, out_ref, bias_grad_ref, decay_scr, small_scr, dq_scr,
):
    cont = cont_ref[...]
    small_low = small_columns(small_ref, bias_ref)
    rows = cont.shape[0]
    width = heads * head_size

    @pl.when(pair == 0)
    def _():
        decay_scr[...] = decay_of(small_low, cont)
        small_scr[...] = jnp.zeros_like(small_scr)

    (
        query_norm, key_norm, value_low, query_factor, key_factor, key_mix, value_mix, key_step,
        value_step,
    ) = prologue(pair, heads, head_size, q_ref, k_ref, v_ref, small_low, cont)
    query = query_norm.astype(BF16) * BF16(head_size**-0.5)
    key = key_norm.astype(BF16)
    opened = jax.nn.sigmoid(gate_ref[...])
    attended = att_ref[...].astype(F32)
    grad_mixed = grad_ref[...].astype(F32)
    grad_low = (grad_mixed * opened).astype(BF16)
    grad_gate = grad_mixed * attended * opened * (1.0 - opened)

    def columns(group):
        at = group * width + pair * LANES
        return pl.ds(pl.multiple_of(at, LANES), LANES)

    out_ref[:, columns(3)] = grad_gate.astype(BF16)
    inner = exact_dot(grad_low.astype(F32) * attended, same_head(head_size))
    decay = exact_dot(decay_scr[...], spread(2 * pair, head_size).astype(F32))
    level_rows = (decay - log_ref[...]).T
    inner_rows = inner.T
    lane = iota((1, LANES), 1)
    ones = jnp.ones((rows, LANES), BF16)
    query_wide = jnp.concatenate([query, ones], axis=1)
    key_wide = jnp.concatenate([key, ones], axis=1)
    key_parts, value_parts, query_parts = [], [], []
    for head in range(2):
        mine = (lane >= head_size) if head else (lane < head_size)
        at = head * head_size
        keys_out, values_out = [], []
        for j in range(rows // block):
            lo, hi = j * block, (j + 1) * block
            span = rows - lo
            visible = iota((block, span), 0) <= iota((block, span), 1)
            scores = dot_f32(
                jnp.where(mine, key[lo:hi], BF16(0.0)), query[lo:], ((1,), (1,))
            )
            scores = scores + level_rows[at : at + 1, lo:] - decay[lo:hi, at : at + 1]
            probs = jnp.where(visible, jnp.exp(scores), 0.0)
            grad_probs = dot_f32(
                jnp.where(mine, value_low[lo:hi], BF16(0.0)), grad_low[lo:], ((1,), (1,))
            )
            grad_scores = (probs * (grad_probs - inner_rows[at : at + 1, lo:])).astype(BF16)
            values_out.append(dot_f32(probs.astype(BF16), grad_low[lo:]))
            keys_out.append(dot_f32(grad_scores, query_wide[lo:]))
            part = dot_f32(grad_scores, key_wide[lo:hi], ((0,), (0,)))
            if j == 0:
                dq_scr[...] = part
            else:
                dq_scr[lo:, :] += part
        key_parts.append(jnp.concatenate(keys_out, axis=0))
        value_parts.append(jnp.concatenate(values_out, axis=0))
        query_parts.append(dq_scr[...])
    first = lane < head_size

    def join(parts):
        return jnp.where(first, parts[0], parts[1])

    grad_query = join([p[:, :LANES] for p in query_parts]) * head_size**-0.5
    grad_key = join([p[:, :LANES] for p in key_parts])
    grad_value = join(value_parts)
    grad_decay = join([p[:, LANES:] for p in query_parts]) - join([p[:, LANES:] for p in key_parts])

    def norm_back(grad, normed, factor):
        return factor * (grad - normed * head_mean(grad * normed, head_size))

    def shift_back(grad, mix):
        return grad * (1.0 - mix) + pltpu.roll(grad * mix * cont, rows - 1, 0)

    grad_query = norm_back(grad_query, query_norm, query_factor)
    grad_shifted = norm_back(grad_key, key_norm, key_factor)
    out_ref[:, columns(0)] = grad_query.astype(BF16)
    out_ref[:, columns(1)] = shift_back(grad_shifted, key_mix).astype(BF16)
    out_ref[:, columns(2)] = shift_back(grad_value, value_mix).astype(BF16)
    key_logit = grad_shifted * key_step * key_mix * (1.0 - key_mix)
    value_logit = grad_value * value_step * value_mix * (1.0 - value_mix)
    single = (lax.rem(lane, head_size) == 0).astype(F32)
    small_scr[...] += (
        exact_dot(grad_decay * single, collect(2 * pair, head_size).astype(F32))
        + exact_dot(key_logit, collect(heads + 2 * pair, head_size).astype(F32))
        + exact_dot(value_logit, collect(2 * heads + 2 * pair, head_size).astype(F32))
    )

    @pl.when(pair == pairs - 1)
    def _():
        grads = small_scr[...]
        forget = running_sum(grads, True) * jax.nn.sigmoid(-small_low.astype(F32))
        result = jnp.where(lane < heads, forget, grads)
        out_ref[:, 4 * width :] = result.astype(BF16)
        bias_grad_ref[...] = jnp.broadcast_to(
            jnp.sum(result, axis=0, keepdims=True), bias_grad_ref.shape
        )


def attention_specs(rows, pairs):
    def block_at(group):
        return pl.BlockSpec((rows, LANES), lambda p: (0, group * pairs + jnp.minimum(p, pairs - 1)))

    def fixed(height, column=0):
        return pl.BlockSpec((height, LANES), lambda p: (0, column))

    base = [block_at(0), block_at(1), block_at(2), block_at(3), fixed(rows, 4 * pairs), fixed(8), fixed(rows)]
    return base, pl.BlockSpec((rows, LANES), lambda p: (0, jnp.minimum(p, pairs - 1)))


def attention_forward(projected, bias, cont, heads, head_size, block):
    rows = projected.shape[0]
    pairs = heads * head_size // LANES
    base, own = attention_specs(rows, pairs)
    wide = jax.ShapeDtypeStruct((rows, heads * head_size), BF16)
    return pl.pallas_call(
        functools.partial(forward_kernel, heads, head_size, block),
        grid=(pairs,),
        in_specs=base,
        out_specs=[own] * 3,
        out_shape=[wide, wide, jax.ShapeDtypeStruct(wide.shape, F32)],
        scratch_shapes=[pltpu.VMEM((rows, LANES), F32)],
        compiler_params=pltpu.CompilerParams(vmem_limit_bytes=48 * 2**20),
    )(*([projected] * 5), bias, cont)


def attention_backward(
    projected, bias, cont, attended, logs, grad, in_full, normed_one, shares, out_part, branches, heads,
    head_size, block, collective_id,
):
    rows = projected.shape[0]
    width = normed_one.shape[1]
    wide, wide_rows = out_part.shape[:2]
    half = wide // 2
    pairs = heads * head_size // LANES
    base, own = attention_specs(rows, pairs)
    columns = 4 * heads * head_size + LANES
    step = min(256, rows)
    row_steps, in_steps = rows // step, width // 256
    steps = 4 + 3 * wide
    part = lambda count: pltpu.VMEM((count, wide_rows, width), BF16)
    shape = jax.ShapeDtypeStruct

    def later(first, count):
        return lambda p: jnp.clip(p - first, 0, count - 1)

    row_at, in_at = later(pairs, row_steps), later(pairs + row_steps, in_steps)
    return pl.pallas_call(
        functools.partial(backward_kernel, heads, head_size, block, wide),
        grid=(pairs + row_steps + in_steps,),
        in_specs=base
        + [own] * 3
        + [
            pl.BlockSpec(in_full.shape, lambda p: (0, 0), pipeline_mode=pl.Buffered(1)),
            pl.BlockSpec((rows, 256), lambda p: (0, in_at(p))),
        ]
        + [ANY] * 6,
        out_specs=[
            pl.BlockSpec((rows, columns), lambda p: (0, 0)),
            pl.BlockSpec((8, LANES), lambda p: (0, 0)),
            pl.BlockSpec((step, width), lambda p: (row_at(p), 0)),
            pl.BlockSpec((256, columns), lambda p: (in_at(p), 0)),
            pl.BlockSpec((wide_rows, width), lambda p: (0, 0)),
        ]
        + [ANY] * 5,
        out_shape=[
            shape((rows, columns), BF16), shape((8, LANES), F32), shape((rows, width), BF16),
            shape((width, columns), BF16), shape((wide_rows, width), BF16),
            *[shape(share.shape, BF16) for share in shares[:2] * 2],
            shape((len(diagonal_steps(wide)),) + branches.shape[1:], BF16),
        ],
        scratch_shapes=[
            pltpu.VMEM((rows, LANES), F32), pltpu.VMEM((rows, LANES), F32),
            pltpu.VMEM((rows, 2 * LANES), F32), part(half), part(half), part(half - 1),
            DMA((steps,)), DMA((steps,)), DMA((half,)),
        ],
        compiler_params=pltpu.CompilerParams(
            collective_id=collective_id, has_side_effects=True, vmem_limit_bytes=60 * 2**20
        ),
    )(
        *([projected] * 5), bias, cont, attended, logs, grad, in_full, normed_one, *shares, out_part,
        branches,
    )


def first_kernel(
    wide, heads, head_size, block, x_ref, in_ref, out_ref, up_ref, grad_ref, down_ref, gain_one_ref,
    gain_two_ref, bias_ref, cont_ref, normed_out, in_out, out_out, proj_out, att_ref, log_ref,
    mixed_rows, middle_ref, normed_two_ref, up_out, up_two, up_one, down_got, grad_got, slot, in_buf,
    out_buf, up_buf, normed, proj, mixed, decay_scr, send, recv, local,
):
    w, z = lax.axis_index("wide"), lax.axis_index("narrow")
    line = [flipped(z, k) for k in range(4)]
    rows, width = x_ref.shape
    own_width = heads * head_size
    part_rows = out_ref.shape[0]
    is_middle = (z == 1) | (z == 2)
    is_end = (z == 0) | (z == 3)
    sender = Sender(send, recv)
    used = []

    def local_copy(src, dst):
        copy = pltpu.make_async_copy(src, dst, local.at[len(used)])
        used.append(copy)
        return copy

    def slot_rows(n):
        return slot.at[pl.ds(pl.multiple_of(n * rows, rows), rows), :]

    def weight_rows(ref, w_of, z_of):
        at = (w_of * 4 + z_of) * part_rows
        return ref.at[pl.ds(pl.multiple_of(at, 16), part_rows), :]

    def wide_rows(ref, w_of):
        at = w_of * 4 * part_rows
        return ref.at[pl.ds(pl.multiple_of(at, 16), 4 * part_rows), :]

    def by_rows(ref):
        return (
            (lambda k: wide_rows(ref, flipped(w, k))),
            (lambda k, to: wide_rows(ref, flipped(w, k))),
        )

    own_in = local_copy(in_ref.at[z], weight_rows(in_buf, w, z))
    own_out = local_copy(out_ref, weight_rows(out_buf, w, z))
    own_x = local_copy(x_ref, slot_rows(z))
    own_up = local_copy(up_ref.at[w], up_buf.at[w])
    for copy in used:
        copy.start()

    index = w * 4 + z
    down_wide = lax.div(lax.rem(index, 2 * wide), 2)
    down_narrow = lax.rem(index, 2) + 2 * lax.div(index, 2 * wide)
    from_index = 2 * wide * lax.div(z, 2) + 2 * w + lax.rem(z, 2)
    from_wide_index, from_narrow_index = lax.div(from_index, 4), lax.rem(from_index, 4)
    moves = jnp.logical_not((down_wide == w) & (down_narrow == z))
    down_push = sender.plan(
        down_ref, down_got, {"wide": down_wide, "narrow": down_narrow}
    )
    down_stay = local_copy(down_ref, down_got)

    barrier = pltpu.get_barrier_semaphore()
    partners = [narrow_device(line[k]) for k in (1, 2, 3)]
    partners += [wide_device(flipped(w, k)) for k in range(1, wide)]
    for device in partners:
        pl.semaphore_signal(barrier, inc=1, device_id=device, device_id_type=MESH)

    @pl.when(moves)
    def _():
        for device in (
            {"wide": from_wide_index, "narrow": from_narrow_index},
            {"wide": down_wide, "narrow": down_narrow},
        ):
            pl.semaphore_signal(barrier, inc=1, device_id=device, device_id_type=MESH)
        pl.semaphore_wait(barrier, len(partners) + 2)

    @pl.when(jnp.logical_not(moves))
    def _():
        pl.semaphore_wait(barrier, len(partners))

    ins = [
        sender.plan(in_ref.at[line[k]], weight_rows(in_buf, w, z), narrow_device(line[k]))
        for k in (2, 3, 1)
    ]
    outs = [
        sender.plan(out_ref, weight_rows(out_buf, w, z), narrow_device(line[k])) for k in (2, 3, 1)
    ]
    ups = [
        sender.plan(up_ref.at[flipped(w, k)], up_buf.at[w], wide_device(flipped(w, k)))
        for k in range(1, wide)
    ]
    grads = {
        k: sender.plan(grad_ref, grad_got.at[k // 2 - 1], wide_device(flipped(w, k)))
        for k in range(2, wide, 2)
    }
    two = sender.plan(x_ref, slot_rows(z), narrow_device(line[2]))
    one = sender.plan(x_ref, slot_rows(z), narrow_device(line[1]))
    middle = sender.plan(x_ref, slot_rows(z), narrow_device(line[3]))
    relay = sender.plan(slot_rows(line[2]), slot_rows(line[2]), narrow_device(line[1]))
    in_wide = WideGather(sender, w, wide, *by_rows(in_buf))
    out_wide = WideGather(sender, w, wide, *by_rows(out_buf))
    up_steps = [
        sender.plan(up_buf, up_two, narrow_device(line[2])),
        sender.plan(up_buf, up_one, narrow_device(line[1])),
    ]
    mixes = [
        sender.plan(
            mixed.at[pl.ds(pl.multiple_of(line[k] * rows, rows), rows), :],
            mixed_rows.at[:, pl.ds(pl.multiple_of(z * own_width, LANES), own_width)],
            narrow_device(line[k]),
        )
        for k in (2, 3, 1)
    ]

    for copy in ins + outs + ups:
        copy.start()
    own_in.wait()
    for copy in ins:
        copy.wait_recv()
    in_wide.start()
    two.start()
    one.start()
    own_out.wait()
    for copy in outs:
        copy.wait_recv()
    out_wide.start()
    in_wide.pass_on()
    for k in diagonal_steps(wide):
        grads[k].start()
    two.wait_recv()

    @pl.when(is_middle)
    def _():
        relay.start()
        middle.start()

    own_up.wait()
    for copy in ups:
        copy.wait_recv()
    up_back = local_copy(up_buf, up_out)
    up_back.start()
    out_wide.pass_on()
    in_wide.received()
    in_back = local_copy(in_buf, in_out)
    in_back.start()
    one.wait_recv()
    own_x.wait()

    @pl.when(is_middle)
    def _():
        middle.wait_recv()

    @pl.when(is_end)
    def _():
        relay.wait_recv()

    for copy in up_steps:
        copy.start()

    @pl.when(moves)
    def _():
        down_push.start()

    @pl.when(jnp.logical_not(moves))
    def _():
        down_stay.start()

    for k in straight_steps(wide):
        grads[k].start()

    def project(n, carry):
        at = pl.ds(pl.multiple_of(n * rows, rows), rows)
        values = slot[at, :].astype(F32)
        low = (values * rms_factor(values) * gain_one_ref[0:1, :]).astype(BF16)
        normed[at, :] = low
        proj[at, :] = dot_f32(low, in_buf[...])
        return carry

    lax.fori_loop(0, slot.shape[0] // rows, project, 0)
    normed_back = local_copy(normed, normed_out)
    proj_back = local_copy(proj, proj_out)
    normed_back.start()
    proj_back.start()

    cont = cont_ref[...]
    groups = own_width // LANES
    small_low = small_columns(proj.at[:, pl.ds(4 * own_width, LANES)], bias_ref)
    decay_scr[...] = decay_of(small_low, cont)

    def attend(pair, carry):
        def at(group):
            return pl.ds(pl.multiple_of((group * groups + pair) * LANES, LANES), LANES)

        forward_pair(
            pair, heads, head_size, block, proj.at[:, at(0)], proj.at[:, at(1)], proj.at[:, at(2)],
            proj.at[:, at(3)], small_low, cont, decay_scr[...], mixed.at[:, at(0)],
            att_ref.at[:, at(0)], log_ref.at[:, at(0)],
        )
        return carry

    lax.fori_loop(0, groups, attend, 0)
    for copy in mixes:
        copy.start()
    mixed_rows[:, pl.ds(pl.multiple_of(z * own_width, LANES), own_width)] = mixed[
        pl.ds(pl.multiple_of(z * rows, rows), rows), :
    ]
    out_wide.received()
    out_back = local_copy(out_buf, out_out)
    out_back.start()
    for copy in mixes:
        copy.wait_recv()
    inputs = slot[pl.ds(pl.multiple_of(z * rows, rows), rows), :].astype(F32)
    values = inputs + dot_f32(mixed_rows[...], out_buf[...])
    middle_ref[...] = values
    normed_two_ref[...] = (values * rms_factor(values) * gain_two_ref[0:1, :]).astype(BF16)

    for copy in up_steps:
        copy.wait()
    for copy in grads.values():
        copy.wait()

    @pl.when(moves)
    def _():
        down_push.wait()

    @pl.when(jnp.logical_not(moves))
    def _():
        down_stay.wait()

    @pl.when(is_middle)
    def _():
        relay.wait_send()
        middle.wait_send()

    for copy in ins + outs + ups + [two, one] + mixes:
        copy.wait_send()
    in_wide.sent()
    out_wide.sent()
    for copy in (up_back, in_back, normed_back, proj_back, out_back):
        copy.wait()


def first_part(
    tokens, in_parts, out_weight, up_parts, cotangent, down_weight, gain_one, gain_two, bias, cont,
    heads, head_size, block, collective_id,
):
    wide = up_parts.shape[0]
    rows, width = tokens.shape
    slot, own_width, columns = 4 * rows, heads * head_size, in_parts.shape[2]
    steps = 3 * wide + 2 * wide + 24
    shape = jax.ShapeDtypeStruct
    return pl.pallas_call(
        functools.partial(first_kernel, wide, heads, head_size, block),
        out_shape=[
            shape((slot, width), BF16), shape((width, columns), BF16), shape((width, width), BF16),
            shape((slot, columns), F32), shape((slot, own_width), BF16),
            shape((slot, own_width), F32), shape((rows, width), BF16), shape((rows, width), F32),
            shape((rows, width), BF16), shape(up_parts.shape, BF16), shape(up_parts.shape, BF16),
            shape(up_parts.shape, BF16), shape(down_weight.shape, BF16),
            shape((wide // 2 - 1, rows, width), BF16),
        ],
        in_specs=[ANY] * 6 + [VMEM] * 4,
        out_specs=[ANY] * 4 + [VMEM] * 5 + [ANY] * 5,
        scratch_shapes=[
            pltpu.VMEM((slot, width), BF16), pltpu.VMEM((width, columns), BF16),
            pltpu.VMEM((width, width), BF16), pltpu.VMEM(up_parts.shape, BF16),
            pltpu.VMEM((slot, width), BF16), pltpu.VMEM((slot, columns), F32),
            pltpu.VMEM((slot, own_width), BF16), pltpu.VMEM((slot, LANES), F32),
            DMA((steps,)), DMA((steps,)), DMA((10,)),
        ],
        compiler_params=pltpu.CompilerParams(
            collective_id=collective_id, has_side_effects=True, vmem_limit_bytes=60 * 2**20
        ),
    )(
        tokens, in_parts, out_weight, up_parts, cotangent, down_weight,
        jnp.broadcast_to(gain_one[None], (8, width)), jnp.broadcast_to(gain_two[None], (8, width)),
        bias, cont,
    )


def second_kernel(
    wide, src_ref, grad_ref, far_grads, up_ref, up_two, up_one, down_ref, norm_sum, branch_sum,
    up_src, down_src, up_acc, down_acc, up_grad_out, down_grad_out, normed, grads, up_full,
    down_full, hidden, mid, rows_buf, core_buf, far_buf, branch_buf, up_join, up_mid, down_join,
    down_mid, up_grad, down_grad, send, recv, local,
):
    w, z = lax.axis_index("wide"), lax.axis_index("narrow")
    line = [flipped(z, k) for k in range(4)]
    rows, width = src_ref.shape
    half = wide // 2
    size = hidden.shape[1]
    unit, part = up_src.shape[1], down_src.shape[1]
    is_middle = (z == 1) | (z == 2)
    is_end = (z == 0) | (z == 3)
    sender = Sender(send, recv)
    sibling = wide_device(flipped(w, 1))

    def at_place(ref, place):
        return ref.at[pl.ds(pl.multiple_of(place * rows, rows), rows), :]

    up_at = lambda n: up_full.at[:, n]
    down_at = lambda n: down_full.at[n]
    moves = [
        (src_ref, at_place(normed, 0)), (up_ref, up_at(z)), (up_two, up_at(line[2])),
        (up_one, up_at(line[1])), (down_ref, down_at(z)), (grad_ref, at_place(grads, 0)),
    ] + [(far_grads.at[n - 1], at_place(grads, n)) for n in range(1, half)]
    own = [pltpu.make_async_copy(src, dst, local.at[n]) for n, (src, dst) in enumerate(moves)]
    for copy in own:
        copy.start()
    greet(
        [wide_device(flipped(w, k)) for k in wide_steps(wide)]
        + [narrow_device(line[k]) for k in (1, 2, 3)]
    )
    gather = WideGather(
        sender, w, wide, lambda k: src_ref if k == 0 else at_place(normed, place_of(k, wide)),
        lambda k, to: at_place(normed, place_of(k ^ to, wide)),
    )
    middle = sender.plan(up_ref, up_at(z), narrow_device(line[3]))
    relay = sender.plan(up_two, up_at(line[2]), narrow_device(line[1]))
    down_two = sender.plan(down_ref, down_at(z), narrow_device(line[2]))
    down_one = sender.plan(down_ref, down_at(z), narrow_device(line[1]))
    down_middle = sender.plan(down_ref, down_at(z), narrow_device(line[3]))
    down_relay = sender.plan(down_at(line[2]), down_at(line[2]), narrow_device(line[1]))
    passed = [
        sender.plan(
            grad_ref if n == 0 else far_grads.at[n - 1], at_place(grads, half + n), sibling
        )
        for n in range(half)
    ]
    core = [
        sender.plan(at_place(rows_buf, half + n), core_buf.at[n], sibling) for n in range(half)
    ]
    far = [
        sender.plan(at_place(rows_buf, n), far_buf.at[n - 1], wide_device(flipped(w, 2 * n)))
        for n in range(1, half)
    ]
    branch_core = [
        sender.plan(at_place(normed, half + n), branch_buf.at[n], sibling) for n in range(half)
    ]

    def up_share(n):
        return up_grad.at[:, pl.ds(pl.multiple_of(n * unit, unit), unit)]

    def down_share(n):
        return down_grad.at[:, pl.ds(pl.multiple_of(n * part, part), part)]

    down_joined = sender.plan(down_share(line[3]), down_join, narrow_device(line[1]))
    down_direct = sender.plan(down_share(line[3]), down_mid, narrow_device(line[3]))
    up_joined = sender.plan(up_share(line[3]), up_join, narrow_device(line[1]))
    up_direct = sender.plan(up_share(line[3]), up_mid, narrow_device(line[3]))

    gather.start()
    down_two.start()

    @pl.when(is_middle)
    def _():
        relay.start()

    down_two.wait_recv()

    @pl.when(is_middle)
    def _():
        down_relay.start()
        middle.start()
        down_middle.start()

    down_one.start()
    for copy in passed:
        copy.start()
    gather.pass_on()
    gather.received()
    for copy in own:
        copy.wait()
    for copy in passed + [down_one]:
        copy.wait_recv()

    @pl.when(is_middle)
    def _():
        middle.wait_recv()
        down_middle.wait_recv()

    @pl.when(is_end)
    def _():
        relay.wait_recv()
        down_relay.wait_recv()

    up_shape = (width, 4 * unit)
    down_shape = (size, width)

    def block(t, carry):
        place = lax.rem(t + half, wide) + jnp.where(t < half, 0, 1)
        place = jnp.where(place == half, jnp.where(t < half, half, 0), place)
        at = pl.ds(pl.multiple_of(place * rows, rows), rows)
        gate_up = dot_f32(normed[at, :], up_full[...].reshape(up_shape))
        grad_hidden = dot_f32(grads[at, :], down_full[...].reshape(down_shape), ((1,), (1,)))
        gate, up = gate_up[:, :size], gate_up[:, size:]
        opened = jax.nn.sigmoid(gate)
        acted = gate * opened
        hidden[at, :] = (acted * up).astype(BF16)
        mid[at, :size] = (grad_hidden * up * (opened * (1.0 + gate * (1.0 - opened)))).astype(BF16)
        mid[at, size:] = (grad_hidden * acted).astype(BF16)
        rows_buf[at, :] = dot_f32(mid[at, :], up_full[...].reshape(up_shape), ((1,), (1,))).astype(
            BF16
        )
        for n in range(half):

            @pl.when(t == n)
            def _():
                core[n].start()

        for n in range(half):

            @pl.when(t == half + lax.rem(n + half - 1, half))
            def _():
                core[n].wait_recv()
                total = rows_buf[n * rows : (n + 1) * rows, :].astype(F32) + core_buf[n].astype(F32)
                rows_buf[n * rows : (n + 1) * rows, :] = total.astype(BF16)
                if n > 0:
                    far[n - 1].start()

        return carry

    lax.fori_loop(0, wide, block, 0)

    step = min(256, size)
    for n in range(size // step):
        cut = slice(n * step, (n + 1) * step)
        down_grad[cut, :] = dot_f32(hidden[:, cut], grads[...], ((0,), (0,))).astype(BF16)

    @pl.when(is_end)
    def _():
        down_joined.start()

    @pl.when(is_middle)
    def _():
        down_direct.start()

    def up_rows(n, carry):
        at = pl.ds(pl.multiple_of(n * 256, 256), 256)
        up_grad[at, :] = dot_f32(normed[:, at], mid[...], ((0,), (0,))).astype(BF16)
        return carry

    lax.fori_loop(0, width // 256, up_rows, 0)

    @pl.when(is_end)
    def _():
        up_joined.start()

    @pl.when(is_middle)
    def _():
        up_direct.start()

    backs = [
        pltpu.make_async_copy(up_grad, up_grad_out, local.at[5 + half]),
        pltpu.make_async_copy(down_grad, down_grad_out, local.at[6 + half]),
        pltpu.make_async_copy(up_share(line[2]), up_src, local.at[7 + half]),
        pltpu.make_async_copy(down_share(line[2]), down_src, local.at[8 + half]),
    ]
    for copy in backs:
        copy.start()
    gather.sent()

    def branch(t, carry):
        place = lax.rem(t + half, wide)
        at = pl.ds(pl.multiple_of(place * rows, rows), rows)
        normed[at, :] = dot_f32(hidden[at, :], down_full[...].reshape(down_shape)).astype(BF16)
        for n in range(half):

            @pl.when(t == n)
            def _():
                branch_core[n].start()

        return carry

    lax.fori_loop(0, wide, branch, 0)
    for n in range(half):
        branch_core[n].wait_recv()
        total = normed[n * rows : (n + 1) * rows, :].astype(F32) + branch_buf[n].astype(F32)
        branch_sum[n] = total.astype(BF16)

    total = rows_buf[:rows, :].astype(F32)
    for n in range(1, half):
        far[n - 1].wait_recv()
        total = total + far_buf[n - 1].astype(F32)
    norm_sum[...] = total
    for copy in backs:
        copy.wait()
    up_acc[...] = up_grad[:, pl.ds(pl.multiple_of(z * unit, unit), unit)]
    down_acc[...] = down_grad[:, pl.ds(pl.multiple_of(z * part, part), part)]

    @pl.when(is_middle)
    def _():
        down_joined.wait_recv()
        down_src[...] = (down_src[...].astype(F32) + down_join[...].astype(F32)).astype(BF16)
        up_joined.wait_recv()
        up_src[...] = (up_src[...].astype(F32) + up_join[...].astype(F32)).astype(BF16)
        down_direct.wait()
        down_acc[...] = (down_acc[...].astype(F32) + down_mid[...].astype(F32)).astype(BF16)
        up_direct.wait()
        up_acc[...] = (up_acc[...].astype(F32) + up_mid[...].astype(F32)).astype(BF16)
        for copy in (relay, middle, down_relay, down_middle):
            copy.wait_send()

    @pl.when(is_end)
    def _():
        down_joined.wait_send()
        up_joined.wait_send()

    for copy in passed + core + far + branch_core + [down_two, down_one]:
        copy.wait_send()


def second_part(normed, grad, far_grads, ups, down, collective_id):
    rows, width = normed.shape
    half = far_grads.shape[0] + 1
    wide = 2 * half
    wide_of_up, part_rows, mid_size = ups[0].shape
    down_rows = down.shape[0]
    size, unit, part = mid_size // 2, mid_size // 4, width // 4
    steps = 6 + wide + 4 * half + 8
    total = wide * rows
    shape = jax.ShapeDtypeStruct
    vmem = lambda *dims: pltpu.VMEM(dims, BF16)
    return pl.pallas_call(
        functools.partial(second_kernel, wide),
        out_shape=[
            shape((rows, width), F32), shape((half, rows, width), BF16),
            shape((width, unit), BF16), shape((size, part), BF16),
            shape((width, unit), BF16), shape((size, part), BF16),
            shape((width, mid_size), BF16), shape((size, width), BF16),
        ],
        in_specs=[ANY] * 7,
        out_specs=[VMEM] * 6 + [ANY] * 2,
        scratch_shapes=[
            vmem(total, width), vmem(total, width), vmem(wide, 4, part_rows, mid_size),
            vmem(4, down_rows, width), vmem(total, size), vmem(total, mid_size), vmem(total, width),
            vmem(half, rows, width), vmem(half - 1, rows, width), vmem(half, rows, width),
            vmem(width, unit), vmem(width, unit), vmem(size, part), vmem(size, part),
            vmem(width, mid_size), vmem(size, width),
            DMA((steps,)), DMA((steps,)), DMA((9 + half,)),
        ],
        compiler_params=pltpu.CompilerParams(
            collective_id=collective_id, has_side_effects=True, vmem_limit_bytes=63 * 2**20
        ),
    )(normed, grad, far_grads, *ups, down)


def add_up(parts):
    total = parts[0].astype(F32)
    for part in parts[1:]:
        total = total + part.astype(F32)
    return total


def on_device(
    tokens, gain_one, in_weight, forget_bias, out_weight, gain_two, gate_up_weight, down_weight,
    segment_ids, cotangent,
):
    wide, narrow = lax.axis_size("wide"), lax.axis_size("narrow")
    w, z = lax.axis_index("wide"), lax.axis_index("narrow")
    rows, width = tokens.shape
    slot = rows * narrow
    heads = forget_bias.shape[0]
    head_size = width // heads
    own_heads = heads // narrow
    own_width = own_heads * head_size
    part_rows = in_weight.shape[0]
    hidden_all = down_weight.shape[0] * wide * narrow
    unit = hidden_all // (2 * wide)
    columns = 4 * own_width + LANES
    base = 4 * width

    small = in_weight[:, base:].reshape(part_rows, 3, narrow, own_heads)
    small = jnp.moveaxis(small, 2, 0).reshape(narrow, part_rows, 3 * own_heads)
    small = jnp.pad(small, ((0, 0), (0, 0), (0, LANES - 3 * own_heads)))
    aligned = unit % LANES == 0

    def split_weights(sources, targets):
        copies = [(sources[1], targets[0].at[:, :, pl.ds(4 * own_width, LANES)])]
        for n in range(narrow):
            for group in range(4):
                copies.append(
                    (
                        sources[0].at[:, pl.ds(group * width + n * own_width, own_width)],
                        targets[0].at[n, :, pl.ds(group * own_width, own_width)],
                    )
                )
        if aligned:
            for n in range(wide):
                for group in range(4):
                    copies.append(
                        (
                            sources[2].at[:, pl.ds((group * wide + n) * unit, unit)],
                            targets[1].at[n, :, pl.ds(group * unit, unit)],
                        )
                    )
        return copies

    shapes = [
        jax.ShapeDtypeStruct((narrow, part_rows, columns), BF16),
        jax.ShapeDtypeStruct((wide, part_rows, 4 * unit), BF16),
    ]
    copies = 4 * narrow + 1
    if aligned:
        in_parts, up_parts = local_copies(
            split_weights, copies + 4 * wide, [in_weight, small, gate_up_weight], shapes, False
        )
    else:
        in_parts = local_copies(split_weights, copies, [in_weight, small], shapes[:1], False)[0]
        up_parts = jnp.moveaxis(gate_up_weight.reshape(part_rows, 4, wide, unit), 2, 0)
        up_parts = up_parts.reshape(wide, part_rows, 4 * unit)

    segments = segment_ids[0]
    joined = (segments[1:] == segments[:-1]).astype(F32)
    cont = jnp.concatenate([jnp.zeros((1,), F32), joined])
    cont = jnp.broadcast_to(cont[:, None], (slot, LANES))
    own_bias = lax.dynamic_slice_in_dim(forget_bias, z * own_heads, own_heads)
    bias = jnp.broadcast_to(jnp.pad(own_bias, (0, LANES - own_heads))[None], (8, LANES))
    block = min(256, slot)
    def row_block(ref, n):
        return ref.at[pl.ds(pl.multiple_of(n * rows, rows), rows), :]

    def column_block(ref, n):
        return ref.at[:, pl.ds(pl.multiple_of(n * own_width, LANES), own_width)]

    straight, diagonal = straight_steps(wide), diagonal_steps(wide)
    inputs = tokens.astype(F32)
    half = wide // 2
    if aligned and part_rows % 16 == 0:
        (
            normed_one, in_full, out_full, projected, attended, logs, mixed_rows, middle, normed_two,
            up_block, up_two, up_one, down_block, grad_got,
        ) = first_part(
            tokens, in_parts, out_weight, up_parts, cotangent, down_weight, gain_one, gain_two,
            bias, cont, own_heads, head_size, block, 0,
        )
    else:
        pairs = []
        for i in range(wide * narrow):
            to_wide = (i % (2 * wide)) // 2
            to_narrow = i % 2 + 2 * (i // (2 * wide))
            pairs.append((i, to_wide * narrow + to_narrow))
        down_block = lax.ppermute(down_weight, ("wide", "narrow"), pairs)

        slot_tokens, in_full, out_full, up_block, grad_far = gather_all(
            tokens, in_parts, out_weight, up_parts, cotangent
        )
        slot_tokens = slot_tokens.reshape(slot, width)
        in_full = in_full.reshape(width, columns)
        out_full = out_full.reshape(width, width)

        up_two = on_line(up_block, LINE_TWO)
        up_one = on_line(up_block, LINE_ONE)

        slot_floats = slot_tokens.astype(F32)
        normed_one = (slot_floats * rms_factor(slot_floats) * gain_one).astype(BF16)
        projected = dot_f32(normed_one, in_full)

        mixed, attended, logs = attention_forward(
            projected, bias, cont, own_heads, head_size, block
        )

        mixed_rows, *grad_near = exchange(
            mixed, row_block, column_block, (rows, width), straight, [cotangent] * len(straight), 1
        )
        grads = {0: cotangent}
        grads.update({k: grad_near[n] for n, k in enumerate(straight)})
        grads.update({k: grad_far[n] for n, k in enumerate(diagonal)})
        grads = [grads[k] for k in range(0, wide, 2)]
        down_block = follow(down_block, mixed_rows)
        down_two = on_line(down_block, LINE_TWO)
        down_one = on_line(down_block, LINE_ONE)
        middle = inputs + dot_f32(mixed_rows, out_full)
        normed_two = (middle * rms_factor(middle) * gain_two).astype(BF16)

    if aligned and part_rows % 16 == 0:
        (
            grad_normed_two, branch_sum, up_src, down_src, up_acc, down_acc, up_one, down_one,
        ) = second_part(
            normed_two, cotangent, grad_got, [up_block, up_two, up_one], down_block, 2
        )
    else:
        ups = [up_block] + [follow(piece, normed_two) for piece in (up_two, up_one)]
        plane_normed, plane_grad, up_full, down_full = gather_rows(
            normed_two, grads, ups, [down_block, down_two, down_one], 2
        )
        plane_normed = plane_normed.reshape(wide * rows, width)
        plane_grad = plane_grad.reshape(wide * rows, width)
        up_full = up_full.reshape(width, 4 * unit)
        down_full = down_full.reshape(2 * unit, width)
        hidden, gate_up_grad, norm_even, norm_odd, branch = feed_forward(
            plane_normed, plane_grad, up_full, down_full, rows
        )
        grad_up_full = dot_f32(plane_normed, gate_up_grad, ((0,), (0,))).astype(BF16)
        grad_down_full = dot_f32(hidden, plane_grad, ((0,), (0,))).astype(BF16)
        if unit % LANES:
            grouped = grad_up_full.reshape(width, 4, unit)
            grad_up_full = jnp.pad(grouped, ((0, 0), (0, 0), (0, LANES - unit))).reshape(width, -1)
        branch = branch.reshape(wide, rows, width)
        fits = wide <= 8
        norm_got = along_wide(norm_odd.reshape(half, rows, width), 1, wide)
        (
            grad_normed_two, branch_sum, up_src, down_src, up_one, down_one, up_acc, down_acc,
        ) = middle_sums(
            norm_even.reshape(half, rows, width), norm_got,
            branch if fits else branch[:2, :16], grad_up_full, grad_down_full, 6,
        )
        if not fits:
            received = along_wide(branch[half:], 1, wide)
            branch_sum = (branch[:half].astype(F32) + received.astype(F32)).astype(BF16)
    upstream = cotangent.astype(F32)
    grad_middle_norm, grad_gain_two = rms_back(middle, gain_two, grad_normed_two)
    grad_middle = upstream + grad_middle_norm
    branch_one_grad = grad_middle.astype(BF16)
    grad_mixed = dot_f32(branch_one_grad, out_full, ((1,), (1,))).astype(BF16)
    slot_grad, *branch_near = exchange(
        grad_mixed, column_block, row_block, (slot, own_width), straight,
        [branch_sum[k // 2] for k in straight], 3,
    )

    wide_rows = width // wide
    out_part = dot_f32(mixed_rows, branch_one_grad, ((0,), (0,))).astype(BF16)
    (
        unused, bias_grad, norm_part, in_part, out_low, up_two, down_two, up_one, down_one,
        branch_far,
    ) = attention_backward(
        projected, bias, cont, attended, logs, slot_grad, in_full, normed_one,
        [up_src, down_src, up_one, down_one], out_part.reshape(wide, wide_rows, width), branch_sum,
        own_heads, head_size, block, 7,
    )
    branches = [branch_sum[0]] + branch_near + [branch_far[n] for n in range(len(diagonal))]
    all_bias = lax.dynamic_update_slice(
        jnp.zeros((width,), F32), bias_grad[0, :own_heads], (z * own_heads,)
    )
    small = jnp.stack([jnp.zeros((width,), F32), grad_gain_two, all_bias])
    small = jnp.pad(small, ((0, 5), (0, 0)))
    low = lambda part: part.astype(BF16)
    output, grad_tokens, grad_in, grad_out, grad_up, grad_down, totals = last_part(
        norm_part, in_part.reshape(wide, wide_rows, columns), out_low, [low(up_acc), up_one, up_two],
        [low(down_acc), down_one, down_two], branches, tokens, middle, grad_middle, gain_one, small,
        own_width, own_heads, (base + 3 * heads) // narrow, 4,
    )
    if not aligned:
        grad_up = grad_up.reshape(wide_rows, wide, LANES)[:, :, :unit]
        grad_up = grad_up.reshape(wide_rows, wide * unit)
    return (
        output,
        grad_tokens,
        totals[0],
        grad_in,
        totals[2, :heads],
        grad_out,
        totals[1],
        grad_up,
        grad_down,
    )


def solution(mesh):
    both = ("wide", "narrow")
    in_specs = (
        P(both, None), P(), P(both, None), P(), P(both, None), P(), P(both, None), P(both, None),
        P("wide", None), P(both, None),
    )
    out_specs = (
        P(both, None), P(both, None), P(), P("wide", "narrow"), P(), P("wide", "narrow"), P(),
        P("wide", "narrow"), P("wide", "narrow"),
    )
    return jax.shard_map(
        on_device, mesh=mesh, in_specs=in_specs, out_specs=out_specs, check_vma=False
    )
```

```python
import functools

import jax
import jax.numpy as jnp
from jax import lax
from jax.experimental import pallas as pl
from jax.experimental.pallas import tpu as pltpu
from jax.sharding import PartitionSpec as P

EPSILON = 1e-06
SEPARATE = 128.0
F32 = jnp.float32
BF16 = jnp.bfloat16
LANES = 128
EXACT = lax.Precision.HIGHEST
ANY = pl.BlockSpec(memory_space=pltpu.HBM)


def dot_f32(left, right, dims=((1,), (0,))):
    return lax.dot_general(left, right, (dims, ((), ())), preferred_element_type=F32)


def along_wide(block, flip, wide):
    return lax.ppermute(block, "wide", [(i, i ^ flip) for i in range(wide)])


def copy_kernel(plan, count, *refs):
    sources, targets, sems = refs[:count], refs[count:-1], refs[-1]
    copies = plan(sources, targets)

    def each(act):
        for n, (src, dst, *when) in enumerate(copies):
            copy = pltpu.make_async_copy(src, dst, sems.at[n])
            if when:
                pl.when(when[0])(functools.partial(act, copy))
            else:
                act(copy)

    each(lambda copy: copy.start())
    each(lambda copy: copy.wait())


def local_copies(plan, copies, sources, shapes, gather):
    moved = sum(s.size * s.dtype.itemsize for s in shapes)
    inside = pl.BlockSpec(memory_space=pltpu.VMEM)
    return pl.pallas_call(
        functools.partial(copy_kernel, plan, len(sources)),
        out_shape=shapes,
        in_specs=[ANY if gather else inside] * len(sources),
        out_specs=[inside if gather else ANY] * len(shapes),
        compiler_params=pltpu.CompilerParams(vmem_limit_bytes=16 * 2**20),
        scratch_shapes=[pltpu.SemaphoreType.DMA((copies,))],
        cost_estimate=pl.CostEstimate(flops=0, bytes_accessed=2 * moved, transcendentals=0),
    )(*sources)


def flipped(me, k):
    out = me
    bit = 1
    while bit <= k:
        if k & bit:
            out = out + bit - 2 * bit * lax.rem(lax.div(out, bit), 2)
        bit *= 2
    return out


LINE_TWO = [(0, 2), (2, 0), (1, 3), (3, 1)]
LINE_ONE = [(0, 1), (1, 0), (2, 3), (3, 2)]
LINE_MIDDLE = [(1, 2), (2, 1)]
LINE_OUT = [(2, 3), (1, 0)]
LINE_IN = [(0, 1), (3, 2)]


def on_line(block, pairs):
    return lax.ppermute(block, "narrow", pairs)


def follow(array, *earlier):
    return lax.optimization_barrier((array, *earlier))[0]


MESH = pl.DeviceIdType.MESH
VMEM = pl.BlockSpec(memory_space=pltpu.VMEM)
DMA = pltpu.SemaphoreType.DMA


def greet(devices):
    barrier = pltpu.get_barrier_semaphore()
    for device in devices:
        pl.semaphore_signal(barrier, inc=1, device_id=device, device_id_type=MESH)
    pl.semaphore_wait(barrier, len(devices))


class Sender:
    def __init__(self, send, recv):
        self.send, self.recv, self.used = send, recv, 0

    def plan(self, src, dst, device):
        n = self.used
        self.used += 1
        return pltpu.make_async_remote_copy(
            src_ref=src, dst_ref=dst, send_sem=self.send.at[n], recv_sem=self.recv.at[n],
            device_id=device, device_id_type=MESH,
        )


def narrow_device(n):
    return {"narrow": n}


def wide_device(n):
    return {"wide": n}


def wide_steps(wide):
    return [1] + list(range(2, wide, 2))


def straight_steps(wide):
    return [k for k in range(2, wide, 2) if k & (k - 1) == 0]


def diagonal_steps(wide):
    return [k for k in range(2, wide, 2) if k & (k - 1)]


def by_device(ref, w):
    return (lambda k: ref.at[flipped(w, k)]), (lambda k, to: ref.at[flipped(w, k)])


class WideGather:
    def __init__(self, sender, w, wide, part, target):
        self.far = list(range(2, wide, 2))
        self.first = {
            k: sender.plan(part(0), target(0, k), wide_device(flipped(w, k)))
            for k in wide_steps(wide)
        }
        sibling = wide_device(flipped(w, 1))
        self.second = {k: sender.plan(part(k), target(k, 1), sibling) for k in self.far}

    def start(self):
        for k in self.far + [1]:
            self.first[k].start()

    def pass_on(self):
        for k in self.far:
            self.first[k].wait_recv()
            self.second[k].start()

    def received(self):
        self.first[1].wait_recv()
        for k in self.far:
            self.second[k].wait_recv()

    def sent(self):
        for copy in list(self.first.values()) + list(self.second.values()):
            copy.wait_send()

    def finish(self):
        self.received()
        self.sent()


def gather_kernel(
    wide, x_ref, in_ref, out_ref, up_ref, grad_ref, slot_ref, in_full, out_full, up_block, grad_far,
    send, recv, local,
):
    w, z = lax.axis_index("wide"), lax.axis_index("narrow")
    line = [flipped(z, k) for k in range(4)]
    sender = Sender(send, recv)
    own = [
        pltpu.make_async_copy(in_ref.at[z], in_full.at[w, z], local.at[0]),
        pltpu.make_async_copy(out_ref, out_full.at[w, z], local.at[1]),
        pltpu.make_async_copy(x_ref, slot_ref.at[z], local.at[2]),
        pltpu.make_async_copy(up_ref.at[w], up_block.at[w], local.at[3]),
    ]
    for copy in own:
        copy.start()
    greet(
        [narrow_device(line[k]) for k in (1, 2, 3)]
        + [wide_device(flipped(w, k)) for k in range(1, wide)]
    )
    ups = [
        sender.plan(up_ref.at[flipped(w, k)], up_block.at[w], wide_device(flipped(w, k)))
        for k in range(1, wide)
    ]
    grads = [
        sender.plan(grad_ref, grad_far.at[n], wide_device(flipped(w, k)))
        for n, k in enumerate(diagonal_steps(wide))
    ]
    is_middle = (z == 1) | (z == 2)
    is_end = (z == 0) | (z == 3)
    ins = [
        sender.plan(in_ref.at[line[k]], in_full.at[w, z], narrow_device(line[k])) for k in (2, 3, 1)
    ]
    outs = [sender.plan(out_ref, out_full.at[w, z], narrow_device(line[k])) for k in (2, 3, 1)]
    two = sender.plan(x_ref, slot_ref.at[z], narrow_device(line[2]))
    one = sender.plan(x_ref, slot_ref.at[z], narrow_device(line[1]))
    middle = sender.plan(x_ref, slot_ref.at[z], narrow_device(line[3]))
    relay = sender.plan(slot_ref.at[line[2]], slot_ref.at[line[2]], narrow_device(line[1]))
    in_wide = WideGather(sender, w, wide, *by_device(in_full, w))
    out_wide = WideGather(sender, w, wide, *by_device(out_full, w))
    for copy in ins + outs + ups:
        copy.start()
    own[0].wait()
    for copy in ins:
        copy.wait_recv()
    in_wide.start()
    two.start()
    one.start()
    own[1].wait()
    for copy in outs:
        copy.wait_recv()
    out_wide.start()
    in_wide.pass_on()
    for copy in grads:
        copy.start()
    two.wait_recv()

    @pl.when(is_middle)
    def _():
        relay.start()
        middle.start()

    out_wide.pass_on()
    one.wait_recv()
    own[2].wait()
    own[3].wait()
    for copy in ups + grads:
        copy.wait()

    @pl.when(is_middle)
    def _():
        middle.wait_recv()
        middle.wait_send()
        relay.wait_send()

    @pl.when(is_end)
    def _():
        relay.wait_recv()

    for copy in ins + outs + [two, one]:
        copy.wait_send()
    in_wide.finish()
    out_wide.finish()


def gather_all(tokens, in_parts, out_weight, up_parts, cotangent):
    narrow, wide = in_parts.shape[0], up_parts.shape[0]
    steps = 10 + 4 * wide
    shapes = [
        (narrow,) + tokens.shape, (wide,) + in_parts.shape, (wide, narrow) + out_weight.shape,
        up_parts.shape, (len(diagonal_steps(wide)),) + cotangent.shape,
    ]
    return pl.pallas_call(
        functools.partial(gather_kernel, wide),
        out_shape=[jax.ShapeDtypeStruct(shape, BF16) for shape in shapes],
        in_specs=[ANY] * 5,
        out_specs=[VMEM] * 5,
        scratch_shapes=[DMA((steps,)), DMA((steps,)), DMA((4,))],
        compiler_params=pltpu.CompilerParams(
            collective_id=0, has_side_effects=True, vmem_limit_bytes=40 * 2**20
        ),
    )(tokens, in_parts, out_weight, up_parts, cotangent)


def exchange_kernel(source, target, steps, *refs):
    count = len(steps)
    src_ref, sides, dst_ref = refs[0], refs[1 : 1 + count], refs[1 + count]
    got = refs[2 + count : 2 + 2 * count]
    send, recv, local = refs[2 + 2 * count :]
    w, z = lax.axis_index("wide"), lax.axis_index("narrow")
    line = [flipped(z, k) for k in range(4)]
    sender = Sender(send, recv)
    own = pltpu.make_async_copy(source(src_ref, z), target(dst_ref, z), local.at[0])
    own.start()
    greet(
        [narrow_device(line[k]) for k in (1, 2, 3)] + [wide_device(flipped(w, k)) for k in steps]
    )
    copies = [
        sender.plan(source(src_ref, line[k]), target(dst_ref, z), narrow_device(line[k]))
        for k in (2, 3, 1)
    ]
    copies += [
        sender.plan(sides[n], got[n], wide_device(flipped(w, k))) for n, k in enumerate(steps)
    ]
    for copy in copies:
        copy.start()
    own.wait()
    for copy in copies:
        copy.wait()


def exchange(array, source, target, shape, steps, sides, collective_id):
    count = len(steps) + 4
    return pl.pallas_call(
        functools.partial(exchange_kernel, source, target, steps),
        out_shape=[jax.ShapeDtypeStruct(shape, array.dtype)]
        + [jax.ShapeDtypeStruct(side.shape, side.dtype) for side in sides],
        in_specs=[ANY] * (1 + len(sides)),
        out_specs=[VMEM] * (1 + len(sides)),
        scratch_shapes=[DMA((count,)), DMA((count,)), DMA((1,))],
        compiler_params=pltpu.CompilerParams(
            collective_id=collective_id, has_side_effects=True, vmem_limit_bytes=16 * 2**20
        ),
    )(array, *sides)


def place_of(k, wide):
    return k // 2 + (k % 2) * (wide // 2)


def rows_kernel(wide, *refs):
    half = wide // 2
    grads = refs[:half]
    (
        src_ref, up_ref, up_two, up_one, down_ref, down_two, down_one, dst_ref, grad_ref, up_full,
        down_full, send, recv, local,
    ) = refs[half:]
    w, z = lax.axis_index("wide"), lax.axis_index("narrow")
    line = [flipped(z, k) for k in range(4)]
    is_middle = (z == 1) | (z == 2)
    is_end = (z == 0) | (z == 3)
    sender = Sender(send, recv)
    up_at = lambda n: up_full.at[:, n]
    down_at = lambda n: down_full.at[n]
    moves = [
        (src_ref, dst_ref.at[0]),
        (down_ref, down_at(z)), (down_two, down_at(line[2])), (down_one, down_at(line[1])),
        (up_ref, up_at(z)), (up_two, up_at(line[2])), (up_one, up_at(line[1])),
    ] + [(grads[n], grad_ref.at[n]) for n in range(half)]
    own = [pltpu.make_async_copy(src, dst, local.at[n]) for n, (src, dst) in enumerate(moves)]
    for copy in own:
        copy.start()
    greet(
        [wide_device(flipped(w, k)) for k in wide_steps(wide)]
        + [narrow_device(line[k]) for k in (1, 3)]
    )
    gather = WideGather(
        sender, w, wide, lambda k: src_ref if k == 0 else dst_ref.at[place_of(k, wide)],
        lambda k, to: dst_ref.at[place_of(k ^ to, wide)],
    )
    middles = [
        sender.plan(up_ref, up_at(z), narrow_device(line[3])),
        sender.plan(down_ref, down_at(z), narrow_device(line[3])),
    ]
    relays = [
        sender.plan(up_two, up_at(line[2]), narrow_device(line[1])),
        sender.plan(down_two, down_at(line[2]), narrow_device(line[1])),
    ]
    gather.start()

    @pl.when(is_middle)
    def _():
        for copy in middles + relays:
            copy.start()

    sibling = wide_device(flipped(w, 1))
    copies = [sender.plan(grads[n], grad_ref.at[half + n], sibling) for n in range(half)]
    for copy in copies:
        copy.start()
    gather.pass_on()

    @pl.when(is_middle)
    def _():
        for copy in middles:
            copy.wait()
        for copy in relays:
            copy.wait_send()

    @pl.when(is_end)
    def _():
        for copy in relays:
            copy.wait_recv()

    for copy in own + copies:
        copy.wait()
    gather.finish()


def gather_rows(array, grads, ups, downs, collective_id):
    half = len(grads)
    wide = 2 * half
    whole = jax.ShapeDtypeStruct((wide,) + array.shape, array.dtype)
    up_shape = ups[0].shape
    full = jax.ShapeDtypeStruct((up_shape[0], 4) + up_shape[1:], BF16)
    return pl.pallas_call(
        functools.partial(rows_kernel, wide),
        out_shape=[whole, whole, full, jax.ShapeDtypeStruct((4,) + downs[0].shape, BF16)],
        in_specs=[ANY] * (half + 7),
        out_specs=[VMEM, ANY if wide > 8 else VMEM, VMEM, VMEM],
        scratch_shapes=[DMA((2 * wide + 4,)), DMA((2 * wide + 4,)), DMA((half + 7,))],
        compiler_params=pltpu.CompilerParams(
            collective_id=collective_id, has_side_effects=True, vmem_limit_bytes=48 * 2**20
        ),
    )(*grads, array, *ups, *downs)


def hidden_kernel(
    half, normed_ref, grad_ref, up_ref, down_ref, hidden_ref, mid_ref, even_ref, odd_ref, branch_ref
):
    size = down_ref.shape[0]
    gate_up = dot_f32(normed_ref[...], up_ref[...])
    grad_hidden = dot_f32(grad_ref[...], down_ref[...], ((1,), (1,)))
    gate, up = gate_up[:, :size], gate_up[:, size:]
    opened = jax.nn.sigmoid(gate)
    acted = gate * opened
    hidden_ref[...] = (acted * up).astype(BF16)
    mid_ref[:, :size] = (grad_hidden * up * (opened * (1.0 + gate * (1.0 - opened)))).astype(BF16)
    mid_ref[:, size:] = (grad_hidden * acted).astype(BF16)
    grad_normed = dot_f32(mid_ref[...], up_ref[...], ((1,), (1,))).astype(BF16)
    branch_ref[...] = dot_f32(hidden_ref[...], down_ref[...]).astype(BF16)
    step = pl.program_id(0)

    @pl.when(step < half)
    def _():
        even_ref[...] = grad_normed

    @pl.when(step >= half)
    def _():
        odd_ref[...] = grad_normed


def feed_forward(normed, grad, up_full, down_full, rows):
    total, width = normed.shape
    blocks = total // rows
    half = blocks // 2
    size = down_full.shape[0]
    row_block = lambda columns: pl.BlockSpec((rows, columns), lambda i: (i, 0))
    fixed = lambda array: pl.BlockSpec(array.shape, lambda i: (0, 0))
    return pl.pallas_call(
        functools.partial(hidden_kernel, half),
        grid=(blocks,),
        in_specs=[row_block(width), row_block(width), fixed(up_full), fixed(down_full)],
        out_specs=[
            row_block(size), row_block(2 * size),
            pl.BlockSpec((rows, width), lambda i: (jnp.minimum(i, half - 1), 0)),
            pl.BlockSpec((rows, width), lambda i: (jnp.maximum(i - half, 0), 0)),
            row_block(width),
        ],
        out_shape=[
            jax.ShapeDtypeStruct((total, size), BF16),
            jax.ShapeDtypeStruct((total, 2 * size), BF16),
            jax.ShapeDtypeStruct((total // 2, width), BF16),
            jax.ShapeDtypeStruct((total // 2, width), BF16),
            jax.ShapeDtypeStruct((total, width), BF16),
        ],
        compiler_params=pltpu.CompilerParams(vmem_limit_bytes=48 * 2**20),
    )(normed, grad, up_full, down_full)


def middle_kernel(
    wide, even_ref, got_ref, branch_ref, up_ref, down_ref, norm_sum, branch_sum, up_src, down_src,
    up_one, down_one, up_acc, down_acc, core_buf, own_buf, far_buf, branch_buf, up_join, up_mid,
    down_join, down_mid, up_own, down_own, send, recv, local,
):
    w, z = lax.axis_index("wide"), lax.axis_index("narrow")
    line = [flipped(z, k) for k in range(4)]
    half = wide // 2
    unit = up_src.shape[1]
    part = down_src.shape[1]
    sender = Sender(send, recv)
    is_middle = (z == 1) | (z == 2)
    is_end = (z == 0) | (z == 3)

    def up_share(n):
        return up_ref.at[:, pl.ds(pl.multiple_of(n * unit, unit), unit)]

    def down_share(n):
        return down_ref.at[:, pl.ds(pl.multiple_of(n * part, part), part)]

    moves = [
        (up_share(line[2]), up_src), (down_share(line[2]), down_src),
        (up_share(z), up_own), (down_share(z), down_own),
        (up_share(line[1]), up_one), (down_share(line[1]), down_one),
    ]
    moves += [(got_ref.at[n], core_buf.at[n]) for n in range(half)]
    moves += [(even_ref.at[n], own_buf.at[n]) for n in range(half)]
    pairs = branch_sum.shape[0]
    moves += [(branch_ref.at[n], branch_sum.at[n]) for n in range(pairs)]
    own = [pltpu.make_async_copy(src, dst, local.at[n]) for n, (src, dst) in enumerate(moves)]
    for copy in own:
        copy.start()
    greet(
        [wide_device(flipped(w, k)) for k in wide_steps(wide)]
        + [narrow_device(line[k]) for k in (1, 3)]
    )
    sibling = wide_device(flipped(w, 1))
    far = [
        sender.plan(own_buf.at[n], far_buf.at[n - 1], wide_device(flipped(w, 2 * n)))
        for n in range(1, half)
    ]
    branch_core = [
        sender.plan(branch_ref.at[pairs + n], branch_buf.at[n], sibling) for n in range(pairs)
    ]
    joins = [
        sender.plan(up_share(line[3]), up_join, narrow_device(line[1])),
        sender.plan(down_share(line[3]), down_join, narrow_device(line[1])),
    ]
    mids = [
        sender.plan(up_share(line[3]), up_mid, narrow_device(line[3])),
        sender.plan(down_share(line[3]), down_mid, narrow_device(line[3])),
    ]
    order = list(range(1, half)) + [0]

    @pl.when(is_end)
    def _():
        for copy in joins:
            copy.start()

    @pl.when(is_middle)
    def _():
        for copy in mids:
            copy.start()

    for n in order:
        own[6 + n].wait()
        own[6 + half + n].wait()
        total = own_buf[n].astype(F32) + core_buf[n].astype(F32)
        own_buf[n] = total.astype(BF16)
        if n > 0:
            far[n - 1].start()
    for copy in branch_core:
        copy.start()
    for n in range(pairs):
        branch_core[n].wait_recv()
        own[6 + 2 * half + n].wait()
        total = branch_sum[n].astype(F32) + branch_buf[n].astype(F32)
        branch_sum[n] = total.astype(BF16)
    for n in range(6):
        own[n].wait()

    @pl.when(is_middle)
    def _():
        for copy in joins:
            copy.wait_recv()
        up_src[...] = (up_src[...].astype(F32) + up_join[...].astype(F32)).astype(BF16)
        down_src[...] = (down_src[...].astype(F32) + down_join[...].astype(F32)).astype(BF16)

    total = own_buf[0].astype(F32)
    for n in range(1, half):
        far[n - 1].wait_recv()
        total = total + far_buf[n - 1].astype(F32)
    norm_sum[...] = total
    up_acc[...] = up_own[...].astype(F32)
    down_acc[...] = down_own[...].astype(F32)

    @pl.when(is_middle)
    def _():
        for copy in mids:
            copy.wait()
        up_acc[...] += up_mid[...].astype(F32)
        down_acc[...] += down_mid[...].astype(F32)

    @pl.when(is_end)
    def _():
        for copy in joins:
            copy.wait_send()

    for copy in far + branch_core:
        copy.wait_send()


def middle_sums(even, got, branch, grad_up, grad_down, collective_id):
    half, rows, width = even.shape
    wide = 2 * half
    unit, part = grad_up.shape[1] // 4, grad_down.shape[1] // 4
    up_shape, down_shape = (grad_up.shape[0], unit), (grad_down.shape[0], part)
    steps = 4 * half + 6
    rows_buf = pltpu.VMEM((half, rows, width), BF16)
    pairs = branch.shape[0] // 2
    return pl.pallas_call(
        functools.partial(middle_kernel, wide),
        out_shape=[
            jax.ShapeDtypeStruct((rows, width), F32),
            jax.ShapeDtypeStruct((pairs,) + branch.shape[1:], BF16),
            *[jax.ShapeDtypeStruct(up_shape, BF16), jax.ShapeDtypeStruct(down_shape, BF16)] * 2,
            jax.ShapeDtypeStruct(up_shape, F32),
            jax.ShapeDtypeStruct(down_shape, F32),
        ],
        in_specs=[ANY] * 5,
        out_specs=[VMEM] * 8,
        scratch_shapes=[
            rows_buf, rows_buf, pltpu.VMEM((half - 1, rows, width), BF16),
            pltpu.VMEM((pairs,) + branch.shape[1:], BF16),
            *[pltpu.VMEM(up_shape, BF16)] * 2, *[pltpu.VMEM(down_shape, BF16)] * 2,
            pltpu.VMEM(up_shape, BF16), pltpu.VMEM(down_shape, BF16),
            DMA((steps,)), DMA((steps,)), DMA((6 + 3 * half,)),
        ],
        compiler_params=pltpu.CompilerParams(
            collective_id=collective_id, has_side_effects=True, vmem_limit_bytes=58 * 2**20
        ),
    )(even, got, branch, grad_up, grad_down)


def last_kernel(
    wide, rows, own_width, own_heads, norm_ref, in_ref, up_parts, down_parts, branch_refs, token_ref,
    middle_ref, grad_ref, gain_ref, small_ref, output, grad_tokens, grad_in, up_got, down_got, totals, join_buf, one_buf, mid_buf, two_buf, two_src, own_norm, norm_sum,
    in_core, in_own, in_far, in_sum, in_got, after_got, tail_buf, up_low, up_bufs, down_low,
    down_bufs, branch_bufs, narrow_buf, wide_buf, sum_buf, send, recv, down_send, down_recv,
    local,
):
    w, z = lax.axis_index("wide"), lax.axis_index("narrow")
    line = [flipped(z, k) for k in range(4)]
    half = wide // 2
    unit = up_low.shape[1]
    wide_rows, width = grad_in.shape[0], token_ref.shape[1]
    sender = Sender(send, recv)
    is_middle = (z == 1) | (z == 2)
    is_end = (z == 0) | (z == 3)

    def norm_block(n):
        return norm_ref.at[pl.ds(pl.multiple_of(n * rows, rows), rows), :]

    def up_rows(n):
        return up_low.at[pl.ds(pl.multiple_of(n * wide_rows, 16), wide_rows), :]

    def up_columns(n):
        return up_got.at[:, pl.ds(pl.multiple_of(n * unit, LANES), unit)]

    def section(n):
        return in_sum.at[:, pl.ds(pl.multiple_of(n * own_width, LANES), own_width)]

    def after_section(n):
        return in_sum.at[:, pl.ds(pl.multiple_of((n + 1) * own_width, LANES), LANES)]

    moves = [(norm_block(line[2]), two_src), (norm_block(z), own_norm)]
    moves += [(in_ref.at[flipped(w, 2 * n)], in_own.at[n]) for n in range(half)]
    ffn_at = len(moves)
    moves += [(ref, up_bufs.at[n]) for n, ref in enumerate(up_parts)]
    moves += [(ref, down_bufs.at[n]) for n, ref in enumerate(down_parts)]
    branch_at = len(moves)
    moves += [(ref, branch_bufs.at[n]) for n, ref in enumerate(branch_refs)]
    own = [pltpu.make_async_copy(src, dst, local.at[n]) for n, (src, dst) in enumerate(moves)]
    for copy in own:
        copy.start()
    greet(
        [narrow_device(line[k]) for k in (1, 2, 3)]
        + [wide_device(flipped(w, k)) for k in range(1, wide)]
    )
    sibling = wide_device(flipped(w, 1))
    joined = sender.plan(norm_block(line[3]), join_buf, narrow_device(line[1]))
    one = sender.plan(norm_block(line[1]), one_buf, narrow_device(line[1]))
    middle = sender.plan(norm_block(line[3]), mid_buf, narrow_device(line[3]))
    two = sender.plan(two_src, two_buf, narrow_device(line[2]))
    core = [
        sender.plan(in_ref.at[flipped(w, 2 * n + 1)], in_core.at[n], sibling) for n in range(half)
    ]
    far = [
        sender.plan(in_own.at[n], in_far.at[n - 1], wide_device(flipped(w, 2 * n)))
        for n in range(1, half)
    ]
    sections = [
        sender.plan(section(line[k]), in_got.at[z], narrow_device(line[k])) for k in (2, 3, 1)
    ]
    afters = [
        (
            (z == 0) | (line[k] == 3), (line[k] == 0) | (z == 3),
            sender.plan(after_section(line[k]), after_got.at[z], narrow_device(line[k])),
        )
        for k in (2, 3, 1)
    ]
    ups = [
        sender.plan(up_rows(flipped(w, k)), up_columns(w), wide_device(flipped(w, k)))
        for k in range(1, wide)
    ]
    first = [
        sender.plan(sum_buf, narrow_buf.at[z], narrow_device(line[k])) for k in (1, 2, 3)
    ]
    second = [
        sender.plan(sum_buf, wide_buf.at[w], wide_device(flipped(w, k))) for k in range(1, wide)
    ]
    parity, target = lax.rem(w, 2), lax.div(w, 2)
    depth = down_low.shape[0] // 2
    down_at = pl.ds(pl.multiple_of(parity * depth, 16), depth)
    downs = []
    for n in range(2):
        owner = target + n * half
        src, dst = down_low.at[pl.ds(n * depth, depth), :], down_got.at[down_at, :]
        push = pltpu.make_async_remote_copy(
            src_ref=src, dst_ref=dst, send_sem=down_send.at[n], recv_sem=down_recv.at[parity],
            device_id=wide_device(owner), device_id_type=MESH,
        )
        stay = pltpu.make_async_copy(src, dst, local.at[len(moves) + 1 + n])
        downs.append((owner == w, push, stay))

    order = list(range(1, half)) + [0]
    for n in order:
        core[n].start()

    @pl.when(is_end)
    def _():
        joined.start()

    @pl.when(is_middle)
    def _():
        middle.start()

    for n in order:
        core[n].wait_recv()
        own[2 + n].wait()
        total = in_own[n].astype(F32) + in_core[n].astype(F32)
        in_own[n] = total.astype(BF16)
        if n > 0:
            far[n - 1].start()
    own[0].wait()

    @pl.when(is_middle)
    def _():
        joined.wait_recv()
        two_src[...] = (two_src[...].astype(F32) + join_buf[...].astype(F32)).astype(BF16)

    two.start()
    one.start()
    for n in range(6):
        own[ffn_at + n].wait()
    up_low[...] = add_up([up_bufs[n] for n in range(3)]).astype(BF16)
    down_low[...] = add_up([down_bufs[n] for n in range(3)]).astype(BF16)
    for copy in ups:
        copy.start()
    for stays, push, stay in downs:
        pl.when(stays)(stay.start)
        pl.when(jnp.logical_not(stays))(push.start)
    up_got[:, pl.ds(pl.multiple_of(w * unit, LANES), unit)] = up_low[
        pl.ds(pl.multiple_of(w * wide_rows, 16), wide_rows), :
    ]
    total = middle_ref[...]
    for n in range(half):
        own[branch_at + n].wait()
        total = total + branch_bufs[n].astype(F32)
    output[...] = total.astype(BF16)

    total = in_own[0].astype(F32)
    for n in range(1, half):
        far[n - 1].wait_recv()
        total = total + in_far[n - 1].astype(F32)
    in_sum[...] = total.astype(BF16)
    mine = pltpu.make_async_copy(section(z), in_got.at[z], local.at[len(moves)])
    mine.start()
    own[1].wait()
    one.wait_recv()
    norm_sum[...] = own_norm[...].astype(F32) + one_buf[...].astype(F32)

    @pl.when(is_middle)
    def _():
        middle.wait()
        norm_sum[...] += mid_buf[...].astype(F32)

    two.wait_recv()
    for copy in sections:
        copy.start()
    for sends, gets, copy in afters:
        pl.when(sends)(copy.start)
    after_got[z] = after_section(z)[...]
    grads = norm_sum[...] + two_buf[...].astype(F32)
    values = token_ref[...].astype(F32)
    factor = rms_factor(values)
    normed = values * factor
    scaled = grads * gain_ref[0:1, :]
    inner = jnp.mean(scaled * normed, axis=-1, keepdims=True)
    grad_tokens[...] = grad_ref[...] + factor * (scaled - normed * inner)
    narrow_buf[z] = small_ref[...]
    narrow_buf[z, 0:1, :] = jnp.sum(grads * normed, axis=0, keepdims=True)
    sum_buf[...] = narrow_buf[z]
    for copy in first:
        copy.start()

    for copy in ups:
        copy.wait_recv()
    for n, (stays, push, stay) in enumerate(downs):
        pl.when(stays)(stay.wait)
        pl.when(jnp.logical_not(stays))(push.wait_send)
    for n in range(2):
        source = lax.rem(2 * w + n, wide)
        arrived = pltpu.make_async_remote_copy(
            src_ref=down_low.at[pl.ds(0, depth), :], dst_ref=down_got.at[pl.ds(n * depth, depth), :],
            send_sem=down_send.at[n], recv_sem=down_recv.at[n], device_id=sibling,
            device_id_type=MESH,
        )
        pl.when(source != w)(arrived.wait_recv)

    for copy in first:
        copy.wait()
    sum_buf[...] = narrow_buf[0] + narrow_buf[1] + narrow_buf[2] + narrow_buf[3]
    for copy in second:
        copy.start()
    wide_buf[w] = sum_buf[...]

    for copy in sections:
        copy.wait_recv()
    mine.wait()
    for sends, gets, copy in afters:
        pl.when(gets)(copy.wait_recv)

    @pl.when(z == 3)
    def _():
        row, lane = iota((LANES, LANES), 0), iota((LANES, LANES), 1)
        last = jnp.zeros((wide_rows, LANES), F32)
        for n in range(4):
            group = lax.div(row, own_heads)
            place = group * (4 * own_heads) + n * own_heads + row - group * own_heads
            spot = ((lane == place) & (row < 3 * own_heads)).astype(BF16)
            last = last + dot_f32(after_got[n], spot)
        tail_buf[...] = last

    @pl.when(z != 3)
    def _():
        tail_buf[...] = after_got[0].astype(F32)

    whole = jnp.concatenate([in_got[n].astype(F32) for n in range(4)] + [tail_buf[...]], axis=1)
    move = whole.shape[1] - (grad_in.shape[1] - width) * z
    grad_in[...] = pltpu.roll(whole, lax.rem(move, whole.shape[1]), 1)[:, : grad_in.shape[1]]

    for copy in second:
        copy.wait()
    total = wide_buf[0]
    for n in range(1, wide):
        total = total + wide_buf[n]
    totals[...] = total

    @pl.when(is_end)
    def _():
        joined.wait_send()

    for sends, gets, copy in afters:
        pl.when(sends)(copy.wait_send)
    for copy in [one, two] + core + far + sections + ups:
        copy.wait_send()


def grouped_last_kernel(wide, rows, own_width, own_heads, *refs):
    own, near, far = refs[8:11]
    branches = [own.at[0]]
    branches += [near.at[n] for n in range(near.shape[0])] + [far.at[n] for n in range(far.shape[0])]
    last_kernel(
        wide, rows, own_width, own_heads, *refs[:2], refs[2:5], refs[5:8], branches, *refs[11:],
    )


def last_part(
    norm_part, in_part, ups, downs, branches, tokens, middle, grad_middle, gain, small, own_width, own_heads,
    shard, collective_id,
):
    wide, wide_rows, columns = in_part.shape
    half = wide // 2
    rows, width = tokens.shape
    unit = ups[0].shape[1]
    steps = 4 + 2 * half + 12 + 2 * wide
    shape = jax.ShapeDtypeStruct
    vmem = lambda *dims: pltpu.VMEM(dims, BF16)
    return pl.pallas_call(
        functools.partial(grouped_last_kernel, wide, rows, own_width, own_heads),
        out_shape=[
            shape((rows, width), BF16), shape((rows, width), F32), shape((wide_rows, shard), F32),
            shape((wide_rows, wide * unit), BF16), shape(downs[0].shape, BF16),
            shape(small.shape, F32),
        ],
        in_specs=[ANY] * 11 + [VMEM] * 5,
        out_specs=[VMEM] * 6,
        scratch_shapes=[
            *[vmem(rows, width)] * 6, pltpu.VMEM((rows, width), F32),
            vmem(half, wide_rows, columns), vmem(half, wide_rows, columns),
            vmem(half - 1, wide_rows, columns), vmem(wide_rows, columns),
            vmem(4, wide_rows, own_width), vmem(4, wide_rows, LANES),
            pltpu.VMEM((wide_rows, LANES), F32), vmem(*ups[0].shape), vmem(3, *ups[0].shape),
            vmem(*downs[0].shape), vmem(3, *downs[0].shape), vmem(half, rows, width),
            pltpu.VMEM((4,) + small.shape, F32), pltpu.VMEM((wide,) + small.shape, F32),
            pltpu.VMEM(small.shape, F32),
            DMA((steps,)), DMA((steps,)), DMA((2,)), DMA((2,)), DMA((12 + 2 * half,)),
        ],
        compiler_params=pltpu.CompilerParams(
            collective_id=collective_id, has_side_effects=True, vmem_limit_bytes=60 * 2**20
        ),
    )(
        norm_part, in_part, *ups, *downs, *branches, tokens, middle, grad_middle,
        jnp.broadcast_to(gain[None], (8, width)), small,
    )


def rms_factor(values):
    return lax.rsqrt(jnp.mean(values * values, axis=-1, keepdims=True) + EPSILON)


def rms_back(values, gain, grad):
    factor = rms_factor(values)
    normed = values * factor
    grad_gain = jnp.sum(grad * normed, axis=0)
    scaled = grad * gain
    inner = jnp.mean(scaled * normed, axis=-1, keepdims=True)
    return (factor * (scaled - normed * inner), grad_gain)


def log_sigmoid(v):
    return jnp.minimum(v, 0.0) - jnp.log1p(jnp.exp(-jnp.abs(v)))


def iota(shape, dim):
    return lax.broadcasted_iota(jnp.int32, shape, dim)


def running_sum(v, reverse):
    rows = v.shape[0]
    index = iota(v.shape, 0)
    step = 1
    while step < rows:
        if reverse:
            v = v + jnp.where(index < rows - step, pltpu.roll(v, rows - step, 0), 0.0)
        else:
            v = v + jnp.where(index >= step, pltpu.roll(v, step, 0), 0.0)
        step *= 2
    return v


def half_of(lane, head_size):
    return (lane >= head_size).astype(jnp.int32)


def spread(first, head_size):
    row, lane = iota((LANES, LANES), 0), iota((LANES, LANES), 1)
    return row == first + half_of(lane, head_size)


def collect(first, head_size):
    row, lane = iota((LANES, LANES), 0), iota((LANES, LANES), 1)
    return lane == first + half_of(row, head_size)


def same_head(head_size):
    row, lane = iota((LANES, LANES), 0), iota((LANES, LANES), 1)
    return (half_of(row, head_size) == half_of(lane, head_size)).astype(F32)


def exact_dot(left, right):
    return lax.dot_general(
        left, right, (((1,), (0,)), ((), ())), precision=EXACT, preferred_element_type=F32
    )


def head_mean(v, head_size):
    return exact_dot(v, same_head(head_size)) * (1.0 / head_size)


def prologue(pair, heads, head_size, q_ref, k_ref, v_ref, small_low, cont):
    spot = lambda group: spread(group * heads + 2 * pair, head_size).astype(BF16)
    key_mix = jax.nn.sigmoid(dot_f32(small_low, spot(1)))
    value_mix = jax.nn.sigmoid(dot_f32(small_low, spot(2)))
    queries = q_ref[...].astype(BF16).astype(F32)
    keys = k_ref[...].astype(BF16).astype(F32)
    values = v_ref[...].astype(BF16).astype(F32)
    key_step = pltpu.roll(keys, 1, 0) * cont - keys
    value_step = pltpu.roll(values, 1, 0) * cont - values
    shifted = keys + key_mix * key_step
    value_low = (values + value_mix * value_step).astype(BF16)
    query_factor = lax.rsqrt(head_mean(queries * queries, head_size) + EPSILON)
    key_factor = lax.rsqrt(head_mean(shifted * shifted, head_size) + EPSILON)
    return (
        queries * query_factor,
        shifted * key_factor,
        value_low,
        query_factor,
        key_factor,
        key_mix,
        value_mix,
        key_step,
        value_step,
    )


def small_columns(small_ref, bias_ref):
    return (small_ref[...] + bias_ref[0:1, :]).astype(BF16)


def decay_of(small_low, cont):
    return running_sum(log_sigmoid(small_low.astype(F32)) - SEPARATE * (1.0 - cont), False)


def forward_pair(
    pair, heads, head_size, block, q_ref, k_ref, v_ref, gate_ref, small_low, cont, decay_all,
    mixed_ref, att_ref, log_ref,
):
    query, key, value_low, *unused = prologue(
        pair, heads, head_size, q_ref, k_ref, v_ref, small_low, cont
    )
    rows = query.shape[0]
    query = query.astype(BF16) * BF16(head_size**-0.5)
    key = key.astype(BF16)
    decay = exact_dot(decay_all, spread(2 * pair, head_size).astype(F32))
    decay_rows = decay.T
    lane = iota((1, LANES), 1)
    ones = jnp.ones((rows, LANES), BF16)
    value_wide = jnp.concatenate([value_low, ones], axis=1)
    for i in range(rows // block):
        lo, hi = i * block, (i + 1) * block
        row_index = iota((block, hi), 0) + lo
        visible = iota((block, hi), 1) <= row_index
        outs, sums = [], []
        for head in range(2):
            mine = (lane >= head_size) if head else (lane < head_size)
            at = head * head_size
            left = jnp.where(mine, query[lo:hi], BF16(0.0))
            scores = dot_f32(left, key[:hi], ((1,), (1,)))
            scores = scores + decay[lo:hi, at : at + 1] - decay_rows[at : at + 1, :hi]
            weights = jnp.where(visible, jnp.exp(scores), 0.0).astype(BF16)
            both = dot_f32(weights, value_wide[:hi])
            outs.append(both[:, :LANES])
            sums.append(both[:, LANES:])
        first = lane < head_size
        total = jnp.where(first, sums[0], sums[1])
        attended = (jnp.where(first, outs[0], outs[1]) / total).astype(BF16)
        att_ref[lo:hi, :] = attended
        log_ref[lo:hi, :] = jnp.log(total)
        opened = jax.nn.sigmoid(gate_ref[lo:hi, :])
        mixed_ref[lo:hi, :] = (attended.astype(F32) * opened).astype(BF16)


def forward_kernel(
    heads, head_size, block, q_ref, k_ref, v_ref, gate_ref, small_ref, bias_ref, cont_ref,
    mixed_ref, att_ref, log_ref, decay_scr,
):
    pair = pl.program_id(0)
    cont = cont_ref[...]
    small_low = small_columns(small_ref, bias_ref)

    @pl.when(pair == 0)
    def _():
        decay_scr[...] = decay_of(small_low, cont)

    forward_pair(
        pair, heads, head_size, block, q_ref, k_ref, v_ref, gate_ref, small_low, cont,
        decay_scr[...], mixed_ref, att_ref, log_ref,
    )


def share_of(ref, like, n):
    size = like.shape[1]
    if ref.shape[1] == size:
        return ref
    return ref.at[:, pl.ds(pl.multiple_of(n * size, size), size)]


def backward_kernel(
    heads, head_size, block, wide, *refs
):
    q_ref, k_ref, v_ref, gate_ref, small_ref, bias_ref, cont_ref, att_ref, log_ref, grad_ref = refs[:10]
    in_ref, normed_ref, up_src, down_src, up_one, down_one, part_ref, branch_ref = refs[10:18]
    out_ref, bias_grad_ref, norm_ref, in_part_ref, grad_out = refs[18:23]
    up_two_got, down_two_got, up_one_got, down_one_got, branch_got = refs[23:28]
    decay_scr, small_scr, dq_scr, part_core, part_own, part_far, part_sum, part_got = refs[28:36]
    send, recv, local = refs[36:]
    pair = pl.program_id(0)
    pairs = heads * head_size // LANES
    half = wide // 2
    row_steps = out_ref.shape[0] // norm_ref.shape[0]
    w, z = lax.axis_index("wide"), lax.axis_index("narrow")
    sender = Sender(send, recv)
    one, two = flipped(z, 1), flipped(z, 2)
    copies = [
        sender.plan(up_src, up_two_got, narrow_device(two)),
        sender.plan(down_src, down_two_got, narrow_device(two)),
        sender.plan(share_of(up_one, up_src, one), up_one_got, narrow_device(one)),
        sender.plan(share_of(down_one, down_src, one), down_one_got, narrow_device(one)),
    ]
    core = [
        sender.plan(part_ref.at[flipped(w, 2 * n + 1)], part_core.at[n], wide_device(flipped(w, 1)))
        for n in range(half)
    ]
    far = [
        sender.plan(part_own.at[n], part_far.at[n - 1], wide_device(flipped(w, 2 * n)))
        for n in range(1, half)
    ]
    branches = [
        sender.plan(branch_ref.at[k // 2], branch_got.at[n], wide_device(flipped(w, k)))
        for n, k in enumerate(diagonal_steps(wide))
    ]
    own = [
        pltpu.make_async_copy(part_ref.at[flipped(w, 2 * n)], part_own.at[n], local.at[n])
        for n in range(half)
    ]
    own_width = heads * head_size

    def part_columns(n):
        return part_sum.at[:, pl.ds(pl.multiple_of(n * own_width, LANES), own_width)]

    outs = [
        sender.plan(part_columns(flipped(z, k)), part_got.at[k - 1], narrow_device(flipped(z, k)))
        for k in (1, 2, 3)
    ]

    @pl.when(pair == 0)
    def _():
        greet(
            [narrow_device(flipped(z, k)) for k in (1, 2, 3)]
            + [wide_device(flipped(w, k)) for k in wide_steps(wide)]
        )
        for copy in copies + core + own:
            copy.start()

    @pl.when(pair == 1)
    def _():
        for n in range(half):
            core[n].wait_recv()
            own[n].wait()
            part_own[n] = (part_own[n].astype(F32) + part_core[n].astype(F32)).astype(BF16)
            if n > 0:
                far[n - 1].start()

    @pl.when(pair == 2)
    def _():
        for copy in branches:
            copy.start()

    @pl.when(pair < pairs)
    def _():
        backward_pair(
            pair, pairs, heads, head_size, block, q_ref, k_ref, v_ref, gate_ref, small_ref,
            bias_ref, cont_ref, att_ref, log_ref, grad_ref, out_ref, bias_grad_ref, decay_scr,
            small_scr, dq_scr,
        )

    @pl.when((pair >= pairs) & (pair < pairs + row_steps))
    def _():
        size = norm_ref.shape[0]
        at = pl.ds(pl.multiple_of((pair - pairs) * size, size), size)
        norm_ref[...] = dot_f32(out_ref[at, :], in_ref[...], ((1,), (1,))).astype(BF16)

    @pl.when(pair == pairs + row_steps)
    def _():
        total = part_own[0].astype(F32)
        for n in range(1, half):
            far[n - 1].wait_recv()
            total = total + part_far[n - 1].astype(F32)
        part_sum[...] = total.astype(BF16)
        for copy in outs:
            copy.start()

    @pl.when(pair >= pairs + row_steps)
    def _():
        in_part_ref[...] = dot_f32(normed_ref[...], out_ref[...], ((0,), (0,))).astype(BF16)

    @pl.when(pair == pl.num_programs(0) - 1)
    def _():
        for copy in outs + copies + branches:
            copy.wait()
        total = part_columns(z)[...].astype(F32)
        for n in range(3):
            total = total + part_got[n].astype(F32)
        grad_out[...] = total
        for copy in core + far:
            copy.wait_send()


def backward_pair(
    pair, pairs, heads, head_size, block, q_ref, k_ref, v_ref, gate_ref, small_ref, bias_ref, cont_ref,
    att_ref, log_ref, grad_ref, out_ref, bias_grad_ref, decay_scr, small_scr, dq_scr,
):
    cont = cont_ref[...]
    small_low = small_columns(small_ref, bias_ref)
    rows = cont.shape[0]
    width = heads * head_size

    @pl.when(pair == 0)
    def _():
        decay_scr[...] = decay_of(small_low, cont)
        small_scr[...] = jnp.zeros_like(small_scr)

    (
        query_norm, key_norm, value_low, query_factor, key_factor, key_mix, value_mix, key_step,
        value_step,
    ) = prologue(pair, heads, head_size, q_ref, k_ref, v_ref, small_low, cont)
    query = query_norm.astype(BF16) * BF16(head_size**-0.5)
    key = key_norm.astype(BF16)
    opened = jax.nn.sigmoid(gate_ref[...])
    attended = att_ref[...].astype(F32)
    grad_mixed = grad_ref[...].astype(F32)
    grad_low = (grad_mixed * opened).astype(BF16)
    grad_gate = grad_mixed * attended * opened * (1.0 - opened)

    def columns(group):
        at = group * width + pair * LANES
        return pl.ds(pl.multiple_of(at, LANES), LANES)

    out_ref[:, columns(3)] = grad_gate.astype(BF16)
    inner = exact_dot(grad_low.astype(F32) * attended, same_head(head_size))
    decay = exact_dot(decay_scr[...], spread(2 * pair, head_size).astype(F32))
    level_rows = (decay - log_ref[...]).T
    inner_rows = inner.T
    lane = iota((1, LANES), 1)
    ones = jnp.ones((rows, LANES), BF16)
    query_wide = jnp.concatenate([query, ones], axis=1)
    key_wide = jnp.concatenate([key, ones], axis=1)
    key_parts, value_parts, query_parts = [], [], []
    for head in range(2):
        mine = (lane >= head_size) if head else (lane < head_size)
        at = head * head_size
        keys_out, values_out = [], []
        for j in range(rows // block):
            lo, hi = j * block, (j + 1) * block
            span = rows - lo
            visible = iota((block, span), 0) <= iota((block, span), 1)
            scores = dot_f32(
                jnp.where(mine, key[lo:hi], BF16(0.0)), query[lo:], ((1,), (1,))
            )
            scores = scores + level_rows[at : at + 1, lo:] - decay[lo:hi, at : at + 1]
            probs = jnp.where(visible, jnp.exp(scores), 0.0)
            grad_probs = dot_f32(
                jnp.where(mine, value_low[lo:hi], BF16(0.0)), grad_low[lo:], ((1,), (1,))
            )
            grad_scores = (probs * (grad_probs - inner_rows[at : at + 1, lo:])).astype(BF16)
            values_out.append(dot_f32(probs.astype(BF16), grad_low[lo:]))
            keys_out.append(dot_f32(grad_scores, query_wide[lo:]))
            part = dot_f32(grad_scores, key_wide[lo:hi], ((0,), (0,)))
            if j == 0:
                dq_scr[...] = part
            else:
                dq_scr[lo:, :] += part
        key_parts.append(jnp.concatenate(keys_out, axis=0))
        value_parts.append(jnp.concatenate(values_out, axis=0))
        query_parts.append(dq_scr[...])
    first = lane < head_size

    def join(parts):
        return jnp.where(first, parts[0], parts[1])

    grad_query = join([p[:, :LANES] for p in query_parts]) * head_size**-0.5
    grad_key = join([p[:, :LANES] for p in key_parts])
    grad_value = join(value_parts)
    grad_decay = join([p[:, LANES:] for p in query_parts]) - join([p[:, LANES:] for p in key_parts])

    def norm_back(grad, normed, factor):
        return factor * (grad - normed * head_mean(grad * normed, head_size))

    def shift_back(grad, mix):
        return grad * (1.0 - mix) + pltpu.roll(grad * mix * cont, rows - 1, 0)

    grad_query = norm_back(grad_query, query_norm, query_factor)
    grad_shifted = norm_back(grad_key, key_norm, key_factor)
    out_ref[:, columns(0)] = grad_query.astype(BF16)
    out_ref[:, columns(1)] = shift_back(grad_shifted, key_mix).astype(BF16)
    out_ref[:, columns(2)] = shift_back(grad_value, value_mix).astype(BF16)
    key_logit = grad_shifted * key_step * key_mix * (1.0 - key_mix)
    value_logit = grad_value * value_step * value_mix * (1.0 - value_mix)
    single = (lax.rem(lane, head_size) == 0).astype(F32)
    small_scr[...] += (
        exact_dot(grad_decay * single, collect(2 * pair, head_size).astype(F32))
        + exact_dot(key_logit, collect(heads + 2 * pair, head_size).astype(F32))
        + exact_dot(value_logit, collect(2 * heads + 2 * pair, head_size).astype(F32))
    )

    @pl.when(pair == pairs - 1)
    def _():
        grads = small_scr[...]
        forget = running_sum(grads, True) * jax.nn.sigmoid(-small_low.astype(F32))
        result = jnp.where(lane < heads, forget, grads)
        out_ref[:, 4 * width :] = result.astype(BF16)
        bias_grad_ref[...] = jnp.broadcast_to(
            jnp.sum(result, axis=0, keepdims=True), bias_grad_ref.shape
        )


def attention_specs(rows, pairs):
    def block_at(group):
        return pl.BlockSpec((rows, LANES), lambda p: (0, group * pairs + jnp.minimum(p, pairs - 1)))

    def fixed(height, column=0):
        return pl.BlockSpec((height, LANES), lambda p: (0, column))

    base = [block_at(0), block_at(1), block_at(2), block_at(3), fixed(rows, 4 * pairs), fixed(8), fixed(rows)]
    return base, pl.BlockSpec((rows, LANES), lambda p: (0, jnp.minimum(p, pairs - 1)))


def attention_forward(projected, bias, cont, heads, head_size, block):
    rows = projected.shape[0]
    pairs = heads * head_size // LANES
    base, own = attention_specs(rows, pairs)
    wide = jax.ShapeDtypeStruct((rows, heads * head_size), BF16)
    return pl.pallas_call(
        functools.partial(forward_kernel, heads, head_size, block),
        grid=(pairs,),
        in_specs=base,
        out_specs=[own] * 3,
        out_shape=[wide, wide, jax.ShapeDtypeStruct(wide.shape, F32)],
        scratch_shapes=[pltpu.VMEM((rows, LANES), F32)],
        compiler_params=pltpu.CompilerParams(vmem_limit_bytes=48 * 2**20),
    )(*([projected] * 5), bias, cont)


def attention_backward(
    projected, bias, cont, attended, logs, grad, in_full, normed_one, shares, out_part, branches, heads,
    head_size, block, collective_id,
):
    rows = projected.shape[0]
    width = normed_one.shape[1]
    wide, wide_rows = out_part.shape[:2]
    half = wide // 2
    pairs = heads * head_size // LANES
    base, own = attention_specs(rows, pairs)
    columns = 4 * heads * head_size + LANES
    step = min(256, rows)
    row_steps, in_steps = rows // step, width // 256
    steps = 8 + 3 * wide
    part = lambda count: pltpu.VMEM((count, wide_rows, width), BF16)
    shape = jax.ShapeDtypeStruct

    def later(first, count):
        return lambda p: jnp.clip(p - first, 0, count - 1)

    row_at, in_at = later(pairs, row_steps), later(pairs + row_steps, in_steps)
    return pl.pallas_call(
        functools.partial(backward_kernel, heads, head_size, block, wide),
        grid=(pairs + row_steps + in_steps,),
        in_specs=base
        + [own] * 3
        + [
            pl.BlockSpec(in_full.shape, lambda p: (0, 0), pipeline_mode=pl.Buffered(1)),
            pl.BlockSpec((rows, 256), lambda p: (0, in_at(p))),
        ]
        + [ANY] * 6,
        out_specs=[
            pl.BlockSpec((rows, columns), lambda p: (0, 0)),
            pl.BlockSpec((8, LANES), lambda p: (0, 0)),
            pl.BlockSpec((step, width), lambda p: (row_at(p), 0)),
            pl.BlockSpec((256, columns), lambda p: (in_at(p), 0)),
            pl.BlockSpec((wide_rows, heads * head_size), lambda p: (0, 0)),
        ]
        + [ANY] * 5,
        out_shape=[
            shape((rows, columns), BF16), shape((8, LANES), F32), shape((rows, width), BF16),
            shape((width, columns), BF16), shape((wide_rows, heads * head_size), F32),
            *[shape(share.shape, BF16) for share in shares[:2] * 2],
            shape((len(diagonal_steps(wide)),) + branches.shape[1:], BF16),
        ],
        scratch_shapes=[
            pltpu.VMEM((rows, LANES), F32), pltpu.VMEM((rows, LANES), F32),
            pltpu.VMEM((rows, 2 * LANES), F32), part(half), part(half), part(half - 1),
            pltpu.VMEM((wide_rows, width), BF16),
            pltpu.VMEM((3, wide_rows, heads * head_size), BF16),
            DMA((steps,)), DMA((steps,)), DMA((half,)),
        ],
        compiler_params=pltpu.CompilerParams(
            collective_id=collective_id, has_side_effects=True, vmem_limit_bytes=60 * 2**20
        ),
    )(
        *([projected] * 5), bias, cont, attended, logs, grad, in_full, normed_one, *shares, out_part,
        branches,
    )


def first_kernel(
    wide, heads, head_size, block, x_ref, in_ref, small_ref, out_ref, up_ref, grad_ref, down_ref, gain_one_ref,
    gain_two_ref, bias_ref, cont_ref, normed_out, in_out, out_out, proj_out, att_ref, log_ref,
    mixed_rows, middle_ref, normed_two_ref, up_out, up_two, up_one, down_got, grad_got, slot, in_buf,
    out_buf, up_buf, normed, proj, mixed, decay_scr, send, recv, local,
):
    w, z = lax.axis_index("wide"), lax.axis_index("narrow")
    line = [flipped(z, k) for k in range(4)]
    rows, width = x_ref.shape
    own_width = heads * head_size
    part_rows = out_ref.shape[0]
    is_middle = (z == 1) | (z == 2)
    is_end = (z == 0) | (z == 3)
    sender = Sender(send, recv)
    used = []

    def local_copy(src, dst):
        copy = pltpu.make_async_copy(src, dst, local.at[len(used)])
        used.append(copy)
        return copy

    def slot_rows(n):
        return slot.at[pl.ds(pl.multiple_of(n * rows, rows), rows), :]

    def weight_rows(ref, w_of, z_of):
        at = (w_of * 4 + z_of) * part_rows
        return ref.at[pl.ds(pl.multiple_of(at, 16), part_rows), :]

    def wide_rows(ref, w_of):
        at = w_of * 4 * part_rows
        return ref.at[pl.ds(pl.multiple_of(at, 16), 4 * part_rows), :]

    def by_rows(ref):
        return (
            (lambda k: wide_rows(ref, flipped(w, k))),
            (lambda k, to: wide_rows(ref, flipped(w, k))),
        )

    unit = up_buf.shape[2] // 4

    def in_pieces(n):
        target = lambda at, size: in_buf.at[
            pl.ds(pl.multiple_of((w * 4 + z) * part_rows, 16), part_rows), pl.ds(at, size)
        ]
        for group in range(4):
            at = pl.multiple_of(group * width + n * own_width, LANES)
            yield in_ref.at[:, pl.ds(at, own_width)], target(group * own_width, own_width)
        yield small_ref.at[n], target(4 * own_width, LANES)

    def up_pieces(n):
        for group in range(4):
            at = pl.multiple_of((group * wide + n) * unit, LANES)
            yield up_ref.at[:, pl.ds(at, unit)], up_buf.at[w, :, pl.ds(group * unit, unit)]

    own_in = [local_copy(*piece) for piece in in_pieces(z)]
    own_up = [local_copy(*piece) for piece in up_pieces(w)]
    own_out = local_copy(out_ref, weight_rows(out_buf, w, z))
    own_x = local_copy(x_ref, slot_rows(z))
    for copy in used:
        copy.start()

    index = w * 4 + z
    down_wide = lax.div(lax.rem(index, 2 * wide), 2)
    down_narrow = lax.rem(index, 2) + 2 * lax.div(index, 2 * wide)
    from_index = 2 * wide * lax.div(z, 2) + 2 * w + lax.rem(z, 2)
    from_wide_index, from_narrow_index = lax.div(from_index, 4), lax.rem(from_index, 4)
    moves = jnp.logical_not((down_wide == w) & (down_narrow == z))
    down_push = sender.plan(
        down_ref, down_got, {"wide": down_wide, "narrow": down_narrow}
    )
    down_stay = local_copy(down_ref, down_got)

    barrier = pltpu.get_barrier_semaphore()
    partners = [narrow_device(line[k]) for k in (1, 2, 3)]
    partners += [wide_device(flipped(w, k)) for k in range(1, wide)]
    for device in partners:
        pl.semaphore_signal(barrier, inc=1, device_id=device, device_id_type=MESH)

    @pl.when(moves)
    def _():
        for device in (
            {"wide": from_wide_index, "narrow": from_narrow_index},
            {"wide": down_wide, "narrow": down_narrow},
        ):
            pl.semaphore_signal(barrier, inc=1, device_id=device, device_id_type=MESH)
        pl.semaphore_wait(barrier, len(partners) + 2)

    @pl.when(jnp.logical_not(moves))
    def _():
        pl.semaphore_wait(barrier, len(partners))

    ins = [
        sender.plan(*piece, narrow_device(line[k])) for k in (2, 3, 1) for piece in in_pieces(line[k])
    ]
    outs = [
        sender.plan(out_ref, weight_rows(out_buf, w, z), narrow_device(line[k])) for k in (2, 3, 1)
    ]
    ups = [
        sender.plan(*piece, wide_device(flipped(w, k)))
        for k in range(1, wide)
        for piece in up_pieces(flipped(w, k))
    ]
    grads = {
        k: sender.plan(grad_ref, grad_got.at[k // 2 - 1], wide_device(flipped(w, k)))
        for k in range(2, wide, 2)
    }
    two = sender.plan(x_ref, slot_rows(z), narrow_device(line[2]))
    one = sender.plan(x_ref, slot_rows(z), narrow_device(line[1]))
    middle = sender.plan(x_ref, slot_rows(z), narrow_device(line[3]))
    relay = sender.plan(slot_rows(line[2]), slot_rows(line[2]), narrow_device(line[1]))
    in_wide = WideGather(sender, w, wide, *by_rows(in_buf))
    out_wide = WideGather(sender, w, wide, *by_rows(out_buf))
    up_steps = [
        sender.plan(up_buf, up_two, narrow_device(line[2])),
        sender.plan(up_buf, up_one, narrow_device(line[1])),
    ]
    mixes = [
        sender.plan(
            mixed.at[pl.ds(pl.multiple_of(line[k] * rows, rows), rows), :],
            mixed_rows.at[:, pl.ds(pl.multiple_of(z * own_width, LANES), own_width)],
            narrow_device(line[k]),
        )
        for k in (2, 3, 1)
    ]

    for copy in ins + outs + ups:
        copy.start()
    for copy in own_in:
        copy.wait()
    for copy in ins:
        copy.wait_recv()
    in_wide.start()
    two.start()
    one.start()
    own_out.wait()
    for copy in outs:
        copy.wait_recv()
    out_wide.start()
    in_wide.pass_on()
    for k in diagonal_steps(wide):
        grads[k].start()
    two.wait_recv()

    @pl.when(is_middle)
    def _():
        relay.start()
        middle.start()

    for copy in own_up:
        copy.wait()
    for copy in ups:
        copy.wait_recv()
    up_back = local_copy(up_buf, up_out)
    up_back.start()
    in_wide.received()
    in_back = local_copy(in_buf, in_out)
    in_back.start()
    own_x.wait()

    def project(t, carry):
        @pl.when(t == 2)
        def _():
            one.wait_recv()

        @pl.when(t == 3)
        def _():
            out_wide.pass_on()

        @pl.when((t == 3) & is_middle)
        def _():
            middle.wait_recv()

        @pl.when((t == 3) & is_end)
        def _():
            relay.wait_recv()

        @pl.when(t == 3)
        def _():
            for copy in up_steps:
                copy.start()
            for k in straight_steps(wide):
                grads[k].start()

        @pl.when((t == 3) & moves)
        def _():
            down_push.start()

        @pl.when((t == 3) & jnp.logical_not(moves))
        def _():
            down_stay.start()

        n = jnp.where(t == 0, z, jnp.where(t == 1, line[2], jnp.where(t == 2, line[1], line[3])))
        at = pl.ds(pl.multiple_of(n * rows, rows), rows)
        values = slot[at, :].astype(F32)
        low = (values * rms_factor(values) * gain_one_ref[0:1, :]).astype(BF16)
        normed[at, :] = low
        proj[at, :] = dot_f32(low, in_buf[...])
        return carry

    lax.fori_loop(0, 4, project, 0)
    normed_back = local_copy(normed, normed_out)
    proj_back = local_copy(proj, proj_out)
    normed_back.start()
    proj_back.start()

    cont = cont_ref[...]
    groups = own_width // LANES
    small_low = small_columns(proj.at[:, pl.ds(4 * own_width, LANES)], bias_ref)
    decay_scr[...] = decay_of(small_low, cont)

    def attend(pair, carry):
        def at(group):
            return pl.ds(pl.multiple_of((group * groups + pair) * LANES, LANES), LANES)

        forward_pair(
            pair, heads, head_size, block, proj.at[:, at(0)], proj.at[:, at(1)], proj.at[:, at(2)],
            proj.at[:, at(3)], small_low, cont, decay_scr[...], mixed.at[:, at(0)],
            att_ref.at[:, at(0)], log_ref.at[:, at(0)],
        )
        return carry

    lax.fori_loop(0, groups, attend, 0)
    for copy in mixes:
        copy.start()
    mixed_rows[:, pl.ds(pl.multiple_of(z * own_width, LANES), own_width)] = mixed[
        pl.ds(pl.multiple_of(z * rows, rows), rows), :
    ]
    out_wide.received()
    out_back = local_copy(out_buf, out_out)
    out_back.start()
    for copy in mixes:
        copy.wait_recv()
    inputs = slot[pl.ds(pl.multiple_of(z * rows, rows), rows), :].astype(F32)
    values = inputs + dot_f32(mixed_rows[...], out_buf[...])
    middle_ref[...] = values
    normed_two_ref[...] = (values * rms_factor(values) * gain_two_ref[0:1, :]).astype(BF16)

    for copy in up_steps:
        copy.wait()
    for copy in grads.values():
        copy.wait()

    @pl.when(moves)
    def _():
        down_push.wait()

    @pl.when(jnp.logical_not(moves))
    def _():
        down_stay.wait()

    @pl.when(is_middle)
    def _():
        relay.wait_send()
        middle.wait_send()

    for copy in ins + outs + ups + [two, one] + mixes:
        copy.wait_send()
    in_wide.sent()
    out_wide.sent()
    for copy in (up_back, in_back, normed_back, proj_back, out_back):
        copy.wait()


def first_part(
    tokens, in_weight, small, out_weight, gate_up_weight, cotangent, down_weight, gain_one, gain_two, bias,
    cont, wide, heads, head_size, block, collective_id,
):
    rows, width = tokens.shape
    slot, own_width = 4 * rows, heads * head_size
    columns = 4 * own_width + LANES
    steps = 8 * wide + 40
    up_shape = (wide, gate_up_weight.shape[0], gate_up_weight.shape[1] // wide)
    shape = jax.ShapeDtypeStruct
    return pl.pallas_call(
        functools.partial(first_kernel, wide, heads, head_size, block),
        out_shape=[
            shape((slot, width), BF16), shape((width, columns), BF16), shape((width, width), BF16),
            shape((slot, columns), F32), shape((slot, own_width), BF16),
            shape((slot, own_width), F32), shape((rows, width), BF16), shape((rows, width), F32),
            shape((rows, width), BF16), shape(up_shape, BF16), shape(up_shape, BF16),
            shape(up_shape, BF16), shape(down_weight.shape, BF16),
            shape((wide // 2 - 1, rows, width), BF16),
        ],
        in_specs=[ANY] * 7 + [VMEM] * 4,
        out_specs=[ANY] * 4 + [VMEM] * 5 + [ANY] * 5,
        scratch_shapes=[
            pltpu.VMEM((slot, width), BF16), pltpu.VMEM((width, columns), BF16),
            pltpu.VMEM((width, width), BF16), pltpu.VMEM(up_shape, BF16),
            pltpu.VMEM((slot, width), BF16), pltpu.VMEM((slot, columns), F32),
            pltpu.VMEM((slot, own_width), BF16), pltpu.VMEM((slot, LANES), F32),
            DMA((steps,)), DMA((steps,)), DMA((20,)),
        ],
        compiler_params=pltpu.CompilerParams(
            collective_id=collective_id, has_side_effects=True, vmem_limit_bytes=60 * 2**20
        ),
    )(
        tokens, in_weight, small, out_weight, gate_up_weight, cotangent, down_weight, jnp.broadcast_to(gain_one[None], (8, width)),
        jnp.broadcast_to(gain_two[None], (8, width)), bias, cont,
    )


def second_kernel(
    wide, src_ref, grad_ref, far_grads, up_ref, up_two, up_one, down_ref, middle_ref, mixed_ref, out_ref,
    gain_ref, grad_middle, gain_grad, slot_grad, branch_sum, up_src, down_src, up_acc, down_acc,
    up_grad_out, down_grad_out, out_part, branch_near, normed, grads, up_full, down_full, hidden, mid,
    rows_buf, core_buf, far_buf, branch_buf, up_join, up_mid, down_join, down_mid, up_grad, down_grad,
    grad_mixed, mixed_buf, send, recv, local,
):
    w, z = lax.axis_index("wide"), lax.axis_index("narrow")
    line = [flipped(z, k) for k in range(4)]
    rows, width = src_ref.shape
    half = wide // 2
    size = hidden.shape[1]
    unit, part = up_src.shape[1], down_src.shape[1]
    is_middle = (z == 1) | (z == 2)
    is_end = (z == 0) | (z == 3)
    sender = Sender(send, recv)
    sibling = wide_device(flipped(w, 1))

    def at_place(ref, place):
        return ref.at[pl.ds(pl.multiple_of(place * rows, rows), rows), :]

    up_at = lambda n: up_full.at[:, n]
    down_at = lambda n: down_full.at[n]
    moves = [
        (src_ref, at_place(normed, 0)), (up_ref, up_at(z)), (up_two, up_at(line[2])),
        (up_one, up_at(line[1])), (down_ref, down_at(z)), (grad_ref, at_place(grads, 0)),
    ] + [(far_grads.at[n - 1], at_place(grads, n)) for n in range(1, half)]
    own = [pltpu.make_async_copy(src, dst, local.at[n]) for n, (src, dst) in enumerate(moves)]
    for copy in own:
        copy.start()
    greet(
        [wide_device(flipped(w, k)) for k in wide_steps(wide)]
        + [narrow_device(line[k]) for k in (1, 2, 3)]
    )
    gather = WideGather(
        sender, w, wide, lambda k: src_ref if k == 0 else at_place(normed, place_of(k, wide)),
        lambda k, to: at_place(normed, place_of(k ^ to, wide)),
    )
    middle = sender.plan(up_ref, up_at(z), narrow_device(line[3]))
    relay = sender.plan(up_two, up_at(line[2]), narrow_device(line[1]))
    down_two = sender.plan(down_ref, down_at(z), narrow_device(line[2]))
    down_one = sender.plan(down_ref, down_at(z), narrow_device(line[1]))
    down_middle = sender.plan(down_ref, down_at(z), narrow_device(line[3]))
    down_relay = sender.plan(down_at(line[2]), down_at(line[2]), narrow_device(line[1]))
    passed = [
        sender.plan(
            grad_ref if n == 0 else far_grads.at[n - 1], at_place(grads, half + n), sibling
        )
        for n in range(half)
    ]
    core = [
        sender.plan(at_place(rows_buf, half + n), core_buf.at[n], sibling) for n in range(half)
    ]
    far = [
        sender.plan(at_place(rows_buf, n), far_buf.at[n - 1], wide_device(flipped(w, 2 * n)))
        for n in range(1, half)
    ]
    branch_core = [
        sender.plan(at_place(normed, half + n), branch_buf.at[n], sibling) for n in range(half)
    ]

    def up_share(n):
        return up_grad.at[:, pl.ds(pl.multiple_of(n * unit, unit), unit)]

    def down_share(n):
        return down_grad.at[:, pl.ds(pl.multiple_of(n * part, part), part)]

    down_joined = sender.plan(down_share(line[3]), down_join, narrow_device(line[1]))
    down_direct = sender.plan(down_share(line[3]), down_mid, narrow_device(line[3]))
    up_joined = sender.plan(up_share(line[3]), up_join, narrow_device(line[1]))
    up_direct = sender.plan(up_share(line[3]), up_mid, narrow_device(line[3]))
    own_width = width // 4
    mixes = [
        sender.plan(
            grad_mixed.at[:, pl.ds(pl.multiple_of(line[k] * own_width, LANES), own_width)],
            slot_grad.at[pl.ds(pl.multiple_of(z * rows, rows), rows), :], narrow_device(line[k]),
        )
        for k in (2, 3, 1)
    ]
    near = [
        sender.plan(branch_sum.at[k // 2], branch_near.at[n], wide_device(flipped(w, k)))
        for n, k in enumerate(straight_steps(wide))
    ]

    gather.start()

    @pl.when(is_middle)
    def _():
        relay.start()
        middle.start()

    down_two.start()
    down_two.wait_recv()

    @pl.when(is_middle)
    def _():
        down_relay.start()
        down_middle.start()

    down_one.start()
    for copy in passed:
        copy.start()
    for copy in own[:4]:
        copy.wait()

    @pl.when(is_middle)
    def _():
        middle.wait_recv()

    @pl.when(is_end)
    def _():
        relay.wait_recv()

    up_shape = (width, 4 * unit)
    down_shape = (size, width)

    def arriving(t, carry):
        @pl.when(t == 1)
        def _():
            gather.first[1].wait_recv()

        for n, k in enumerate(gather.far):

            @pl.when(t == 2 + n)
            def _():
                gather.first[k].wait_recv()
                gather.second[k].start()

            @pl.when(t == half + 1 + n)
            def _():
                gather.second[k].wait_recv()

        place = jnp.where(t < 2, t * half, jnp.where(t < half + 1, t - 1, t))
        at = pl.ds(pl.multiple_of(place * rows, rows), rows)
        mid[at, :] = dot_f32(normed[at, :], up_full[...].reshape(up_shape)).astype(BF16)
        return carry

    lax.fori_loop(0, wide, arriving, 0)
    for copy in own[4:]:
        copy.wait()
    for copy in passed + [down_one]:
        copy.wait_recv()

    @pl.when(is_middle)
    def _():
        down_middle.wait_recv()

    @pl.when(is_end)
    def _():
        down_relay.wait_recv()

    def block(t, carry):
        place = lax.rem(t + half, wide) + jnp.where(t < half, 0, 1)
        place = jnp.where(place == half, jnp.where(t < half, half, 0), place)
        at = pl.ds(pl.multiple_of(place * rows, rows), rows)
        gate_up = mid[at, :].astype(F32)
        grad_hidden = dot_f32(grads[at, :], down_full[...].reshape(down_shape), ((1,), (1,)))
        gate, up = gate_up[:, :size], gate_up[:, size:]
        opened = jax.nn.sigmoid(gate)
        acted = gate * opened
        hidden[at, :] = (acted * up).astype(BF16)
        mid[at, :size] = (grad_hidden * up * (opened * (1.0 + gate * (1.0 - opened)))).astype(BF16)
        mid[at, size:] = (grad_hidden * acted).astype(BF16)
        rows_buf[at, :] = dot_f32(mid[at, :], up_full[...].reshape(up_shape), ((1,), (1,))).astype(
            BF16
        )
        for n in range(half):

            @pl.when(t == n)
            def _():
                core[n].start()

        for n in range(half):

            @pl.when(t == half + lax.rem(n + half - 1, half))
            def _():
                core[n].wait_recv()
                total = rows_buf[n * rows : (n + 1) * rows, :].astype(F32) + core_buf[n].astype(F32)
                rows_buf[n * rows : (n + 1) * rows, :] = total.astype(BF16)
                if n > 0:
                    far[n - 1].start()

        return carry

    lax.fori_loop(0, wide, block, 0)

    step = min(256, size)
    for n in range(size // step):
        cut = slice(n * step, (n + 1) * step)
        down_grad[cut, :] = dot_f32(hidden[:, cut], grads[...], ((0,), (0,))).astype(BF16)

    @pl.when(is_end)
    def _():
        down_joined.start()

    @pl.when(is_middle)
    def _():
        down_direct.start()

    reloads = [
        pltpu.make_async_copy(out_ref, grads.at[pl.ds(0, width), :], local.at[9 + half]),
        pltpu.make_async_copy(grad_ref, grads.at[pl.ds(width, rows), :], local.at[10 + half]),
        pltpu.make_async_copy(mixed_ref, mixed_buf, local.at[11 + half]),
        pltpu.make_async_copy(middle_ref, grad_middle, local.at[12 + half]),
    ]
    for copy in reloads:
        copy.start()

    def up_rows(n, carry):
        at = pl.ds(pl.multiple_of(n * 256, 256), 256)
        up_grad[at, :] = dot_f32(normed[:, at], mid[...], ((0,), (0,))).astype(BF16)
        return carry

    lax.fori_loop(0, width // 256, up_rows, 0)

    @pl.when(is_end)
    def _():
        up_joined.start()

    @pl.when(is_middle)
    def _():
        up_direct.start()

    backs = [
        pltpu.make_async_copy(up_grad, up_grad_out, local.at[5 + half]),
        pltpu.make_async_copy(down_grad, down_grad_out, local.at[6 + half]),
        pltpu.make_async_copy(up_share(line[2]), up_src, local.at[7 + half]),
        pltpu.make_async_copy(down_share(line[2]), down_src, local.at[8 + half]),
    ]
    for copy in backs:
        copy.start()
    gather.sent()

    def branch(t, carry):
        place = lax.rem(t + half, wide)
        at = pl.ds(pl.multiple_of(place * rows, rows), rows)
        normed[at, :] = dot_f32(hidden[at, :], down_full[...].reshape(down_shape)).astype(BF16)
        for n in range(half):

            @pl.when(t == n)
            def _():
                branch_core[n].start()

        return carry

    lax.fori_loop(0, wide, branch, 0)
    for n in range(half):
        branch_core[n].wait_recv()
        total = normed[n * rows : (n + 1) * rows, :].astype(F32) + branch_buf[n].astype(F32)
        branch_sum[n] = total.astype(BF16)

    total = rows_buf[:rows, :].astype(F32)
    for n in range(1, half):
        far[n - 1].wait_recv()
        total = total + far_buf[n - 1].astype(F32)
    for copy in core + far:
        copy.wait_send()
    for copy in reloads:
        copy.wait()
    values = grad_middle[...]
    factor = rms_factor(values)
    values = values * factor
    gain_grad[...] = jnp.broadcast_to(
        jnp.sum(total * values, axis=0, keepdims=True), gain_grad.shape
    )
    total = total * gain_ref[0:1, :]
    inner = jnp.mean(total * values, axis=-1, keepdims=True)
    total = grads[width : width + rows, :].astype(F32) + factor * (total - values * inner)
    grad_middle[...] = total
    branch_grad = total.astype(BF16)
    grad_mixed[...] = dot_f32(branch_grad, grads[:width, :], ((1,), (1,))).astype(BF16)
    for copy in mixes + near:
        copy.start()
    slot_grad[pl.ds(pl.multiple_of(z * rows, rows), rows), :] = grad_mixed[
        :, pl.ds(pl.multiple_of(z * own_width, LANES), own_width)
    ]
    for n in range(width // 256):
        cut = slice(n * 256, (n + 1) * 256)
        rows_buf[cut, :] = dot_f32(mixed_buf[:, cut], branch_grad, ((0,), (0,))).astype(BF16)
    out_back = pltpu.make_async_copy(
        rows_buf.at[pl.ds(0, width), :], out_part, local.at[13 + half]
    )
    out_back.start()
    for copy in backs:
        copy.wait()
    up_acc[...] = up_grad[:, pl.ds(pl.multiple_of(z * unit, unit), unit)]
    down_acc[...] = down_grad[:, pl.ds(pl.multiple_of(z * part, part), part)]

    @pl.when(is_middle)
    def _():
        down_joined.wait_recv()
        down_src[...] = (down_src[...].astype(F32) + down_join[...].astype(F32)).astype(BF16)
        up_joined.wait_recv()
        up_src[...] = (up_src[...].astype(F32) + up_join[...].astype(F32)).astype(BF16)
        down_direct.wait()
        down_acc[...] = (down_acc[...].astype(F32) + down_mid[...].astype(F32)).astype(BF16)
        up_direct.wait()
        up_acc[...] = (up_acc[...].astype(F32) + up_mid[...].astype(F32)).astype(BF16)
        for copy in (relay, middle, down_relay, down_middle):
            copy.wait_send()

    @pl.when(is_end)
    def _():
        down_joined.wait_send()
        up_joined.wait_send()

    for copy in mixes + near:
        copy.wait()
    out_back.wait()
    for copy in passed + branch_core + [down_two, down_one]:
        copy.wait_send()


def second_part(
    normed, grad, far_grads, ups, down, middle, mixed_rows, out_full, gain, collective_id
):
    rows, width = normed.shape
    half = far_grads.shape[0] + 1
    wide = 2 * half
    wide_of_up, part_rows, mid_size = ups[0].shape
    down_rows = down.shape[0]
    size, unit, part = mid_size // 2, mid_size // 4, width // 4
    steps = 9 + 2 * wide + 4 * half + 8
    total = wide * rows
    shape = jax.ShapeDtypeStruct
    vmem = lambda *dims: pltpu.VMEM(dims, BF16)
    return pl.pallas_call(
        functools.partial(second_kernel, wide),
        out_shape=[
            shape((rows, width), F32), shape((8, width), F32), shape((4 * rows, part), BF16),
            shape((half, rows, width), BF16),
            shape((width, unit), BF16), shape((size, part), BF16),
            shape((width, unit), BF16), shape((size, part), BF16),
            shape((width, mid_size), BF16), shape((size, width), BF16),
            shape((width, width), BF16), shape((len(straight_steps(wide)), rows, width), BF16),
        ],
        in_specs=[ANY] * 10 + [VMEM],
        out_specs=[VMEM] * 8 + [ANY] * 4,
        scratch_shapes=[
            vmem(total, width), vmem(total, width), vmem(wide, 4, part_rows, mid_size),
            vmem(4, down_rows, width), vmem(total, size), vmem(total, mid_size), vmem(total, width),
            vmem(half, rows, width), vmem(half - 1, rows, width), vmem(half, rows, width),
            vmem(width, unit), vmem(width, unit), vmem(size, part), vmem(size, part),
            vmem(width, mid_size), vmem(size, width), vmem(rows, width), vmem(rows, width),
            DMA((steps,)), DMA((steps,)), DMA((14 + half,)),
        ],
        compiler_params=pltpu.CompilerParams(
            collective_id=collective_id, has_side_effects=True, vmem_limit_bytes=63 * 2**20
        ),
    )(
        normed, grad, far_grads, *ups, down, middle, mixed_rows, out_full,
        jnp.broadcast_to(gain[None], (8, width)),
    )


def add_up(parts):
    total = parts[0].astype(F32)
    for part in parts[1:]:
        total = total + part.astype(F32)
    return total


def on_device(
    tokens, gain_one, in_weight, forget_bias, out_weight, gain_two, gate_up_weight, down_weight,
    segment_ids, cotangent,
):
    wide, narrow = lax.axis_size("wide"), lax.axis_size("narrow")
    w, z = lax.axis_index("wide"), lax.axis_index("narrow")
    rows, width = tokens.shape
    slot = rows * narrow
    heads = forget_bias.shape[0]
    head_size = width // heads
    own_heads = heads // narrow
    own_width = own_heads * head_size
    part_rows = in_weight.shape[0]
    hidden_all = down_weight.shape[0] * wide * narrow
    unit = hidden_all // (2 * wide)
    columns = 4 * own_width + LANES
    base = 4 * width

    small = in_weight[:, base:].reshape(part_rows, 3, narrow, own_heads)
    small = jnp.moveaxis(small, 2, 0).reshape(narrow, part_rows, 3 * own_heads)
    small = jnp.pad(small, ((0, 0), (0, 0), (0, LANES - 3 * own_heads)))
    aligned = unit % LANES == 0

    def split_weights(sources, targets):
        copies = [(sources[1], targets[0].at[:, :, pl.ds(4 * own_width, LANES)])]
        for n in range(narrow):
            for group in range(4):
                copies.append(
                    (
                        sources[0].at[:, pl.ds(group * width + n * own_width, own_width)],
                        targets[0].at[n, :, pl.ds(group * own_width, own_width)],
                    )
                )
        return copies

    shapes = [
        jax.ShapeDtypeStruct((narrow, part_rows, columns), BF16),
        jax.ShapeDtypeStruct((wide, part_rows, 4 * unit), BF16),
    ]
    copies = 4 * narrow + 1
    fused = aligned and part_rows % 16 == 0
    if not fused:
        in_parts = local_copies(split_weights, copies, [in_weight, small], shapes[:1], False)[0]
        up_parts = jnp.moveaxis(gate_up_weight.reshape(part_rows, 4, wide, unit), 2, 0)
        up_parts = up_parts.reshape(wide, part_rows, 4 * unit)

    segments = segment_ids[0]
    joined = (segments[1:] == segments[:-1]).astype(F32)
    cont = jnp.concatenate([jnp.zeros((1,), F32), joined])
    cont = jnp.broadcast_to(cont[:, None], (slot, LANES))
    own_bias = lax.dynamic_slice_in_dim(forget_bias, z * own_heads, own_heads)
    bias = jnp.broadcast_to(jnp.pad(own_bias, (0, LANES - own_heads))[None], (8, LANES))
    block = min(256, slot)
    def row_block(ref, n):
        return ref.at[pl.ds(pl.multiple_of(n * rows, rows), rows), :]

    def column_block(ref, n):
        return ref.at[:, pl.ds(pl.multiple_of(n * own_width, LANES), own_width)]

    straight, diagonal = straight_steps(wide), diagonal_steps(wide)
    inputs = tokens.astype(F32)
    half = wide // 2
    if fused:
        (
            normed_one, in_full, out_full, projected, attended, logs, mixed_rows, middle, normed_two,
            up_block, up_two, up_one, down_block, grad_got,
        ) = first_part(
            tokens, in_weight, small, out_weight, gate_up_weight, cotangent, down_weight, gain_one,
            gain_two, bias, cont, wide, own_heads, head_size, block, 0,
        )
    else:
        pairs = []
        for i in range(wide * narrow):
            to_wide = (i % (2 * wide)) // 2
            to_narrow = i % 2 + 2 * (i // (2 * wide))
            pairs.append((i, to_wide * narrow + to_narrow))
        down_block = lax.ppermute(down_weight, ("wide", "narrow"), pairs)

        slot_tokens, in_full, out_full, up_block, grad_far = gather_all(
            tokens, in_parts, out_weight, up_parts, cotangent
        )
        slot_tokens = slot_tokens.reshape(slot, width)
        in_full = in_full.reshape(width, columns)
        out_full = out_full.reshape(width, width)

        up_two = on_line(up_block, LINE_TWO)
        up_one = on_line(up_block, LINE_ONE)

        slot_floats = slot_tokens.astype(F32)
        normed_one = (slot_floats * rms_factor(slot_floats) * gain_one).astype(BF16)
        projected = dot_f32(normed_one, in_full)

        mixed, attended, logs = attention_forward(
            projected, bias, cont, own_heads, head_size, block
        )

        mixed_rows, *grad_near = exchange(
            mixed, row_block, column_block, (rows, width), straight, [cotangent] * len(straight), 1
        )
        grads = {0: cotangent}
        grads.update({k: grad_near[n] for n, k in enumerate(straight)})
        grads.update({k: grad_far[n] for n, k in enumerate(diagonal)})
        grads = [grads[k] for k in range(0, wide, 2)]
        down_block = follow(down_block, mixed_rows)
        down_two = on_line(down_block, LINE_TWO)
        down_one = on_line(down_block, LINE_ONE)
        middle = inputs + dot_f32(mixed_rows, out_full)
        normed_two = (middle * rms_factor(middle) * gain_two).astype(BF16)

    if fused:
        (
            grad_middle, grad_gain_two, slot_grad, branch_sum, up_src, down_src, up_acc, down_acc,
            up_one, down_one, out_part, branch_near,
        ) = second_part(
            normed_two, cotangent, grad_got, [up_block, up_two, up_one], down_block, middle,
            mixed_rows, out_full, gain_two, 2,
        )
        grad_gain_two = grad_gain_two[0]
    else:
        ups = [up_block] + [follow(piece, normed_two) for piece in (up_two, up_one)]
        plane_normed, plane_grad, up_full, down_full = gather_rows(
            normed_two, grads, ups, [down_block, down_two, down_one], 2
        )
        plane_normed = plane_normed.reshape(wide * rows, width)
        plane_grad = plane_grad.reshape(wide * rows, width)
        up_full = up_full.reshape(width, 4 * unit)
        down_full = down_full.reshape(2 * unit, width)
        hidden, gate_up_grad, norm_even, norm_odd, branch = feed_forward(
            plane_normed, plane_grad, up_full, down_full, rows
        )
        grad_up_full = dot_f32(plane_normed, gate_up_grad, ((0,), (0,))).astype(BF16)
        grad_down_full = dot_f32(hidden, plane_grad, ((0,), (0,))).astype(BF16)
        if unit % LANES:
            grouped = grad_up_full.reshape(width, 4, unit)
            grad_up_full = jnp.pad(grouped, ((0, 0), (0, 0), (0, LANES - unit))).reshape(width, -1)
        branch = branch.reshape(wide, rows, width)
        fits = wide <= 8
        norm_got = along_wide(norm_odd.reshape(half, rows, width), 1, wide)
        (
            grad_normed_two, branch_sum, up_src, down_src, up_one, down_one, up_acc, down_acc,
        ) = middle_sums(
            norm_even.reshape(half, rows, width), norm_got,
            branch if fits else branch[:2, :16], grad_up_full, grad_down_full, 6,
        )
        if not fits:
            received = along_wide(branch[half:], 1, wide)
            branch_sum = (branch[:half].astype(F32) + received.astype(F32)).astype(BF16)
        upstream = cotangent.astype(F32)
        grad_middle_norm, grad_gain_two = rms_back(middle, gain_two, grad_normed_two)
        grad_middle = upstream + grad_middle_norm
        branch_one_grad = grad_middle.astype(BF16)
        grad_mixed = dot_f32(branch_one_grad, out_full, ((1,), (1,))).astype(BF16)
        slot_grad, *branch_near = exchange(
            grad_mixed, column_block, row_block, (slot, own_width), straight,
            [branch_sum[k // 2] for k in straight], 3,
        )
        branch_near = jnp.stack(branch_near)
        out_part = dot_f32(mixed_rows, branch_one_grad, ((0,), (0,))).astype(BF16)
    wide_rows = width // wide
    (
        unused, bias_grad, norm_part, in_part, grad_out, up_two, down_two, up_one, down_one,
        branch_far,
    ) = attention_backward(
        projected, bias, cont, attended, logs, slot_grad, in_full, normed_one,
        [up_src, down_src, up_one, down_one], out_part.reshape(wide, wide_rows, width), branch_sum,
        own_heads, head_size, block, 7,
    )
    branches = [branch_sum, branch_near, branch_far]
    all_bias = lax.dynamic_update_slice(
        jnp.zeros((width,), F32), bias_grad[0, :own_heads], (z * own_heads,)
    )
    small = jnp.stack([jnp.zeros((width,), F32), grad_gain_two, all_bias])
    small = jnp.pad(small, ((0, 5), (0, 0)))
    low = lambda part: part.astype(BF16)
    output, grad_tokens, grad_in, grad_up, grad_down, totals = last_part(
        norm_part, in_part.reshape(wide, wide_rows, columns), [low(up_acc), up_one, up_two],
        [low(down_acc), down_one, down_two], branches, tokens, middle, grad_middle, gain_one, small,
        own_width, own_heads, (base + 3 * heads) // narrow, 4,
    )
    if not aligned:
        grad_up = grad_up.reshape(wide_rows, wide, LANES)[:, :, :unit]
        grad_up = grad_up.reshape(wide_rows, wide * unit)
    grad_up, grad_down = grad_up.astype(F32), grad_down.astype(F32)
    return (
        output,
        grad_tokens,
        totals[0],
        grad_in,
        totals[2, :heads],
        grad_out,
        totals[1],
        grad_up,
        grad_down,
    )


def solution(mesh):
    both = ("wide", "narrow")
    in_specs = (
        P(both, None), P(), P(both, None), P(), P(both, None), P(), P(both, None), P(both, None),
        P("wide", None), P(both, None),
    )
    out_specs = (
        P(both, None), P(both, None), P(), P("wide", "narrow"), P(), P("wide", "narrow"), P(),
        P("wide", "narrow"), P("wide", "narrow"),
    )
    return jax.shard_map(
        on_device, mesh=mesh, in_specs=in_specs, out_specs=out_specs, check_vma=False
    )
```

```python
import functools

import jax
import jax.numpy as jnp
from jax import lax
from jax.experimental import pallas as pl
from jax.experimental.pallas import tpu as pltpu
from jax.sharding import PartitionSpec as P

EPSILON = 1e-06
SEPARATE = 128.0
F32 = jnp.float32
BF16 = jnp.bfloat16
LANES = 128
EXACT = lax.Precision.HIGHEST
ANY = pl.BlockSpec(memory_space=pltpu.HBM)


def dot_f32(left, right, dims=((1,), (0,))):
    return lax.dot_general(left, right, (dims, ((), ())), preferred_element_type=F32)


def along_wide(block, flip, wide):
    return lax.ppermute(block, "wide", [(i, i ^ flip) for i in range(wide)])


def copy_kernel(plan, count, *refs):
    sources, targets, sems = refs[:count], refs[count:-1], refs[-1]
    copies = plan(sources, targets)

    def each(act):
        for n, (src, dst, *when) in enumerate(copies):
            copy = pltpu.make_async_copy(src, dst, sems.at[n])
            if when:
                pl.when(when[0])(functools.partial(act, copy))
            else:
                act(copy)

    each(lambda copy: copy.start())
    each(lambda copy: copy.wait())


def local_copies(plan, copies, sources, shapes, gather):
    moved = sum(s.size * s.dtype.itemsize for s in shapes)
    inside = pl.BlockSpec(memory_space=pltpu.VMEM)
    return pl.pallas_call(
        functools.partial(copy_kernel, plan, len(sources)),
        out_shape=shapes,
        in_specs=[ANY if gather else inside] * len(sources),
        out_specs=[inside if gather else ANY] * len(shapes),
        compiler_params=pltpu.CompilerParams(vmem_limit_bytes=16 * 2**20),
        scratch_shapes=[pltpu.SemaphoreType.DMA((copies,))],
        cost_estimate=pl.CostEstimate(flops=0, bytes_accessed=2 * moved, transcendentals=0),
    )(*sources)


def flipped(me, k):
    out = me
    bit = 1
    while bit <= k:
        if k & bit:
            out = out + bit - 2 * bit * lax.rem(lax.div(out, bit), 2)
        bit *= 2
    return out


LINE_TWO = [(0, 2), (2, 0), (1, 3), (3, 1)]
LINE_ONE = [(0, 1), (1, 0), (2, 3), (3, 2)]
LINE_MIDDLE = [(1, 2), (2, 1)]
LINE_OUT = [(2, 3), (1, 0)]
LINE_IN = [(0, 1), (3, 2)]


def on_line(block, pairs):
    return lax.ppermute(block, "narrow", pairs)


def follow(array, *earlier):
    return lax.optimization_barrier((array, *earlier))[0]


MESH = pl.DeviceIdType.MESH
VMEM = pl.BlockSpec(memory_space=pltpu.VMEM)
DMA = pltpu.SemaphoreType.DMA


def greet(devices):
    barrier = pltpu.get_barrier_semaphore()
    for device in devices:
        pl.semaphore_signal(barrier, inc=1, device_id=device, device_id_type=MESH)
    pl.semaphore_wait(barrier, len(devices))


class Sender:
    def __init__(self, send, recv):
        self.send, self.recv, self.used = send, recv, 0

    def plan(self, src, dst, device):
        n = self.used
        self.used += 1
        return pltpu.make_async_remote_copy(
            src_ref=src, dst_ref=dst, send_sem=self.send.at[n], recv_sem=self.recv.at[n],
            device_id=device, device_id_type=MESH,
        )


def narrow_device(n):
    return {"narrow": n}


def wide_device(n):
    return {"wide": n}


def wide_steps(wide):
    return [1] + list(range(2, wide, 2))


def straight_steps(wide):
    return [k for k in range(2, wide, 2) if k & (k - 1) == 0]


def diagonal_steps(wide):
    return [k for k in range(2, wide, 2) if k & (k - 1)]


def by_device(ref, w):
    return (lambda k: ref.at[flipped(w, k)]), (lambda k, to: ref.at[flipped(w, k)])


class WideGather:
    def __init__(self, sender, w, wide, part, target):
        self.far = list(range(2, wide, 2))
        self.first = {
            k: sender.plan(part(0), target(0, k), wide_device(flipped(w, k)))
            for k in wide_steps(wide)
        }
        sibling = wide_device(flipped(w, 1))
        self.second = {k: sender.plan(part(k), target(k, 1), sibling) for k in self.far}

    def start(self):
        for k in self.far + [1]:
            self.first[k].start()

    def pass_on(self):
        for k in self.far:
            self.first[k].wait_recv()
            self.second[k].start()

    def received(self):
        self.first[1].wait_recv()
        for k in self.far:
            self.second[k].wait_recv()

    def sent(self):
        for copy in list(self.first.values()) + list(self.second.values()):
            copy.wait_send()

    def finish(self):
        self.received()
        self.sent()


def gather_kernel(
    wide, x_ref, in_ref, out_ref, up_ref, grad_ref, slot_ref, in_full, out_full, up_block, grad_far,
    send, recv, local,
):
    w, z = lax.axis_index("wide"), lax.axis_index("narrow")
    line = [flipped(z, k) for k in range(4)]
    sender = Sender(send, recv)
    own = [
        pltpu.make_async_copy(in_ref.at[z], in_full.at[w, z], local.at[0]),
        pltpu.make_async_copy(out_ref, out_full.at[w, z], local.at[1]),
        pltpu.make_async_copy(x_ref, slot_ref.at[z], local.at[2]),
        pltpu.make_async_copy(up_ref.at[w], up_block.at[w], local.at[3]),
    ]
    for copy in own:
        copy.start()
    greet(
        [narrow_device(line[k]) for k in (1, 2, 3)]
        + [wide_device(flipped(w, k)) for k in range(1, wide)]
    )
    ups = [
        sender.plan(up_ref.at[flipped(w, k)], up_block.at[w], wide_device(flipped(w, k)))
        for k in range(1, wide)
    ]
    grads = [
        sender.plan(grad_ref, grad_far.at[n], wide_device(flipped(w, k)))
        for n, k in enumerate(diagonal_steps(wide))
    ]
    is_middle = (z == 1) | (z == 2)
    is_end = (z == 0) | (z == 3)
    ins = [
        sender.plan(in_ref.at[line[k]], in_full.at[w, z], narrow_device(line[k])) for k in (2, 3, 1)
    ]
    outs = [sender.plan(out_ref, out_full.at[w, z], narrow_device(line[k])) for k in (2, 3, 1)]
    two = sender.plan(x_ref, slot_ref.at[z], narrow_device(line[2]))
    one = sender.plan(x_ref, slot_ref.at[z], narrow_device(line[1]))
    middle = sender.plan(x_ref, slot_ref.at[z], narrow_device(line[3]))
    relay = sender.plan(slot_ref.at[line[2]], slot_ref.at[line[2]], narrow_device(line[1]))
    in_wide = WideGather(sender, w, wide, *by_device(in_full, w))
    out_wide = WideGather(sender, w, wide, *by_device(out_full, w))
    for copy in ins + outs + ups:
        copy.start()
    own[0].wait()
    for copy in ins:
        copy.wait_recv()
    in_wide.start()
    two.start()
    one.start()
    own[1].wait()
    for copy in outs:
        copy.wait_recv()
    out_wide.start()
    in_wide.pass_on()
    for copy in grads:
        copy.start()
    two.wait_recv()

    @pl.when(is_middle)
    def _():
        relay.start()
        middle.start()

    out_wide.pass_on()
    one.wait_recv()
    own[2].wait()
    own[3].wait()
    for copy in ups + grads:
        copy.wait()

    @pl.when(is_middle)
    def _():
        middle.wait_recv()
        middle.wait_send()
        relay.wait_send()

    @pl.when(is_end)
    def _():
        relay.wait_recv()

    for copy in ins + outs + [two, one]:
        copy.wait_send()
    in_wide.finish()
    out_wide.finish()


def gather_all(tokens, in_parts, out_weight, up_parts, cotangent):
    narrow, wide = in_parts.shape[0], up_parts.shape[0]
    steps = 10 + 4 * wide
    shapes = [
        (narrow,) + tokens.shape, (wide,) + in_parts.shape, (wide, narrow) + out_weight.shape,
        up_parts.shape, (len(diagonal_steps(wide)),) + cotangent.shape,
    ]
    return pl.pallas_call(
        functools.partial(gather_kernel, wide),
        out_shape=[jax.ShapeDtypeStruct(shape, BF16) for shape in shapes],
        in_specs=[ANY] * 5,
        out_specs=[VMEM] * 5,
        scratch_shapes=[DMA((steps,)), DMA((steps,)), DMA((4,))],
        compiler_params=pltpu.CompilerParams(
            collective_id=0, has_side_effects=True, vmem_limit_bytes=40 * 2**20
        ),
    )(tokens, in_parts, out_weight, up_parts, cotangent)


def exchange_kernel(source, target, steps, *refs):
    count = len(steps)
    src_ref, sides, dst_ref = refs[0], refs[1 : 1 + count], refs[1 + count]
    got = refs[2 + count : 2 + 2 * count]
    send, recv, local = refs[2 + 2 * count :]
    w, z = lax.axis_index("wide"), lax.axis_index("narrow")
    line = [flipped(z, k) for k in range(4)]
    sender = Sender(send, recv)
    own = pltpu.make_async_copy(source(src_ref, z), target(dst_ref, z), local.at[0])
    own.start()
    greet(
        [narrow_device(line[k]) for k in (1, 2, 3)] + [wide_device(flipped(w, k)) for k in steps]
    )
    copies = [
        sender.plan(source(src_ref, line[k]), target(dst_ref, z), narrow_device(line[k]))
        for k in (2, 3, 1)
    ]
    copies += [
        sender.plan(sides[n], got[n], wide_device(flipped(w, k))) for n, k in enumerate(steps)
    ]
    for copy in copies:
        copy.start()
    own.wait()
    for copy in copies:
        copy.wait()


def exchange(array, source, target, shape, steps, sides, collective_id):
    count = len(steps) + 4
    return pl.pallas_call(
        functools.partial(exchange_kernel, source, target, steps),
        out_shape=[jax.ShapeDtypeStruct(shape, array.dtype)]
        + [jax.ShapeDtypeStruct(side.shape, side.dtype) for side in sides],
        in_specs=[ANY] * (1 + len(sides)),
        out_specs=[VMEM] * (1 + len(sides)),
        scratch_shapes=[DMA((count,)), DMA((count,)), DMA((1,))],
        compiler_params=pltpu.CompilerParams(
            collective_id=collective_id, has_side_effects=True, vmem_limit_bytes=16 * 2**20
        ),
    )(array, *sides)


def place_of(k, wide):
    return k // 2 + (k % 2) * (wide // 2)


def rows_kernel(wide, *refs):
    half = wide // 2
    grads = refs[:half]
    (
        src_ref, up_ref, up_two, up_one, down_ref, down_two, down_one, dst_ref, grad_ref, up_full,
        down_full, send, recv, local,
    ) = refs[half:]
    w, z = lax.axis_index("wide"), lax.axis_index("narrow")
    line = [flipped(z, k) for k in range(4)]
    is_middle = (z == 1) | (z == 2)
    is_end = (z == 0) | (z == 3)
    sender = Sender(send, recv)
    up_at = lambda n: up_full.at[:, n]
    down_at = lambda n: down_full.at[n]
    moves = [
        (src_ref, dst_ref.at[0]),
        (down_ref, down_at(z)), (down_two, down_at(line[2])), (down_one, down_at(line[1])),
        (up_ref, up_at(z)), (up_two, up_at(line[2])), (up_one, up_at(line[1])),
    ] + [(grads[n], grad_ref.at[n]) for n in range(half)]
    own = [pltpu.make_async_copy(src, dst, local.at[n]) for n, (src, dst) in enumerate(moves)]
    for copy in own:
        copy.start()
    greet(
        [wide_device(flipped(w, k)) for k in wide_steps(wide)]
        + [narrow_device(line[k]) for k in (1, 3)]
    )
    gather = WideGather(
        sender, w, wide, lambda k: src_ref if k == 0 else dst_ref.at[place_of(k, wide)],
        lambda k, to: dst_ref.at[place_of(k ^ to, wide)],
    )
    middles = [
        sender.plan(up_ref, up_at(z), narrow_device(line[3])),
        sender.plan(down_ref, down_at(z), narrow_device(line[3])),
    ]
    relays = [
        sender.plan(up_two, up_at(line[2]), narrow_device(line[1])),
        sender.plan(down_two, down_at(line[2]), narrow_device(line[1])),
    ]
    gather.start()

    @pl.when(is_middle)
    def _():
        for copy in middles + relays:
            copy.start()

    sibling = wide_device(flipped(w, 1))
    copies = [sender.plan(grads[n], grad_ref.at[half + n], sibling) for n in range(half)]
    for copy in copies:
        copy.start()
    gather.pass_on()

    @pl.when(is_middle)
    def _():
        for copy in middles:
            copy.wait()
        for copy in relays:
            copy.wait_send()

    @pl.when(is_end)
    def _():
        for copy in relays:
            copy.wait_recv()

    for copy in own + copies:
        copy.wait()
    gather.finish()


def gather_rows(array, grads, ups, downs, collective_id):
    half = len(grads)
    wide = 2 * half
    whole = jax.ShapeDtypeStruct((wide,) + array.shape, array.dtype)
    up_shape = ups[0].shape
    full = jax.ShapeDtypeStruct((up_shape[0], 4) + up_shape[1:], BF16)
    return pl.pallas_call(
        functools.partial(rows_kernel, wide),
        out_shape=[whole, whole, full, jax.ShapeDtypeStruct((4,) + downs[0].shape, BF16)],
        in_specs=[ANY] * (half + 7),
        out_specs=[VMEM, ANY if wide > 8 else VMEM, VMEM, VMEM],
        scratch_shapes=[DMA((2 * wide + 4,)), DMA((2 * wide + 4,)), DMA((half + 7,))],
        compiler_params=pltpu.CompilerParams(
            collective_id=collective_id, has_side_effects=True, vmem_limit_bytes=48 * 2**20
        ),
    )(*grads, array, *ups, *downs)


def hidden_kernel(
    half, normed_ref, grad_ref, up_ref, down_ref, hidden_ref, mid_ref, even_ref, odd_ref, branch_ref
):
    size = down_ref.shape[0]
    gate_up = dot_f32(normed_ref[...], up_ref[...])
    grad_hidden = dot_f32(grad_ref[...], down_ref[...], ((1,), (1,)))
    gate, up = gate_up[:, :size], gate_up[:, size:]
    opened = jax.nn.sigmoid(gate)
    acted = gate * opened
    hidden_ref[...] = (acted * up).astype(BF16)
    mid_ref[:, :size] = (grad_hidden * up * (opened * (1.0 + gate * (1.0 - opened)))).astype(BF16)
    mid_ref[:, size:] = (grad_hidden * acted).astype(BF16)
    grad_normed = dot_f32(mid_ref[...], up_ref[...], ((1,), (1,))).astype(BF16)
    branch_ref[...] = dot_f32(hidden_ref[...], down_ref[...]).astype(BF16)
    step = pl.program_id(0)

    @pl.when(step < half)
    def _():
        even_ref[...] = grad_normed

    @pl.when(step >= half)
    def _():
        odd_ref[...] = grad_normed


def feed_forward(normed, grad, up_full, down_full, rows):
    total, width = normed.shape
    blocks = total // rows
    half = blocks // 2
    size = down_full.shape[0]
    row_block = lambda columns: pl.BlockSpec((rows, columns), lambda i: (i, 0))
    fixed = lambda array: pl.BlockSpec(array.shape, lambda i: (0, 0))
    return pl.pallas_call(
        functools.partial(hidden_kernel, half),
        grid=(blocks,),
        in_specs=[row_block(width), row_block(width), fixed(up_full), fixed(down_full)],
        out_specs=[
            row_block(size), row_block(2 * size),
            pl.BlockSpec((rows, width), lambda i: (jnp.minimum(i, half - 1), 0)),
            pl.BlockSpec((rows, width), lambda i: (jnp.maximum(i - half, 0), 0)),
            row_block(width),
        ],
        out_shape=[
            jax.ShapeDtypeStruct((total, size), BF16),
            jax.ShapeDtypeStruct((total, 2 * size), BF16),
            jax.ShapeDtypeStruct((total // 2, width), BF16),
            jax.ShapeDtypeStruct((total // 2, width), BF16),
            jax.ShapeDtypeStruct((total, width), BF16),
        ],
        compiler_params=pltpu.CompilerParams(vmem_limit_bytes=48 * 2**20),
    )(normed, grad, up_full, down_full)


def middle_kernel(
    wide, even_ref, got_ref, branch_ref, up_ref, down_ref, norm_sum, branch_sum, up_src, down_src,
    up_one, down_one, up_acc, down_acc, core_buf, own_buf, far_buf, branch_buf, up_join, up_mid,
    down_join, down_mid, up_own, down_own, send, recv, local,
):
    w, z = lax.axis_index("wide"), lax.axis_index("narrow")
    line = [flipped(z, k) for k in range(4)]
    half = wide // 2
    unit = up_src.shape[1]
    part = down_src.shape[1]
    sender = Sender(send, recv)
    is_middle = (z == 1) | (z == 2)
    is_end = (z == 0) | (z == 3)

    def up_share(n):
        return up_ref.at[:, pl.ds(pl.multiple_of(n * unit, unit), unit)]

    def down_share(n):
        return down_ref.at[:, pl.ds(pl.multiple_of(n * part, part), part)]

    moves = [
        (up_share(line[2]), up_src), (down_share(line[2]), down_src),
        (up_share(z), up_own), (down_share(z), down_own),
        (up_share(line[1]), up_one), (down_share(line[1]), down_one),
    ]
    moves += [(got_ref.at[n], core_buf.at[n]) for n in range(half)]
    moves += [(even_ref.at[n], own_buf.at[n]) for n in range(half)]
    pairs = branch_sum.shape[0]
    moves += [(branch_ref.at[n], branch_sum.at[n]) for n in range(pairs)]
    own = [pltpu.make_async_copy(src, dst, local.at[n]) for n, (src, dst) in enumerate(moves)]
    for copy in own:
        copy.start()
    greet(
        [wide_device(flipped(w, k)) for k in wide_steps(wide)]
        + [narrow_device(line[k]) for k in (1, 3)]
    )
    sibling = wide_device(flipped(w, 1))
    far = [
        sender.plan(own_buf.at[n], far_buf.at[n - 1], wide_device(flipped(w, 2 * n)))
        for n in range(1, half)
    ]
    branch_core = [
        sender.plan(branch_ref.at[pairs + n], branch_buf.at[n], sibling) for n in range(pairs)
    ]
    joins = [
        sender.plan(up_share(line[3]), up_join, narrow_device(line[1])),
        sender.plan(down_share(line[3]), down_join, narrow_device(line[1])),
    ]
    mids = [
        sender.plan(up_share(line[3]), up_mid, narrow_device(line[3])),
        sender.plan(down_share(line[3]), down_mid, narrow_device(line[3])),
    ]
    order = list(range(1, half)) + [0]

    @pl.when(is_end)
    def _():
        for copy in joins:
            copy.start()

    @pl.when(is_middle)
    def _():
        for copy in mids:
            copy.start()

    for n in order:
        own[6 + n].wait()
        own[6 + half + n].wait()
        total = own_buf[n].astype(F32) + core_buf[n].astype(F32)
        own_buf[n] = total.astype(BF16)
        if n > 0:
            far[n - 1].start()
    for copy in branch_core:
        copy.start()
    for n in range(pairs):
        branch_core[n].wait_recv()
        own[6 + 2 * half + n].wait()
        total = branch_sum[n].astype(F32) + branch_buf[n].astype(F32)
        branch_sum[n] = total.astype(BF16)
    for n in range(6):
        own[n].wait()

    @pl.when(is_middle)
    def _():
        for copy in joins:
            copy.wait_recv()
        up_src[...] = (up_src[...].astype(F32) + up_join[...].astype(F32)).astype(BF16)
        down_src[...] = (down_src[...].astype(F32) + down_join[...].astype(F32)).astype(BF16)

    total = own_buf[0].astype(F32)
    for n in range(1, half):
        far[n - 1].wait_recv()
        total = total + far_buf[n - 1].astype(F32)
    norm_sum[...] = total
    up_acc[...] = up_own[...].astype(F32)
    down_acc[...] = down_own[...].astype(F32)

    @pl.when(is_middle)
    def _():
        for copy in mids:
            copy.wait()
        up_acc[...] += up_mid[...].astype(F32)
        down_acc[...] += down_mid[...].astype(F32)

    @pl.when(is_end)
    def _():
        for copy in joins:
            copy.wait_send()

    for copy in far + branch_core:
        copy.wait_send()


def middle_sums(even, got, branch, grad_up, grad_down, collective_id):
    half, rows, width = even.shape
    wide = 2 * half
    unit, part = grad_up.shape[1] // 4, grad_down.shape[1] // 4
    up_shape, down_shape = (grad_up.shape[0], unit), (grad_down.shape[0], part)
    steps = 4 * half + 6
    rows_buf = pltpu.VMEM((half, rows, width), BF16)
    pairs = branch.shape[0] // 2
    return pl.pallas_call(
        functools.partial(middle_kernel, wide),
        out_shape=[
            jax.ShapeDtypeStruct((rows, width), F32),
            jax.ShapeDtypeStruct((pairs,) + branch.shape[1:], BF16),
            *[jax.ShapeDtypeStruct(up_shape, BF16), jax.ShapeDtypeStruct(down_shape, BF16)] * 2,
            jax.ShapeDtypeStruct(up_shape, F32),
            jax.ShapeDtypeStruct(down_shape, F32),
        ],
        in_specs=[ANY] * 5,
        out_specs=[VMEM] * 8,
        scratch_shapes=[
            rows_buf, rows_buf, pltpu.VMEM((half - 1, rows, width), BF16),
            pltpu.VMEM((pairs,) + branch.shape[1:], BF16),
            *[pltpu.VMEM(up_shape, BF16)] * 2, *[pltpu.VMEM(down_shape, BF16)] * 2,
            pltpu.VMEM(up_shape, BF16), pltpu.VMEM(down_shape, BF16),
            DMA((steps,)), DMA((steps,)), DMA((6 + 3 * half,)),
        ],
        compiler_params=pltpu.CompilerParams(
            collective_id=collective_id, has_side_effects=True, vmem_limit_bytes=58 * 2**20
        ),
    )(even, got, branch, grad_up, grad_down)


def last_kernel(
    wide, rows, own_width, own_heads, norm_ref, in_ref, up_parts, down_parts, branch_refs, token_ref,
    middle_ref, grad_ref, gain_ref, small_ref, output, grad_tokens, grad_in, up_got, down_got, totals, join_buf, one_buf, mid_buf, two_buf, two_src, own_norm, norm_sum,
    in_core, in_own, in_far, in_sum, in_got, after_got, tail_buf, up_low, up_bufs, down_low,
    down_bufs, branch_bufs, narrow_buf, wide_buf, sum_buf, send, recv, down_send, down_recv,
    local,
):
    w, z = lax.axis_index("wide"), lax.axis_index("narrow")
    line = [flipped(z, k) for k in range(4)]
    half = wide // 2
    unit = up_low.shape[1]
    wide_rows, width = grad_in.shape[0], token_ref.shape[1]
    sender = Sender(send, recv)
    is_middle = (z == 1) | (z == 2)
    is_end = (z == 0) | (z == 3)

    def norm_block(n):
        return norm_ref.at[pl.ds(pl.multiple_of(n * rows, rows), rows), :]

    def up_rows(n):
        return up_low.at[pl.ds(pl.multiple_of(n * wide_rows, 16), wide_rows), :]

    def up_columns(n):
        return up_got.at[:, pl.ds(pl.multiple_of(n * unit, LANES), unit)]

    def section(n):
        return in_sum.at[:, pl.ds(pl.multiple_of(n * own_width, LANES), own_width)]

    def after_section(n):
        return in_sum.at[:, pl.ds(pl.multiple_of((n + 1) * own_width, LANES), LANES)]

    moves = [(norm_block(line[2]), two_src), (norm_block(z), own_norm)]
    moves += [(in_ref.at[flipped(w, 2 * n)], in_own.at[n]) for n in range(half)]
    ffn_at = len(moves)
    moves += [(ref, up_bufs.at[n]) for n, ref in enumerate(up_parts)]
    moves += [(ref, down_bufs.at[n]) for n, ref in enumerate(down_parts)]
    branch_at = len(moves)
    moves += [(ref, branch_bufs.at[n]) for n, ref in enumerate(branch_refs)]
    own = [pltpu.make_async_copy(src, dst, local.at[n]) for n, (src, dst) in enumerate(moves)]
    for copy in own:
        copy.start()
    greet(
        [narrow_device(line[k]) for k in (1, 2, 3)]
        + [wide_device(flipped(w, k)) for k in range(1, wide)]
    )
    sibling = wide_device(flipped(w, 1))
    joined = sender.plan(norm_block(line[3]), join_buf, narrow_device(line[1]))
    one = sender.plan(norm_block(line[1]), one_buf, narrow_device(line[1]))
    middle = sender.plan(norm_block(line[3]), mid_buf, narrow_device(line[3]))
    two = sender.plan(two_src, two_buf, narrow_device(line[2]))
    core = [
        sender.plan(in_ref.at[flipped(w, 2 * n + 1)], in_core.at[n], sibling) for n in range(half)
    ]
    far = [
        sender.plan(in_own.at[n], in_far.at[n - 1], wide_device(flipped(w, 2 * n)))
        for n in range(1, half)
    ]
    sections = [
        sender.plan(section(line[k]), in_got.at[z], narrow_device(line[k])) for k in (2, 3, 1)
    ]
    afters = [
        (
            (z == 0) | (line[k] == 3), (line[k] == 0) | (z == 3),
            sender.plan(after_section(line[k]), after_got.at[z], narrow_device(line[k])),
        )
        for k in (2, 3, 1)
    ]
    ups = [
        sender.plan(up_rows(flipped(w, k)), up_columns(w), wide_device(flipped(w, k)))
        for k in range(1, wide)
    ]
    first = [
        sender.plan(sum_buf, narrow_buf.at[z], narrow_device(line[k])) for k in (1, 2, 3)
    ]
    second = [
        sender.plan(sum_buf, wide_buf.at[w], wide_device(flipped(w, k))) for k in range(1, wide)
    ]
    parity, target = lax.rem(w, 2), lax.div(w, 2)
    depth = down_low.shape[0] // 2
    down_at = pl.ds(pl.multiple_of(parity * depth, 16), depth)
    downs = []
    for n in range(2):
        owner = target + n * half
        src, dst = down_low.at[pl.ds(n * depth, depth), :], down_got.at[down_at, :]
        push = pltpu.make_async_remote_copy(
            src_ref=src, dst_ref=dst, send_sem=down_send.at[n], recv_sem=down_recv.at[parity],
            device_id=wide_device(owner), device_id_type=MESH,
        )
        stay = pltpu.make_async_copy(src, dst, local.at[len(moves) + 1 + n])
        downs.append((owner == w, push, stay))

    order = list(range(1, half)) + [0]
    for n in order:
        core[n].start()

    @pl.when(is_end)
    def _():
        joined.start()

    @pl.when(is_middle)
    def _():
        middle.start()

    for n in order:
        core[n].wait_recv()
        own[2 + n].wait()
        total = in_own[n].astype(F32) + in_core[n].astype(F32)
        in_own[n] = total.astype(BF16)
        if n > 0:
            far[n - 1].start()
    own[0].wait()

    @pl.when(is_middle)
    def _():
        joined.wait_recv()
        two_src[...] = (two_src[...].astype(F32) + join_buf[...].astype(F32)).astype(BF16)

    two.start()
    one.start()
    for n in range(6):
        own[ffn_at + n].wait()
    up_low[...] = add_up([up_bufs[n] for n in range(3)]).astype(BF16)
    down_low[...] = add_up([down_bufs[n] for n in range(3)]).astype(BF16)
    for copy in ups:
        copy.start()
    for stays, push, stay in downs:
        pl.when(stays)(stay.start)
        pl.when(jnp.logical_not(stays))(push.start)
    up_got[:, pl.ds(pl.multiple_of(w * unit, LANES), unit)] = up_low[
        pl.ds(pl.multiple_of(w * wide_rows, 16), wide_rows), :
    ]
    total = middle_ref[...]
    for n in range(half):
        own[branch_at + n].wait()
        total = total + branch_bufs[n].astype(F32)
    output[...] = total.astype(BF16)

    total = in_own[0].astype(F32)
    for n in range(1, half):
        far[n - 1].wait_recv()
        total = total + in_far[n - 1].astype(F32)
    in_sum[...] = total.astype(BF16)
    mine = pltpu.make_async_copy(section(z), in_got.at[z], local.at[len(moves)])
    mine.start()
    own[1].wait()
    one.wait_recv()
    norm_sum[...] = own_norm[...].astype(F32) + one_buf[...].astype(F32)

    @pl.when(is_middle)
    def _():
        middle.wait()
        norm_sum[...] += mid_buf[...].astype(F32)

    two.wait_recv()
    for copy in sections:
        copy.start()
    for sends, gets, copy in afters:
        pl.when(sends)(copy.start)
    after_got[z] = after_section(z)[...]
    grads = norm_sum[...] + two_buf[...].astype(F32)
    values = token_ref[...].astype(F32)
    factor = rms_factor(values)
    normed = values * factor
    scaled = grads * gain_ref[0:1, :]
    inner = jnp.mean(scaled * normed, axis=-1, keepdims=True)
    grad_tokens[...] = grad_ref[...] + factor * (scaled - normed * inner)
    narrow_buf[z] = small_ref[...]
    narrow_buf[z, 0:1, :] = jnp.sum(grads * normed, axis=0, keepdims=True)
    sum_buf[...] = narrow_buf[z]
    for copy in first:
        copy.start()

    for copy in ups:
        copy.wait_recv()
    for n, (stays, push, stay) in enumerate(downs):
        pl.when(stays)(stay.wait)
        pl.when(jnp.logical_not(stays))(push.wait_send)
    for n in range(2):
        source = lax.rem(2 * w + n, wide)
        arrived = pltpu.make_async_remote_copy(
            src_ref=down_low.at[pl.ds(0, depth), :], dst_ref=down_got.at[pl.ds(n * depth, depth), :],
            send_sem=down_send.at[n], recv_sem=down_recv.at[n], device_id=sibling,
            device_id_type=MESH,
        )
        pl.when(source != w)(arrived.wait_recv)

    for copy in first:
        copy.wait()
    sum_buf[...] = narrow_buf[0] + narrow_buf[1] + narrow_buf[2] + narrow_buf[3]
    for copy in second:
        copy.start()
    wide_buf[w] = sum_buf[...]

    for copy in sections:
        copy.wait_recv()
    mine.wait()
    for sends, gets, copy in afters:
        pl.when(gets)(copy.wait_recv)

    @pl.when(z == 3)
    def _():
        row, lane = iota((LANES, LANES), 0), iota((LANES, LANES), 1)
        last = jnp.zeros((wide_rows, LANES), F32)
        for n in range(4):
            group = lax.div(row, own_heads)
            place = group * (4 * own_heads) + n * own_heads + row - group * own_heads
            spot = ((lane == place) & (row < 3 * own_heads)).astype(BF16)
            last = last + dot_f32(after_got[n], spot)
        tail_buf[...] = last

    @pl.when(z != 3)
    def _():
        tail_buf[...] = after_got[0].astype(F32)

    whole = jnp.concatenate([in_got[n].astype(F32) for n in range(4)] + [tail_buf[...]], axis=1)
    move = whole.shape[1] - (grad_in.shape[1] - width) * z
    grad_in[...] = pltpu.roll(whole, lax.rem(move, whole.shape[1]), 1)[:, : grad_in.shape[1]]

    for copy in second:
        copy.wait()
    total = wide_buf[0]
    for n in range(1, wide):
        total = total + wide_buf[n]
    totals[...] = total

    @pl.when(is_end)
    def _():
        joined.wait_send()

    for sends, gets, copy in afters:
        pl.when(sends)(copy.wait_send)
    for copy in [one, two] + core + far + sections + ups:
        copy.wait_send()


def grouped_last_kernel(wide, rows, own_width, own_heads, *refs):
    own, near, far = refs[8:11]
    branches = [own.at[0]]
    branches += [near.at[n] for n in range(near.shape[0])] + [far.at[n] for n in range(far.shape[0])]
    last_kernel(
        wide, rows, own_width, own_heads, *refs[:2], refs[2:5], refs[5:8], branches, *refs[11:],
    )


def last_part(
    norm_part, in_part, ups, downs, branches, tokens, middle, grad_middle, gain, small, own_width, own_heads,
    shard, collective_id,
):
    wide, wide_rows, columns = in_part.shape
    half = wide // 2
    rows, width = tokens.shape
    unit = ups[0].shape[1]
    steps = 4 + 2 * half + 12 + 2 * wide
    shape = jax.ShapeDtypeStruct
    vmem = lambda *dims: pltpu.VMEM(dims, BF16)
    return pl.pallas_call(
        functools.partial(grouped_last_kernel, wide, rows, own_width, own_heads),
        out_shape=[
            shape((rows, width), BF16), shape((rows, width), F32), shape((wide_rows, shard), F32),
            shape((wide_rows, wide * unit), BF16), shape(downs[0].shape, BF16),
            shape(small.shape, F32),
        ],
        in_specs=[ANY] * 11 + [VMEM] * 5,
        out_specs=[VMEM] * 6,
        scratch_shapes=[
            *[vmem(rows, width)] * 6, pltpu.VMEM((rows, width), F32),
            vmem(half, wide_rows, columns), vmem(half, wide_rows, columns),
            vmem(half - 1, wide_rows, columns), vmem(wide_rows, columns),
            vmem(4, wide_rows, own_width), vmem(4, wide_rows, LANES),
            pltpu.VMEM((wide_rows, LANES), F32), vmem(*ups[0].shape), vmem(3, *ups[0].shape),
            vmem(*downs[0].shape), vmem(3, *downs[0].shape), vmem(half, rows, width),
            pltpu.VMEM((4,) + small.shape, F32), pltpu.VMEM((wide,) + small.shape, F32),
            pltpu.VMEM(small.shape, F32),
            DMA((steps,)), DMA((steps,)), DMA((2,)), DMA((2,)), DMA((12 + 2 * half,)),
        ],
        compiler_params=pltpu.CompilerParams(
            collective_id=collective_id, has_side_effects=True, vmem_limit_bytes=60 * 2**20
        ),
    )(
        norm_part, in_part, *ups, *downs, *branches, tokens, middle, grad_middle,
        jnp.broadcast_to(gain[None], (8, width)), small,
    )


def rms_factor(values):
    return lax.rsqrt(jnp.mean(values * values, axis=-1, keepdims=True) + EPSILON)


def rms_back(values, gain, grad):
    factor = rms_factor(values)
    normed = values * factor
    grad_gain = jnp.sum(grad * normed, axis=0)
    scaled = grad * gain
    inner = jnp.mean(scaled * normed, axis=-1, keepdims=True)
    return (factor * (scaled - normed * inner), grad_gain)


def log_sigmoid(v):
    return jnp.minimum(v, 0.0) - jnp.log1p(jnp.exp(-jnp.abs(v)))


def iota(shape, dim):
    return lax.broadcasted_iota(jnp.int32, shape, dim)


def running_sum(v, reverse):
    rows = v.shape[0]
    index = iota(v.shape, 0)
    step = 1
    while step < rows:
        if reverse:
            v = v + jnp.where(index < rows - step, pltpu.roll(v, rows - step, 0), 0.0)
        else:
            v = v + jnp.where(index >= step, pltpu.roll(v, step, 0), 0.0)
        step *= 2
    return v


def half_of(lane, head_size):
    return (lane >= head_size).astype(jnp.int32)


def spread(first, head_size):
    row, lane = iota((LANES, LANES), 0), iota((LANES, LANES), 1)
    return row == first + half_of(lane, head_size)


def collect(first, head_size):
    row, lane = iota((LANES, LANES), 0), iota((LANES, LANES), 1)
    return lane == first + half_of(row, head_size)


def same_head(head_size):
    row, lane = iota((LANES, LANES), 0), iota((LANES, LANES), 1)
    return (half_of(row, head_size) == half_of(lane, head_size)).astype(F32)


def exact_dot(left, right):
    return lax.dot_general(
        left, right, (((1,), (0,)), ((), ())), precision=EXACT, preferred_element_type=F32
    )


def head_mean(v, head_size):
    return exact_dot(v, same_head(head_size)) * (1.0 / head_size)


def prologue(pair, heads, head_size, q_ref, k_ref, v_ref, small_low, cont):
    spot = lambda group: spread(group * heads + 2 * pair, head_size).astype(BF16)
    key_mix = jax.nn.sigmoid(dot_f32(small_low, spot(1)))
    value_mix = jax.nn.sigmoid(dot_f32(small_low, spot(2)))
    queries = q_ref[...].astype(BF16).astype(F32)
    keys = k_ref[...].astype(BF16).astype(F32)
    values = v_ref[...].astype(BF16).astype(F32)
    key_step = pltpu.roll(keys, 1, 0) * cont - keys
    value_step = pltpu.roll(values, 1, 0) * cont - values
    shifted = keys + key_mix * key_step
    value_low = (values + value_mix * value_step).astype(BF16)
    query_factor = lax.rsqrt(head_mean(queries * queries, head_size) + EPSILON)
    key_factor = lax.rsqrt(head_mean(shifted * shifted, head_size) + EPSILON)
    return (
        queries * query_factor,
        shifted * key_factor,
        value_low,
        query_factor,
        key_factor,
        key_mix,
        value_mix,
        key_step,
        value_step,
    )


def small_columns(small_ref, bias_ref):
    return (small_ref[...] + bias_ref[0:1, :]).astype(BF16)


def decay_of(small_low, cont):
    return running_sum(log_sigmoid(small_low.astype(F32)) - SEPARATE * (1.0 - cont), False)


def forward_pair(
    pair, heads, head_size, block, q_ref, k_ref, v_ref, gate_ref, small_low, cont, decay_all,
    mixed_ref, att_ref, log_ref,
):
    query, key, value_low, *unused = prologue(
        pair, heads, head_size, q_ref, k_ref, v_ref, small_low, cont
    )
    rows = query.shape[0]
    query = query.astype(BF16) * BF16(head_size**-0.5)
    key = key.astype(BF16)
    decay = exact_dot(decay_all, spread(2 * pair, head_size).astype(F32))
    decay_rows = decay.T
    lane = iota((1, LANES), 1)
    ones = jnp.ones((rows, LANES), BF16)
    value_wide = jnp.concatenate([value_low, ones], axis=1)
    for i in range(rows // block):
        lo, hi = i * block, (i + 1) * block
        row_index = iota((block, hi), 0) + lo
        visible = iota((block, hi), 1) <= row_index
        outs, sums = [], []
        for head in range(2):
            mine = (lane >= head_size) if head else (lane < head_size)
            at = head * head_size
            left = jnp.where(mine, query[lo:hi], BF16(0.0))
            scores = dot_f32(left, key[:hi], ((1,), (1,)))
            scores = scores + decay[lo:hi, at : at + 1] - decay_rows[at : at + 1, :hi]
            weights = jnp.where(visible, jnp.exp(scores), 0.0).astype(BF16)
            both = dot_f32(weights, value_wide[:hi])
            outs.append(both[:, :LANES])
            sums.append(both[:, LANES:])
        first = lane < head_size
        total = jnp.where(first, sums[0], sums[1])
        attended = (jnp.where(first, outs[0], outs[1]) / total).astype(BF16)
        att_ref[lo:hi, :] = attended
        log_ref[lo:hi, :] = jnp.log(total)
        opened = jax.nn.sigmoid(gate_ref[lo:hi, :])
        mixed_ref[lo:hi, :] = (attended.astype(F32) * opened).astype(BF16)


def forward_kernel(
    heads, head_size, block, q_ref, k_ref, v_ref, gate_ref, small_ref, bias_ref, cont_ref,
    mixed_ref, att_ref, log_ref, decay_scr,
):
    pair = pl.program_id(0)
    cont = cont_ref[...]
    small_low = small_columns(small_ref, bias_ref)

    @pl.when(pair == 0)
    def _():
        decay_scr[...] = decay_of(small_low, cont)

    forward_pair(
        pair, heads, head_size, block, q_ref, k_ref, v_ref, gate_ref, small_low, cont,
        decay_scr[...], mixed_ref, att_ref, log_ref,
    )


def share_of(ref, like, n):
    size = like.shape[1]
    if ref.shape[1] == size:
        return ref
    return ref.at[:, pl.ds(pl.multiple_of(n * size, size), size)]


def backward_kernel(
    heads, head_size, block, wide, *refs
):
    q_ref, k_ref, v_ref, gate_ref, small_ref, bias_ref, cont_ref, att_ref, log_ref, grad_ref = refs[:10]
    in_ref, normed_ref, up_src, down_src, up_one, down_one, part_ref, branch_ref = refs[10:18]
    out_ref, bias_grad_ref, norm_ref, in_part_ref, grad_out = refs[18:23]
    up_two_got, down_two_got, up_one_got, down_one_got, branch_got = refs[23:28]
    decay_scr, small_scr, dq_scr, part_core, part_own, part_far, part_sum, part_got = refs[28:36]
    send, recv, local = refs[36:]
    pair = pl.program_id(0)
    pairs = heads * head_size // LANES
    half = wide // 2
    row_steps = out_ref.shape[0] // norm_ref.shape[0]
    w, z = lax.axis_index("wide"), lax.axis_index("narrow")
    sender = Sender(send, recv)
    one, two = flipped(z, 1), flipped(z, 2)
    copies = [
        sender.plan(up_src, up_two_got, narrow_device(two)),
        sender.plan(down_src, down_two_got, narrow_device(two)),
        sender.plan(share_of(up_one, up_src, one), up_one_got, narrow_device(one)),
        sender.plan(share_of(down_one, down_src, one), down_one_got, narrow_device(one)),
    ]
    core = [
        sender.plan(part_ref.at[flipped(w, 2 * n + 1)], part_core.at[n], wide_device(flipped(w, 1)))
        for n in range(half)
    ]
    far = [
        sender.plan(part_own.at[n], part_far.at[n - 1], wide_device(flipped(w, 2 * n)))
        for n in range(1, half)
    ]
    branches = [
        sender.plan(branch_ref.at[k // 2], branch_got.at[n], wide_device(flipped(w, k)))
        for n, k in enumerate(diagonal_steps(wide))
    ]
    own = [
        pltpu.make_async_copy(part_ref.at[flipped(w, 2 * n)], part_own.at[n], local.at[n])
        for n in range(half)
    ]
    own_width = heads * head_size

    def part_columns(n):
        return part_sum.at[:, pl.ds(pl.multiple_of(n * own_width, LANES), own_width)]

    outs = [
        sender.plan(part_columns(flipped(z, k)), part_got.at[k - 1], narrow_device(flipped(z, k)))
        for k in (1, 2, 3)
    ]

    @pl.when(pair == 0)
    def _():
        greet(
            [narrow_device(flipped(z, k)) for k in (1, 2, 3)]
            + [wide_device(flipped(w, k)) for k in wide_steps(wide)]
        )
        for copy in copies + core + own:
            copy.start()

    @pl.when(pair == 1)
    def _():
        for n in range(half):
            core[n].wait_recv()
            own[n].wait()
            part_own[n] = (part_own[n].astype(F32) + part_core[n].astype(F32)).astype(BF16)
            if n > 0:
                far[n - 1].start()

    @pl.when(pair < pairs)
    def _():
        backward_pair(
            pair, pairs, heads, head_size, block, q_ref, k_ref, v_ref, gate_ref, small_ref,
            bias_ref, cont_ref, att_ref, log_ref, grad_ref, out_ref, bias_grad_ref, decay_scr,
            small_scr, dq_scr,
        )

    @pl.when((pair >= pairs) & (pair < pairs + row_steps))
    def _():
        size = norm_ref.shape[0]
        at = pl.ds(pl.multiple_of((pair - pairs) * size, size), size)
        norm_ref[...] = dot_f32(out_ref[at, :], in_ref[...], ((1,), (1,))).astype(BF16)

    @pl.when(pair == pairs + row_steps)
    def _():
        total = part_own[0].astype(F32)
        for n in range(1, half):
            far[n - 1].wait_recv()
            total = total + part_far[n - 1].astype(F32)
        part_sum[...] = total.astype(BF16)
        for copy in outs + branches:
            copy.start()

    @pl.when(pair >= pairs + row_steps)
    def _():
        in_part_ref[...] = dot_f32(normed_ref[...], out_ref[...], ((0,), (0,))).astype(BF16)

    @pl.when(pair == pl.num_programs(0) - 1)
    def _():
        for copy in outs + copies + branches:
            copy.wait()
        total = part_columns(z)[...].astype(F32)
        for n in range(3):
            total = total + part_got[n].astype(F32)
        grad_out[...] = total
        for copy in core + far:
            copy.wait_send()


def backward_pair(
    pair, pairs, heads, head_size, block, q_ref, k_ref, v_ref, gate_ref, small_ref, bias_ref, cont_ref,
    att_ref, log_ref, grad_ref, out_ref, bias_grad_ref, decay_scr, small_scr, dq_scr,
):
    cont = cont_ref[...]
    small_low = small_columns(small_ref, bias_ref)
    rows = cont.shape[0]
    width = heads * head_size

    @pl.when(pair == 0)
    def _():
        decay_scr[...] = decay_of(small_low, cont)
        small_scr[...] = jnp.zeros_like(small_scr)

    (
        query_norm, key_norm, value_low, query_factor, key_factor, key_mix, value_mix, key_step,
        value_step,
    ) = prologue(pair, heads, head_size, q_ref, k_ref, v_ref, small_low, cont)
    query = query_norm.astype(BF16) * BF16(head_size**-0.5)
    key = key_norm.astype(BF16)
    opened = jax.nn.sigmoid(gate_ref[...])
    attended = att_ref[...].astype(F32)
    grad_mixed = grad_ref[...].astype(F32)
    grad_low = (grad_mixed * opened).astype(BF16)
    grad_gate = grad_mixed * attended * opened * (1.0 - opened)

    def columns(group):
        at = group * width + pair * LANES
        return pl.ds(pl.multiple_of(at, LANES), LANES)

    out_ref[:, columns(3)] = grad_gate.astype(BF16)
    inner = exact_dot(grad_low.astype(F32) * attended, same_head(head_size))
    decay = exact_dot(decay_scr[...], spread(2 * pair, head_size).astype(F32))
    level_rows = (decay - log_ref[...]).T
    inner_rows = inner.T
    lane = iota((1, LANES), 1)
    ones = jnp.ones((rows, LANES), BF16)
    query_wide = jnp.concatenate([query, ones], axis=1)
    key_wide = jnp.concatenate([key, ones], axis=1)
    key_parts, value_parts, query_parts = [], [], []
    for head in range(2):
        mine = (lane >= head_size) if head else (lane < head_size)
        at = head * head_size
        keys_out, values_out = [], []
        for j in range(rows // block):
            lo, hi = j * block, (j + 1) * block
            span = rows - lo
            visible = iota((block, span), 0) <= iota((block, span), 1)
            scores = dot_f32(
                jnp.where(mine, key[lo:hi], BF16(0.0)), query[lo:], ((1,), (1,))
            )
            scores = scores + level_rows[at : at + 1, lo:] - decay[lo:hi, at : at + 1]
            probs = jnp.where(visible, jnp.exp(scores), 0.0)
            grad_probs = dot_f32(
                jnp.where(mine, value_low[lo:hi], BF16(0.0)), grad_low[lo:], ((1,), (1,))
            )
            grad_scores = (probs * (grad_probs - inner_rows[at : at + 1, lo:])).astype(BF16)
            values_out.append(dot_f32(probs.astype(BF16), grad_low[lo:]))
            keys_out.append(dot_f32(grad_scores, query_wide[lo:]))
            part = dot_f32(grad_scores, key_wide[lo:hi], ((0,), (0,)))
            if j == 0:
                dq_scr[...] = part
            else:
                dq_scr[lo:, :] += part
        key_parts.append(jnp.concatenate(keys_out, axis=0))
        value_parts.append(jnp.concatenate(values_out, axis=0))
        query_parts.append(dq_scr[...])
    first = lane < head_size

    def join(parts):
        return jnp.where(first, parts[0], parts[1])

    grad_query = join([p[:, :LANES] for p in query_parts]) * head_size**-0.5
    grad_key = join([p[:, :LANES] for p in key_parts])
    grad_value = join(value_parts)
    grad_decay = join([p[:, LANES:] for p in query_parts]) - join([p[:, LANES:] for p in key_parts])

    def norm_back(grad, normed, factor):
        return factor * (grad - normed * head_mean(grad * normed, head_size))

    def shift_back(grad, mix):
        return grad * (1.0 - mix) + pltpu.roll(grad * mix * cont, rows - 1, 0)

    grad_query = norm_back(grad_query, query_norm, query_factor)
    grad_shifted = norm_back(grad_key, key_norm, key_factor)
    out_ref[:, columns(0)] = grad_query.astype(BF16)
    out_ref[:, columns(1)] = shift_back(grad_shifted, key_mix).astype(BF16)
    out_ref[:, columns(2)] = shift_back(grad_value, value_mix).astype(BF16)
    key_logit = grad_shifted * key_step * key_mix * (1.0 - key_mix)
    value_logit = grad_value * value_step * value_mix * (1.0 - value_mix)
    single = (lax.rem(lane, head_size) == 0).astype(F32)
    small_scr[...] += (
        exact_dot(grad_decay * single, collect(2 * pair, head_size).astype(F32))
        + exact_dot(key_logit, collect(heads + 2 * pair, head_size).astype(F32))
        + exact_dot(value_logit, collect(2 * heads + 2 * pair, head_size).astype(F32))
    )

    @pl.when(pair == pairs - 1)
    def _():
        grads = small_scr[...]
        forget = running_sum(grads, True) * jax.nn.sigmoid(-small_low.astype(F32))
        result = jnp.where(lane < heads, forget, grads)
        out_ref[:, 4 * width :] = result.astype(BF16)
        bias_grad_ref[...] = jnp.broadcast_to(
            jnp.sum(result, axis=0, keepdims=True), bias_grad_ref.shape
        )


def attention_specs(rows, pairs):
    def block_at(group):
        return pl.BlockSpec((rows, LANES), lambda p: (0, group * pairs + jnp.minimum(p, pairs - 1)))

    def fixed(height, column=0):
        return pl.BlockSpec((height, LANES), lambda p: (0, column))

    base = [block_at(0), block_at(1), block_at(2), block_at(3), fixed(rows, 4 * pairs), fixed(8), fixed(rows)]
    return base, pl.BlockSpec((rows, LANES), lambda p: (0, jnp.minimum(p, pairs - 1)))


def attention_forward(projected, bias, cont, heads, head_size, block):
    rows = projected.shape[0]
    pairs = heads * head_size // LANES
    base, own = attention_specs(rows, pairs)
    wide = jax.ShapeDtypeStruct((rows, heads * head_size), BF16)
    return pl.pallas_call(
        functools.partial(forward_kernel, heads, head_size, block),
        grid=(pairs,),
        in_specs=base,
        out_specs=[own] * 3,
        out_shape=[wide, wide, jax.ShapeDtypeStruct(wide.shape, F32)],
        scratch_shapes=[pltpu.VMEM((rows, LANES), F32)],
        compiler_params=pltpu.CompilerParams(vmem_limit_bytes=48 * 2**20),
    )(*([projected] * 5), bias, cont)


def attention_backward(
    projected, bias, cont, attended, logs, grad, in_full, normed_one, shares, out_part, branches, heads,
    head_size, block, collective_id,
):
    rows = projected.shape[0]
    width = normed_one.shape[1]
    wide, wide_rows = out_part.shape[:2]
    half = wide // 2
    pairs = heads * head_size // LANES
    base, own = attention_specs(rows, pairs)
    columns = 4 * heads * head_size + LANES
    step = min(256, rows)
    row_steps, in_steps = rows // step, width // 256
    steps = 8 + 3 * wide
    part = lambda count: pltpu.VMEM((count, wide_rows, width), BF16)
    shape = jax.ShapeDtypeStruct

    def later(first, count):
        return lambda p: jnp.clip(p - first, 0, count - 1)

    row_at, in_at = later(pairs, row_steps), later(pairs + row_steps, in_steps)
    return pl.pallas_call(
        functools.partial(backward_kernel, heads, head_size, block, wide),
        grid=(pairs + row_steps + in_steps,),
        in_specs=base
        + [own] * 3
        + [
            pl.BlockSpec(in_full.shape, lambda p: (0, 0), pipeline_mode=pl.Buffered(1)),
            pl.BlockSpec((rows, 256), lambda p: (0, in_at(p))),
        ]
        + [ANY] * 6,
        out_specs=[
            pl.BlockSpec((rows, columns), lambda p: (0, 0)),
            pl.BlockSpec((8, LANES), lambda p: (0, 0)),
            pl.BlockSpec((step, width), lambda p: (row_at(p), 0)),
            pl.BlockSpec((256, columns), lambda p: (in_at(p), 0)),
            pl.BlockSpec((wide_rows, heads * head_size), lambda p: (0, 0)),
        ]
        + [ANY] * 5,
        out_shape=[
            shape((rows, columns), BF16), shape((8, LANES), F32), shape((rows, width), BF16),
            shape((width, columns), BF16), shape((wide_rows, heads * head_size), F32),
            *[shape(share.shape, BF16) for share in shares[:2] * 2],
            shape((len(diagonal_steps(wide)),) + branches.shape[1:], BF16),
        ],
        scratch_shapes=[
            pltpu.VMEM((rows, LANES), F32), pltpu.VMEM((rows, LANES), F32),
            pltpu.VMEM((rows, 2 * LANES), F32), part(half), part(half), part(half - 1),
            pltpu.VMEM((wide_rows, width), BF16),
            pltpu.VMEM((3, wide_rows, heads * head_size), BF16),
            DMA((steps,)), DMA((steps,)), DMA((half,)),
        ],
        compiler_params=pltpu.CompilerParams(
            collective_id=collective_id, has_side_effects=True, vmem_limit_bytes=60 * 2**20
        ),
    )(
        *([projected] * 5), bias, cont, attended, logs, grad, in_full, normed_one, *shares, out_part,
        branches,
    )


def first_kernel(
    wide, heads, head_size, block, x_ref, in_ref, small_ref, out_ref, up_ref, grad_ref, down_ref, gain_one_ref,
    gain_two_ref, bias_ref, cont_ref, normed_out, in_out, out_out, proj_out, att_ref, log_ref,
    mixed_rows, middle_ref, normed_two_ref, up_out, up_two, up_one, down_got, grad_got, slot, in_buf,
    out_buf, up_buf, normed, proj, mixed, decay_scr, send, recv, local,
):
    w, z = lax.axis_index("wide"), lax.axis_index("narrow")
    line = [flipped(z, k) for k in range(4)]
    rows, width = x_ref.shape
    own_width = heads * head_size
    part_rows = out_ref.shape[0]
    is_middle = (z == 1) | (z == 2)
    is_end = (z == 0) | (z == 3)
    sender = Sender(send, recv)
    used = []

    def local_copy(src, dst):
        copy = pltpu.make_async_copy(src, dst, local.at[len(used)])
        used.append(copy)
        return copy

    def slot_rows(n):
        return slot.at[pl.ds(pl.multiple_of(n * rows, rows), rows), :]

    def weight_rows(ref, w_of, z_of):
        at = (w_of * 4 + z_of) * part_rows
        return ref.at[pl.ds(pl.multiple_of(at, 16), part_rows), :]

    def wide_rows(ref, w_of):
        at = w_of * 4 * part_rows
        return ref.at[pl.ds(pl.multiple_of(at, 16), 4 * part_rows), :]

    def by_rows(ref):
        return (
            (lambda k: wide_rows(ref, flipped(w, k))),
            (lambda k, to: wide_rows(ref, flipped(w, k))),
        )

    unit = up_buf.shape[2] // 4

    def in_pieces(n):
        target = lambda at, size: in_buf.at[
            pl.ds(pl.multiple_of((w * 4 + z) * part_rows, 16), part_rows), pl.ds(at, size)
        ]
        for group in range(4):
            at = pl.multiple_of(group * width + n * own_width, LANES)
            yield in_ref.at[:, pl.ds(at, own_width)], target(group * own_width, own_width)
        yield small_ref.at[n], target(4 * own_width, LANES)

    def up_pieces(n):
        for group in range(4):
            at = pl.multiple_of((group * wide + n) * unit, LANES)
            yield up_ref.at[:, pl.ds(at, unit)], up_buf.at[w, :, pl.ds(group * unit, unit)]

    own_in = [local_copy(*piece) for piece in in_pieces(z)]
    own_up = [local_copy(*piece) for piece in up_pieces(w)]
    own_out = local_copy(out_ref, weight_rows(out_buf, w, z))
    own_x = local_copy(x_ref, slot_rows(z))
    for copy in used:
        copy.start()

    index = w * 4 + z
    down_wide = lax.div(lax.rem(index, 2 * wide), 2)
    down_narrow = lax.rem(index, 2) + 2 * lax.div(index, 2 * wide)
    from_index = 2 * wide * lax.div(z, 2) + 2 * w + lax.rem(z, 2)
    from_wide_index, from_narrow_index = lax.div(from_index, 4), lax.rem(from_index, 4)
    moves = jnp.logical_not((down_wide == w) & (down_narrow == z))
    down_push = sender.plan(
        down_ref, down_got, {"wide": down_wide, "narrow": down_narrow}
    )
    down_stay = local_copy(down_ref, down_got)

    barrier = pltpu.get_barrier_semaphore()
    partners = [narrow_device(line[k]) for k in (1, 2, 3)]
    partners += [wide_device(flipped(w, k)) for k in range(1, wide)]
    for device in partners:
        pl.semaphore_signal(barrier, inc=1, device_id=device, device_id_type=MESH)

    @pl.when(moves)
    def _():
        for device in (
            {"wide": from_wide_index, "narrow": from_narrow_index},
            {"wide": down_wide, "narrow": down_narrow},
        ):
            pl.semaphore_signal(barrier, inc=1, device_id=device, device_id_type=MESH)
        pl.semaphore_wait(barrier, len(partners) + 2)

    @pl.when(jnp.logical_not(moves))
    def _():
        pl.semaphore_wait(barrier, len(partners))

    ins = [
        sender.plan(*piece, narrow_device(line[k])) for k in (2, 3, 1) for piece in in_pieces(line[k])
    ]
    outs = [
        sender.plan(out_ref, weight_rows(out_buf, w, z), narrow_device(line[k])) for k in (2, 3, 1)
    ]
    ups = [
        sender.plan(*piece, wide_device(flipped(w, k)))
        for k in range(1, wide)
        for piece in up_pieces(flipped(w, k))
    ]
    grads = {
        k: sender.plan(grad_ref, grad_got.at[k // 2 - 1], wide_device(flipped(w, k)))
        for k in range(2, wide, 2)
    }
    two = sender.plan(x_ref, slot_rows(z), narrow_device(line[2]))
    one = sender.plan(x_ref, slot_rows(z), narrow_device(line[1]))
    middle = sender.plan(x_ref, slot_rows(z), narrow_device(line[3]))
    relay = sender.plan(slot_rows(line[2]), slot_rows(line[2]), narrow_device(line[1]))
    in_wide = WideGather(sender, w, wide, *by_rows(in_buf))
    out_wide = WideGather(sender, w, wide, *by_rows(out_buf))
    up_steps = [
        sender.plan(up_buf, up_two, narrow_device(line[2])),
        sender.plan(up_buf, up_one, narrow_device(line[1])),
    ]
    mixes = [
        sender.plan(
            mixed.at[pl.ds(pl.multiple_of(line[k] * rows, rows), rows), :],
            mixed_rows.at[:, pl.ds(pl.multiple_of(z * own_width, LANES), own_width)],
            narrow_device(line[k]),
        )
        for k in (2, 3, 1)
    ]

    for copy in ins + outs + ups:
        copy.start()
    for copy in own_in:
        copy.wait()
    for copy in ins:
        copy.wait_recv()
    in_wide.start()
    two.start()
    one.start()
    own_out.wait()
    for copy in outs:
        copy.wait_recv()
    out_wide.start()
    in_wide.pass_on()
    for k in diagonal_steps(wide):
        grads[k].start()
    two.wait_recv()

    @pl.when(is_middle)
    def _():
        relay.start()
        middle.start()

    for copy in own_up:
        copy.wait()
    for copy in ups:
        copy.wait_recv()
    up_back = local_copy(up_buf, up_out)
    up_back.start()
    in_wide.received()
    in_back = local_copy(in_buf, in_out)
    in_back.start()
    own_x.wait()

    def project(t, carry):
        @pl.when(t == 2)
        def _():
            one.wait_recv()

        @pl.when(t == 3)
        def _():
            out_wide.pass_on()

        @pl.when((t == 3) & is_middle)
        def _():
            middle.wait_recv()

        @pl.when((t == 3) & is_end)
        def _():
            relay.wait_recv()

        @pl.when(t == 3)
        def _():
            for copy in up_steps:
                copy.start()
            for k in straight_steps(wide):
                grads[k].start()

        @pl.when((t == 3) & moves)
        def _():
            down_push.start()

        @pl.when((t == 3) & jnp.logical_not(moves))
        def _():
            down_stay.start()

        n = jnp.where(t == 0, z, jnp.where(t == 1, line[2], jnp.where(t == 2, line[1], line[3])))
        at = pl.ds(pl.multiple_of(n * rows, rows), rows)
        values = slot[at, :].astype(F32)
        low = (values * rms_factor(values) * gain_one_ref[0:1, :]).astype(BF16)
        normed[at, :] = low
        proj[at, :] = dot_f32(low, in_buf[...])
        return carry

    lax.fori_loop(0, 4, project, 0)
    normed_back = local_copy(normed, normed_out)
    proj_back = local_copy(proj, proj_out)
    normed_back.start()
    proj_back.start()

    cont = cont_ref[...]
    groups = own_width // LANES
    small_low = small_columns(proj.at[:, pl.ds(4 * own_width, LANES)], bias_ref)
    decay_scr[...] = decay_of(small_low, cont)

    def attend(pair, carry):
        def at(group):
            return pl.ds(pl.multiple_of((group * groups + pair) * LANES, LANES), LANES)

        forward_pair(
            pair, heads, head_size, block, proj.at[:, at(0)], proj.at[:, at(1)], proj.at[:, at(2)],
            proj.at[:, at(3)], small_low, cont, decay_scr[...], mixed.at[:, at(0)],
            att_ref.at[:, at(0)], log_ref.at[:, at(0)],
        )
        return carry

    lax.fori_loop(0, groups, attend, 0)
    for copy in mixes:
        copy.start()
    mixed_rows[:, pl.ds(pl.multiple_of(z * own_width, LANES), own_width)] = mixed[
        pl.ds(pl.multiple_of(z * rows, rows), rows), :
    ]
    out_wide.received()
    out_back = local_copy(out_buf, out_out)
    out_back.start()
    for copy in mixes:
        copy.wait_recv()
    inputs = slot[pl.ds(pl.multiple_of(z * rows, rows), rows), :].astype(F32)
    values = inputs + dot_f32(mixed_rows[...], out_buf[...])
    middle_ref[...] = values
    normed_two_ref[...] = (values * rms_factor(values) * gain_two_ref[0:1, :]).astype(BF16)

    for copy in up_steps:
        copy.wait()
    for copy in grads.values():
        copy.wait()

    @pl.when(moves)
    def _():
        down_push.wait()

    @pl.when(jnp.logical_not(moves))
    def _():
        down_stay.wait()

    @pl.when(is_middle)
    def _():
        relay.wait_send()
        middle.wait_send()

    for copy in ins + outs + ups + [two, one] + mixes:
        copy.wait_send()
    in_wide.sent()
    out_wide.sent()
    for copy in (up_back, in_back, normed_back, proj_back, out_back):
        copy.wait()


def first_part(
    tokens, in_weight, small, out_weight, gate_up_weight, cotangent, down_weight, gain_one, gain_two, bias,
    cont, wide, heads, head_size, block, collective_id,
):
    rows, width = tokens.shape
    slot, own_width = 4 * rows, heads * head_size
    columns = 4 * own_width + LANES
    steps = 8 * wide + 40
    up_shape = (wide, gate_up_weight.shape[0], gate_up_weight.shape[1] // wide)
    shape = jax.ShapeDtypeStruct
    return pl.pallas_call(
        functools.partial(first_kernel, wide, heads, head_size, block),
        out_shape=[
            shape((slot, width), BF16), shape((width, columns), BF16), shape((width, width), BF16),
            shape((slot, columns), F32), shape((slot, own_width), BF16),
            shape((slot, own_width), F32), shape((rows, width), BF16), shape((rows, width), F32),
            shape((rows, width), BF16), shape(up_shape, BF16), shape(up_shape, BF16),
            shape(up_shape, BF16), shape(down_weight.shape, BF16),
            shape((wide // 2 - 1, rows, width), BF16),
        ],
        in_specs=[ANY] * 7 + [VMEM] * 4,
        out_specs=[ANY] * 4 + [VMEM] * 5 + [ANY] * 5,
        scratch_shapes=[
            pltpu.VMEM((slot, width), BF16), pltpu.VMEM((width, columns), BF16),
            pltpu.VMEM((width, width), BF16), pltpu.VMEM(up_shape, BF16),
            pltpu.VMEM((slot, width), BF16), pltpu.VMEM((slot, columns), F32),
            pltpu.VMEM((slot, own_width), BF16), pltpu.VMEM((slot, LANES), F32),
            DMA((steps,)), DMA((steps,)), DMA((20,)),
        ],
        compiler_params=pltpu.CompilerParams(
            collective_id=collective_id, has_side_effects=True, vmem_limit_bytes=60 * 2**20
        ),
    )(
        tokens, in_weight, small, out_weight, gate_up_weight, cotangent, down_weight, jnp.broadcast_to(gain_one[None], (8, width)),
        jnp.broadcast_to(gain_two[None], (8, width)), bias, cont,
    )


def second_kernel(
    wide, src_ref, grad_ref, far_grads, up_ref, up_two, up_one, down_ref, middle_ref, mixed_ref, out_ref,
    gain_ref, grad_middle, gain_grad, slot_grad, branch_sum, up_src, down_src, up_acc, down_acc,
    up_grad_out, down_grad_out, out_part, branch_near, normed, grads, up_full, down_full, hidden, mid,
    rows_buf, core_buf, far_buf, branch_buf, up_join, up_mid, down_join, down_mid, up_grad, down_grad,
    grad_mixed, mixed_buf, send, recv, local,
):
    w, z = lax.axis_index("wide"), lax.axis_index("narrow")
    line = [flipped(z, k) for k in range(4)]
    rows, width = src_ref.shape
    half = wide // 2
    size = hidden.shape[1]
    unit, part = up_src.shape[1], down_src.shape[1]
    is_middle = (z == 1) | (z == 2)
    is_end = (z == 0) | (z == 3)
    sender = Sender(send, recv)
    sibling = wide_device(flipped(w, 1))

    def at_place(ref, place):
        return ref.at[pl.ds(pl.multiple_of(place * rows, rows), rows), :]

    up_at = lambda n: up_full.at[:, n]
    down_at = lambda n: down_full.at[n]
    moves = [
        (src_ref, at_place(normed, 0)), (up_ref, up_at(z)), (up_two, up_at(line[2])),
        (up_one, up_at(line[1])), (down_ref, down_at(z)), (grad_ref, at_place(grads, 0)),
    ] + [(far_grads.at[n - 1], at_place(grads, n)) for n in range(1, half)]
    own = [pltpu.make_async_copy(src, dst, local.at[n]) for n, (src, dst) in enumerate(moves)]
    for copy in own:
        copy.start()
    greet(
        [wide_device(flipped(w, k)) for k in wide_steps(wide)]
        + [narrow_device(line[k]) for k in (1, 2, 3)]
    )
    gather = WideGather(
        sender, w, wide, lambda k: src_ref if k == 0 else at_place(normed, place_of(k, wide)),
        lambda k, to: at_place(normed, place_of(k ^ to, wide)),
    )
    middle = sender.plan(up_ref, up_at(z), narrow_device(line[3]))
    relay = sender.plan(up_two, up_at(line[2]), narrow_device(line[1]))
    down_two = sender.plan(down_ref, down_at(z), narrow_device(line[2]))
    down_one = sender.plan(down_ref, down_at(z), narrow_device(line[1]))
    down_middle = sender.plan(down_ref, down_at(z), narrow_device(line[3]))
    down_relay = sender.plan(down_at(line[2]), down_at(line[2]), narrow_device(line[1]))
    passed = [
        sender.plan(
            grad_ref if n == 0 else far_grads.at[n - 1], at_place(grads, half + n), sibling
        )
        for n in range(half)
    ]
    core = [
        sender.plan(at_place(rows_buf, half + n), core_buf.at[n], sibling) for n in range(half)
    ]
    far = [
        sender.plan(at_place(rows_buf, n), far_buf.at[n - 1], wide_device(flipped(w, 2 * n)))
        for n in range(1, half)
    ]
    branch_core = [
        sender.plan(at_place(normed, half + n), branch_buf.at[n], sibling) for n in range(half)
    ]

    def up_share(n):
        return up_grad.at[:, pl.ds(pl.multiple_of(n * unit, unit), unit)]

    def down_share(n):
        return down_grad.at[:, pl.ds(pl.multiple_of(n * part, part), part)]

    down_joined = sender.plan(down_share(line[3]), down_join, narrow_device(line[1]))
    down_direct = sender.plan(down_share(line[3]), down_mid, narrow_device(line[3]))
    up_joined = sender.plan(up_share(line[3]), up_join, narrow_device(line[1]))
    up_direct = sender.plan(up_share(line[3]), up_mid, narrow_device(line[3]))
    own_width = width // 4
    mixes = [
        sender.plan(
            grad_mixed.at[:, pl.ds(pl.multiple_of(line[k] * own_width, LANES), own_width)],
            slot_grad.at[pl.ds(pl.multiple_of(z * rows, rows), rows), :], narrow_device(line[k]),
        )
        for k in (2, 3, 1)
    ]
    near = [
        sender.plan(branch_sum.at[k // 2], branch_near.at[n], wide_device(flipped(w, k)))
        for n, k in enumerate(straight_steps(wide))
    ]

    gather.start()

    @pl.when(is_middle)
    def _():
        relay.start()
        middle.start()

    down_two.start()
    down_two.wait_recv()

    @pl.when(is_middle)
    def _():
        down_relay.start()
        down_middle.start()

    down_one.start()
    for copy in passed:
        copy.start()
    for copy in own[:4]:
        copy.wait()

    @pl.when(is_middle)
    def _():
        middle.wait_recv()

    @pl.when(is_end)
    def _():
        relay.wait_recv()

    up_shape = (width, 4 * unit)
    down_shape = (size, width)

    def arriving(t, carry):
        @pl.when(t == 1)
        def _():
            gather.first[1].wait_recv()

        for n, k in enumerate(gather.far):

            @pl.when(t == 2 + n)
            def _():
                gather.first[k].wait_recv()
                gather.second[k].start()

            @pl.when(t == half + 1 + n)
            def _():
                gather.second[k].wait_recv()

        place = jnp.where(t < 2, t * half, jnp.where(t < half + 1, t - 1, t))
        at = pl.ds(pl.multiple_of(place * rows, rows), rows)
        mid[at, :] = dot_f32(normed[at, :], up_full[...].reshape(up_shape)).astype(BF16)
        return carry

    lax.fori_loop(0, wide, arriving, 0)
    for copy in own[4:]:
        copy.wait()
    for copy in passed + [down_one]:
        copy.wait_recv()

    @pl.when(is_middle)
    def _():
        down_middle.wait_recv()

    @pl.when(is_end)
    def _():
        down_relay.wait_recv()

    def block(t, carry):
        pick = half - 1 - lax.div(t, 2)
        place = jnp.where(lax.rem(t, 2) == 0, half + pick, pick)
        at = pl.ds(pl.multiple_of(place * rows, rows), rows)
        gate_up = mid[at, :].astype(F32)
        grad_hidden = dot_f32(grads[at, :], down_full[...].reshape(down_shape), ((1,), (1,)))
        gate, up = gate_up[:, :size], gate_up[:, size:]
        opened = jax.nn.sigmoid(gate)
        acted = gate * opened
        hidden[at, :] = (acted * up).astype(BF16)
        mid[at, :size] = (grad_hidden * up * (opened * (1.0 + gate * (1.0 - opened)))).astype(BF16)
        mid[at, size:] = (grad_hidden * acted).astype(BF16)
        rows_buf[at, :] = dot_f32(mid[at, :], up_full[...].reshape(up_shape), ((1,), (1,))).astype(
            BF16
        )
        for n in range(half):

            @pl.when(t == 2 * (half - 1 - n))
            def _():
                core[n].start()

        for n in range(half):

            @pl.when(t == 2 * (half - 1 - n) + 1)
            def _():
                core[n].wait_recv()
                total = rows_buf[n * rows : (n + 1) * rows, :].astype(F32) + core_buf[n].astype(F32)
                rows_buf[n * rows : (n + 1) * rows, :] = total.astype(BF16)
                if n > 0:
                    far[n - 1].start()

        return carry

    lax.fori_loop(0, wide, block, 0)

    step = min(256, size)
    for n in range(size // step):
        cut = slice(n * step, (n + 1) * step)
        down_grad[cut, :] = dot_f32(hidden[:, cut], grads[...], ((0,), (0,))).astype(BF16)

    @pl.when(is_end)
    def _():
        down_joined.start()

    @pl.when(is_middle)
    def _():
        down_direct.start()

    reloads = [
        pltpu.make_async_copy(out_ref, grads.at[pl.ds(0, width), :], local.at[9 + half]),
        pltpu.make_async_copy(grad_ref, grads.at[pl.ds(width, rows), :], local.at[10 + half]),
        pltpu.make_async_copy(mixed_ref, mixed_buf, local.at[11 + half]),
        pltpu.make_async_copy(middle_ref, grad_middle, local.at[12 + half]),
    ]
    for copy in reloads:
        copy.start()

    def up_rows(n, carry):
        at = pl.ds(pl.multiple_of(n * 256, 256), 256)
        up_grad[at, :] = dot_f32(normed[:, at], mid[...], ((0,), (0,))).astype(BF16)
        return carry

    lax.fori_loop(0, width // 256, up_rows, 0)

    @pl.when(is_end)
    def _():
        up_joined.start()

    @pl.when(is_middle)
    def _():
        up_direct.start()

    backs = [
        pltpu.make_async_copy(up_grad, up_grad_out, local.at[5 + half]),
        pltpu.make_async_copy(down_grad, down_grad_out, local.at[6 + half]),
        pltpu.make_async_copy(up_share(line[2]), up_src, local.at[7 + half]),
        pltpu.make_async_copy(down_share(line[2]), down_src, local.at[8 + half]),
    ]
    for copy in backs:
        copy.start()
    gather.sent()

    def branch(t, carry):
        place = lax.rem(t + half, wide)
        at = pl.ds(pl.multiple_of(place * rows, rows), rows)
        normed[at, :] = dot_f32(hidden[at, :], down_full[...].reshape(down_shape)).astype(BF16)
        for n in range(half):

            @pl.when(t == n)
            def _():
                branch_core[n].start()

        return carry

    lax.fori_loop(0, wide, branch, 0)
    for n in range(half):
        branch_core[n].wait_recv()
        total = normed[n * rows : (n + 1) * rows, :].astype(F32) + branch_buf[n].astype(F32)
        branch_sum[n] = total.astype(BF16)

    total = rows_buf[:rows, :].astype(F32)
    for n in range(1, half):
        far[n - 1].wait_recv()
        total = total + far_buf[n - 1].astype(F32)
    for copy in core + far:
        copy.wait_send()
    for copy in reloads:
        copy.wait()
    values = grad_middle[...]
    factor = rms_factor(values)
    values = values * factor
    gain_grad[...] = jnp.broadcast_to(
        jnp.sum(total * values, axis=0, keepdims=True), gain_grad.shape
    )
    total = total * gain_ref[0:1, :]
    inner = jnp.mean(total * values, axis=-1, keepdims=True)
    total = grads[width : width + rows, :].astype(F32) + factor * (total - values * inner)
    grad_middle[...] = total
    branch_grad = total.astype(BF16)
    grad_mixed[...] = dot_f32(branch_grad, grads[:width, :], ((1,), (1,))).astype(BF16)
    for copy in mixes + near:
        copy.start()
    slot_grad[pl.ds(pl.multiple_of(z * rows, rows), rows), :] = grad_mixed[
        :, pl.ds(pl.multiple_of(z * own_width, LANES), own_width)
    ]
    for n in range(width // 256):
        cut = slice(n * 256, (n + 1) * 256)
        rows_buf[cut, :] = dot_f32(mixed_buf[:, cut], branch_grad, ((0,), (0,))).astype(BF16)
    out_back = pltpu.make_async_copy(
        rows_buf.at[pl.ds(0, width), :], out_part, local.at[13 + half]
    )
    out_back.start()
    for copy in backs:
        copy.wait()
    up_acc[...] = up_grad[:, pl.ds(pl.multiple_of(z * unit, unit), unit)]
    down_acc[...] = down_grad[:, pl.ds(pl.multiple_of(z * part, part), part)]

    @pl.when(is_middle)
    def _():
        down_joined.wait_recv()
        down_src[...] = (down_src[...].astype(F32) + down_join[...].astype(F32)).astype(BF16)
        up_joined.wait_recv()
        up_src[...] = (up_src[...].astype(F32) + up_join[...].astype(F32)).astype(BF16)
        down_direct.wait()
        down_acc[...] = (down_acc[...].astype(F32) + down_mid[...].astype(F32)).astype(BF16)
        up_direct.wait()
        up_acc[...] = (up_acc[...].astype(F32) + up_mid[...].astype(F32)).astype(BF16)
        for copy in (relay, middle, down_relay, down_middle):
            copy.wait_send()

    @pl.when(is_end)
    def _():
        down_joined.wait_send()
        up_joined.wait_send()

    for copy in mixes + near:
        copy.wait()
    out_back.wait()
    for copy in passed + branch_core + [down_two, down_one]:
        copy.wait_send()


def second_part(
    normed, grad, far_grads, ups, down, middle, mixed_rows, out_full, gain, collective_id
):
    rows, width = normed.shape
    half = far_grads.shape[0] + 1
    wide = 2 * half
    wide_of_up, part_rows, mid_size = ups[0].shape
    down_rows = down.shape[0]
    size, unit, part = mid_size // 2, mid_size // 4, width // 4
    steps = 9 + 2 * wide + 4 * half + 8
    total = wide * rows
    shape = jax.ShapeDtypeStruct
    vmem = lambda *dims: pltpu.VMEM(dims, BF16)
    return pl.pallas_call(
        functools.partial(second_kernel, wide),
        out_shape=[
            shape((rows, width), F32), shape((8, width), F32), shape((4 * rows, part), BF16),
            shape((half, rows, width), BF16),
            shape((width, unit), BF16), shape((size, part), BF16),
            shape((width, unit), BF16), shape((size, part), BF16),
            shape((width, mid_size), BF16), shape((size, width), BF16),
            shape((width, width), BF16), shape((len(straight_steps(wide)), rows, width), BF16),
        ],
        in_specs=[ANY] * 10 + [VMEM],
        out_specs=[VMEM] * 8 + [ANY] * 4,
        scratch_shapes=[
            vmem(total, width), vmem(total, width), vmem(wide, 4, part_rows, mid_size),
            vmem(4, down_rows, width), vmem(total, size), vmem(total, mid_size), vmem(total, width),
            vmem(half, rows, width), vmem(half - 1, rows, width), vmem(half, rows, width),
            vmem(width, unit), vmem(width, unit), vmem(size, part), vmem(size, part),
            vmem(width, mid_size), vmem(size, width), vmem(rows, width), vmem(rows, width),
            DMA((steps,)), DMA((steps,)), DMA((14 + half,)),
        ],
        compiler_params=pltpu.CompilerParams(
            collective_id=collective_id, has_side_effects=True, vmem_limit_bytes=63 * 2**20
        ),
    )(
        normed, grad, far_grads, *ups, down, middle, mixed_rows, out_full,
        jnp.broadcast_to(gain[None], (8, width)),
    )


def add_up(parts):
    total = parts[0].astype(F32)
    for part in parts[1:]:
        total = total + part.astype(F32)
    return total


def on_device(
    tokens, gain_one, in_weight, forget_bias, out_weight, gain_two, gate_up_weight, down_weight,
    segment_ids, cotangent,
):
    wide, narrow = lax.axis_size("wide"), lax.axis_size("narrow")
    w, z = lax.axis_index("wide"), lax.axis_index("narrow")
    rows, width = tokens.shape
    slot = rows * narrow
    heads = forget_bias.shape[0]
    head_size = width // heads
    own_heads = heads // narrow
    own_width = own_heads * head_size
    part_rows = in_weight.shape[0]
    hidden_all = down_weight.shape[0] * wide * narrow
    unit = hidden_all // (2 * wide)
    columns = 4 * own_width + LANES
    base = 4 * width

    small = in_weight[:, base:].reshape(part_rows, 3, narrow, own_heads)
    small = jnp.moveaxis(small, 2, 0).reshape(narrow, part_rows, 3 * own_heads)
    small = jnp.pad(small, ((0, 0), (0, 0), (0, LANES - 3 * own_heads)))
    aligned = unit % LANES == 0

    def split_weights(sources, targets):
        copies = [(sources[1], targets[0].at[:, :, pl.ds(4 * own_width, LANES)])]
        for n in range(narrow):
            for group in range(4):
                copies.append(
                    (
                        sources[0].at[:, pl.ds(group * width + n * own_width, own_width)],
                        targets[0].at[n, :, pl.ds(group * own_width, own_width)],
                    )
                )
        return copies

    shapes = [
        jax.ShapeDtypeStruct((narrow, part_rows, columns), BF16),
        jax.ShapeDtypeStruct((wide, part_rows, 4 * unit), BF16),
    ]
    copies = 4 * narrow + 1
    fused = aligned and part_rows % 16 == 0
    if not fused:
        in_parts = local_copies(split_weights, copies, [in_weight, small], shapes[:1], False)[0]
        up_parts = jnp.moveaxis(gate_up_weight.reshape(part_rows, 4, wide, unit), 2, 0)
        up_parts = up_parts.reshape(wide, part_rows, 4 * unit)

    segments = segment_ids[0]
    joined = (segments[1:] == segments[:-1]).astype(F32)
    cont = jnp.concatenate([jnp.zeros((1,), F32), joined])
    cont = jnp.broadcast_to(cont[:, None], (slot, LANES))
    own_bias = lax.dynamic_slice_in_dim(forget_bias, z * own_heads, own_heads)
    bias = jnp.broadcast_to(jnp.pad(own_bias, (0, LANES - own_heads))[None], (8, LANES))
    block = min(256, slot)
    def row_block(ref, n):
        return ref.at[pl.ds(pl.multiple_of(n * rows, rows), rows), :]

    def column_block(ref, n):
        return ref.at[:, pl.ds(pl.multiple_of(n * own_width, LANES), own_width)]

    straight, diagonal = straight_steps(wide), diagonal_steps(wide)
    inputs = tokens.astype(F32)
    half = wide // 2
    if fused:
        (
            normed_one, in_full, out_full, projected, attended, logs, mixed_rows, middle, normed_two,
            up_block, up_two, up_one, down_block, grad_got,
        ) = first_part(
            tokens, in_weight, small, out_weight, gate_up_weight, cotangent, down_weight, gain_one,
            gain_two, bias, cont, wide, own_heads, head_size, block, 0,
        )
    else:
        pairs = []
        for i in range(wide * narrow):
            to_wide = (i % (2 * wide)) // 2
            to_narrow = i % 2 + 2 * (i // (2 * wide))
            pairs.append((i, to_wide * narrow + to_narrow))
        down_block = lax.ppermute(down_weight, ("wide", "narrow"), pairs)

        slot_tokens, in_full, out_full, up_block, grad_far = gather_all(
            tokens, in_parts, out_weight, up_parts, cotangent
        )
        slot_tokens = slot_tokens.reshape(slot, width)
        in_full = in_full.reshape(width, columns)
        out_full = out_full.reshape(width, width)

        up_two = on_line(up_block, LINE_TWO)
        up_one = on_line(up_block, LINE_ONE)

        slot_floats = slot_tokens.astype(F32)
        normed_one = (slot_floats * rms_factor(slot_floats) * gain_one).astype(BF16)
        projected = dot_f32(normed_one, in_full)

        mixed, attended, logs = attention_forward(
            projected, bias, cont, own_heads, head_size, block
        )

        mixed_rows, *grad_near = exchange(
            mixed, row_block, column_block, (rows, width), straight, [cotangent] * len(straight), 1
        )
        grads = {0: cotangent}
        grads.update({k: grad_near[n] for n, k in enumerate(straight)})
        grads.update({k: grad_far[n] for n, k in enumerate(diagonal)})
        grads = [grads[k] for k in range(0, wide, 2)]
        down_block = follow(down_block, mixed_rows)
        down_two = on_line(down_block, LINE_TWO)
        down_one = on_line(down_block, LINE_ONE)
        middle = inputs + dot_f32(mixed_rows, out_full)
        normed_two = (middle * rms_factor(middle) * gain_two).astype(BF16)

    if fused:
        (
            grad_middle, grad_gain_two, slot_grad, branch_sum, up_src, down_src, up_acc, down_acc,
            up_one, down_one, out_part, branch_near,
        ) = second_part(
            normed_two, cotangent, grad_got, [up_block, up_two, up_one], down_block, middle,
            mixed_rows, out_full, gain_two, 2,
        )
        grad_gain_two = grad_gain_two[0]
    else:
        ups = [up_block] + [follow(piece, normed_two) for piece in (up_two, up_one)]
        plane_normed, plane_grad, up_full, down_full = gather_rows(
            normed_two, grads, ups, [down_block, down_two, down_one], 2
        )
        plane_normed = plane_normed.reshape(wide * rows, width)
        plane_grad = plane_grad.reshape(wide * rows, width)
        up_full = up_full.reshape(width, 4 * unit)
        down_full = down_full.reshape(2 * unit, width)
        hidden, gate_up_grad, norm_even, norm_odd, branch = feed_forward(
            plane_normed, plane_grad, up_full, down_full, rows
        )
        grad_up_full = dot_f32(plane_normed, gate_up_grad, ((0,), (0,))).astype(BF16)
        grad_down_full = dot_f32(hidden, plane_grad, ((0,), (0,))).astype(BF16)
        if unit % LANES:
            grouped = grad_up_full.reshape(width, 4, unit)
            grad_up_full = jnp.pad(grouped, ((0, 0), (0, 0), (0, LANES - unit))).reshape(width, -1)
        branch = branch.reshape(wide, rows, width)
        fits = wide <= 8
        norm_got = along_wide(norm_odd.reshape(half, rows, width), 1, wide)
        (
            grad_normed_two, branch_sum, up_src, down_src, up_one, down_one, up_acc, down_acc,
        ) = middle_sums(
            norm_even.reshape(half, rows, width), norm_got,
            branch if fits else branch[:2, :16], grad_up_full, grad_down_full, 6,
        )
        if not fits:
            received = along_wide(branch[half:], 1, wide)
            branch_sum = (branch[:half].astype(F32) + received.astype(F32)).astype(BF16)
        upstream = cotangent.astype(F32)
        grad_middle_norm, grad_gain_two = rms_back(middle, gain_two, grad_normed_two)
        grad_middle = upstream + grad_middle_norm
        branch_one_grad = grad_middle.astype(BF16)
        grad_mixed = dot_f32(branch_one_grad, out_full, ((1,), (1,))).astype(BF16)
        slot_grad, *branch_near = exchange(
            grad_mixed, column_block, row_block, (slot, own_width), straight,
            [branch_sum[k // 2] for k in straight], 3,
        )
        branch_near = jnp.stack(branch_near)
        out_part = dot_f32(mixed_rows, branch_one_grad, ((0,), (0,))).astype(BF16)
    wide_rows = width // wide
    (
        unused, bias_grad, norm_part, in_part, grad_out, up_two, down_two, up_one, down_one,
        branch_far,
    ) = attention_backward(
        projected, bias, cont, attended, logs, slot_grad, in_full, normed_one,
        [up_src, down_src, up_one, down_one], out_part.reshape(wide, wide_rows, width), branch_sum,
        own_heads, head_size, block, 7,
    )
    branches = [branch_sum, branch_near, branch_far]
    all_bias = lax.dynamic_update_slice(
        jnp.zeros((width,), F32), bias_grad[0, :own_heads], (z * own_heads,)
    )
    small = jnp.stack([jnp.zeros((width,), F32), grad_gain_two, all_bias])
    small = jnp.pad(small, ((0, 5), (0, 0)))
    low = lambda part: part.astype(BF16)
    output, grad_tokens, grad_in, grad_up, grad_down, totals = last_part(
        norm_part, in_part.reshape(wide, wide_rows, columns), [low(up_acc), up_one, up_two],
        [low(down_acc), down_one, down_two], branches, tokens, middle, grad_middle, gain_one, small,
        own_width, own_heads, (base + 3 * heads) // narrow, 4,
    )
    if not aligned:
        grad_up = grad_up.reshape(wide_rows, wide, LANES)[:, :, :unit]
        grad_up = grad_up.reshape(wide_rows, wide * unit)
    grad_up, grad_down = grad_up.astype(F32), grad_down.astype(F32)
    return (
        output,
        grad_tokens,
        totals[0],
        grad_in,
        totals[2, :heads],
        grad_out,
        totals[1],
        grad_up,
        grad_down,
    )


def solution(mesh):
    both = ("wide", "narrow")
    in_specs = (
        P(both, None), P(), P(both, None), P(), P(both, None), P(), P(both, None), P(both, None),
        P("wide", None), P(both, None),
    )
    out_specs = (
        P(both, None), P(both, None), P(), P("wide", "narrow"), P(), P("wide", "narrow"), P(),
        P("wide", "narrow"), P("wide", "narrow"),
    )
    return jax.shard_map(
        on_device, mesh=mesh, in_specs=in_specs, out_specs=out_specs, check_vma=False
    )
```

```python
import functools

import jax
import jax.numpy as jnp
from jax import lax
from jax.experimental import pallas as pl
from jax.experimental.pallas import tpu as pltpu
from jax.sharding import PartitionSpec as P

EPSILON = 1e-06
SEPARATE = 128.0
F32 = jnp.float32
BF16 = jnp.bfloat16
LANES = 128
EXACT = lax.Precision.HIGHEST
ANY = pl.BlockSpec(memory_space=pltpu.HBM)


def dot_f32(left, right, dims=((1,), (0,))):
    return lax.dot_general(left, right, (dims, ((), ())), preferred_element_type=F32)


def along_wide(block, flip, wide):
    return lax.ppermute(block, "wide", [(i, i ^ flip) for i in range(wide)])


def copy_kernel(plan, count, *refs):
    sources, targets, sems = refs[:count], refs[count:-1], refs[-1]
    copies = plan(sources, targets)

    def each(act):
        for n, (src, dst, *when) in enumerate(copies):
            copy = pltpu.make_async_copy(src, dst, sems.at[n])
            if when:
                pl.when(when[0])(functools.partial(act, copy))
            else:
                act(copy)

    each(lambda copy: copy.start())
    each(lambda copy: copy.wait())


def local_copies(plan, copies, sources, shapes, gather):
    moved = sum(s.size * s.dtype.itemsize for s in shapes)
    inside = pl.BlockSpec(memory_space=pltpu.VMEM)
    return pl.pallas_call(
        functools.partial(copy_kernel, plan, len(sources)),
        out_shape=shapes,
        in_specs=[ANY if gather else inside] * len(sources),
        out_specs=[inside if gather else ANY] * len(shapes),
        compiler_params=pltpu.CompilerParams(vmem_limit_bytes=16 * 2**20),
        scratch_shapes=[pltpu.SemaphoreType.DMA((copies,))],
        cost_estimate=pl.CostEstimate(flops=0, bytes_accessed=2 * moved, transcendentals=0),
    )(*sources)


def flipped(me, k):
    out = me
    bit = 1
    while bit <= k:
        if k & bit:
            out = out + bit - 2 * bit * lax.rem(lax.div(out, bit), 2)
        bit *= 2
    return out


LINE_TWO = [(0, 2), (2, 0), (1, 3), (3, 1)]
LINE_ONE = [(0, 1), (1, 0), (2, 3), (3, 2)]
LINE_MIDDLE = [(1, 2), (2, 1)]
LINE_OUT = [(2, 3), (1, 0)]
LINE_IN = [(0, 1), (3, 2)]


def on_line(block, pairs):
    return lax.ppermute(block, "narrow", pairs)


def follow(array, *earlier):
    return lax.optimization_barrier((array, *earlier))[0]


MESH = pl.DeviceIdType.MESH
VMEM = pl.BlockSpec(memory_space=pltpu.VMEM)
DMA = pltpu.SemaphoreType.DMA


def greet(devices):
    barrier = pltpu.get_barrier_semaphore()
    for device in devices:
        pl.semaphore_signal(barrier, inc=1, device_id=device, device_id_type=MESH)
    pl.semaphore_wait(barrier, len(devices))


class Sender:
    def __init__(self, send, recv):
        self.send, self.recv, self.used = send, recv, 0

    def plan(self, src, dst, device):
        n = self.used
        self.used += 1
        return pltpu.make_async_remote_copy(
            src_ref=src, dst_ref=dst, send_sem=self.send.at[n], recv_sem=self.recv.at[n],
            device_id=device, device_id_type=MESH,
        )


def narrow_device(n):
    return {"narrow": n}


def wide_device(n):
    return {"wide": n}


def wide_steps(wide):
    return [1] + list(range(2, wide, 2))


def straight_steps(wide):
    return [k for k in range(2, wide, 2) if k & (k - 1) == 0]


def diagonal_steps(wide):
    return [k for k in range(2, wide, 2) if k & (k - 1)]


def by_device(ref, w):
    return (lambda k: ref.at[flipped(w, k)]), (lambda k, to: ref.at[flipped(w, k)])


class WideGather:
    def __init__(self, sender, w, wide, part, target):
        self.far = list(range(2, wide, 2))
        self.first = {
            k: sender.plan(part(0), target(0, k), wide_device(flipped(w, k)))
            for k in wide_steps(wide)
        }
        sibling = wide_device(flipped(w, 1))
        self.second = {k: sender.plan(part(k), target(k, 1), sibling) for k in self.far}

    def start(self):
        for k in self.far + [1]:
            self.first[k].start()

    def pass_on(self):
        for k in self.far:
            self.first[k].wait_recv()
            self.second[k].start()

    def received(self):
        self.first[1].wait_recv()
        for k in self.far:
            self.second[k].wait_recv()

    def sent(self):
        for copy in list(self.first.values()) + list(self.second.values()):
            copy.wait_send()

    def finish(self):
        self.received()
        self.sent()


def gather_kernel(
    wide, x_ref, in_ref, out_ref, up_ref, grad_ref, slot_ref, in_full, out_full, up_block, grad_far,
    send, recv, local,
):
    w, z = lax.axis_index("wide"), lax.axis_index("narrow")
    line = [flipped(z, k) for k in range(4)]
    sender = Sender(send, recv)
    own = [
        pltpu.make_async_copy(in_ref.at[z], in_full.at[w, z], local.at[0]),
        pltpu.make_async_copy(out_ref, out_full.at[w, z], local.at[1]),
        pltpu.make_async_copy(x_ref, slot_ref.at[z], local.at[2]),
        pltpu.make_async_copy(up_ref.at[w], up_block.at[w], local.at[3]),
    ]
    for copy in own:
        copy.start()
    greet(
        [narrow_device(line[k]) for k in (1, 2, 3)]
        + [wide_device(flipped(w, k)) for k in range(1, wide)]
    )
    ups = [
        sender.plan(up_ref.at[flipped(w, k)], up_block.at[w], wide_device(flipped(w, k)))
        for k in range(1, wide)
    ]
    grads = [
        sender.plan(grad_ref, grad_far.at[n], wide_device(flipped(w, k)))
        for n, k in enumerate(diagonal_steps(wide))
    ]
    is_middle = (z == 1) | (z == 2)
    is_end = (z == 0) | (z == 3)
    ins = [
        sender.plan(in_ref.at[line[k]], in_full.at[w, z], narrow_device(line[k])) for k in (2, 3, 1)
    ]
    outs = [sender.plan(out_ref, out_full.at[w, z], narrow_device(line[k])) for k in (2, 3, 1)]
    two = sender.plan(x_ref, slot_ref.at[z], narrow_device(line[2]))
    one = sender.plan(x_ref, slot_ref.at[z], narrow_device(line[1]))
    middle = sender.plan(x_ref, slot_ref.at[z], narrow_device(line[3]))
    relay = sender.plan(slot_ref.at[line[2]], slot_ref.at[line[2]], narrow_device(line[1]))
    in_wide = WideGather(sender, w, wide, *by_device(in_full, w))
    out_wide = WideGather(sender, w, wide, *by_device(out_full, w))
    for copy in ins + outs + ups:
        copy.start()
    own[0].wait()
    for copy in ins:
        copy.wait_recv()
    in_wide.start()
    two.start()
    one.start()
    own[1].wait()
    for copy in outs:
        copy.wait_recv()
    out_wide.start()
    in_wide.pass_on()
    for copy in grads:
        copy.start()
    two.wait_recv()

    @pl.when(is_middle)
    def _():
        relay.start()
        middle.start()

    out_wide.pass_on()
    one.wait_recv()
    own[2].wait()
    own[3].wait()
    for copy in ups + grads:
        copy.wait()

    @pl.when(is_middle)
    def _():
        middle.wait_recv()
        middle.wait_send()
        relay.wait_send()

    @pl.when(is_end)
    def _():
        relay.wait_recv()

    for copy in ins + outs + [two, one]:
        copy.wait_send()
    in_wide.finish()
    out_wide.finish()


def gather_all(tokens, in_parts, out_weight, up_parts, cotangent):
    narrow, wide = in_parts.shape[0], up_parts.shape[0]
    steps = 10 + 4 * wide
    shapes = [
        (narrow,) + tokens.shape, (wide,) + in_parts.shape, (wide, narrow) + out_weight.shape,
        up_parts.shape, (len(diagonal_steps(wide)),) + cotangent.shape,
    ]
    return pl.pallas_call(
        functools.partial(gather_kernel, wide),
        out_shape=[jax.ShapeDtypeStruct(shape, BF16) for shape in shapes],
        in_specs=[ANY] * 5,
        out_specs=[VMEM] * 5,
        scratch_shapes=[DMA((steps,)), DMA((steps,)), DMA((4,))],
        compiler_params=pltpu.CompilerParams(
            collective_id=0, has_side_effects=True, vmem_limit_bytes=40 * 2**20
        ),
    )(tokens, in_parts, out_weight, up_parts, cotangent)


def exchange_kernel(source, target, steps, *refs):
    count = len(steps)
    src_ref, sides, dst_ref = refs[0], refs[1 : 1 + count], refs[1 + count]
    got = refs[2 + count : 2 + 2 * count]
    send, recv, local = refs[2 + 2 * count :]
    w, z = lax.axis_index("wide"), lax.axis_index("narrow")
    line = [flipped(z, k) for k in range(4)]
    sender = Sender(send, recv)
    own = pltpu.make_async_copy(source(src_ref, z), target(dst_ref, z), local.at[0])
    own.start()
    greet(
        [narrow_device(line[k]) for k in (1, 2, 3)] + [wide_device(flipped(w, k)) for k in steps]
    )
    copies = [
        sender.plan(source(src_ref, line[k]), target(dst_ref, z), narrow_device(line[k]))
        for k in (2, 3, 1)
    ]
    copies += [
        sender.plan(sides[n], got[n], wide_device(flipped(w, k))) for n, k in enumerate(steps)
    ]
    for copy in copies:
        copy.start()
    own.wait()
    for copy in copies:
        copy.wait()


def exchange(array, source, target, shape, steps, sides, collective_id):
    count = len(steps) + 4
    return pl.pallas_call(
        functools.partial(exchange_kernel, source, target, steps),
        out_shape=[jax.ShapeDtypeStruct(shape, array.dtype)]
        + [jax.ShapeDtypeStruct(side.shape, side.dtype) for side in sides],
        in_specs=[ANY] * (1 + len(sides)),
        out_specs=[VMEM] * (1 + len(sides)),
        scratch_shapes=[DMA((count,)), DMA((count,)), DMA((1,))],
        compiler_params=pltpu.CompilerParams(
            collective_id=collective_id, has_side_effects=True, vmem_limit_bytes=16 * 2**20
        ),
    )(array, *sides)


def place_of(k, wide):
    return k // 2 + (k % 2) * (wide // 2)


def rows_kernel(wide, *refs):
    half = wide // 2
    grads = refs[:half]
    (
        src_ref, up_ref, up_two, up_one, down_ref, down_two, down_one, dst_ref, grad_ref, up_full,
        down_full, send, recv, local,
    ) = refs[half:]
    w, z = lax.axis_index("wide"), lax.axis_index("narrow")
    line = [flipped(z, k) for k in range(4)]
    is_middle = (z == 1) | (z == 2)
    is_end = (z == 0) | (z == 3)
    sender = Sender(send, recv)
    up_at = lambda n: up_full.at[:, n]
    down_at = lambda n: down_full.at[n]
    moves = [
        (src_ref, dst_ref.at[0]),
        (down_ref, down_at(z)), (down_two, down_at(line[2])), (down_one, down_at(line[1])),
        (up_ref, up_at(z)), (up_two, up_at(line[2])), (up_one, up_at(line[1])),
    ] + [(grads[n], grad_ref.at[n]) for n in range(half)]
    own = [pltpu.make_async_copy(src, dst, local.at[n]) for n, (src, dst) in enumerate(moves)]
    for copy in own:
        copy.start()
    greet(
        [wide_device(flipped(w, k)) for k in wide_steps(wide)]
        + [narrow_device(line[k]) for k in (1, 3)]
    )
    gather = WideGather(
        sender, w, wide, lambda k: src_ref if k == 0 else dst_ref.at[place_of(k, wide)],
        lambda k, to: dst_ref.at[place_of(k ^ to, wide)],
    )
    middles = [
        sender.plan(up_ref, up_at(z), narrow_device(line[3])),
        sender.plan(down_ref, down_at(z), narrow_device(line[3])),
    ]
    relays = [
        sender.plan(up_two, up_at(line[2]), narrow_device(line[1])),
        sender.plan(down_two, down_at(line[2]), narrow_device(line[1])),
    ]
    gather.start()

    @pl.when(is_middle)
    def _():
        for copy in middles + relays:
            copy.start()

    sibling = wide_device(flipped(w, 1))
    copies = [sender.plan(grads[n], grad_ref.at[half + n], sibling) for n in range(half)]
    for copy in copies:
        copy.start()
    gather.pass_on()

    @pl.when(is_middle)
    def _():
        for copy in middles:
            copy.wait()
        for copy in relays:
            copy.wait_send()

    @pl.when(is_end)
    def _():
        for copy in relays:
            copy.wait_recv()

    for copy in own + copies:
        copy.wait()
    gather.finish()


def gather_rows(array, grads, ups, downs, collective_id):
    half = len(grads)
    wide = 2 * half
    whole = jax.ShapeDtypeStruct((wide,) + array.shape, array.dtype)
    up_shape = ups[0].shape
    full = jax.ShapeDtypeStruct((up_shape[0], 4) + up_shape[1:], BF16)
    return pl.pallas_call(
        functools.partial(rows_kernel, wide),
        out_shape=[whole, whole, full, jax.ShapeDtypeStruct((4,) + downs[0].shape, BF16)],
        in_specs=[ANY] * (half + 7),
        out_specs=[VMEM, ANY if wide > 8 else VMEM, VMEM, VMEM],
        scratch_shapes=[DMA((2 * wide + 4,)), DMA((2 * wide + 4,)), DMA((half + 7,))],
        compiler_params=pltpu.CompilerParams(
            collective_id=collective_id, has_side_effects=True, vmem_limit_bytes=48 * 2**20
        ),
    )(*grads, array, *ups, *downs)


def hidden_kernel(
    half, normed_ref, grad_ref, up_ref, down_ref, hidden_ref, mid_ref, even_ref, odd_ref, branch_ref
):
    size = down_ref.shape[0]
    gate_up = dot_f32(normed_ref[...], up_ref[...])
    grad_hidden = dot_f32(grad_ref[...], down_ref[...], ((1,), (1,)))
    gate, up = gate_up[:, :size], gate_up[:, size:]
    opened = jax.nn.sigmoid(gate)
    acted = gate * opened
    hidden_ref[...] = (acted * up).astype(BF16)
    mid_ref[:, :size] = (grad_hidden * up * (opened * (1.0 + gate * (1.0 - opened)))).astype(BF16)
    mid_ref[:, size:] = (grad_hidden * acted).astype(BF16)
    grad_normed = dot_f32(mid_ref[...], up_ref[...], ((1,), (1,))).astype(BF16)
    branch_ref[...] = dot_f32(hidden_ref[...], down_ref[...]).astype(BF16)
    step = pl.program_id(0)

    @pl.when(step < half)
    def _():
        even_ref[...] = grad_normed

    @pl.when(step >= half)
    def _():
        odd_ref[...] = grad_normed


def feed_forward(normed, grad, up_full, down_full, rows):
    total, width = normed.shape
    blocks = total // rows
    half = blocks // 2
    size = down_full.shape[0]
    row_block = lambda columns: pl.BlockSpec((rows, columns), lambda i: (i, 0))
    fixed = lambda array: pl.BlockSpec(array.shape, lambda i: (0, 0))
    return pl.pallas_call(
        functools.partial(hidden_kernel, half),
        grid=(blocks,),
        in_specs=[row_block(width), row_block(width), fixed(up_full), fixed(down_full)],
        out_specs=[
            row_block(size), row_block(2 * size),
            pl.BlockSpec((rows, width), lambda i: (jnp.minimum(i, half - 1), 0)),
            pl.BlockSpec((rows, width), lambda i: (jnp.maximum(i - half, 0), 0)),
            row_block(width),
        ],
        out_shape=[
            jax.ShapeDtypeStruct((total, size), BF16),
            jax.ShapeDtypeStruct((total, 2 * size), BF16),
            jax.ShapeDtypeStruct((total // 2, width), BF16),
            jax.ShapeDtypeStruct((total // 2, width), BF16),
            jax.ShapeDtypeStruct((total, width), BF16),
        ],
        compiler_params=pltpu.CompilerParams(vmem_limit_bytes=48 * 2**20),
    )(normed, grad, up_full, down_full)


def middle_kernel(
    wide, even_ref, got_ref, branch_ref, up_ref, down_ref, norm_sum, branch_sum, up_src, down_src,
    up_one, down_one, up_acc, down_acc, core_buf, own_buf, far_buf, branch_buf, up_join, up_mid,
    down_join, down_mid, up_own, down_own, send, recv, local,
):
    w, z = lax.axis_index("wide"), lax.axis_index("narrow")
    line = [flipped(z, k) for k in range(4)]
    half = wide // 2
    unit = up_src.shape[1]
    part = down_src.shape[1]
    sender = Sender(send, recv)
    is_middle = (z == 1) | (z == 2)
    is_end = (z == 0) | (z == 3)

    def up_share(n):
        return up_ref.at[:, pl.ds(pl.multiple_of(n * unit, unit), unit)]

    def down_share(n):
        return down_ref.at[:, pl.ds(pl.multiple_of(n * part, part), part)]

    moves = [
        (up_share(line[2]), up_src), (down_share(line[2]), down_src),
        (up_share(z), up_own), (down_share(z), down_own),
        (up_share(line[1]), up_one), (down_share(line[1]), down_one),
    ]
    moves += [(got_ref.at[n], core_buf.at[n]) for n in range(half)]
    moves += [(even_ref.at[n], own_buf.at[n]) for n in range(half)]
    pairs = branch_sum.shape[0]
    moves += [(branch_ref.at[n], branch_sum.at[n]) for n in range(pairs)]
    own = [pltpu.make_async_copy(src, dst, local.at[n]) for n, (src, dst) in enumerate(moves)]
    for copy in own:
        copy.start()
    greet(
        [wide_device(flipped(w, k)) for k in wide_steps(wide)]
        + [narrow_device(line[k]) for k in (1, 3)]
    )
    sibling = wide_device(flipped(w, 1))
    far = [
        sender.plan(own_buf.at[n], far_buf.at[n - 1], wide_device(flipped(w, 2 * n)))
        for n in range(1, half)
    ]
    branch_core = [
        sender.plan(branch_ref.at[pairs + n], branch_buf.at[n], sibling) for n in range(pairs)
    ]
    joins = [
        sender.plan(up_share(line[3]), up_join, narrow_device(line[1])),
        sender.plan(down_share(line[3]), down_join, narrow_device(line[1])),
    ]
    mids = [
        sender.plan(up_share(line[3]), up_mid, narrow_device(line[3])),
        sender.plan(down_share(line[3]), down_mid, narrow_device(line[3])),
    ]
    order = list(range(1, half)) + [0]

    @pl.when(is_end)
    def _():
        for copy in joins:
            copy.start()

    @pl.when(is_middle)
    def _():
        for copy in mids:
            copy.start()

    for n in order:
        own[6 + n].wait()
        own[6 + half + n].wait()
        total = own_buf[n].astype(F32) + core_buf[n].astype(F32)
        own_buf[n] = total.astype(BF16)
        if n > 0:
            far[n - 1].start()
    for copy in branch_core:
        copy.start()
    for n in range(pairs):
        branch_core[n].wait_recv()
        own[6 + 2 * half + n].wait()
        total = branch_sum[n].astype(F32) + branch_buf[n].astype(F32)
        branch_sum[n] = total.astype(BF16)
    for n in range(6):
        own[n].wait()

    @pl.when(is_middle)
    def _():
        for copy in joins:
            copy.wait_recv()
        up_src[...] = (up_src[...].astype(F32) + up_join[...].astype(F32)).astype(BF16)
        down_src[...] = (down_src[...].astype(F32) + down_join[...].astype(F32)).astype(BF16)

    total = own_buf[0].astype(F32)
    for n in range(1, half):
        far[n - 1].wait_recv()
        total = total + far_buf[n - 1].astype(F32)
    norm_sum[...] = total
    up_acc[...] = up_own[...].astype(F32)
    down_acc[...] = down_own[...].astype(F32)

    @pl.when(is_middle)
    def _():
        for copy in mids:
            copy.wait()
        up_acc[...] += up_mid[...].astype(F32)
        down_acc[...] += down_mid[...].astype(F32)

    @pl.when(is_end)
    def _():
        for copy in joins:
            copy.wait_send()

    for copy in far + branch_core:
        copy.wait_send()


def middle_sums(even, got, branch, grad_up, grad_down, collective_id):
    half, rows, width = even.shape
    wide = 2 * half
    unit, part = grad_up.shape[1] // 4, grad_down.shape[1] // 4
    up_shape, down_shape = (grad_up.shape[0], unit), (grad_down.shape[0], part)
    steps = 4 * half + 6
    rows_buf = pltpu.VMEM((half, rows, width), BF16)
    pairs = branch.shape[0] // 2
    return pl.pallas_call(
        functools.partial(middle_kernel, wide),
        out_shape=[
            jax.ShapeDtypeStruct((rows, width), F32),
            jax.ShapeDtypeStruct((pairs,) + branch.shape[1:], BF16),
            *[jax.ShapeDtypeStruct(up_shape, BF16), jax.ShapeDtypeStruct(down_shape, BF16)] * 2,
            jax.ShapeDtypeStruct(up_shape, F32),
            jax.ShapeDtypeStruct(down_shape, F32),
        ],
        in_specs=[ANY] * 5,
        out_specs=[VMEM] * 8,
        scratch_shapes=[
            rows_buf, rows_buf, pltpu.VMEM((half - 1, rows, width), BF16),
            pltpu.VMEM((pairs,) + branch.shape[1:], BF16),
            *[pltpu.VMEM(up_shape, BF16)] * 2, *[pltpu.VMEM(down_shape, BF16)] * 2,
            pltpu.VMEM(up_shape, BF16), pltpu.VMEM(down_shape, BF16),
            DMA((steps,)), DMA((steps,)), DMA((6 + 3 * half,)),
        ],
        compiler_params=pltpu.CompilerParams(
            collective_id=collective_id, has_side_effects=True, vmem_limit_bytes=58 * 2**20
        ),
    )(even, got, branch, grad_up, grad_down)


def last_kernel(
    wide, rows, own_width, own_heads, norm_ref, in_ref, up_parts, down_parts, branch_refs, token_ref,
    middle_ref, grad_ref, gain_ref, small_ref, output, grad_tokens, grad_in, grad_up, grad_down, totals, join_buf, one_buf, mid_buf, two_buf, two_src, own_norm, norm_sum,
    in_core, in_own, in_far, in_sum, in_got, after_got, tail_buf, up_low, up_bufs, up_got, down_low,
    down_bufs, down_got, branch_bufs, narrow_buf, wide_buf, sum_buf, send, recv, down_send, down_recv,
    local,
):
    w, z = lax.axis_index("wide"), lax.axis_index("narrow")
    line = [flipped(z, k) for k in range(4)]
    half = wide // 2
    unit = up_low.shape[1]
    wide_rows, width = grad_in.shape[0], token_ref.shape[1]
    sender = Sender(send, recv)
    is_middle = (z == 1) | (z == 2)
    is_end = (z == 0) | (z == 3)

    def norm_block(n):
        return norm_ref.at[pl.ds(pl.multiple_of(n * rows, rows), rows), :]

    def up_rows(n):
        return up_low.at[pl.ds(pl.multiple_of(n * wide_rows, 16), wide_rows), :]

    def up_columns(n):
        return up_got.at[:, pl.ds(pl.multiple_of(n * unit, LANES), unit)]

    def section(n):
        return in_sum.at[:, pl.ds(pl.multiple_of(n * own_width, LANES), own_width)]

    def after_section(n):
        return in_sum.at[:, pl.ds(pl.multiple_of((n + 1) * own_width, LANES), LANES)]

    moves = [(norm_block(line[2]), two_src), (norm_block(z), own_norm)]
    moves += [(in_ref.at[flipped(w, 2 * n)], in_own.at[n]) for n in range(half)]
    ffn_at = len(moves)
    moves += [(ref, up_bufs.at[n]) for n, ref in enumerate(up_parts)]
    moves += [(ref, down_bufs.at[n]) for n, ref in enumerate(down_parts)]
    branch_at = len(moves)
    moves += [(ref, branch_bufs.at[n]) for n, ref in enumerate(branch_refs)]
    own = [pltpu.make_async_copy(src, dst, local.at[n]) for n, (src, dst) in enumerate(moves)]
    for copy in own:
        copy.start()
    greet(
        [narrow_device(line[k]) for k in (1, 2, 3)]
        + [wide_device(flipped(w, k)) for k in range(1, wide)]
    )
    sibling = wide_device(flipped(w, 1))
    joined = sender.plan(norm_block(line[3]), join_buf, narrow_device(line[1]))
    one = sender.plan(norm_block(line[1]), one_buf, narrow_device(line[1]))
    middle = sender.plan(norm_block(line[3]), mid_buf, narrow_device(line[3]))
    two = sender.plan(two_src, two_buf, narrow_device(line[2]))
    core = [
        sender.plan(in_ref.at[flipped(w, 2 * n + 1)], in_core.at[n], sibling) for n in range(half)
    ]
    far = [
        sender.plan(in_own.at[n], in_far.at[n - 1], wide_device(flipped(w, 2 * n)))
        for n in range(1, half)
    ]
    sections = [
        sender.plan(section(line[k]), in_got.at[z], narrow_device(line[k])) for k in (2, 3, 1)
    ]
    afters = [
        (
            (z == 0) | (line[k] == 3), (line[k] == 0) | (z == 3),
            sender.plan(after_section(line[k]), after_got.at[z], narrow_device(line[k])),
        )
        for k in (2, 3, 1)
    ]
    ups = [
        sender.plan(up_rows(flipped(w, k)), up_columns(w), wide_device(flipped(w, k)))
        for k in range(1, wide)
    ]
    first = [
        sender.plan(sum_buf, narrow_buf.at[z], narrow_device(line[k])) for k in (1, 2, 3)
    ]
    second = [
        sender.plan(sum_buf, wide_buf.at[w], wide_device(flipped(w, k))) for k in range(1, wide)
    ]
    parity, target = lax.rem(w, 2), lax.div(w, 2)
    depth = down_low.shape[0] // 2
    down_at = pl.ds(pl.multiple_of(parity * depth, 16), depth)
    downs = []
    for n in range(2):
        owner = target + n * half
        src, dst = down_low.at[pl.ds(n * depth, depth), :], down_got.at[down_at, :]
        push = pltpu.make_async_remote_copy(
            src_ref=src, dst_ref=dst, send_sem=down_send.at[n], recv_sem=down_recv.at[parity],
            device_id=wide_device(owner), device_id_type=MESH,
        )
        stay = pltpu.make_async_copy(src, dst, local.at[len(moves) + 1 + n])
        downs.append((owner == w, push, stay))

    order = list(range(1, half)) + [0]
    for n in order:
        core[n].start()

    @pl.when(is_end)
    def _():
        joined.start()

    @pl.when(is_middle)
    def _():
        middle.start()

    for n in order:
        core[n].wait_recv()
        own[2 + n].wait()
        total = in_own[n].astype(F32) + in_core[n].astype(F32)
        in_own[n] = total.astype(BF16)
        if n > 0:
            far[n - 1].start()
    own[0].wait()

    @pl.when(is_middle)
    def _():
        joined.wait_recv()
        two_src[...] = (two_src[...].astype(F32) + join_buf[...].astype(F32)).astype(BF16)

    two.start()
    one.start()
    for n in range(6):
        own[ffn_at + n].wait()
    up_low[...] = add_up([up_bufs[n] for n in range(3)]).astype(BF16)
    down_low[...] = add_up([down_bufs[n] for n in range(3)]).astype(BF16)
    for copy in ups:
        copy.start()
    for stays, push, stay in downs:
        pl.when(stays)(stay.start)
        pl.when(jnp.logical_not(stays))(push.start)
    up_got[:, pl.ds(pl.multiple_of(w * unit, LANES), unit)] = up_low[
        pl.ds(pl.multiple_of(w * wide_rows, 16), wide_rows), :
    ]
    total = middle_ref[...]
    for n in range(half):
        own[branch_at + n].wait()
        total = total + branch_bufs[n].astype(F32)
    output[...] = total.astype(BF16)

    total = in_own[0].astype(F32)
    for n in range(1, half):
        far[n - 1].wait_recv()
        total = total + in_far[n - 1].astype(F32)
    in_sum[...] = total.astype(BF16)
    mine = pltpu.make_async_copy(section(z), in_got.at[z], local.at[len(moves)])
    mine.start()
    own[1].wait()
    one.wait_recv()
    norm_sum[...] = own_norm[...].astype(F32) + one_buf[...].astype(F32)

    @pl.when(is_middle)
    def _():
        middle.wait()
        norm_sum[...] += mid_buf[...].astype(F32)

    two.wait_recv()
    for copy in sections:
        copy.start()
    for sends, gets, copy in afters:
        pl.when(sends)(copy.start)
    after_got[z] = after_section(z)[...]
    grads = norm_sum[...] + two_buf[...].astype(F32)
    values = token_ref[...].astype(F32)
    factor = rms_factor(values)
    normed = values * factor
    scaled = grads * gain_ref[...].reshape(1, width)
    inner = jnp.mean(scaled * normed, axis=-1, keepdims=True)
    grad_tokens[...] = grad_ref[...] + factor * (scaled - normed * inner)
    narrow_buf[z] = small_ref[...]
    narrow_buf[z, 0:1, :] = jnp.sum(grads * normed, axis=0, keepdims=True)
    sum_buf[...] = narrow_buf[z]
    for copy in first:
        copy.start()

    for copy in ups:
        copy.wait_recv()
    grad_up[...] = up_got[...].astype(F32)
    for n, (stays, push, stay) in enumerate(downs):
        pl.when(stays)(stay.wait)
        pl.when(jnp.logical_not(stays))(push.wait_send)
    for n in range(2):
        source = lax.rem(2 * w + n, wide)
        arrived = pltpu.make_async_remote_copy(
            src_ref=down_low.at[pl.ds(0, depth), :], dst_ref=down_got.at[pl.ds(n * depth, depth), :],
            send_sem=down_send.at[n], recv_sem=down_recv.at[n], device_id=sibling,
            device_id_type=MESH,
        )
        pl.when(source != w)(arrived.wait_recv)
    grad_down[...] = down_got[...].astype(F32)

    for copy in first:
        copy.wait()
    sum_buf[...] = narrow_buf[0] + narrow_buf[1] + narrow_buf[2] + narrow_buf[3]
    for copy in second:
        copy.start()
    wide_buf[w] = sum_buf[...]

    for copy in sections:
        copy.wait_recv()
    mine.wait()
    for sends, gets, copy in afters:
        pl.when(gets)(copy.wait_recv)

    @pl.when(z == 3)
    def _():
        row, lane = iota((LANES, LANES), 0), iota((LANES, LANES), 1)
        last = jnp.zeros((wide_rows, LANES), F32)
        for n in range(4):
            group = lax.div(row, own_heads)
            place = group * (4 * own_heads) + n * own_heads + row - group * own_heads
            spot = ((lane == place) & (row < 3 * own_heads)).astype(BF16)
            last = last + dot_f32(after_got[n], spot)
        tail_buf[...] = last

    @pl.when(z != 3)
    def _():
        tail_buf[...] = after_got[0].astype(F32)

    whole = jnp.concatenate([in_got[n].astype(F32) for n in range(4)] + [tail_buf[...]], axis=1)
    move = whole.shape[1] - (grad_in.shape[1] - width) * z
    grad_in[...] = pltpu.roll(whole, lax.rem(move, whole.shape[1]), 1)[:, : grad_in.shape[1]]

    for copy in second:
        copy.wait()
    total = wide_buf[0]
    for n in range(1, wide):
        total = total + wide_buf[n]
    totals[...] = total

    @pl.when(is_end)
    def _():
        joined.wait_send()

    for sends, gets, copy in afters:
        pl.when(sends)(copy.wait_send)
    for copy in [one, two] + core + far + sections + ups:
        copy.wait_send()


def grouped_last_kernel(wide, rows, own_width, own_heads, *refs):
    own, near, far = refs[8:11]
    branches = [own.at[0]]
    branches += [near.at[n] for n in range(near.shape[0])] + [far.at[n] for n in range(far.shape[0])]
    last_kernel(
        wide, rows, own_width, own_heads, *refs[:2], refs[2:5], refs[5:8], branches, *refs[11:],
    )


def last_part(
    norm_part, in_part, ups, downs, branches, tokens, middle, grad_middle, gain, small, own_width, own_heads,
    shard, collective_id,
):
    wide, wide_rows, columns = in_part.shape
    half = wide // 2
    rows, width = tokens.shape
    unit = ups[0].shape[1]
    steps = 4 + 2 * half + 12 + 2 * wide
    shape = jax.ShapeDtypeStruct
    vmem = lambda *dims: pltpu.VMEM(dims, BF16)
    return pl.pallas_call(
        functools.partial(grouped_last_kernel, wide, rows, own_width, own_heads),
        out_shape=[
            shape((rows, width), BF16), shape((rows, width), F32), shape((wide_rows, shard), F32),
            shape((wide_rows, wide * unit), F32), shape(downs[0].shape, F32),
            shape(small.shape, F32),
        ],
        in_specs=[ANY] * 11 + [VMEM] * 5,
        out_specs=[VMEM] * 6,
        scratch_shapes=[
            *[vmem(rows, width)] * 6, pltpu.VMEM((rows, width), F32),
            vmem(half, wide_rows, columns), vmem(half, wide_rows, columns),
            vmem(half - 1, wide_rows, columns), vmem(wide_rows, columns),
            vmem(4, wide_rows, own_width), vmem(4, wide_rows, LANES),
            pltpu.VMEM((wide_rows, LANES), F32), vmem(*ups[0].shape), vmem(3, *ups[0].shape),
            vmem(wide_rows, wide * unit), vmem(*downs[0].shape), vmem(3, *downs[0].shape),
            vmem(*downs[0].shape), vmem(half, rows, width),
            pltpu.VMEM((4,) + small.shape, F32), pltpu.VMEM((wide,) + small.shape, F32),
            pltpu.VMEM(small.shape, F32),
            DMA((steps,)), DMA((steps,)), DMA((2,)), DMA((2,)), DMA((12 + 2 * half,)),
        ],
        compiler_params=pltpu.CompilerParams(
            collective_id=collective_id, has_side_effects=True, vmem_limit_bytes=60 * 2**20
        ),
    )(
        norm_part, in_part, *ups, *downs, *branches, tokens, middle, grad_middle,
        gain, small,
    )


def rms_factor(values):
    return lax.rsqrt(jnp.mean(values * values, axis=-1, keepdims=True) + EPSILON)


def rms_back(values, gain, grad):
    factor = rms_factor(values)
    normed = values * factor
    grad_gain = jnp.sum(grad * normed, axis=0)
    scaled = grad * gain
    inner = jnp.mean(scaled * normed, axis=-1, keepdims=True)
    return (factor * (scaled - normed * inner), grad_gain)


def log_sigmoid(v):
    return jnp.minimum(v, 0.0) - jnp.log1p(jnp.exp(-jnp.abs(v)))


def iota(shape, dim):
    return lax.broadcasted_iota(jnp.int32, shape, dim)


def running_sum(v, reverse):
    rows = v.shape[0]
    index = iota(v.shape, 0)
    step = 1
    while step < rows:
        if reverse:
            v = v + jnp.where(index < rows - step, pltpu.roll(v, rows - step, 0), 0.0)
        else:
            v = v + jnp.where(index >= step, pltpu.roll(v, step, 0), 0.0)
        step *= 2
    return v


def half_of(lane, head_size):
    return (lane >= head_size).astype(jnp.int32)


def spread(first, head_size):
    row, lane = iota((LANES, LANES), 0), iota((LANES, LANES), 1)
    return row == first + half_of(lane, head_size)


def collect(first, head_size):
    row, lane = iota((LANES, LANES), 0), iota((LANES, LANES), 1)
    return lane == first + half_of(row, head_size)


def same_head(head_size):
    row, lane = iota((LANES, LANES), 0), iota((LANES, LANES), 1)
    return (half_of(row, head_size) == half_of(lane, head_size)).astype(F32)


def exact_dot(left, right):
    return lax.dot_general(
        left, right, (((1,), (0,)), ((), ())), precision=EXACT, preferred_element_type=F32
    )


def head_mean(v, head_size):
    return exact_dot(v, same_head(head_size)) * (1.0 / head_size)


def prologue(pair, heads, head_size, q_ref, k_ref, v_ref, small_low, cont):
    spot = lambda group: spread(group * heads + 2 * pair, head_size).astype(BF16)
    key_mix = jax.nn.sigmoid(dot_f32(small_low, spot(1)))
    value_mix = jax.nn.sigmoid(dot_f32(small_low, spot(2)))
    queries = q_ref[...].astype(BF16).astype(F32)
    keys = k_ref[...].astype(BF16).astype(F32)
    values = v_ref[...].astype(BF16).astype(F32)
    key_step = pltpu.roll(keys, 1, 0) * cont - keys
    value_step = pltpu.roll(values, 1, 0) * cont - values
    shifted = keys + key_mix * key_step
    value_low = (values + value_mix * value_step).astype(BF16)
    query_factor = lax.rsqrt(head_mean(queries * queries, head_size) + EPSILON)
    key_factor = lax.rsqrt(head_mean(shifted * shifted, head_size) + EPSILON)
    return (
        queries * query_factor,
        shifted * key_factor,
        value_low,
        query_factor,
        key_factor,
        key_mix,
        value_mix,
        key_step,
        value_step,
    )


def small_columns(small_ref, bias_ref):
    return (small_ref[...] + bias_ref[0:1, :]).astype(BF16)


def decay_of(small_low, cont):
    return running_sum(log_sigmoid(small_low.astype(F32)) - SEPARATE * (1.0 - cont), False)


def forward_pair(
    pair, heads, head_size, block, q_ref, k_ref, v_ref, gate_ref, small_low, cont, decay_all,
    mixed_ref, att_ref, log_ref,
):
    query, key, value_low, *unused = prologue(
        pair, heads, head_size, q_ref, k_ref, v_ref, small_low, cont
    )
    rows = query.shape[0]
    query = query.astype(BF16) * BF16(head_size**-0.5)
    key = key.astype(BF16)
    decay = exact_dot(decay_all, spread(2 * pair, head_size).astype(F32))
    decay_rows = decay.T
    lane = iota((1, LANES), 1)
    ones = jnp.ones((rows, LANES), BF16)
    value_wide = jnp.concatenate([value_low, ones], axis=1)
    for i in range(rows // block):
        lo, hi = i * block, (i + 1) * block
        row_index = iota((block, hi), 0) + lo
        visible = iota((block, hi), 1) <= row_index
        outs, sums = [], []
        for head in range(2):
            mine = (lane >= head_size) if head else (lane < head_size)
            at = head * head_size
            left = jnp.where(mine, query[lo:hi], BF16(0.0))
            scores = dot_f32(left, key[:hi], ((1,), (1,)))
            scores = scores + decay[lo:hi, at : at + 1] - decay_rows[at : at + 1, :hi]
            weights = jnp.where(visible, jnp.exp(scores), 0.0).astype(BF16)
            both = dot_f32(weights, value_wide[:hi])
            outs.append(both[:, :LANES])
            sums.append(both[:, LANES:])
        first = lane < head_size
        total = jnp.where(first, sums[0], sums[1])
        attended = (jnp.where(first, outs[0], outs[1]) / total).astype(BF16)
        att_ref[lo:hi, :] = attended
        log_ref[lo:hi, :] = jnp.log(total)
        opened = jax.nn.sigmoid(gate_ref[lo:hi, :])
        mixed_ref[lo:hi, :] = (attended.astype(F32) * opened).astype(BF16)


def forward_kernel(
    heads, head_size, block, q_ref, k_ref, v_ref, gate_ref, small_ref, bias_ref, cont_ref,
    mixed_ref, att_ref, log_ref, decay_scr,
):
    pair = pl.program_id(0)
    cont = cont_ref[...]
    small_low = small_columns(small_ref, bias_ref)

    @pl.when(pair == 0)
    def _():
        decay_scr[...] = decay_of(small_low, cont)

    forward_pair(
        pair, heads, head_size, block, q_ref, k_ref, v_ref, gate_ref, small_low, cont,
        decay_scr[...], mixed_ref, att_ref, log_ref,
    )


def share_of(ref, like, n):
    size = like.shape[1]
    if ref.shape[1] == size:
        return ref
    return ref.at[:, pl.ds(pl.multiple_of(n * size, size), size)]


def backward_kernel(
    heads, head_size, block, wide, *refs
):
    q_ref, k_ref, v_ref, gate_ref, small_ref, bias_ref, cont_ref, att_ref, log_ref, grad_ref = refs[:10]
    in_ref, normed_ref, up_src, down_src, up_one, down_one, part_ref, branch_ref = refs[10:18]
    out_ref, bias_grad_ref, norm_ref, in_part_ref, grad_out = refs[18:23]
    up_two_got, down_two_got, up_one_got, down_one_got, branch_got = refs[23:28]
    decay_scr, small_scr, dq_scr, part_core, part_own, part_far, part_sum, part_got = refs[28:36]
    send, recv, local = refs[36:]
    pair = pl.program_id(0)
    pairs = heads * head_size // LANES
    half = wide // 2
    row_steps = out_ref.shape[0] // norm_ref.shape[0]
    w, z = lax.axis_index("wide"), lax.axis_index("narrow")
    sender = Sender(send, recv)
    one, two = flipped(z, 1), flipped(z, 2)
    copies = [
        sender.plan(up_src, up_two_got, narrow_device(two)),
        sender.plan(down_src, down_two_got, narrow_device(two)),
        sender.plan(share_of(up_one, up_src, one), up_one_got, narrow_device(one)),
        sender.plan(share_of(down_one, down_src, one), down_one_got, narrow_device(one)),
    ]
    core = [
        sender.plan(part_ref.at[flipped(w, 2 * n + 1)], part_core.at[n], wide_device(flipped(w, 1)))
        for n in range(half)
    ]
    far = [
        sender.plan(part_own.at[n], part_far.at[n - 1], wide_device(flipped(w, 2 * n)))
        for n in range(1, half)
    ]
    branches = [
        sender.plan(branch_ref.at[k // 2], branch_got.at[n], wide_device(flipped(w, k)))
        for n, k in enumerate(diagonal_steps(wide))
    ]
    own = [
        pltpu.make_async_copy(part_ref.at[flipped(w, 2 * n)], part_own.at[n], local.at[n])
        for n in range(half)
    ]
    own_width = heads * head_size

    def part_columns(n):
        return part_sum.at[:, pl.ds(pl.multiple_of(n * own_width, LANES), own_width)]

    outs = [
        sender.plan(part_columns(flipped(z, k)), part_got.at[k - 1], narrow_device(flipped(z, k)))
        for k in (1, 2, 3)
    ]

    @pl.when(pair == 0)
    def _():
        greet(
            [narrow_device(flipped(z, k)) for k in (1, 2, 3)]
            + [wide_device(flipped(w, k)) for k in wide_steps(wide)]
        )
        for copy in copies + core + own:
            copy.start()

    @pl.when(pair == 1)
    def _():
        for n in range(half):
            core[n].wait_recv()
            own[n].wait()
            part_own[n] = (part_own[n].astype(F32) + part_core[n].astype(F32)).astype(BF16)
            if n > 0:
                far[n - 1].start()

    @pl.when(pair < pairs)
    def _():
        backward_pair(
            pair, pairs, heads, head_size, block, q_ref, k_ref, v_ref, gate_ref, small_ref,
            bias_ref, cont_ref, att_ref, log_ref, grad_ref, out_ref, bias_grad_ref, decay_scr,
            small_scr, dq_scr,
        )

    @pl.when((pair >= pairs) & (pair < pairs + row_steps))
    def _():
        size = norm_ref.shape[0]
        at = pl.ds(pl.multiple_of((pair - pairs) * size, size), size)
        norm_ref[...] = dot_f32(out_ref[at, :], in_ref[...], ((1,), (1,))).astype(BF16)

    @pl.when(pair == pairs + row_steps)
    def _():
        total = part_own[0].astype(F32)
        for n in range(1, half):
            far[n - 1].wait_recv()
            total = total + part_far[n - 1].astype(F32)
        part_sum[...] = total.astype(BF16)
        for copy in outs + branches:
            copy.start()

    @pl.when(pair >= pairs + row_steps)
    def _():
        in_part_ref[...] = dot_f32(normed_ref[...], out_ref[...], ((0,), (0,))).astype(BF16)

    @pl.when(pair == pl.num_programs(0) - 1)
    def _():
        for copy in outs + copies + branches:
            copy.wait()
        total = part_columns(z)[...].astype(F32)
        for n in range(3):
            total = total + part_got[n].astype(F32)
        grad_out[...] = total
        for copy in core + far:
            copy.wait_send()


def backward_pair(
    pair, pairs, heads, head_size, block, q_ref, k_ref, v_ref, gate_ref, small_ref, bias_ref, cont_ref,
    att_ref, log_ref, grad_ref, out_ref, bias_grad_ref, decay_scr, small_scr, dq_scr,
):
    cont = cont_ref[...]
    small_low = small_columns(small_ref, bias_ref)
    rows = cont.shape[0]
    width = heads * head_size

    @pl.when(pair == 0)
    def _():
        decay_scr[...] = decay_of(small_low, cont)
        small_scr[...] = jnp.zeros_like(small_scr)

    (
        query_norm, key_norm, value_low, query_factor, key_factor, key_mix, value_mix, key_step,
        value_step,
    ) = prologue(pair, heads, head_size, q_ref, k_ref, v_ref, small_low, cont)
    query = query_norm.astype(BF16) * BF16(head_size**-0.5)
    key = key_norm.astype(BF16)
    opened = jax.nn.sigmoid(gate_ref[...])
    attended = att_ref[...].astype(F32)
    grad_mixed = grad_ref[...].astype(F32)
    grad_low = (grad_mixed * opened).astype(BF16)
    grad_gate = grad_mixed * attended * opened * (1.0 - opened)

    def columns(group):
        at = group * width + pair * LANES
        return pl.ds(pl.multiple_of(at, LANES), LANES)

    out_ref[:, columns(3)] = grad_gate.astype(BF16)
    inner = exact_dot(grad_low.astype(F32) * attended, same_head(head_size))
    decay = exact_dot(decay_scr[...], spread(2 * pair, head_size).astype(F32))
    level_rows = (decay - log_ref[...]).T
    inner_rows = inner.T
    lane = iota((1, LANES), 1)
    ones = jnp.ones((rows, LANES), BF16)
    query_wide = jnp.concatenate([query, ones], axis=1)
    key_wide = jnp.concatenate([key, ones], axis=1)
    key_parts, value_parts, query_parts = [], [], []
    for head in range(2):
        mine = (lane >= head_size) if head else (lane < head_size)
        at = head * head_size
        keys_out, values_out = [], []
        for j in range(rows // block):
            lo, hi = j * block, (j + 1) * block
            span = rows - lo
            visible = iota((block, span), 0) <= iota((block, span), 1)
            scores = dot_f32(
                jnp.where(mine, key[lo:hi], BF16(0.0)), query[lo:], ((1,), (1,))
            )
            scores = scores + level_rows[at : at + 1, lo:] - decay[lo:hi, at : at + 1]
            probs = jnp.where(visible, jnp.exp(scores), 0.0)
            grad_probs = dot_f32(
                jnp.where(mine, value_low[lo:hi], BF16(0.0)), grad_low[lo:], ((1,), (1,))
            )
            grad_scores = (probs * (grad_probs - inner_rows[at : at + 1, lo:])).astype(BF16)
            values_out.append(dot_f32(probs.astype(BF16), grad_low[lo:]))
            keys_out.append(dot_f32(grad_scores, query_wide[lo:]))
            part = dot_f32(grad_scores, key_wide[lo:hi], ((0,), (0,)))
            if j == 0:
                dq_scr[...] = part
            else:
                dq_scr[lo:, :] += part
        key_parts.append(jnp.concatenate(keys_out, axis=0))
        value_parts.append(jnp.concatenate(values_out, axis=0))
        query_parts.append(dq_scr[...])
    first = lane < head_size

    def join(parts):
        return jnp.where(first, parts[0], parts[1])

    grad_query = join([p[:, :LANES] for p in query_parts]) * head_size**-0.5
    grad_key = join([p[:, :LANES] for p in key_parts])
    grad_value = join(value_parts)
    grad_decay = join([p[:, LANES:] for p in query_parts]) - join([p[:, LANES:] for p in key_parts])

    def norm_back(grad, normed, factor):
        return factor * (grad - normed * head_mean(grad * normed, head_size))

    def shift_back(grad, mix):
        return grad * (1.0 - mix) + pltpu.roll(grad * mix * cont, rows - 1, 0)

    grad_query = norm_back(grad_query, query_norm, query_factor)
    grad_shifted = norm_back(grad_key, key_norm, key_factor)
    out_ref[:, columns(0)] = grad_query.astype(BF16)
    out_ref[:, columns(1)] = shift_back(grad_shifted, key_mix).astype(BF16)
    out_ref[:, columns(2)] = shift_back(grad_value, value_mix).astype(BF16)
    key_logit = grad_shifted * key_step * key_mix * (1.0 - key_mix)
    value_logit = grad_value * value_step * value_mix * (1.0 - value_mix)
    single = (lax.rem(lane, head_size) == 0).astype(F32)
    small_scr[...] += (
        exact_dot(grad_decay * single, collect(2 * pair, head_size).astype(F32))
        + exact_dot(key_logit, collect(heads + 2 * pair, head_size).astype(F32))
        + exact_dot(value_logit, collect(2 * heads + 2 * pair, head_size).astype(F32))
    )

    @pl.when(pair == pairs - 1)
    def _():
        grads = small_scr[...]
        forget = running_sum(grads, True) * jax.nn.sigmoid(-small_low.astype(F32))
        result = jnp.where(lane < heads, forget, grads)
        out_ref[:, 4 * width :] = result.astype(BF16)
        bias_grad_ref[...] = jnp.broadcast_to(
            jnp.sum(result, axis=0, keepdims=True), bias_grad_ref.shape
        )


def attention_specs(rows, pairs):
    def block_at(group):
        return pl.BlockSpec((rows, LANES), lambda p: (0, group * pairs + jnp.minimum(p, pairs - 1)))

    def fixed(height, column=0):
        return pl.BlockSpec((height, LANES), lambda p: (0, column))

    base = [block_at(0), block_at(1), block_at(2), block_at(3), fixed(rows, 4 * pairs), fixed(8), fixed(rows)]
    return base, pl.BlockSpec((rows, LANES), lambda p: (0, jnp.minimum(p, pairs - 1)))


def attention_forward(projected, bias, cont, heads, head_size, block):
    rows = projected.shape[0]
    pairs = heads * head_size // LANES
    base, own = attention_specs(rows, pairs)
    wide = jax.ShapeDtypeStruct((rows, heads * head_size), BF16)
    return pl.pallas_call(
        functools.partial(forward_kernel, heads, head_size, block),
        grid=(pairs,),
        in_specs=base,
        out_specs=[own] * 3,
        out_shape=[wide, wide, jax.ShapeDtypeStruct(wide.shape, F32)],
        scratch_shapes=[pltpu.VMEM((rows, LANES), F32)],
        compiler_params=pltpu.CompilerParams(vmem_limit_bytes=48 * 2**20),
    )(*([projected] * 5), bias, cont)


def attention_backward(
    projected, bias, cont, attended, logs, grad, in_full, normed_one, shares, out_part, branches, heads,
    head_size, block, collective_id,
):
    rows = projected.shape[0]
    width = normed_one.shape[1]
    wide, wide_rows = out_part.shape[:2]
    half = wide // 2
    pairs = heads * head_size // LANES
    base, own = attention_specs(rows, pairs)
    columns = 4 * heads * head_size + LANES
    step = min(256, rows)
    row_steps, in_steps = rows // step, width // 256
    steps = 8 + 3 * wide
    part = lambda count: pltpu.VMEM((count, wide_rows, width), BF16)
    shape = jax.ShapeDtypeStruct

    def later(first, count):
        return lambda p: jnp.clip(p - first, 0, count - 1)

    row_at, in_at = later(pairs, row_steps), later(pairs + row_steps, in_steps)
    return pl.pallas_call(
        functools.partial(backward_kernel, heads, head_size, block, wide),
        grid=(pairs + row_steps + in_steps,),
        in_specs=base
        + [own] * 3
        + [
            pl.BlockSpec(in_full.shape, lambda p: (0, 0), pipeline_mode=pl.Buffered(1)),
            pl.BlockSpec((rows, 256), lambda p: (0, in_at(p))),
        ]
        + [ANY] * 6,
        out_specs=[
            pl.BlockSpec((rows, columns), lambda p: (0, 0)),
            pl.BlockSpec((8, LANES), lambda p: (0, 0)),
            pl.BlockSpec((step, width), lambda p: (row_at(p), 0)),
            pl.BlockSpec((256, columns), lambda p: (in_at(p), 0)),
            pl.BlockSpec((wide_rows, heads * head_size), lambda p: (0, 0)),
        ]
        + [ANY] * 5,
        out_shape=[
            shape((rows, columns), BF16), shape((8, LANES), F32), shape((rows, width), BF16),
            shape((width, columns), BF16), shape((wide_rows, heads * head_size), F32),
            *[shape(share.shape, BF16) for share in shares[:2] * 2],
            shape((len(diagonal_steps(wide)),) + branches.shape[1:], BF16),
        ],
        scratch_shapes=[
            pltpu.VMEM((rows, LANES), F32), pltpu.VMEM((rows, LANES), F32),
            pltpu.VMEM((rows, 2 * LANES), F32), part(half), part(half), part(half - 1),
            pltpu.VMEM((wide_rows, width), BF16),
            pltpu.VMEM((3, wide_rows, heads * head_size), BF16),
            DMA((steps,)), DMA((steps,)), DMA((half,)),
        ],
        compiler_params=pltpu.CompilerParams(
            collective_id=collective_id, has_side_effects=True, vmem_limit_bytes=60 * 2**20
        ),
    )(
        *([projected] * 5), bias, cont, attended, logs, grad, in_full, normed_one, *shares, out_part,
        branches,
    )


def first_kernel(
    wide, heads, head_size, block, x_ref, in_ref, small_ref, out_ref, up_ref, grad_ref, down_ref, gain_one_ref,
    gain_two_ref, bias_ref, cont_ref, normed_out, in_out, out_out, proj_out, att_ref, log_ref,
    mixed_rows, middle_ref, normed_two_ref, up_out, up_two, up_one, down_got, grad_got, slot, in_buf,
    out_buf, up_buf, normed, proj, mixed, decay_scr, send, recv, local,
):
    w, z = lax.axis_index("wide"), lax.axis_index("narrow")
    line = [flipped(z, k) for k in range(4)]
    rows, width = x_ref.shape
    own_width = heads * head_size
    part_rows = out_ref.shape[0]
    is_middle = (z == 1) | (z == 2)
    is_end = (z == 0) | (z == 3)
    sender = Sender(send, recv)
    used = []

    def local_copy(src, dst):
        copy = pltpu.make_async_copy(src, dst, local.at[len(used)])
        used.append(copy)
        return copy

    def slot_rows(n):
        return slot.at[pl.ds(pl.multiple_of(n * rows, rows), rows), :]

    def weight_rows(ref, w_of, z_of):
        at = (w_of * 4 + z_of) * part_rows
        return ref.at[pl.ds(pl.multiple_of(at, 16), part_rows), :]

    def wide_rows(ref, w_of):
        at = w_of * 4 * part_rows
        return ref.at[pl.ds(pl.multiple_of(at, 16), 4 * part_rows), :]

    def by_rows(ref):
        return (
            (lambda k: wide_rows(ref, flipped(w, k))),
            (lambda k, to: wide_rows(ref, flipped(w, k))),
        )

    unit = up_buf.shape[2] // 4

    def in_pieces(n):
        target = lambda at, size: in_buf.at[
            pl.ds(pl.multiple_of((w * 4 + z) * part_rows, 16), part_rows), pl.ds(at, size)
        ]
        for group in range(4):
            at = pl.multiple_of(group * width + n * own_width, LANES)
            yield in_ref.at[:, pl.ds(at, own_width)], target(group * own_width, own_width)
        yield small_ref.at[n], target(4 * own_width, LANES)

    def up_pieces(n):
        for group in range(4):
            at = pl.multiple_of((group * wide + n) * unit, LANES)
            yield up_ref.at[:, pl.ds(at, unit)], up_buf.at[w, :, pl.ds(group * unit, unit)]

    own_in = [local_copy(*piece) for piece in in_pieces(z)]
    own_up = [local_copy(*piece) for piece in up_pieces(w)]
    own_out = local_copy(out_ref, weight_rows(out_buf, w, z))
    own_x = local_copy(x_ref, slot_rows(z))
    for copy in used:
        copy.start()

    index = w * 4 + z
    down_wide = lax.div(lax.rem(index, 2 * wide), 2)
    down_narrow = lax.rem(index, 2) + 2 * lax.div(index, 2 * wide)
    from_index = 2 * wide * lax.div(z, 2) + 2 * w + lax.rem(z, 2)
    from_wide_index, from_narrow_index = lax.div(from_index, 4), lax.rem(from_index, 4)
    moves = jnp.logical_not((down_wide == w) & (down_narrow == z))
    down_push = sender.plan(
        down_ref, down_got, {"wide": down_wide, "narrow": down_narrow}
    )
    down_stay = local_copy(down_ref, down_got)

    barrier = pltpu.get_barrier_semaphore()
    partners = [narrow_device(line[k]) for k in (1, 2, 3)]
    partners += [wide_device(flipped(w, k)) for k in range(1, wide)]
    for device in partners:
        pl.semaphore_signal(barrier, inc=1, device_id=device, device_id_type=MESH)

    @pl.when(moves)
    def _():
        for device in (
            {"wide": from_wide_index, "narrow": from_narrow_index},
            {"wide": down_wide, "narrow": down_narrow},
        ):
            pl.semaphore_signal(barrier, inc=1, device_id=device, device_id_type=MESH)
        pl.semaphore_wait(barrier, len(partners) + 2)

    @pl.when(jnp.logical_not(moves))
    def _():
        pl.semaphore_wait(barrier, len(partners))

    ins = [
        sender.plan(*piece, narrow_device(line[k])) for k in (2, 3, 1) for piece in in_pieces(line[k])
    ]
    outs = [
        sender.plan(out_ref, weight_rows(out_buf, w, z), narrow_device(line[k])) for k in (2, 1)
    ]
    out_middle = sender.plan(out_ref, weight_rows(out_buf, w, z), narrow_device(line[3]))
    out_relay = sender.plan(
        weight_rows(out_buf, w, line[2]), weight_rows(out_buf, w, line[2]), narrow_device(line[1])
    )
    ups = [
        sender.plan(*piece, wide_device(flipped(w, k)))
        for k in range(1, wide)
        for piece in up_pieces(flipped(w, k))
    ]
    grads = {
        k: sender.plan(grad_ref, grad_got.at[k // 2 - 1], wide_device(flipped(w, k)))
        for k in range(2, wide, 2)
    }
    two = sender.plan(x_ref, slot_rows(z), narrow_device(line[2]))
    one = sender.plan(x_ref, slot_rows(z), narrow_device(line[1]))
    middle = sender.plan(x_ref, slot_rows(z), narrow_device(line[3]))
    relay = sender.plan(slot_rows(line[2]), slot_rows(line[2]), narrow_device(line[1]))
    in_wide = WideGather(sender, w, wide, *by_rows(in_buf))
    out_wide = WideGather(sender, w, wide, *by_rows(out_buf))
    up_steps = [
        sender.plan(up_buf, up_two, narrow_device(line[2])),
        sender.plan(up_buf, up_one, narrow_device(line[1])),
    ]
    mixes = [
        sender.plan(
            mixed.at[pl.ds(pl.multiple_of(line[k] * rows, rows), rows), :],
            mixed_rows.at[:, pl.ds(pl.multiple_of(z * own_width, LANES), own_width)],
            narrow_device(line[k]),
        )
        for k in (2, 3, 1)
    ]

    for copy in ins + outs + ups:
        copy.start()
    for copy in own_in:
        copy.wait()
    for copy in ins:
        copy.wait_recv()
    in_wide.start()
    two.start()
    one.start()
    own_out.wait()
    outs[0].wait_recv()

    @pl.when(is_middle)
    def _():
        out_relay.start()
        out_middle.start()

    in_wide.pass_on()
    outs[1].wait_recv()

    @pl.when(is_middle)
    def _():
        out_middle.wait_recv()

    @pl.when(is_end)
    def _():
        out_relay.wait_recv()

    out_wide.start()
    for k in diagonal_steps(wide):
        grads[k].start()
    two.wait_recv()

    @pl.when(is_middle)
    def _():
        relay.start()
        middle.start()

    for copy in own_up:
        copy.wait()
    for copy in ups:
        copy.wait_recv()
    up_back = local_copy(up_buf, up_out)
    up_back.start()
    in_wide.received()
    in_back = local_copy(in_buf, in_out)
    in_back.start()
    own_x.wait()

    def project(t, carry):
        @pl.when(t == 2)
        def _():
            one.wait_recv()

        @pl.when((t == 3) & is_middle)
        def _():
            middle.wait_recv()

        @pl.when((t == 3) & is_end)
        def _():
            relay.wait_recv()

        @pl.when(t == 3)
        def _():
            for copy in up_steps:
                copy.start()
            for k in straight_steps(wide):
                grads[k].start()

        @pl.when((t == 3) & moves)
        def _():
            down_push.start()

        @pl.when((t == 3) & jnp.logical_not(moves))
        def _():
            down_stay.start()

        n = jnp.where(t == 0, z, jnp.where(t == 1, line[2], jnp.where(t == 2, line[1], line[3])))
        at = pl.ds(pl.multiple_of(n * rows, rows), rows)
        values = slot[at, :].astype(F32)
        low = (values * rms_factor(values) * gain_one_ref[...].reshape(1, width)).astype(BF16)
        normed[at, :] = low
        proj[at, :] = dot_f32(low, in_buf[...])
        return carry

    lax.fori_loop(0, 4, project, 0)
    normed_back = local_copy(normed, normed_out)
    proj_back = local_copy(proj, proj_out)
    normed_back.start()
    proj_back.start()

    cont = cont_ref[...]
    groups = own_width // LANES
    small_low = small_columns(proj.at[:, pl.ds(4 * own_width, LANES)], bias_ref)
    decay_scr[...] = decay_of(small_low, cont)

    def attend(pair, carry):
        def at(group):
            return pl.ds(pl.multiple_of((group * groups + pair) * LANES, LANES), LANES)

        forward_pair(
            pair, heads, head_size, block, proj.at[:, at(0)], proj.at[:, at(1)], proj.at[:, at(2)],
            proj.at[:, at(3)], small_low, cont, decay_scr[...], mixed.at[:, at(0)],
            att_ref.at[:, at(0)], log_ref.at[:, at(0)],
        )
        return carry

    lax.fori_loop(0, groups, attend, 0)
    for copy in mixes:
        copy.start()
    out_wide.pass_on()
    mixed_rows[:, pl.ds(pl.multiple_of(z * own_width, LANES), own_width)] = mixed[
        pl.ds(pl.multiple_of(z * rows, rows), rows), :
    ]
    out_wide.received()
    out_back = local_copy(out_buf, out_out)
    out_back.start()
    for copy in mixes:
        copy.wait_recv()
    inputs = slot[pl.ds(pl.multiple_of(z * rows, rows), rows), :].astype(F32)
    values = inputs + dot_f32(mixed_rows[...], out_buf[...])
    middle_ref[...] = values
    normed_two_ref[...] = (values * rms_factor(values) * gain_two_ref[...].reshape(1, width)).astype(BF16)

    for copy in up_steps:
        copy.wait()
    for copy in grads.values():
        copy.wait()

    @pl.when(moves)
    def _():
        down_push.wait()

    @pl.when(jnp.logical_not(moves))
    def _():
        down_stay.wait()

    @pl.when(is_middle)
    def _():
        relay.wait_send()
        middle.wait_send()
        out_relay.wait_send()
        out_middle.wait_send()

    for copy in ins + outs + ups + [two, one] + mixes:
        copy.wait_send()
    in_wide.sent()
    out_wide.sent()
    for copy in (up_back, in_back, normed_back, proj_back, out_back):
        copy.wait()


def first_part(
    tokens, in_weight, small, out_weight, gate_up_weight, cotangent, down_weight, gain_one, gain_two, bias,
    cont, wide, heads, head_size, block, collective_id,
):
    rows, width = tokens.shape
    slot, own_width = 4 * rows, heads * head_size
    columns = 4 * own_width + LANES
    steps = 8 * wide + 40
    up_shape = (wide, gate_up_weight.shape[0], gate_up_weight.shape[1] // wide)
    shape = jax.ShapeDtypeStruct
    return pl.pallas_call(
        functools.partial(first_kernel, wide, heads, head_size, block),
        out_shape=[
            shape((slot, width), BF16), shape((width, columns), BF16), shape((width, width), BF16),
            shape((slot, columns), F32), shape((slot, own_width), BF16),
            shape((slot, own_width), F32), shape((rows, width), BF16), shape((rows, width), F32),
            shape((rows, width), BF16), shape(up_shape, BF16), shape(up_shape, BF16),
            shape(up_shape, BF16), shape(down_weight.shape, BF16),
            shape((wide // 2 - 1, rows, width), BF16),
        ],
        in_specs=[ANY] * 7 + [VMEM] * 4,
        out_specs=[ANY] * 4 + [VMEM] * 5 + [ANY] * 5,
        scratch_shapes=[
            pltpu.VMEM((slot, width), BF16), pltpu.VMEM((width, columns), BF16),
            pltpu.VMEM((width, width), BF16), pltpu.VMEM(up_shape, BF16),
            pltpu.VMEM((slot, width), BF16), pltpu.VMEM((slot, columns), F32),
            pltpu.VMEM((slot, own_width), BF16), pltpu.VMEM((slot, LANES), F32),
            DMA((steps,)), DMA((steps,)), DMA((20,)),
        ],
        compiler_params=pltpu.CompilerParams(
            collective_id=collective_id, has_side_effects=True, vmem_limit_bytes=60 * 2**20
        ),
    )(
        tokens, in_weight, small, out_weight, gate_up_weight, cotangent, down_weight, gain_one,
        gain_two, bias, cont,
    )


def second_kernel(
    wide, src_ref, grad_ref, far_grads, up_ref, up_two, up_one, down_ref, middle_ref, mixed_ref, out_ref,
    gain_ref, grad_middle, gain_grad, slot_grad, branch_sum, up_src, down_src, up_acc, down_acc,
    up_grad_out, down_grad_out, out_part, branch_near, normed, grads, up_full, down_full, hidden, mid,
    rows_buf, core_buf, far_buf, branch_buf, up_join, up_mid, down_join, down_mid, up_grad, down_grad,
    grad_mixed, mixed_buf, send, recv, local,
):
    w, z = lax.axis_index("wide"), lax.axis_index("narrow")
    line = [flipped(z, k) for k in range(4)]
    rows, width = src_ref.shape
    half = wide // 2
    size = hidden.shape[1]
    unit, part = up_src.shape[1], down_src.shape[1]
    is_middle = (z == 1) | (z == 2)
    is_end = (z == 0) | (z == 3)
    sender = Sender(send, recv)
    sibling = wide_device(flipped(w, 1))

    def at_place(ref, place):
        return ref.at[pl.ds(pl.multiple_of(place * rows, rows), rows), :]

    up_at = lambda n: up_full.at[:, n]
    down_at = lambda n: down_full.at[n]
    moves = [
        (src_ref, at_place(normed, 0)), (up_ref, up_at(z)), (up_two, up_at(line[2])),
        (up_one, up_at(line[1])), (down_ref, down_at(z)), (grad_ref, at_place(grads, 0)),
    ] + [(far_grads.at[n - 1], at_place(grads, n)) for n in range(1, half)]
    own = [pltpu.make_async_copy(src, dst, local.at[n]) for n, (src, dst) in enumerate(moves)]
    for copy in own:
        copy.start()
    greet(
        [wide_device(flipped(w, k)) for k in wide_steps(wide)]
        + [narrow_device(line[k]) for k in (1, 2, 3)]
    )
    gather = WideGather(
        sender, w, wide, lambda k: src_ref if k == 0 else at_place(normed, place_of(k, wide)),
        lambda k, to: at_place(normed, place_of(k ^ to, wide)),
    )
    middle = sender.plan(up_ref, up_at(z), narrow_device(line[3]))
    relay = sender.plan(up_two, up_at(line[2]), narrow_device(line[1]))
    down_two = sender.plan(down_ref, down_at(z), narrow_device(line[2]))
    down_one = sender.plan(down_ref, down_at(z), narrow_device(line[1]))
    down_middle = sender.plan(down_ref, down_at(z), narrow_device(line[3]))
    down_relay = sender.plan(down_at(line[2]), down_at(line[2]), narrow_device(line[1]))
    passed = [
        sender.plan(
            grad_ref if n == 0 else far_grads.at[n - 1], at_place(grads, half + n), sibling
        )
        for n in range(half)
    ]
    core = [
        sender.plan(at_place(rows_buf, half + n), core_buf.at[n], sibling) for n in range(half)
    ]
    far = [
        sender.plan(at_place(rows_buf, n), far_buf.at[n - 1], wide_device(flipped(w, 2 * n)))
        for n in range(1, half)
    ]
    branch_core = [
        sender.plan(at_place(normed, half + n), branch_buf.at[n], sibling) for n in range(half)
    ]

    def up_share(n):
        return up_grad.at[:, pl.ds(pl.multiple_of(n * unit, unit), unit)]

    def down_share(n):
        return down_grad.at[:, pl.ds(pl.multiple_of(n * part, part), part)]

    down_joined = sender.plan(down_share(line[3]), down_join, narrow_device(line[1]))
    down_direct = sender.plan(down_share(line[3]), down_mid, narrow_device(line[3]))
    up_joined = sender.plan(up_share(line[3]), up_join, narrow_device(line[1]))
    up_direct = sender.plan(up_share(line[3]), up_mid, narrow_device(line[3]))
    own_width = width // 4
    mixes = [
        sender.plan(
            grad_mixed.at[:, pl.ds(pl.multiple_of(line[k] * own_width, LANES), own_width)],
            slot_grad.at[pl.ds(pl.multiple_of(z * rows, rows), rows), :], narrow_device(line[k]),
        )
        for k in (2, 3, 1)
    ]
    near = [
        sender.plan(branch_sum.at[k // 2], branch_near.at[n], wide_device(flipped(w, k)))
        for n, k in enumerate(straight_steps(wide))
    ]

    gather.start()

    @pl.when(is_middle)
    def _():
        relay.start()
        middle.start()

    down_two.start()
    down_two.wait_recv()

    @pl.when(is_middle)
    def _():
        down_relay.start()
        down_middle.start()

    down_one.start()
    for copy in passed:
        copy.start()
    for copy in own[:4]:
        copy.wait()

    @pl.when(is_middle)
    def _():
        middle.wait_recv()

    @pl.when(is_end)
    def _():
        relay.wait_recv()

    up_shape = (width, 4 * unit)
    down_shape = (size, width)

    def arriving(t, carry):
        @pl.when(t == 1)
        def _():
            gather.first[1].wait_recv()

        for n, k in enumerate(gather.far):

            @pl.when(t == 2 + n)
            def _():
                gather.first[k].wait_recv()
                gather.second[k].start()

            @pl.when(t == half + 1 + n)
            def _():
                gather.second[k].wait_recv()

        place = jnp.where(t < 2, t * half, jnp.where(t < half + 1, t - 1, t))
        at = pl.ds(pl.multiple_of(place * rows, rows), rows)
        mid[at, :] = dot_f32(normed[at, :], up_full[...].reshape(up_shape)).astype(BF16)
        return carry

    lax.fori_loop(0, wide, arriving, 0)
    for copy in own[4:]:
        copy.wait()
    for copy in passed + [down_one]:
        copy.wait_recv()

    @pl.when(is_middle)
    def _():
        down_middle.wait_recv()

    @pl.when(is_end)
    def _():
        down_relay.wait_recv()

    def block(t, carry):
        pick = half - 1 - lax.div(t, 2)
        place = jnp.where(lax.rem(t, 2) == 0, half + pick, pick)
        at = pl.ds(pl.multiple_of(place * rows, rows), rows)
        gate_up = mid[at, :].astype(F32)
        grad_hidden = dot_f32(grads[at, :], down_full[...].reshape(down_shape), ((1,), (1,)))
        gate, up = gate_up[:, :size], gate_up[:, size:]
        opened = jax.nn.sigmoid(gate)
        acted = gate * opened
        hidden[at, :] = (acted * up).astype(BF16)
        mid[at, :size] = (grad_hidden * up * (opened * (1.0 + gate * (1.0 - opened)))).astype(BF16)
        mid[at, size:] = (grad_hidden * acted).astype(BF16)
        rows_buf[at, :] = dot_f32(mid[at, :], up_full[...].reshape(up_shape), ((1,), (1,))).astype(
            BF16
        )
        for n in range(half):

            @pl.when(t == 2 * (half - 1 - n))
            def _():
                core[n].start()

        for n in range(half):

            @pl.when(t == 2 * (half - 1 - n) + 1)
            def _():
                core[n].wait_recv()
                total = rows_buf[n * rows : (n + 1) * rows, :].astype(F32) + core_buf[n].astype(F32)
                rows_buf[n * rows : (n + 1) * rows, :] = total.astype(BF16)
                if n > 0:
                    far[n - 1].start()

        return carry

    lax.fori_loop(0, wide, block, 0)

    step = min(256, size)
    for n in range(size // step):
        cut = slice(n * step, (n + 1) * step)
        down_grad[cut, :] = dot_f32(hidden[:, cut], grads[...], ((0,), (0,))).astype(BF16)

    @pl.when(is_end)
    def _():
        down_joined.start()

    @pl.when(is_middle)
    def _():
        down_direct.start()

    reloads = [
        pltpu.make_async_copy(out_ref, grads.at[pl.ds(0, width), :], local.at[9 + half]),
        pltpu.make_async_copy(grad_ref, grads.at[pl.ds(width, rows), :], local.at[10 + half]),
        pltpu.make_async_copy(mixed_ref, mixed_buf, local.at[11 + half]),
        pltpu.make_async_copy(middle_ref, grad_middle, local.at[12 + half]),
    ]
    for copy in reloads:
        copy.start()

    def up_rows(n, carry):
        at = pl.ds(pl.multiple_of(n * 256, 256), 256)
        up_grad[at, :] = dot_f32(normed[:, at], mid[...], ((0,), (0,))).astype(BF16)
        return carry

    lax.fori_loop(0, width // 256, up_rows, 0)

    @pl.when(is_end)
    def _():
        up_joined.start()

    @pl.when(is_middle)
    def _():
        up_direct.start()

    backs = [
        pltpu.make_async_copy(up_grad, up_grad_out, local.at[5 + half]),
        pltpu.make_async_copy(down_grad, down_grad_out, local.at[6 + half]),
        pltpu.make_async_copy(up_share(line[2]), up_src, local.at[7 + half]),
        pltpu.make_async_copy(down_share(line[2]), down_src, local.at[8 + half]),
    ]
    for copy in backs:
        copy.start()
    gather.sent()

    def branch(t, carry):
        place = lax.rem(t + half, wide)
        at = pl.ds(pl.multiple_of(place * rows, rows), rows)
        normed[at, :] = dot_f32(hidden[at, :], down_full[...].reshape(down_shape)).astype(BF16)
        for n in range(half):

            @pl.when(t == n)
            def _():
                branch_core[n].start()

        return carry

    lax.fori_loop(0, wide, branch, 0)
    for n in range(half):
        branch_core[n].wait_recv()
        total = normed[n * rows : (n + 1) * rows, :].astype(F32) + branch_buf[n].astype(F32)
        branch_sum[n] = total.astype(BF16)

    total = rows_buf[:rows, :].astype(F32)
    for n in range(1, half):
        far[n - 1].wait_recv()
        total = total + far_buf[n - 1].astype(F32)
    for copy in core + far:
        copy.wait_send()
    for copy in reloads:
        copy.wait()
    values = grad_middle[...]
    factor = rms_factor(values)
    values = values * factor
    gain_grad[...] = jnp.broadcast_to(
        jnp.sum(total * values, axis=0, keepdims=True), gain_grad.shape
    )
    total = total * gain_ref[...].reshape(1, width)
    inner = jnp.mean(total * values, axis=-1, keepdims=True)
    total = grads[width : width + rows, :].astype(F32) + factor * (total - values * inner)
    grad_middle[...] = total
    branch_grad = total.astype(BF16)
    grad_mixed[...] = dot_f32(branch_grad, grads[:width, :], ((1,), (1,))).astype(BF16)
    for copy in mixes + near:
        copy.start()
    slot_grad[pl.ds(pl.multiple_of(z * rows, rows), rows), :] = grad_mixed[
        :, pl.ds(pl.multiple_of(z * own_width, LANES), own_width)
    ]
    for n in range(width // 256):
        cut = slice(n * 256, (n + 1) * 256)
        rows_buf[cut, :] = dot_f32(mixed_buf[:, cut], branch_grad, ((0,), (0,))).astype(BF16)
    out_back = pltpu.make_async_copy(
        rows_buf.at[pl.ds(0, width), :], out_part, local.at[13 + half]
    )
    out_back.start()
    for copy in backs:
        copy.wait()
    up_acc[...] = up_grad[:, pl.ds(pl.multiple_of(z * unit, unit), unit)]
    down_acc[...] = down_grad[:, pl.ds(pl.multiple_of(z * part, part), part)]

    @pl.when(is_middle)
    def _():
        down_joined.wait_recv()
        down_src[...] = (down_src[...].astype(F32) + down_join[...].astype(F32)).astype(BF16)
        up_joined.wait_recv()
        up_src[...] = (up_src[...].astype(F32) + up_join[...].astype(F32)).astype(BF16)
        down_direct.wait()
        down_acc[...] = (down_acc[...].astype(F32) + down_mid[...].astype(F32)).astype(BF16)
        up_direct.wait()
        up_acc[...] = (up_acc[...].astype(F32) + up_mid[...].astype(F32)).astype(BF16)
        for copy in (relay, middle, down_relay, down_middle):
            copy.wait_send()

    @pl.when(is_end)
    def _():
        down_joined.wait_send()
        up_joined.wait_send()

    for copy in mixes + near:
        copy.wait()
    out_back.wait()
    for copy in passed + branch_core + [down_two, down_one]:
        copy.wait_send()


def second_part(
    normed, grad, far_grads, ups, down, middle, mixed_rows, out_full, gain, collective_id
):
    rows, width = normed.shape
    half = far_grads.shape[0] + 1
    wide = 2 * half
    wide_of_up, part_rows, mid_size = ups[0].shape
    down_rows = down.shape[0]
    size, unit, part = mid_size // 2, mid_size // 4, width // 4
    steps = 9 + 2 * wide + 4 * half + 8
    total = wide * rows
    shape = jax.ShapeDtypeStruct
    vmem = lambda *dims: pltpu.VMEM(dims, BF16)
    return pl.pallas_call(
        functools.partial(second_kernel, wide),
        out_shape=[
            shape((rows, width), F32), shape((8, width), F32), shape((4 * rows, part), BF16),
            shape((half, rows, width), BF16),
            shape((width, unit), BF16), shape((size, part), BF16),
            shape((width, unit), BF16), shape((size, part), BF16),
            shape((width, mid_size), BF16), shape((size, width), BF16),
            shape((width, width), BF16), shape((len(straight_steps(wide)), rows, width), BF16),
        ],
        in_specs=[ANY] * 10 + [VMEM],
        out_specs=[VMEM] * 8 + [ANY] * 4,
        scratch_shapes=[
            vmem(total, width), vmem(total, width), vmem(wide, 4, part_rows, mid_size),
            vmem(4, down_rows, width), vmem(total, size), vmem(total, mid_size), vmem(total, width),
            vmem(half, rows, width), vmem(half - 1, rows, width), vmem(half, rows, width),
            vmem(width, unit), vmem(width, unit), vmem(size, part), vmem(size, part),
            vmem(width, mid_size), vmem(size, width), vmem(rows, width), vmem(rows, width),
            DMA((steps,)), DMA((steps,)), DMA((14 + half,)),
        ],
        compiler_params=pltpu.CompilerParams(
            collective_id=collective_id, has_side_effects=True, vmem_limit_bytes=63 * 2**20
        ),
    )(
        normed, grad, far_grads, *ups, down, middle, mixed_rows, out_full,
        gain,
    )


def add_up(parts):
    total = parts[0].astype(F32)
    for part in parts[1:]:
        total = total + part.astype(F32)
    return total


def on_device(
    tokens, gain_one, in_weight, forget_bias, out_weight, gain_two, gate_up_weight, down_weight,
    segment_ids, cotangent,
):
    wide, narrow = lax.axis_size("wide"), lax.axis_size("narrow")
    w, z = lax.axis_index("wide"), lax.axis_index("narrow")
    rows, width = tokens.shape
    slot = rows * narrow
    heads = forget_bias.shape[0]
    head_size = width // heads
    own_heads = heads // narrow
    own_width = own_heads * head_size
    part_rows = in_weight.shape[0]
    hidden_all = down_weight.shape[0] * wide * narrow
    unit = hidden_all // (2 * wide)
    columns = 4 * own_width + LANES
    base = 4 * width

    small = in_weight[:, base:].reshape(part_rows, 3, narrow, own_heads)
    small = jnp.moveaxis(small, 2, 0).reshape(narrow, part_rows, 3 * own_heads)
    small = jnp.pad(small, ((0, 0), (0, 0), (0, LANES - 3 * own_heads)))
    aligned = unit % LANES == 0

    def split_weights(sources, targets):
        copies = [(sources[1], targets[0].at[:, :, pl.ds(4 * own_width, LANES)])]
        for n in range(narrow):
            for group in range(4):
                copies.append(
                    (
                        sources[0].at[:, pl.ds(group * width + n * own_width, own_width)],
                        targets[0].at[n, :, pl.ds(group * own_width, own_width)],
                    )
                )
        return copies

    shapes = [
        jax.ShapeDtypeStruct((narrow, part_rows, columns), BF16),
        jax.ShapeDtypeStruct((wide, part_rows, 4 * unit), BF16),
    ]
    copies = 4 * narrow + 1
    fused = aligned and part_rows % 16 == 0
    if not fused:
        in_parts = local_copies(split_weights, copies, [in_weight, small], shapes[:1], False)[0]
        up_parts = jnp.moveaxis(gate_up_weight.reshape(part_rows, 4, wide, unit), 2, 0)
        up_parts = up_parts.reshape(wide, part_rows, 4 * unit)

    segments = segment_ids[0]
    joined = (segments[1:] == segments[:-1]).astype(F32)
    cont = jnp.concatenate([jnp.zeros((1,), F32), joined])
    cont = jnp.broadcast_to(cont[:, None], (slot, LANES))
    own_bias = lax.dynamic_slice_in_dim(forget_bias, z * own_heads, own_heads)
    bias = jnp.broadcast_to(jnp.pad(own_bias, (0, LANES - own_heads))[None], (8, LANES))
    block = min(256, slot)
    def row_block(ref, n):
        return ref.at[pl.ds(pl.multiple_of(n * rows, rows), rows), :]

    def column_block(ref, n):
        return ref.at[:, pl.ds(pl.multiple_of(n * own_width, LANES), own_width)]

    straight, diagonal = straight_steps(wide), diagonal_steps(wide)
    inputs = tokens.astype(F32)
    half = wide // 2
    if fused:
        (
            normed_one, in_full, out_full, projected, attended, logs, mixed_rows, middle, normed_two,
            up_block, up_two, up_one, down_block, grad_got,
        ) = first_part(
            tokens, in_weight, small, out_weight, gate_up_weight, cotangent, down_weight, gain_one,
            gain_two, bias, cont, wide, own_heads, head_size, block, 0,
        )
    else:
        pairs = []
        for i in range(wide * narrow):
            to_wide = (i % (2 * wide)) // 2
            to_narrow = i % 2 + 2 * (i // (2 * wide))
            pairs.append((i, to_wide * narrow + to_narrow))
        down_block = lax.ppermute(down_weight, ("wide", "narrow"), pairs)

        slot_tokens, in_full, out_full, up_block, grad_far = gather_all(
            tokens, in_parts, out_weight, up_parts, cotangent
        )
        slot_tokens = slot_tokens.reshape(slot, width)
        in_full = in_full.reshape(width, columns)
        out_full = out_full.reshape(width, width)

        up_two = on_line(up_block, LINE_TWO)
        up_one = on_line(up_block, LINE_ONE)

        slot_floats = slot_tokens.astype(F32)
        normed_one = (slot_floats * rms_factor(slot_floats) * gain_one).astype(BF16)
        projected = dot_f32(normed_one, in_full)

        mixed, attended, logs = attention_forward(
            projected, bias, cont, own_heads, head_size, block
        )

        mixed_rows, *grad_near = exchange(
            mixed, row_block, column_block, (rows, width), straight, [cotangent] * len(straight), 1
        )
        grads = {0: cotangent}
        grads.update({k: grad_near[n] for n, k in enumerate(straight)})
        grads.update({k: grad_far[n] for n, k in enumerate(diagonal)})
        grads = [grads[k] for k in range(0, wide, 2)]
        down_block = follow(down_block, mixed_rows)
        down_two = on_line(down_block, LINE_TWO)
        down_one = on_line(down_block, LINE_ONE)
        middle = inputs + dot_f32(mixed_rows, out_full)
        normed_two = (middle * rms_factor(middle) * gain_two).astype(BF16)

    if fused:
        (
            grad_middle, grad_gain_two, slot_grad, branch_sum, up_src, down_src, up_acc, down_acc,
            up_one, down_one, out_part, branch_near,
        ) = second_part(
            normed_two, cotangent, grad_got, [up_block, up_two, up_one], down_block, middle,
            mixed_rows, out_full, gain_two, 2,
        )
        grad_gain_two = grad_gain_two[0]
    else:
        ups = [up_block] + [follow(piece, normed_two) for piece in (up_two, up_one)]
        plane_normed, plane_grad, up_full, down_full = gather_rows(
            normed_two, grads, ups, [down_block, down_two, down_one], 2
        )
        plane_normed = plane_normed.reshape(wide * rows, width)
        plane_grad = plane_grad.reshape(wide * rows, width)
        up_full = up_full.reshape(width, 4 * unit)
        down_full = down_full.reshape(2 * unit, width)
        hidden, gate_up_grad, norm_even, norm_odd, branch = feed_forward(
            plane_normed, plane_grad, up_full, down_full, rows
        )
        grad_up_full = dot_f32(plane_normed, gate_up_grad, ((0,), (0,))).astype(BF16)
        grad_down_full = dot_f32(hidden, plane_grad, ((0,), (0,))).astype(BF16)
        if unit % LANES:
            grouped = grad_up_full.reshape(width, 4, unit)
            grad_up_full = jnp.pad(grouped, ((0, 0), (0, 0), (0, LANES - unit))).reshape(width, -1)
        branch = branch.reshape(wide, rows, width)
        fits = wide <= 8
        norm_got = along_wide(norm_odd.reshape(half, rows, width), 1, wide)
        (
            grad_normed_two, branch_sum, up_src, down_src, up_one, down_one, up_acc, down_acc,
        ) = middle_sums(
            norm_even.reshape(half, rows, width), norm_got,
            branch if fits else branch[:2, :16], grad_up_full, grad_down_full, 6,
        )
        if not fits:
            received = along_wide(branch[half:], 1, wide)
            branch_sum = (branch[:half].astype(F32) + received.astype(F32)).astype(BF16)
        upstream = cotangent.astype(F32)
        grad_middle_norm, grad_gain_two = rms_back(middle, gain_two, grad_normed_two)
        grad_middle = upstream + grad_middle_norm
        branch_one_grad = grad_middle.astype(BF16)
        grad_mixed = dot_f32(branch_one_grad, out_full, ((1,), (1,))).astype(BF16)
        slot_grad, *branch_near = exchange(
            grad_mixed, column_block, row_block, (slot, own_width), straight,
            [branch_sum[k // 2] for k in straight], 3,
        )
        branch_near = jnp.stack(branch_near)
        out_part = dot_f32(mixed_rows, branch_one_grad, ((0,), (0,))).astype(BF16)
    wide_rows = width // wide
    (
        unused, bias_grad, norm_part, in_part, grad_out, up_two, down_two, up_one, down_one,
        branch_far,
    ) = attention_backward(
        projected, bias, cont, attended, logs, slot_grad, in_full, normed_one,
        [up_src, down_src, up_one, down_one], out_part.reshape(wide, wide_rows, width), branch_sum,
        own_heads, head_size, block, 7,
    )
    branches = [branch_sum, branch_near, branch_far]
    all_bias = lax.dynamic_update_slice(
        jnp.zeros((width,), F32), bias_grad[0, :own_heads], (z * own_heads,)
    )
    small = jnp.stack([jnp.zeros((width,), F32), grad_gain_two, all_bias])
    small = jnp.pad(small, ((0, 5), (0, 0)))
    low = lambda part: part.astype(BF16)
    output, grad_tokens, grad_in, grad_up, grad_down, totals = last_part(
        norm_part, in_part.reshape(wide, wide_rows, columns), [low(up_acc), up_one, up_two],
        [low(down_acc), down_one, down_two], branches, tokens, middle, grad_middle, gain_one, small,
        own_width, own_heads, (base + 3 * heads) // narrow, 4,
    )
    if not aligned:
        grad_up = grad_up.reshape(wide_rows, wide, LANES)[:, :, :unit]
        grad_up = grad_up.reshape(wide_rows, wide * unit)
    return (
        output,
        grad_tokens,
        totals[0],
        grad_in,
        totals[2, :heads],
        grad_out,
        totals[1],
        grad_up,
        grad_down,
    )


def solution(mesh):
    both = ("wide", "narrow")
    in_specs = (
        P(both, None), P(), P(both, None), P(), P(both, None), P(), P(both, None), P(both, None),
        P("wide", None), P(both, None),
    )
    out_specs = (
        P(both, None), P(both, None), P(), P("wide", "narrow"), P(), P("wide", "narrow"), P(),
        P("wide", "narrow"), P("wide", "narrow"),
    )
    return jax.shard_map(
        on_device, mesh=mesh, in_specs=in_specs, out_specs=out_specs, check_vma=False
    )
```

```python
import functools

import jax
import jax.numpy as jnp
from jax import lax
from jax.experimental import pallas as pl
from jax.experimental.pallas import tpu as pltpu
from jax.sharding import PartitionSpec as P

EPSILON = 1e-06
SEPARATE = 128.0
F32 = jnp.float32
BF16 = jnp.bfloat16
LANES = 128
EXACT = lax.Precision.HIGHEST
ANY = pl.BlockSpec(memory_space=pltpu.HBM)


def dot_f32(left, right, dims=((1,), (0,))):
    return lax.dot_general(left, right, (dims, ((), ())), preferred_element_type=F32)


def along_wide(block, flip, wide):
    return lax.ppermute(block, "wide", [(i, i ^ flip) for i in range(wide)])


def copy_kernel(plan, count, *refs):
    sources, targets, sems = refs[:count], refs[count:-1], refs[-1]
    copies = plan(sources, targets)

    def each(act):
        for n, (src, dst, *when) in enumerate(copies):
            copy = pltpu.make_async_copy(src, dst, sems.at[n])
            if when:
                pl.when(when[0])(functools.partial(act, copy))
            else:
                act(copy)

    each(lambda copy: copy.start())
    each(lambda copy: copy.wait())


def local_copies(plan, copies, sources, shapes, gather):
    moved = sum(s.size * s.dtype.itemsize for s in shapes)
    inside = pl.BlockSpec(memory_space=pltpu.VMEM)
    return pl.pallas_call(
        functools.partial(copy_kernel, plan, len(sources)),
        out_shape=shapes,
        in_specs=[ANY if gather else inside] * len(sources),
        out_specs=[inside if gather else ANY] * len(shapes),
        compiler_params=pltpu.CompilerParams(vmem_limit_bytes=16 * 2**20),
        scratch_shapes=[pltpu.SemaphoreType.DMA((copies,))],
        cost_estimate=pl.CostEstimate(flops=0, bytes_accessed=2 * moved, transcendentals=0),
    )(*sources)


def flipped(me, k):
    out = me
    bit = 1
    while bit <= k:
        if k & bit:
            out = out + bit - 2 * bit * lax.rem(lax.div(out, bit), 2)
        bit *= 2
    return out


LINE_TWO = [(0, 2), (2, 0), (1, 3), (3, 1)]
LINE_ONE = [(0, 1), (1, 0), (2, 3), (3, 2)]
LINE_MIDDLE = [(1, 2), (2, 1)]
LINE_OUT = [(2, 3), (1, 0)]
LINE_IN = [(0, 1), (3, 2)]


def on_line(block, pairs):
    return lax.ppermute(block, "narrow", pairs)


def follow(array, *earlier):
    return lax.optimization_barrier((array, *earlier))[0]


MESH = pl.DeviceIdType.MESH
VMEM = pl.BlockSpec(memory_space=pltpu.VMEM)
DMA = pltpu.SemaphoreType.DMA


def greet(devices):
    barrier = pltpu.get_barrier_semaphore()
    for device in devices:
        pl.semaphore_signal(barrier, inc=1, device_id=device, device_id_type=MESH)
    pl.semaphore_wait(barrier, len(devices))


class Sender:
    def __init__(self, send, recv):
        self.send, self.recv, self.used = send, recv, 0

    def plan(self, src, dst, device):
        n = self.used
        self.used += 1
        return pltpu.make_async_remote_copy(
            src_ref=src, dst_ref=dst, send_sem=self.send.at[n], recv_sem=self.recv.at[n],
            device_id=device, device_id_type=MESH,
        )


def narrow_device(n):
    return {"narrow": n}


def wide_device(n):
    return {"wide": n}


def wide_steps(wide):
    return [1] + list(range(2, wide, 2))


def straight_steps(wide):
    return [k for k in range(2, wide, 2) if k & (k - 1) == 0]


def diagonal_steps(wide):
    return [k for k in range(2, wide, 2) if k & (k - 1)]


def by_device(ref, w):
    return (lambda k: ref.at[flipped(w, k)]), (lambda k, to: ref.at[flipped(w, k)])


class WideGather:
    def __init__(self, sender, w, wide, part, target):
        self.far = list(range(2, wide, 2))
        self.first = {
            k: sender.plan(part(0), target(0, k), wide_device(flipped(w, k)))
            for k in wide_steps(wide)
        }
        sibling = wide_device(flipped(w, 1))
        self.second = {k: sender.plan(part(k), target(k, 1), sibling) for k in self.far}

    def start(self):
        for k in self.far + [1]:
            self.first[k].start()

    def pass_on(self):
        for k in self.far:
            self.first[k].wait_recv()
            self.second[k].start()

    def received(self):
        self.first[1].wait_recv()
        for k in self.far:
            self.second[k].wait_recv()

    def sent(self):
        for copy in list(self.first.values()) + list(self.second.values()):
            copy.wait_send()

    def finish(self):
        self.received()
        self.sent()


def gather_kernel(
    wide, x_ref, in_ref, out_ref, up_ref, grad_ref, slot_ref, in_full, out_full, up_block, grad_far,
    send, recv, local,
):
    w, z = lax.axis_index("wide"), lax.axis_index("narrow")
    line = [flipped(z, k) for k in range(4)]
    sender = Sender(send, recv)
    own = [
        pltpu.make_async_copy(in_ref.at[z], in_full.at[w, z], local.at[0]),
        pltpu.make_async_copy(out_ref, out_full.at[w, z], local.at[1]),
        pltpu.make_async_copy(x_ref, slot_ref.at[z], local.at[2]),
        pltpu.make_async_copy(up_ref.at[w], up_block.at[w], local.at[3]),
    ]
    for copy in own:
        copy.start()
    greet(
        [narrow_device(line[k]) for k in (1, 2, 3)]
        + [wide_device(flipped(w, k)) for k in range(1, wide)]
    )
    ups = [
        sender.plan(up_ref.at[flipped(w, k)], up_block.at[w], wide_device(flipped(w, k)))
        for k in range(1, wide)
    ]
    grads = [
        sender.plan(grad_ref, grad_far.at[n], wide_device(flipped(w, k)))
        for n, k in enumerate(diagonal_steps(wide))
    ]
    is_middle = (z == 1) | (z == 2)
    is_end = (z == 0) | (z == 3)
    ins = [
        sender.plan(in_ref.at[line[k]], in_full.at[w, z], narrow_device(line[k])) for k in (2, 3, 1)
    ]
    outs = [sender.plan(out_ref, out_full.at[w, z], narrow_device(line[k])) for k in (2, 3, 1)]
    two = sender.plan(x_ref, slot_ref.at[z], narrow_device(line[2]))
    one = sender.plan(x_ref, slot_ref.at[z], narrow_device(line[1]))
    middle = sender.plan(x_ref, slot_ref.at[z], narrow_device(line[3]))
    relay = sender.plan(slot_ref.at[line[2]], slot_ref.at[line[2]], narrow_device(line[1]))
    in_wide = WideGather(sender, w, wide, *by_device(in_full, w))
    out_wide = WideGather(sender, w, wide, *by_device(out_full, w))
    for copy in ins + outs + ups:
        copy.start()
    own[0].wait()
    for copy in ins:
        copy.wait_recv()
    in_wide.start()
    two.start()
    one.start()
    own[1].wait()
    for copy in outs:
        copy.wait_recv()
    out_wide.start()
    in_wide.pass_on()
    for copy in grads:
        copy.start()
    two.wait_recv()

    @pl.when(is_middle)
    def _():
        relay.start()
        middle.start()

    out_wide.pass_on()
    one.wait_recv()
    own[2].wait()
    own[3].wait()
    for copy in ups + grads:
        copy.wait()

    @pl.when(is_middle)
    def _():
        middle.wait_recv()
        middle.wait_send()
        relay.wait_send()

    @pl.when(is_end)
    def _():
        relay.wait_recv()

    for copy in ins + outs + [two, one]:
        copy.wait_send()
    in_wide.finish()
    out_wide.finish()


def gather_all(tokens, in_parts, out_weight, up_parts, cotangent):
    narrow, wide = in_parts.shape[0], up_parts.shape[0]
    steps = 10 + 4 * wide
    shapes = [
        (narrow,) + tokens.shape, (wide,) + in_parts.shape, (wide, narrow) + out_weight.shape,
        up_parts.shape, (len(diagonal_steps(wide)),) + cotangent.shape,
    ]
    return pl.pallas_call(
        functools.partial(gather_kernel, wide),
        out_shape=[jax.ShapeDtypeStruct(shape, BF16) for shape in shapes],
        in_specs=[ANY] * 5,
        out_specs=[VMEM] * 5,
        scratch_shapes=[DMA((steps,)), DMA((steps,)), DMA((4,))],
        compiler_params=pltpu.CompilerParams(
            collective_id=0, has_side_effects=True, vmem_limit_bytes=40 * 2**20
        ),
    )(tokens, in_parts, out_weight, up_parts, cotangent)


def exchange_kernel(source, target, steps, *refs):
    count = len(steps)
    src_ref, sides, dst_ref = refs[0], refs[1 : 1 + count], refs[1 + count]
    got = refs[2 + count : 2 + 2 * count]
    send, recv, local = refs[2 + 2 * count :]
    w, z = lax.axis_index("wide"), lax.axis_index("narrow")
    line = [flipped(z, k) for k in range(4)]
    sender = Sender(send, recv)
    own = pltpu.make_async_copy(source(src_ref, z), target(dst_ref, z), local.at[0])
    own.start()
    greet(
        [narrow_device(line[k]) for k in (1, 2, 3)] + [wide_device(flipped(w, k)) for k in steps]
    )
    copies = [
        sender.plan(source(src_ref, line[k]), target(dst_ref, z), narrow_device(line[k]))
        for k in (2, 3, 1)
    ]
    copies += [
        sender.plan(sides[n], got[n], wide_device(flipped(w, k))) for n, k in enumerate(steps)
    ]
    for copy in copies:
        copy.start()
    own.wait()
    for copy in copies:
        copy.wait()


def exchange(array, source, target, shape, steps, sides, collective_id):
    count = len(steps) + 4
    return pl.pallas_call(
        functools.partial(exchange_kernel, source, target, steps),
        out_shape=[jax.ShapeDtypeStruct(shape, array.dtype)]
        + [jax.ShapeDtypeStruct(side.shape, side.dtype) for side in sides],
        in_specs=[ANY] * (1 + len(sides)),
        out_specs=[VMEM] * (1 + len(sides)),
        scratch_shapes=[DMA((count,)), DMA((count,)), DMA((1,))],
        compiler_params=pltpu.CompilerParams(
            collective_id=collective_id, has_side_effects=True, vmem_limit_bytes=16 * 2**20
        ),
    )(array, *sides)


def place_of(k, wide):
    return k // 2 + (k % 2) * (wide // 2)


def rows_kernel(wide, *refs):
    half = wide // 2
    grads = refs[:half]
    (
        src_ref, up_ref, up_two, up_one, down_ref, down_two, down_one, dst_ref, grad_ref, up_full,
        down_full, send, recv, local,
    ) = refs[half:]
    w, z = lax.axis_index("wide"), lax.axis_index("narrow")
    line = [flipped(z, k) for k in range(4)]
    is_middle = (z == 1) | (z == 2)
    is_end = (z == 0) | (z == 3)
    sender = Sender(send, recv)
    up_at = lambda n: up_full.at[:, n]
    down_at = lambda n: down_full.at[n]
    moves = [
        (src_ref, dst_ref.at[0]),
        (down_ref, down_at(z)), (down_two, down_at(line[2])), (down_one, down_at(line[1])),
        (up_ref, up_at(z)), (up_two, up_at(line[2])), (up_one, up_at(line[1])),
    ] + [(grads[n], grad_ref.at[n]) for n in range(half)]
    own = [pltpu.make_async_copy(src, dst, local.at[n]) for n, (src, dst) in enumerate(moves)]
    for copy in own:
        copy.start()
    greet(
        [wide_device(flipped(w, k)) for k in wide_steps(wide)]
        + [narrow_device(line[k]) for k in (1, 3)]
    )
    gather = WideGather(
        sender, w, wide, lambda k: src_ref if k == 0 else dst_ref.at[place_of(k, wide)],
        lambda k, to: dst_ref.at[place_of(k ^ to, wide)],
    )
    middles = [
        sender.plan(up_ref, up_at(z), narrow_device(line[3])),
        sender.plan(down_ref, down_at(z), narrow_device(line[3])),
    ]
    relays = [
        sender.plan(up_two, up_at(line[2]), narrow_device(line[1])),
        sender.plan(down_two, down_at(line[2]), narrow_device(line[1])),
    ]
    gather.start()

    @pl.when(is_middle)
    def _():
        for copy in middles + relays:
            copy.start()

    sibling = wide_device(flipped(w, 1))
    copies = [sender.plan(grads[n], grad_ref.at[half + n], sibling) for n in range(half)]
    for copy in copies:
        copy.start()
    gather.pass_on()

    @pl.when(is_middle)
    def _():
        for copy in middles:
            copy.wait()
        for copy in relays:
            copy.wait_send()

    @pl.when(is_end)
    def _():
        for copy in relays:
            copy.wait_recv()

    for copy in own + copies:
        copy.wait()
    gather.finish()


def gather_rows(array, grads, ups, downs, collective_id):
    half = len(grads)
    wide = 2 * half
    whole = jax.ShapeDtypeStruct((wide,) + array.shape, array.dtype)
    up_shape = ups[0].shape
    full = jax.ShapeDtypeStruct((up_shape[0], 4) + up_shape[1:], BF16)
    return pl.pallas_call(
        functools.partial(rows_kernel, wide),
        out_shape=[whole, whole, full, jax.ShapeDtypeStruct((4,) + downs[0].shape, BF16)],
        in_specs=[ANY] * (half + 7),
        out_specs=[VMEM, ANY if wide > 8 else VMEM, VMEM, VMEM],
        scratch_shapes=[DMA((2 * wide + 4,)), DMA((2 * wide + 4,)), DMA((half + 7,))],
        compiler_params=pltpu.CompilerParams(
            collective_id=collective_id, has_side_effects=True, vmem_limit_bytes=48 * 2**20
        ),
    )(*grads, array, *ups, *downs)


def hidden_kernel(
    half, normed_ref, grad_ref, up_ref, down_ref, hidden_ref, mid_ref, even_ref, odd_ref, branch_ref
):
    size = down_ref.shape[0]
    gate_up = dot_f32(normed_ref[...], up_ref[...])
    grad_hidden = dot_f32(grad_ref[...], down_ref[...], ((1,), (1,)))
    gate, up = gate_up[:, :size], gate_up[:, size:]
    opened = jax.nn.sigmoid(gate)
    acted = gate * opened
    hidden_ref[...] = (acted * up).astype(BF16)
    mid_ref[:, :size] = (grad_hidden * up * (opened * (1.0 + gate * (1.0 - opened)))).astype(BF16)
    mid_ref[:, size:] = (grad_hidden * acted).astype(BF16)
    grad_normed = dot_f32(mid_ref[...], up_ref[...], ((1,), (1,))).astype(BF16)
    branch_ref[...] = dot_f32(hidden_ref[...], down_ref[...]).astype(BF16)
    step = pl.program_id(0)

    @pl.when(step < half)
    def _():
        even_ref[...] = grad_normed

    @pl.when(step >= half)
    def _():
        odd_ref[...] = grad_normed


def feed_forward(normed, grad, up_full, down_full, rows):
    total, width = normed.shape
    blocks = total // rows
    half = blocks // 2
    size = down_full.shape[0]
    row_block = lambda columns: pl.BlockSpec((rows, columns), lambda i: (i, 0))
    fixed = lambda array: pl.BlockSpec(array.shape, lambda i: (0, 0))
    return pl.pallas_call(
        functools.partial(hidden_kernel, half),
        grid=(blocks,),
        in_specs=[row_block(width), row_block(width), fixed(up_full), fixed(down_full)],
        out_specs=[
            row_block(size), row_block(2 * size),
            pl.BlockSpec((rows, width), lambda i: (jnp.minimum(i, half - 1), 0)),
            pl.BlockSpec((rows, width), lambda i: (jnp.maximum(i - half, 0), 0)),
            row_block(width),
        ],
        out_shape=[
            jax.ShapeDtypeStruct((total, size), BF16),
            jax.ShapeDtypeStruct((total, 2 * size), BF16),
            jax.ShapeDtypeStruct((total // 2, width), BF16),
            jax.ShapeDtypeStruct((total // 2, width), BF16),
            jax.ShapeDtypeStruct((total, width), BF16),
        ],
        compiler_params=pltpu.CompilerParams(vmem_limit_bytes=48 * 2**20),
    )(normed, grad, up_full, down_full)


def middle_kernel(
    wide, even_ref, got_ref, branch_ref, up_ref, down_ref, norm_sum, branch_sum, up_src, down_src,
    up_one, down_one, up_acc, down_acc, core_buf, own_buf, far_buf, branch_buf, up_join, up_mid,
    down_join, down_mid, up_own, down_own, send, recv, local,
):
    w, z = lax.axis_index("wide"), lax.axis_index("narrow")
    line = [flipped(z, k) for k in range(4)]
    half = wide // 2
    unit = up_src.shape[1]
    part = down_src.shape[1]
    sender = Sender(send, recv)
    is_middle = (z == 1) | (z == 2)
    is_end = (z == 0) | (z == 3)

    def up_share(n):
        return up_ref.at[:, pl.ds(pl.multiple_of(n * unit, unit), unit)]

    def down_share(n):
        return down_ref.at[:, pl.ds(pl.multiple_of(n * part, part), part)]

    moves = [
        (up_share(line[2]), up_src), (down_share(line[2]), down_src),
        (up_share(z), up_own), (down_share(z), down_own),
        (up_share(line[1]), up_one), (down_share(line[1]), down_one),
    ]
    moves += [(got_ref.at[n], core_buf.at[n]) for n in range(half)]
    moves += [(even_ref.at[n], own_buf.at[n]) for n in range(half)]
    pairs = branch_sum.shape[0]
    moves += [(branch_ref.at[n], branch_sum.at[n]) for n in range(pairs)]
    own = [pltpu.make_async_copy(src, dst, local.at[n]) for n, (src, dst) in enumerate(moves)]
    for copy in own:
        copy.start()
    greet(
        [wide_device(flipped(w, k)) for k in wide_steps(wide)]
        + [narrow_device(line[k]) for k in (1, 3)]
    )
    sibling = wide_device(flipped(w, 1))
    far = [
        sender.plan(own_buf.at[n], far_buf.at[n - 1], wide_device(flipped(w, 2 * n)))
        for n in range(1, half)
    ]
    branch_core = [
        sender.plan(branch_ref.at[pairs + n], branch_buf.at[n], sibling) for n in range(pairs)
    ]
    joins = [
        sender.plan(up_share(line[3]), up_join, narrow_device(line[1])),
        sender.plan(down_share(line[3]), down_join, narrow_device(line[1])),
    ]
    mids = [
        sender.plan(up_share(line[3]), up_mid, narrow_device(line[3])),
        sender.plan(down_share(line[3]), down_mid, narrow_device(line[3])),
    ]
    order = list(range(1, half)) + [0]

    @pl.when(is_end)
    def _():
        for copy in joins:
            copy.start()

    @pl.when(is_middle)
    def _():
        for copy in mids:
            copy.start()

    for n in order:
        own[6 + n].wait()
        own[6 + half + n].wait()
        total = own_buf[n].astype(F32) + core_buf[n].astype(F32)
        own_buf[n] = total.astype(BF16)
        if n > 0:
            far[n - 1].start()
    for copy in branch_core:
        copy.start()
    for n in range(pairs):
        branch_core[n].wait_recv()
        own[6 + 2 * half + n].wait()
        total = branch_sum[n].astype(F32) + branch_buf[n].astype(F32)
        branch_sum[n] = total.astype(BF16)
    for n in range(6):
        own[n].wait()

    @pl.when(is_middle)
    def _():
        for copy in joins:
            copy.wait_recv()
        up_src[...] = (up_src[...].astype(F32) + up_join[...].astype(F32)).astype(BF16)
        down_src[...] = (down_src[...].astype(F32) + down_join[...].astype(F32)).astype(BF16)

    total = own_buf[0].astype(F32)
    for n in range(1, half):
        far[n - 1].wait_recv()
        total = total + far_buf[n - 1].astype(F32)
    norm_sum[...] = total
    up_acc[...] = up_own[...].astype(F32)
    down_acc[...] = down_own[...].astype(F32)

    @pl.when(is_middle)
    def _():
        for copy in mids:
            copy.wait()
        up_acc[...] += up_mid[...].astype(F32)
        down_acc[...] += down_mid[...].astype(F32)

    @pl.when(is_end)
    def _():
        for copy in joins:
            copy.wait_send()

    for copy in far + branch_core:
        copy.wait_send()


def middle_sums(even, got, branch, grad_up, grad_down, collective_id):
    half, rows, width = even.shape
    wide = 2 * half
    unit, part = grad_up.shape[1] // 4, grad_down.shape[1] // 4
    up_shape, down_shape = (grad_up.shape[0], unit), (grad_down.shape[0], part)
    steps = 4 * half + 6
    rows_buf = pltpu.VMEM((half, rows, width), BF16)
    pairs = branch.shape[0] // 2
    return pl.pallas_call(
        functools.partial(middle_kernel, wide),
        out_shape=[
            jax.ShapeDtypeStruct((rows, width), F32),
            jax.ShapeDtypeStruct((pairs,) + branch.shape[1:], BF16),
            *[jax.ShapeDtypeStruct(up_shape, BF16), jax.ShapeDtypeStruct(down_shape, BF16)] * 2,
            jax.ShapeDtypeStruct(up_shape, F32),
            jax.ShapeDtypeStruct(down_shape, F32),
        ],
        in_specs=[ANY] * 5,
        out_specs=[VMEM] * 8,
        scratch_shapes=[
            rows_buf, rows_buf, pltpu.VMEM((half - 1, rows, width), BF16),
            pltpu.VMEM((pairs,) + branch.shape[1:], BF16),
            *[pltpu.VMEM(up_shape, BF16)] * 2, *[pltpu.VMEM(down_shape, BF16)] * 2,
            pltpu.VMEM(up_shape, BF16), pltpu.VMEM(down_shape, BF16),
            DMA((steps,)), DMA((steps,)), DMA((6 + 3 * half,)),
        ],
        compiler_params=pltpu.CompilerParams(
            collective_id=collective_id, has_side_effects=True, vmem_limit_bytes=58 * 2**20
        ),
    )(even, got, branch, grad_up, grad_down)


def last_kernel(
    wide, rows, own_width, own_heads, norm_ref, in_ref, up_parts, down_parts, branch_refs, token_ref,
    middle_ref, grad_ref, gain_ref, small_ref, output, grad_tokens, grad_in, grad_up, grad_down, totals, join_buf, one_buf, mid_buf, two_buf, two_src, own_norm, norm_sum,
    in_core, in_own, in_far, in_sum, in_got, after_got, tail_buf, up_low, up_bufs, up_got, down_low,
    down_bufs, down_got, branch_bufs, narrow_buf, wide_buf, sum_buf, send, recv, down_send, down_recv,
    local,
):
    w, z = lax.axis_index("wide"), lax.axis_index("narrow")
    line = [flipped(z, k) for k in range(4)]
    half = wide // 2
    unit = up_low.shape[1]
    wide_rows, width = grad_in.shape[0], token_ref.shape[1]
    sender = Sender(send, recv)
    is_middle = (z == 1) | (z == 2)
    is_end = (z == 0) | (z == 3)

    def norm_block(n):
        return norm_ref.at[pl.ds(pl.multiple_of(n * rows, rows), rows), :]

    def up_rows(n):
        return up_low.at[pl.ds(pl.multiple_of(n * wide_rows, 16), wide_rows), :]

    def up_columns(n):
        return up_got.at[:, pl.ds(pl.multiple_of(n * unit, LANES), unit)]

    def section(n):
        return in_sum.at[:, pl.ds(pl.multiple_of(n * own_width, LANES), own_width)]

    def after_section(n):
        return in_sum.at[:, pl.ds(pl.multiple_of((n + 1) * own_width, LANES), LANES)]

    moves = [(norm_block(line[2]), two_src), (norm_block(z), own_norm)]
    moves += [(in_ref.at[flipped(w, 2 * n)], in_own.at[n]) for n in range(half)]
    ffn_at = len(moves)
    moves += [(ref, up_bufs.at[n]) for n, ref in enumerate(up_parts)]
    moves += [(ref, down_bufs.at[n]) for n, ref in enumerate(down_parts)]
    branch_at = len(moves)
    moves += [(ref, branch_bufs.at[n]) for n, ref in enumerate(branch_refs)]
    own = [pltpu.make_async_copy(src, dst, local.at[n]) for n, (src, dst) in enumerate(moves)]
    for copy in own:
        copy.start()
    greet(
        [narrow_device(line[k]) for k in (1, 2, 3)]
        + [wide_device(flipped(w, k)) for k in range(1, wide)]
    )
    sibling = wide_device(flipped(w, 1))
    joined = sender.plan(norm_block(line[3]), join_buf, narrow_device(line[1]))
    one = sender.plan(norm_block(line[1]), one_buf, narrow_device(line[1]))
    middle = sender.plan(norm_block(line[3]), mid_buf, narrow_device(line[3]))
    two = sender.plan(two_src, two_buf, narrow_device(line[2]))
    core = [
        sender.plan(in_ref.at[flipped(w, 2 * n + 1)], in_core.at[n], sibling) for n in range(half)
    ]
    far = [
        sender.plan(in_own.at[n], in_far.at[n - 1], wide_device(flipped(w, 2 * n)))
        for n in range(1, half)
    ]
    sections = [
        sender.plan(section(line[k]), in_got.at[z], narrow_device(line[k])) for k in (2, 3, 1)
    ]
    afters = [
        (
            (z == 0) | (line[k] == 3), (line[k] == 0) | (z == 3),
            sender.plan(after_section(line[k]), after_got.at[z], narrow_device(line[k])),
        )
        for k in (2, 3, 1)
    ]
    ups = [
        sender.plan(up_rows(flipped(w, k)), up_columns(w), wide_device(flipped(w, k)))
        for k in range(1, wide)
    ]
    first = [
        sender.plan(sum_buf, narrow_buf.at[z], narrow_device(line[k])) for k in (1, 2, 3)
    ]
    second = [
        sender.plan(sum_buf, wide_buf.at[w], wide_device(flipped(w, k))) for k in range(1, wide)
    ]
    parity, target = lax.rem(w, 2), lax.div(w, 2)
    depth = down_low.shape[0] // 2
    down_at = pl.ds(pl.multiple_of(parity * depth, 16), depth)
    downs = []
    for n in range(2):
        owner = target + n * half
        src, dst = down_low.at[pl.ds(n * depth, depth), :], down_got.at[down_at, :]
        push = pltpu.make_async_remote_copy(
            src_ref=src, dst_ref=dst, send_sem=down_send.at[n], recv_sem=down_recv.at[parity],
            device_id=wide_device(owner), device_id_type=MESH,
        )
        stay = pltpu.make_async_copy(src, dst, local.at[len(moves) + 1 + n])
        downs.append((owner == w, push, stay))

    order = list(range(1, half)) + [0]
    for n in order:
        core[n].start()

    @pl.when(is_end)
    def _():
        joined.start()

    @pl.when(is_middle)
    def _():
        middle.start()

    for n in order:
        core[n].wait_recv()
        own[2 + n].wait()
        total = in_own[n].astype(F32) + in_core[n].astype(F32)
        in_own[n] = total.astype(BF16)
        if n > 0:
            far[n - 1].start()
    own[0].wait()

    @pl.when(is_middle)
    def _():
        joined.wait_recv()
        two_src[...] = (two_src[...].astype(F32) + join_buf[...].astype(F32)).astype(BF16)

    two.start()
    one.start()
    for n in range(6):
        own[ffn_at + n].wait()
    up_low[...] = add_up([up_bufs[n] for n in range(3)]).astype(BF16)
    down_low[...] = add_up([down_bufs[n] for n in range(3)]).astype(BF16)
    for copy in ups:
        copy.start()
    for stays, push, stay in downs:
        pl.when(stays)(stay.start)
        pl.when(jnp.logical_not(stays))(push.start)
    up_got[:, pl.ds(pl.multiple_of(w * unit, LANES), unit)] = up_low[
        pl.ds(pl.multiple_of(w * wide_rows, 16), wide_rows), :
    ]
    total = middle_ref[...]
    for n in range(half):
        own[branch_at + n].wait()
        total = total + branch_bufs[n].astype(F32)
    output[...] = total.astype(BF16)

    total = in_own[0].astype(F32)
    for n in range(1, half):
        far[n - 1].wait_recv()
        total = total + in_far[n - 1].astype(F32)
    in_sum[...] = total.astype(BF16)
    mine = pltpu.make_async_copy(section(z), in_got.at[z], local.at[len(moves)])
    mine.start()
    own[1].wait()
    one.wait_recv()
    norm_sum[...] = own_norm[...].astype(F32) + one_buf[...].astype(F32)

    @pl.when(is_middle)
    def _():
        middle.wait()
        norm_sum[...] += mid_buf[...].astype(F32)

    two.wait_recv()
    for copy in sections:
        copy.start()
    for sends, gets, copy in afters:
        pl.when(sends)(copy.start)
    after_got[z] = after_section(z)[...]
    grads = norm_sum[...] + two_buf[...].astype(F32)
    values = token_ref[...].astype(F32)
    factor = rms_factor(values)
    normed = values * factor
    scaled = grads * gain_ref[...].reshape(1, width)
    inner = jnp.mean(scaled * normed, axis=-1, keepdims=True)
    grad_tokens[...] = grad_ref[...] + factor * (scaled - normed * inner)
    narrow_buf[z] = small_ref[...]
    narrow_buf[z, 0:1, :] = jnp.sum(grads * normed, axis=0, keepdims=True)
    sum_buf[...] = narrow_buf[z]
    for copy in first:
        copy.start()

    for copy in ups:
        copy.wait_recv()
    grad_up[...] = up_got[...].astype(F32)
    for n, (stays, push, stay) in enumerate(downs):
        pl.when(stays)(stay.wait)
        pl.when(jnp.logical_not(stays))(push.wait_send)
    for n in range(2):
        source = lax.rem(2 * w + n, wide)
        arrived = pltpu.make_async_remote_copy(
            src_ref=down_low.at[pl.ds(0, depth), :], dst_ref=down_got.at[pl.ds(n * depth, depth), :],
            send_sem=down_send.at[n], recv_sem=down_recv.at[n], device_id=sibling,
            device_id_type=MESH,
        )
        pl.when(source != w)(arrived.wait_recv)
    grad_down[...] = down_got[...].astype(F32)

    for copy in first:
        copy.wait()
    sum_buf[...] = narrow_buf[0] + narrow_buf[1] + narrow_buf[2] + narrow_buf[3]
    for copy in second:
        copy.start()
    wide_buf[w] = sum_buf[...]

    for copy in sections:
        copy.wait_recv()
    mine.wait()
    for sends, gets, copy in afters:
        pl.when(gets)(copy.wait_recv)

    @pl.when(z == 3)
    def _():
        row, lane = iota((LANES, LANES), 0), iota((LANES, LANES), 1)
        last = jnp.zeros((wide_rows, LANES), F32)
        for n in range(4):
            group = lax.div(row, own_heads)
            place = group * (4 * own_heads) + n * own_heads + row - group * own_heads
            spot = ((lane == place) & (row < 3 * own_heads)).astype(BF16)
            last = last + dot_f32(after_got[n], spot)
        tail_buf[...] = last

    @pl.when(z != 3)
    def _():
        tail_buf[...] = after_got[0].astype(F32)

    whole = jnp.concatenate([in_got[n].astype(F32) for n in range(4)] + [tail_buf[...]], axis=1)
    move = whole.shape[1] - (grad_in.shape[1] - width) * z
    grad_in[...] = pltpu.roll(whole, lax.rem(move, whole.shape[1]), 1)[:, : grad_in.shape[1]]

    for copy in second:
        copy.wait()
    total = wide_buf[0]
    for n in range(1, wide):
        total = total + wide_buf[n]
    totals[...] = total

    @pl.when(is_end)
    def _():
        joined.wait_send()

    for sends, gets, copy in afters:
        pl.when(sends)(copy.wait_send)
    for copy in [one, two] + core + far + sections + ups:
        copy.wait_send()


def grouped_last_kernel(wide, rows, own_width, own_heads, *refs):
    own, near, far = refs[8:11]
    branches = [own.at[0]]
    branches += [near.at[n] for n in range(near.shape[0])] + [far.at[n] for n in range(far.shape[0])]
    last_kernel(
        wide, rows, own_width, own_heads, *refs[:2], refs[2:5], refs[5:8], branches, *refs[11:],
    )


def last_part(
    norm_part, in_part, ups, downs, branches, tokens, middle, grad_middle, gain, small, own_width, own_heads,
    shard, collective_id,
):
    wide, wide_rows, columns = in_part.shape
    half = wide // 2
    rows, width = tokens.shape
    unit = ups[0].shape[1]
    steps = 4 + 2 * half + 12 + 2 * wide
    shape = jax.ShapeDtypeStruct
    vmem = lambda *dims: pltpu.VMEM(dims, BF16)
    return pl.pallas_call(
        functools.partial(grouped_last_kernel, wide, rows, own_width, own_heads),
        out_shape=[
            shape((rows, width), BF16), shape((rows, width), F32), shape((wide_rows, shard), F32),
            shape((wide_rows, wide * unit), F32), shape(downs[0].shape, F32),
            shape(small.shape, F32),
        ],
        in_specs=[ANY] * 11 + [VMEM] * 5,
        out_specs=[VMEM] * 6,
        scratch_shapes=[
            *[vmem(rows, width)] * 6, pltpu.VMEM((rows, width), F32),
            vmem(half, wide_rows, columns), vmem(half, wide_rows, columns),
            vmem(half - 1, wide_rows, columns), vmem(wide_rows, columns),
            vmem(4, wide_rows, own_width), vmem(4, wide_rows, LANES),
            pltpu.VMEM((wide_rows, LANES), F32), vmem(*ups[0].shape), vmem(3, *ups[0].shape),
            vmem(wide_rows, wide * unit), vmem(*downs[0].shape), vmem(3, *downs[0].shape),
            vmem(*downs[0].shape), vmem(half, rows, width),
            pltpu.VMEM((4,) + small.shape, F32), pltpu.VMEM((wide,) + small.shape, F32),
            pltpu.VMEM(small.shape, F32),
            DMA((steps,)), DMA((steps,)), DMA((2,)), DMA((2,)), DMA((12 + 2 * half,)),
        ],
        compiler_params=pltpu.CompilerParams(
            collective_id=collective_id, has_side_effects=True, vmem_limit_bytes=60 * 2**20
        ),
    )(
        norm_part, in_part, *ups, *downs, *branches, tokens, middle, grad_middle,
        gain, small,
    )


def rms_factor(values):
    return lax.rsqrt(jnp.mean(values * values, axis=-1, keepdims=True) + EPSILON)


def rms_back(values, gain, grad):
    factor = rms_factor(values)
    normed = values * factor
    grad_gain = jnp.sum(grad * normed, axis=0)
    scaled = grad * gain
    inner = jnp.mean(scaled * normed, axis=-1, keepdims=True)
    return (factor * (scaled - normed * inner), grad_gain)


def log_sigmoid(v):
    return jnp.minimum(v, 0.0) - jnp.log1p(jnp.exp(-jnp.abs(v)))


def iota(shape, dim):
    return lax.broadcasted_iota(jnp.int32, shape, dim)


def running_sum(v, reverse):
    rows = v.shape[0]
    index = iota(v.shape, 0)
    step = 1
    while step < rows:
        if reverse:
            v = v + jnp.where(index < rows - step, pltpu.roll(v, rows - step, 0), 0.0)
        else:
            v = v + jnp.where(index >= step, pltpu.roll(v, step, 0), 0.0)
        step *= 2
    return v


def half_of(lane, head_size):
    return (lane >= head_size).astype(jnp.int32)


def spread(first, head_size):
    row, lane = iota((LANES, LANES), 0), iota((LANES, LANES), 1)
    return row == first + half_of(lane, head_size)


def collect(first, head_size):
    row, lane = iota((LANES, LANES), 0), iota((LANES, LANES), 1)
    return lane == first + half_of(row, head_size)


def same_head(head_size):
    row, lane = iota((LANES, LANES), 0), iota((LANES, LANES), 1)
    return (half_of(row, head_size) == half_of(lane, head_size)).astype(F32)


def exact_dot(left, right):
    return lax.dot_general(
        left, right, (((1,), (0,)), ((), ())), precision=EXACT, preferred_element_type=F32
    )


def head_mean(v, head_size):
    return exact_dot(v, same_head(head_size)) * (1.0 / head_size)


def prologue(pair, heads, head_size, q_ref, k_ref, v_ref, small_low, cont):
    spot = lambda group: spread(group * heads + 2 * pair, head_size).astype(BF16)
    key_mix = jax.nn.sigmoid(dot_f32(small_low, spot(1)))
    value_mix = jax.nn.sigmoid(dot_f32(small_low, spot(2)))
    queries = q_ref[...].astype(BF16).astype(F32)
    keys = k_ref[...].astype(BF16).astype(F32)
    values = v_ref[...].astype(BF16).astype(F32)
    key_step = pltpu.roll(keys, 1, 0) * cont - keys
    value_step = pltpu.roll(values, 1, 0) * cont - values
    shifted = keys + key_mix * key_step
    value_low = (values + value_mix * value_step).astype(BF16)
    query_factor = lax.rsqrt(head_mean(queries * queries, head_size) + EPSILON)
    key_factor = lax.rsqrt(head_mean(shifted * shifted, head_size) + EPSILON)
    return (
        queries * query_factor,
        shifted * key_factor,
        value_low,
        query_factor,
        key_factor,
        key_mix,
        value_mix,
        key_step,
        value_step,
    )


def small_columns(small_ref, bias_ref):
    return (small_ref[...] + bias_ref[0:1, :]).astype(BF16)


def decay_of(small_low, cont):
    return running_sum(log_sigmoid(small_low.astype(F32)) - SEPARATE * (1.0 - cont), False)


def forward_pair(
    pair, heads, head_size, block, q_ref, k_ref, v_ref, gate_ref, small_low, cont, decay_all,
    mixed_ref, att_ref, log_ref,
):
    query, key, value_low, *unused = prologue(
        pair, heads, head_size, q_ref, k_ref, v_ref, small_low, cont
    )
    rows = query.shape[0]
    query = query.astype(BF16) * BF16(head_size**-0.5)
    key = key.astype(BF16)
    decay = exact_dot(decay_all, spread(2 * pair, head_size).astype(F32))
    decay_rows = decay.T
    lane = iota((1, LANES), 1)
    ones = jnp.ones((rows, LANES), BF16)
    value_wide = jnp.concatenate([value_low, ones], axis=1)
    for i in range(rows // block):
        lo, hi = i * block, (i + 1) * block
        row_index = iota((block, hi), 0) + lo
        visible = iota((block, hi), 1) <= row_index
        outs, sums = [], []
        for head in range(2):
            mine = (lane >= head_size) if head else (lane < head_size)
            at = head * head_size
            left = jnp.where(mine, query[lo:hi], BF16(0.0))
            scores = dot_f32(left, key[:hi], ((1,), (1,)))
            scores = scores + decay[lo:hi, at : at + 1] - decay_rows[at : at + 1, :hi]
            weights = jnp.where(visible, jnp.exp(scores), 0.0).astype(BF16)
            both = dot_f32(weights, value_wide[:hi])
            outs.append(both[:, :LANES])
            sums.append(both[:, LANES:])
        first = lane < head_size
        total = jnp.where(first, sums[0], sums[1])
        attended = (jnp.where(first, outs[0], outs[1]) / total).astype(BF16)
        att_ref[lo:hi, :] = attended
        log_ref[lo:hi, :] = jnp.log(total)
        opened = jax.nn.sigmoid(gate_ref[lo:hi, :])
        mixed_ref[lo:hi, :] = (attended.astype(F32) * opened).astype(BF16)


def forward_kernel(
    heads, head_size, block, q_ref, k_ref, v_ref, gate_ref, small_ref, bias_ref, cont_ref,
    mixed_ref, att_ref, log_ref, decay_scr,
):
    pair = pl.program_id(0)
    cont = cont_ref[...]
    small_low = small_columns(small_ref, bias_ref)

    @pl.when(pair == 0)
    def _():
        decay_scr[...] = decay_of(small_low, cont)

    forward_pair(
        pair, heads, head_size, block, q_ref, k_ref, v_ref, gate_ref, small_low, cont,
        decay_scr[...], mixed_ref, att_ref, log_ref,
    )


def share_of(ref, like, n):
    size = like.shape[1]
    if ref.shape[1] == size:
        return ref
    return ref.at[:, pl.ds(pl.multiple_of(n * size, size), size)]


def backward_kernel(
    heads, head_size, block, wide, *refs
):
    q_ref, k_ref, v_ref, gate_ref, small_ref, bias_ref, cont_ref, att_ref, log_ref, grad_ref = refs[:10]
    in_ref, normed_ref, up_src, down_src, up_one, down_one, part_ref, branch_ref = refs[10:18]
    out_ref, bias_grad_ref, norm_ref, in_part_ref, grad_out = refs[18:23]
    up_two_got, down_two_got, up_one_got, down_one_got, branch_got = refs[23:28]
    decay_scr, small_scr, dq_scr, part_core, part_own, part_far, part_sum, part_got = refs[28:36]
    in_buf, send, recv, local = refs[36:]
    pair = pl.program_id(0)
    pairs = heads * head_size // LANES
    half = wide // 2
    row_steps = out_ref.shape[0] // norm_ref.shape[0]
    w, z = lax.axis_index("wide"), lax.axis_index("narrow")
    sender = Sender(send, recv)
    one, two = flipped(z, 1), flipped(z, 2)
    copies = [
        sender.plan(up_src, up_two_got, narrow_device(two)),
        sender.plan(down_src, down_two_got, narrow_device(two)),
        sender.plan(share_of(up_one, up_src, one), up_one_got, narrow_device(one)),
        sender.plan(share_of(down_one, down_src, one), down_one_got, narrow_device(one)),
    ]
    core = [
        sender.plan(part_ref.at[flipped(w, 2 * n + 1)], part_core.at[n], wide_device(flipped(w, 1)))
        for n in range(half)
    ]
    far = [
        sender.plan(part_own.at[n], part_far.at[n - 1], wide_device(flipped(w, 2 * n)))
        for n in range(1, half)
    ]
    branches = [
        sender.plan(branch_ref.at[k // 2], branch_got.at[n], wide_device(flipped(w, k)))
        for n, k in enumerate(diagonal_steps(wide))
    ]
    own = [
        pltpu.make_async_copy(part_ref.at[flipped(w, 2 * n)], part_own.at[n], local.at[n])
        for n in range(half)
    ]
    in_copy = pltpu.make_async_copy(in_ref, in_buf, local.at[half])
    own_width = heads * head_size

    def part_columns(n):
        return part_sum.at[:, pl.ds(pl.multiple_of(n * own_width, LANES), own_width)]

    outs = [
        sender.plan(part_columns(flipped(z, k)), part_got.at[k - 1], narrow_device(flipped(z, k)))
        for k in (1, 2, 3)
    ]

    @pl.when(pair == 0)
    def _():
        greet(
            [narrow_device(flipped(z, k)) for k in (1, 2, 3)]
            + [wide_device(flipped(w, k)) for k in wide_steps(wide)]
        )
        for copy in copies + core + own + [in_copy]:
            copy.start()

    @pl.when(pair == 1)
    def _():
        for n in range(half):
            core[n].wait_recv()
            own[n].wait()
            part_own[n] = (part_own[n].astype(F32) + part_core[n].astype(F32)).astype(BF16)
            if n > 0:
                far[n - 1].start()

    @pl.when(pair < pairs)
    def _():
        backward_pair(
            pair, pairs, heads, head_size, block, q_ref, k_ref, v_ref, gate_ref, small_ref,
            bias_ref, cont_ref, att_ref, log_ref, grad_ref, out_ref, bias_grad_ref, decay_scr,
            small_scr, dq_scr,
        )

    @pl.when(pair == pairs)
    def _():
        in_copy.wait()

    @pl.when((pair >= pairs) & (pair < pairs + row_steps))
    def _():
        size = norm_ref.shape[0]
        at = pl.ds(pl.multiple_of((pair - pairs) * size, size), size)
        norm_ref[...] = dot_f32(out_ref[at, :], in_buf[...], ((1,), (1,))).astype(BF16)

    @pl.when(pair == pairs + row_steps)
    def _():
        total = part_own[0].astype(F32)
        for n in range(1, half):
            far[n - 1].wait_recv()
            total = total + part_far[n - 1].astype(F32)
        part_sum[...] = total.astype(BF16)
        for copy in outs + branches:
            copy.start()

    @pl.when(pair >= pairs + row_steps)
    def _():
        in_part_ref[...] = dot_f32(normed_ref[...], out_ref[...], ((0,), (0,))).astype(BF16)

    @pl.when(pair == pl.num_programs(0) - 1)
    def _():
        for copy in outs + copies + branches:
            copy.wait()
        total = part_columns(z)[...].astype(F32)
        for n in range(3):
            total = total + part_got[n].astype(F32)
        grad_out[...] = total
        for copy in core + far:
            copy.wait_send()


def backward_pair(
    pair, pairs, heads, head_size, block, q_ref, k_ref, v_ref, gate_ref, small_ref, bias_ref, cont_ref,
    att_ref, log_ref, grad_ref, out_ref, bias_grad_ref, decay_scr, small_scr, dq_scr,
):
    cont = cont_ref[...]
    small_low = small_columns(small_ref, bias_ref)
    rows = cont.shape[0]
    width = heads * head_size

    @pl.when(pair == 0)
    def _():
        decay_scr[...] = decay_of(small_low, cont)
        small_scr[...] = jnp.zeros_like(small_scr)

    (
        query_norm, key_norm, value_low, query_factor, key_factor, key_mix, value_mix, key_step,
        value_step,
    ) = prologue(pair, heads, head_size, q_ref, k_ref, v_ref, small_low, cont)
    query = query_norm.astype(BF16) * BF16(head_size**-0.5)
    key = key_norm.astype(BF16)
    opened = jax.nn.sigmoid(gate_ref[...])
    attended = att_ref[...].astype(F32)
    grad_mixed = grad_ref[...].astype(F32)
    grad_low = (grad_mixed * opened).astype(BF16)
    grad_gate = grad_mixed * attended * opened * (1.0 - opened)

    def columns(group):
        at = group * width + pair * LANES
        return pl.ds(pl.multiple_of(at, LANES), LANES)

    out_ref[:, columns(3)] = grad_gate.astype(BF16)
    inner = exact_dot(grad_low.astype(F32) * attended, same_head(head_size))
    decay = exact_dot(decay_scr[...], spread(2 * pair, head_size).astype(F32))
    level_rows = (decay - log_ref[...]).T
    inner_rows = inner.T
    lane = iota((1, LANES), 1)
    ones = jnp.ones((rows, LANES), BF16)
    query_wide = jnp.concatenate([query, ones], axis=1)
    key_wide = jnp.concatenate([key, ones], axis=1)
    key_parts, value_parts, query_parts = [], [], []
    for head in range(2):
        mine = (lane >= head_size) if head else (lane < head_size)
        at = head * head_size
        keys_out, values_out = [], []
        for j in range(rows // block):
            lo, hi = j * block, (j + 1) * block
            span = rows - lo
            visible = iota((block, span), 0) <= iota((block, span), 1)
            scores = dot_f32(
                jnp.where(mine, key[lo:hi], BF16(0.0)), query[lo:], ((1,), (1,))
            )
            scores = scores + level_rows[at : at + 1, lo:] - decay[lo:hi, at : at + 1]
            probs = jnp.where(visible, jnp.exp(scores), 0.0)
            grad_probs = dot_f32(
                jnp.where(mine, value_low[lo:hi], BF16(0.0)), grad_low[lo:], ((1,), (1,))
            )
            grad_scores = (probs * (grad_probs - inner_rows[at : at + 1, lo:])).astype(BF16)
            values_out.append(dot_f32(probs.astype(BF16), grad_low[lo:]))
            keys_out.append(dot_f32(grad_scores, query_wide[lo:]))
            part = dot_f32(grad_scores, key_wide[lo:hi], ((0,), (0,)))
            if j == 0:
                dq_scr[...] = part
            else:
                dq_scr[lo:, :] += part
        key_parts.append(jnp.concatenate(keys_out, axis=0))
        value_parts.append(jnp.concatenate(values_out, axis=0))
        query_parts.append(dq_scr[...])
    first = lane < head_size

    def join(parts):
        return jnp.where(first, parts[0], parts[1])

    grad_query = join([p[:, :LANES] for p in query_parts]) * head_size**-0.5
    grad_key = join([p[:, :LANES] for p in key_parts])
    grad_value = join(value_parts)
    grad_decay = join([p[:, LANES:] for p in query_parts]) - join([p[:, LANES:] for p in key_parts])

    def norm_back(grad, normed, factor):
        return factor * (grad - normed * head_mean(grad * normed, head_size))

    def shift_back(grad, mix):
        return grad * (1.0 - mix) + pltpu.roll(grad * mix * cont, rows - 1, 0)

    grad_query = norm_back(grad_query, query_norm, query_factor)
    grad_shifted = norm_back(grad_key, key_norm, key_factor)
    out_ref[:, columns(0)] = grad_query.astype(BF16)
    out_ref[:, columns(1)] = shift_back(grad_shifted, key_mix).astype(BF16)
    out_ref[:, columns(2)] = shift_back(grad_value, value_mix).astype(BF16)
    key_logit = grad_shifted * key_step * key_mix * (1.0 - key_mix)
    value_logit = grad_value * value_step * value_mix * (1.0 - value_mix)
    single = (lax.rem(lane, head_size) == 0).astype(F32)
    small_scr[...] += (
        exact_dot(grad_decay * single, collect(2 * pair, head_size).astype(F32))
        + exact_dot(key_logit, collect(heads + 2 * pair, head_size).astype(F32))
        + exact_dot(value_logit, collect(2 * heads + 2 * pair, head_size).astype(F32))
    )

    @pl.when(pair == pairs - 1)
    def _():
        grads = small_scr[...]
        forget = running_sum(grads, True) * jax.nn.sigmoid(-small_low.astype(F32))
        result = jnp.where(lane < heads, forget, grads)
        out_ref[:, 4 * width :] = result.astype(BF16)
        bias_grad_ref[...] = jnp.broadcast_to(
            jnp.sum(result, axis=0, keepdims=True), bias_grad_ref.shape
        )


def attention_specs(rows, pairs):
    def block_at(group):
        return pl.BlockSpec((rows, LANES), lambda p: (0, group * pairs + jnp.minimum(p, pairs - 1)))

    def fixed(height, column=0):
        return pl.BlockSpec((height, LANES), lambda p: (0, column))

    base = [block_at(0), block_at(1), block_at(2), block_at(3), fixed(rows, 4 * pairs), fixed(8), fixed(rows)]
    return base, pl.BlockSpec((rows, LANES), lambda p: (0, jnp.minimum(p, pairs - 1)))


def attention_forward(projected, bias, cont, heads, head_size, block):
    rows = projected.shape[0]
    pairs = heads * head_size // LANES
    base, own = attention_specs(rows, pairs)
    wide = jax.ShapeDtypeStruct((rows, heads * head_size), BF16)
    return pl.pallas_call(
        functools.partial(forward_kernel, heads, head_size, block),
        grid=(pairs,),
        in_specs=base,
        out_specs=[own] * 3,
        out_shape=[wide, wide, jax.ShapeDtypeStruct(wide.shape, F32)],
        scratch_shapes=[pltpu.VMEM((rows, LANES), F32)],
        compiler_params=pltpu.CompilerParams(vmem_limit_bytes=48 * 2**20),
    )(*([projected] * 5), bias, cont)


def attention_backward(
    projected, bias, cont, attended, logs, grad, in_full, normed_one, shares, out_part, branches, heads,
    head_size, block, collective_id,
):
    rows = projected.shape[0]
    width = normed_one.shape[1]
    wide, wide_rows = out_part.shape[:2]
    half = wide // 2
    pairs = heads * head_size // LANES
    base, own = attention_specs(rows, pairs)
    columns = 4 * heads * head_size + LANES
    step = min(256, rows)
    row_steps, in_steps = rows // step, width // 256
    steps = 8 + 3 * wide
    part = lambda count: pltpu.VMEM((count, wide_rows, width), BF16)
    shape = jax.ShapeDtypeStruct

    def later(first, count):
        return lambda p: jnp.clip(p - first, 0, count - 1)

    row_at, in_at = later(pairs, row_steps), later(pairs + row_steps, in_steps)
    return pl.pallas_call(
        functools.partial(backward_kernel, heads, head_size, block, wide),
        grid=(pairs + row_steps + in_steps,),
        in_specs=base
        + [own] * 3
        + [
            ANY,
            pl.BlockSpec((rows, 256), lambda p: (0, in_at(p))),
        ]
        + [ANY] * 6,
        out_specs=[
            pl.BlockSpec((rows, columns), lambda p: (0, 0)),
            pl.BlockSpec((8, LANES), lambda p: (0, 0)),
            pl.BlockSpec((step, width), lambda p: (row_at(p), 0)),
            pl.BlockSpec((256, columns), lambda p: (in_at(p), 0)),
            pl.BlockSpec((wide_rows, heads * head_size), lambda p: (0, 0)),
        ]
        + [ANY] * 5,
        out_shape=[
            shape((rows, columns), BF16), shape((8, LANES), F32), shape((rows, width), BF16),
            shape((width, columns), BF16), shape((wide_rows, heads * head_size), F32),
            *[shape(share.shape, BF16) for share in shares[:2] * 2],
            shape((len(diagonal_steps(wide)),) + branches.shape[1:], BF16),
        ],
        scratch_shapes=[
            pltpu.VMEM((rows, LANES), F32), pltpu.VMEM((rows, LANES), F32),
            pltpu.VMEM((rows, 2 * LANES), F32), part(half), part(half), part(half - 1),
            pltpu.VMEM((wide_rows, width), BF16),
            pltpu.VMEM((3, wide_rows, heads * head_size), BF16),
            pltpu.VMEM(in_full.shape, BF16),
            DMA((steps,)), DMA((steps,)), DMA((half + 1,)),
        ],
        compiler_params=pltpu.CompilerParams(
            collective_id=collective_id, has_side_effects=True, vmem_limit_bytes=60 * 2**20
        ),
    )(
        *([projected] * 5), bias, cont, attended, logs, grad, in_full, normed_one, *shares, out_part,
        branches,
    )


def first_kernel(
    wide, heads, head_size, block, x_ref, in_ref, small_ref, out_ref, up_ref, grad_ref, down_ref, gain_one_ref,
    gain_two_ref, bias_ref, cont_ref, normed_out, in_out, out_out, proj_out, att_ref, log_ref,
    mixed_rows, middle_ref, normed_two_ref, up_out, up_two, up_one, down_got, grad_got, slot, in_buf,
    out_buf, up_buf, normed, proj, mixed, decay_scr, send, recv, local,
):
    w, z = lax.axis_index("wide"), lax.axis_index("narrow")
    line = [flipped(z, k) for k in range(4)]
    rows, width = x_ref.shape
    own_width = heads * head_size
    part_rows = out_ref.shape[0]
    is_middle = (z == 1) | (z == 2)
    is_end = (z == 0) | (z == 3)
    sender = Sender(send, recv)
    used = []

    def local_copy(src, dst):
        copy = pltpu.make_async_copy(src, dst, local.at[len(used)])
        used.append(copy)
        return copy

    def slot_rows(n):
        return slot.at[pl.ds(pl.multiple_of(n * rows, rows), rows), :]

    def weight_rows(ref, w_of, z_of):
        at = (w_of * 4 + z_of) * part_rows
        return ref.at[pl.ds(pl.multiple_of(at, 16), part_rows), :]

    def wide_rows(ref, w_of):
        at = w_of * 4 * part_rows
        return ref.at[pl.ds(pl.multiple_of(at, 16), 4 * part_rows), :]

    def by_rows(ref):
        return (
            (lambda k: wide_rows(ref, flipped(w, k))),
            (lambda k, to: wide_rows(ref, flipped(w, k))),
        )

    unit = up_buf.shape[2] // 4

    def in_pieces(n):
        target = lambda at, size: in_buf.at[
            pl.ds(pl.multiple_of((w * 4 + z) * part_rows, 16), part_rows), pl.ds(at, size)
        ]
        for group in range(4):
            at = pl.multiple_of(group * width + n * own_width, LANES)
            yield in_ref.at[:, pl.ds(at, own_width)], target(group * own_width, own_width)
        yield small_ref.at[n], target(4 * own_width, LANES)

    def up_pieces(n):
        for group in range(4):
            at = pl.multiple_of((group * wide + n) * unit, LANES)
            yield up_ref.at[:, pl.ds(at, unit)], up_buf.at[w, :, pl.ds(group * unit, unit)]

    own_in = [local_copy(*piece) for piece in in_pieces(z)]
    own_up = [local_copy(*piece) for piece in up_pieces(w)]
    own_out = local_copy(out_ref, weight_rows(out_buf, w, z))
    own_x = local_copy(x_ref, slot_rows(z))
    for copy in used:
        copy.start()

    index = w * 4 + z
    down_wide = lax.div(lax.rem(index, 2 * wide), 2)
    down_narrow = lax.rem(index, 2) + 2 * lax.div(index, 2 * wide)
    from_index = 2 * wide * lax.div(z, 2) + 2 * w + lax.rem(z, 2)
    from_wide_index, from_narrow_index = lax.div(from_index, 4), lax.rem(from_index, 4)
    moves = jnp.logical_not((down_wide == w) & (down_narrow == z))
    down_push = sender.plan(
        down_ref, down_got, {"wide": down_wide, "narrow": down_narrow}
    )
    down_stay = local_copy(down_ref, down_got)

    barrier = pltpu.get_barrier_semaphore()
    partners = [narrow_device(line[k]) for k in (1, 2, 3)]
    partners += [wide_device(flipped(w, k)) for k in range(1, wide)]
    for device in partners:
        pl.semaphore_signal(barrier, inc=1, device_id=device, device_id_type=MESH)

    @pl.when(moves)
    def _():
        for device in (
            {"wide": from_wide_index, "narrow": from_narrow_index},
            {"wide": down_wide, "narrow": down_narrow},
        ):
            pl.semaphore_signal(barrier, inc=1, device_id=device, device_id_type=MESH)
        pl.semaphore_wait(barrier, len(partners) + 2)

    @pl.when(jnp.logical_not(moves))
    def _():
        pl.semaphore_wait(barrier, len(partners))

    ins = [
        sender.plan(*piece, narrow_device(line[k])) for k in (2, 3, 1) for piece in in_pieces(line[k])
    ]
    outs = [
        sender.plan(out_ref, weight_rows(out_buf, w, z), narrow_device(line[k])) for k in (2, 1)
    ]
    out_middle = sender.plan(out_ref, weight_rows(out_buf, w, z), narrow_device(line[3]))
    out_relay = sender.plan(
        weight_rows(out_buf, w, line[2]), weight_rows(out_buf, w, line[2]), narrow_device(line[1])
    )
    ups = [
        sender.plan(*piece, wide_device(flipped(w, k)))
        for k in range(1, wide)
        for piece in up_pieces(flipped(w, k))
    ]
    grads = {
        k: sender.plan(grad_ref, grad_got.at[k // 2 - 1], wide_device(flipped(w, k)))
        for k in range(2, wide, 2)
    }
    two = sender.plan(x_ref, slot_rows(z), narrow_device(line[2]))
    one = sender.plan(x_ref, slot_rows(z), narrow_device(line[1]))
    middle = sender.plan(x_ref, slot_rows(z), narrow_device(line[3]))
    relay = sender.plan(slot_rows(line[2]), slot_rows(line[2]), narrow_device(line[1]))
    in_wide = WideGather(sender, w, wide, *by_rows(in_buf))
    out_wide = WideGather(sender, w, wide, *by_rows(out_buf))
    up_steps = [
        sender.plan(up_buf, up_two, narrow_device(line[2])),
        sender.plan(up_buf, up_one, narrow_device(line[1])),
    ]
    mixes = [
        sender.plan(
            mixed.at[pl.ds(pl.multiple_of(line[k] * rows, rows), rows), :],
            mixed_rows.at[:, pl.ds(pl.multiple_of(z * own_width, LANES), own_width)],
            narrow_device(line[k]),
        )
        for k in (2, 3, 1)
    ]

    for copy in ins + outs + ups + [two]:
        copy.start()
    for copy in own_in:
        copy.wait()
    for copy in ins:
        copy.wait_recv()
    in_wide.start()
    one.start()
    own_out.wait()
    outs[0].wait_recv()

    @pl.when(is_middle)
    def _():
        out_relay.start()
        out_middle.start()

    in_wide.pass_on()
    outs[1].wait_recv()

    @pl.when(is_middle)
    def _():
        out_middle.wait_recv()

    @pl.when(is_end)
    def _():
        out_relay.wait_recv()

    out_wide.start()
    for k in diagonal_steps(wide):
        grads[k].start()
    two.wait_recv()

    @pl.when(is_middle)
    def _():
        relay.start()
        middle.start()

    for copy in own_up:
        copy.wait()
    for copy in ups:
        copy.wait_recv()
    up_back = local_copy(up_buf, up_out)
    up_back.start()
    in_wide.received()
    in_back = local_copy(in_buf, in_out)
    in_back.start()
    own_x.wait()

    def project(t, carry):
        @pl.when(t == 2)
        def _():
            one.wait_recv()

        @pl.when((t == 3) & is_middle)
        def _():
            middle.wait_recv()

        @pl.when((t == 3) & is_end)
        def _():
            relay.wait_recv()

        @pl.when(t == 3)
        def _():
            for copy in up_steps:
                copy.start()
            for k in straight_steps(wide):
                grads[k].start()

        @pl.when((t == 3) & moves)
        def _():
            down_push.start()

        @pl.when((t == 3) & jnp.logical_not(moves))
        def _():
            down_stay.start()

        n = jnp.where(t == 0, z, jnp.where(t == 1, line[2], jnp.where(t == 2, line[1], line[3])))
        at = pl.ds(pl.multiple_of(n * rows, rows), rows)
        values = slot[at, :].astype(F32)
        low = (values * rms_factor(values) * gain_one_ref[...].reshape(1, width)).astype(BF16)
        normed[at, :] = low
        proj[at, :] = dot_f32(low, in_buf[...])
        return carry

    lax.fori_loop(0, 4, project, 0)
    normed_back = local_copy(normed, normed_out)
    proj_back = local_copy(proj, proj_out)
    normed_back.start()
    proj_back.start()

    cont = cont_ref[...]
    groups = own_width // LANES
    small_low = small_columns(proj.at[:, pl.ds(4 * own_width, LANES)], bias_ref)
    decay_scr[...] = decay_of(small_low, cont)

    def attend(pair, carry):
        def at(group):
            return pl.ds(pl.multiple_of((group * groups + pair) * LANES, LANES), LANES)

        forward_pair(
            pair, heads, head_size, block, proj.at[:, at(0)], proj.at[:, at(1)], proj.at[:, at(2)],
            proj.at[:, at(3)], small_low, cont, decay_scr[...], mixed.at[:, at(0)],
            att_ref.at[:, at(0)], log_ref.at[:, at(0)],
        )
        return carry

    lax.fori_loop(0, groups, attend, 0)
    for copy in mixes:
        copy.start()
    out_wide.pass_on()
    mixed_rows[:, pl.ds(pl.multiple_of(z * own_width, LANES), own_width)] = mixed[
        pl.ds(pl.multiple_of(z * rows, rows), rows), :
    ]
    out_wide.received()
    out_back = local_copy(out_buf, out_out)
    out_back.start()
    for copy in mixes:
        copy.wait_recv()
    inputs = slot[pl.ds(pl.multiple_of(z * rows, rows), rows), :].astype(F32)
    values = inputs + dot_f32(mixed_rows[...], out_buf[...])
    middle_ref[...] = values
    normed_two_ref[...] = (values * rms_factor(values) * gain_two_ref[...].reshape(1, width)).astype(BF16)

    for copy in up_steps:
        copy.wait()
    for copy in grads.values():
        copy.wait()

    @pl.when(moves)
    def _():
        down_push.wait()

    @pl.when(jnp.logical_not(moves))
    def _():
        down_stay.wait()

    @pl.when(is_middle)
    def _():
        relay.wait_send()
        middle.wait_send()
        out_relay.wait_send()
        out_middle.wait_send()

    for copy in ins + outs + ups + [two, one] + mixes:
        copy.wait_send()
    in_wide.sent()
    out_wide.sent()
    for copy in (up_back, in_back, normed_back, proj_back, out_back):
        copy.wait()


def first_part(
    tokens, in_weight, small, out_weight, gate_up_weight, cotangent, down_weight, gain_one, gain_two, bias,
    cont, wide, heads, head_size, block, collective_id,
):
    rows, width = tokens.shape
    slot, own_width = 4 * rows, heads * head_size
    columns = 4 * own_width + LANES
    steps = 8 * wide + 40
    up_shape = (wide, gate_up_weight.shape[0], gate_up_weight.shape[1] // wide)
    shape = jax.ShapeDtypeStruct
    return pl.pallas_call(
        functools.partial(first_kernel, wide, heads, head_size, block),
        out_shape=[
            shape((slot, width), BF16), shape((width, columns), BF16), shape((width, width), BF16),
            shape((slot, columns), F32), shape((slot, own_width), BF16),
            shape((slot, own_width), F32), shape((rows, width), BF16), shape((rows, width), F32),
            shape((rows, width), BF16), shape(up_shape, BF16), shape(up_shape, BF16),
            shape(up_shape, BF16), shape(down_weight.shape, BF16),
            shape((wide // 2 - 1, rows, width), BF16),
        ],
        in_specs=[ANY] * 7 + [VMEM] * 4,
        out_specs=[ANY] * 4 + [VMEM] * 5 + [ANY] * 5,
        scratch_shapes=[
            pltpu.VMEM((slot, width), BF16), pltpu.VMEM((width, columns), BF16),
            pltpu.VMEM((width, width), BF16), pltpu.VMEM(up_shape, BF16),
            pltpu.VMEM((slot, width), BF16), pltpu.VMEM((slot, columns), F32),
            pltpu.VMEM((slot, own_width), BF16), pltpu.VMEM((slot, LANES), F32),
            DMA((steps,)), DMA((steps,)), DMA((20,)),
        ],
        compiler_params=pltpu.CompilerParams(
            collective_id=collective_id, has_side_effects=True, vmem_limit_bytes=60 * 2**20
        ),
    )(
        tokens, in_weight, small, out_weight, gate_up_weight, cotangent, down_weight, gain_one,
        gain_two, bias, cont,
    )


def second_kernel(
    wide, src_ref, grad_ref, far_grads, up_ref, up_two, up_one, down_ref, middle_ref, mixed_ref, out_ref,
    gain_ref, grad_middle, gain_grad, slot_grad, branch_sum, up_src, down_src, up_acc, down_acc,
    up_grad_out, down_grad_out, out_part, branch_near, normed, grads, up_full, down_full, hidden, mid,
    rows_buf, core_buf, far_buf, branch_buf, up_join, up_mid, down_join, down_mid, up_grad, down_grad,
    grad_mixed, mixed_buf, send, recv, local,
):
    w, z = lax.axis_index("wide"), lax.axis_index("narrow")
    line = [flipped(z, k) for k in range(4)]
    rows, width = src_ref.shape
    half = wide // 2
    size = hidden.shape[1]
    unit, part = up_src.shape[1], down_src.shape[1]
    is_middle = (z == 1) | (z == 2)
    is_end = (z == 0) | (z == 3)
    sender = Sender(send, recv)
    sibling = wide_device(flipped(w, 1))

    def at_place(ref, place):
        return ref.at[pl.ds(pl.multiple_of(place * rows, rows), rows), :]

    up_at = lambda n: up_full.at[:, n]
    down_at = lambda n: down_full.at[n]
    moves = [
        (src_ref, at_place(normed, 0)), (up_ref, up_at(z)), (up_two, up_at(line[2])),
        (up_one, up_at(line[1])), (down_ref, down_at(z)), (grad_ref, at_place(grads, 0)),
    ] + [(far_grads.at[n - 1], at_place(grads, n)) for n in range(1, half)]
    own = [pltpu.make_async_copy(src, dst, local.at[n]) for n, (src, dst) in enumerate(moves)]
    for copy in own:
        copy.start()
    greet(
        [wide_device(flipped(w, k)) for k in wide_steps(wide)]
        + [narrow_device(line[k]) for k in (1, 2, 3)]
    )
    gather = WideGather(
        sender, w, wide, lambda k: src_ref if k == 0 else at_place(normed, place_of(k, wide)),
        lambda k, to: at_place(normed, place_of(k ^ to, wide)),
    )
    middle = sender.plan(up_ref, up_at(z), narrow_device(line[3]))
    relay = sender.plan(up_two, up_at(line[2]), narrow_device(line[1]))
    down_two = sender.plan(down_ref, down_at(z), narrow_device(line[2]))
    down_one = sender.plan(down_ref, down_at(z), narrow_device(line[1]))
    down_middle = sender.plan(down_ref, down_at(z), narrow_device(line[3]))
    down_relay = sender.plan(down_at(line[2]), down_at(line[2]), narrow_device(line[1]))
    passed = [
        sender.plan(
            grad_ref if n == 0 else far_grads.at[n - 1], at_place(grads, half + n), sibling
        )
        for n in range(half)
    ]
    core = [
        sender.plan(at_place(rows_buf, half + n), core_buf.at[n], sibling) for n in range(half)
    ]
    far = [
        sender.plan(at_place(rows_buf, n), far_buf.at[n - 1], wide_device(flipped(w, 2 * n)))
        for n in range(1, half)
    ]
    branch_core = [
        sender.plan(at_place(normed, half + n), branch_buf.at[n], sibling) for n in range(half)
    ]

    def up_share(n):
        return up_grad.at[:, pl.ds(pl.multiple_of(n * unit, unit), unit)]

    def down_share(n):
        return down_grad.at[:, pl.ds(pl.multiple_of(n * part, part), part)]

    down_joined = sender.plan(down_share(line[3]), down_join, narrow_device(line[1]))
    down_direct = sender.plan(down_share(line[3]), down_mid, narrow_device(line[3]))
    up_joined = sender.plan(up_share(line[3]), up_join, narrow_device(line[1]))
    up_direct = sender.plan(up_share(line[3]), up_mid, narrow_device(line[3]))
    own_width = width // 4
    mixes = [
        sender.plan(
            grad_mixed.at[:, pl.ds(pl.multiple_of(line[k] * own_width, LANES), own_width)],
            slot_grad.at[pl.ds(pl.multiple_of(z * rows, rows), rows), :], narrow_device(line[k]),
        )
        for k in (2, 3, 1)
    ]
    near = [
        sender.plan(branch_sum.at[k // 2], branch_near.at[n], wide_device(flipped(w, k)))
        for n, k in enumerate(straight_steps(wide))
    ]

    gather.start()

    @pl.when(is_middle)
    def _():
        relay.start()
        middle.start()

    down_two.start()
    down_two.wait_recv()

    @pl.when(is_middle)
    def _():
        down_relay.start()
        down_middle.start()

    down_one.start()
    for copy in passed:
        copy.start()
    for copy in own[:4]:
        copy.wait()

    @pl.when(is_middle)
    def _():
        middle.wait_recv()

    @pl.when(is_end)
    def _():
        relay.wait_recv()

    up_shape = (width, 4 * unit)
    down_shape = (size, width)

    def arriving(t, carry):
        @pl.when(t == 1)
        def _():
            gather.first[1].wait_recv()

        for n, k in enumerate(gather.far):

            @pl.when(t == 2 + n)
            def _():
                gather.first[k].wait_recv()
                gather.second[k].start()

            @pl.when(t == half + 1 + n)
            def _():
                gather.second[k].wait_recv()

        place = jnp.where(t < 2, t * half, jnp.where(t < half + 1, t - 1, t))
        at = pl.ds(pl.multiple_of(place * rows, rows), rows)
        mid[at, :] = dot_f32(normed[at, :], up_full[...].reshape(up_shape)).astype(BF16)
        return carry

    lax.fori_loop(0, wide, arriving, 0)
    for copy in own[4:]:
        copy.wait()
    for copy in passed + [down_one]:
        copy.wait_recv()

    @pl.when(is_middle)
    def _():
        down_middle.wait_recv()

    @pl.when(is_end)
    def _():
        down_relay.wait_recv()

    def block(t, carry):
        pick = half - 1 - lax.div(t, 2)
        place = jnp.where(lax.rem(t, 2) == 0, half + pick, pick)
        at = pl.ds(pl.multiple_of(place * rows, rows), rows)
        gate_up = mid[at, :].astype(F32)
        grad_hidden = dot_f32(grads[at, :], down_full[...].reshape(down_shape), ((1,), (1,)))
        gate, up = gate_up[:, :size], gate_up[:, size:]
        opened = jax.nn.sigmoid(gate)
        acted = gate * opened
        hidden[at, :] = (acted * up).astype(BF16)
        mid[at, :size] = (grad_hidden * up * (opened * (1.0 + gate * (1.0 - opened)))).astype(BF16)
        mid[at, size:] = (grad_hidden * acted).astype(BF16)
        rows_buf[at, :] = dot_f32(mid[at, :], up_full[...].reshape(up_shape), ((1,), (1,))).astype(
            BF16
        )
        for n in range(half):

            @pl.when(t == 2 * (half - 1 - n))
            def _():
                core[n].start()

        for n in range(half):

            @pl.when(t == 2 * (half - 1 - n) + 1)
            def _():
                core[n].wait_recv()
                total = rows_buf[n * rows : (n + 1) * rows, :].astype(F32) + core_buf[n].astype(F32)
                rows_buf[n * rows : (n + 1) * rows, :] = total.astype(BF16)
                if n > 0:
                    far[n - 1].start()

        return carry

    lax.fori_loop(0, wide, block, 0)

    step = min(256, size)
    for n in range(size // step):
        cut = slice(n * step, (n + 1) * step)
        down_grad[cut, :] = dot_f32(hidden[:, cut], grads[...], ((0,), (0,))).astype(BF16)

    @pl.when(is_end)
    def _():
        down_joined.start()

    @pl.when(is_middle)
    def _():
        down_direct.start()

    reloads = [
        pltpu.make_async_copy(out_ref, grads.at[pl.ds(0, width), :], local.at[9 + half]),
        pltpu.make_async_copy(grad_ref, grads.at[pl.ds(width, rows), :], local.at[10 + half]),
        pltpu.make_async_copy(mixed_ref, mixed_buf, local.at[11 + half]),
        pltpu.make_async_copy(middle_ref, grad_middle, local.at[12 + half]),
    ]
    for copy in reloads:
        copy.start()

    def up_rows(n, carry):
        at = pl.ds(pl.multiple_of(n * 256, 256), 256)
        up_grad[at, :] = dot_f32(normed[:, at], mid[...], ((0,), (0,))).astype(BF16)
        return carry

    lax.fori_loop(0, width // 256, up_rows, 0)

    @pl.when(is_end)
    def _():
        up_joined.start()

    @pl.when(is_middle)
    def _():
        up_direct.start()

    backs = [
        pltpu.make_async_copy(up_grad, up_grad_out, local.at[5 + half]),
        pltpu.make_async_copy(down_grad, down_grad_out, local.at[6 + half]),
        pltpu.make_async_copy(up_share(line[2]), up_src, local.at[7 + half]),
        pltpu.make_async_copy(down_share(line[2]), down_src, local.at[8 + half]),
    ]
    for copy in backs:
        copy.start()
    gather.sent()

    def branch(t, carry):
        place = lax.rem(t + half, wide)
        at = pl.ds(pl.multiple_of(place * rows, rows), rows)
        normed[at, :] = dot_f32(hidden[at, :], down_full[...].reshape(down_shape)).astype(BF16)
        for n in range(half):

            @pl.when(t == n)
            def _():
                branch_core[n].start()

        return carry

    lax.fori_loop(0, wide, branch, 0)
    for n in range(half):
        branch_core[n].wait_recv()
        total = normed[n * rows : (n + 1) * rows, :].astype(F32) + branch_buf[n].astype(F32)
        branch_sum[n] = total.astype(BF16)

    total = rows_buf[:rows, :].astype(F32)
    for n in range(1, half):
        far[n - 1].wait_recv()
        total = total + far_buf[n - 1].astype(F32)
    for copy in core + far:
        copy.wait_send()
    for copy in reloads:
        copy.wait()
    values = grad_middle[...]
    factor = rms_factor(values)
    values = values * factor
    gain_grad[...] = jnp.broadcast_to(
        jnp.sum(total * values, axis=0, keepdims=True), gain_grad.shape
    )
    total = total * gain_ref[...].reshape(1, width)
    inner = jnp.mean(total * values, axis=-1, keepdims=True)
    total = grads[width : width + rows, :].astype(F32) + factor * (total - values * inner)
    grad_middle[...] = total
    branch_grad = total.astype(BF16)
    grad_mixed[...] = dot_f32(branch_grad, grads[:width, :], ((1,), (1,))).astype(BF16)
    for copy in mixes + near:
        copy.start()
    slot_grad[pl.ds(pl.multiple_of(z * rows, rows), rows), :] = grad_mixed[
        :, pl.ds(pl.multiple_of(z * own_width, LANES), own_width)
    ]
    for n in range(width // 256):
        cut = slice(n * 256, (n + 1) * 256)
        rows_buf[cut, :] = dot_f32(mixed_buf[:, cut], branch_grad, ((0,), (0,))).astype(BF16)
    out_back = pltpu.make_async_copy(
        rows_buf.at[pl.ds(0, width), :], out_part, local.at[13 + half]
    )
    out_back.start()
    for copy in backs:
        copy.wait()
    up_acc[...] = up_grad[:, pl.ds(pl.multiple_of(z * unit, unit), unit)]
    down_acc[...] = down_grad[:, pl.ds(pl.multiple_of(z * part, part), part)]

    @pl.when(is_middle)
    def _():
        down_joined.wait_recv()
        down_src[...] = (down_src[...].astype(F32) + down_join[...].astype(F32)).astype(BF16)
        up_joined.wait_recv()
        up_src[...] = (up_src[...].astype(F32) + up_join[...].astype(F32)).astype(BF16)
        down_direct.wait()
        down_acc[...] = (down_acc[...].astype(F32) + down_mid[...].astype(F32)).astype(BF16)
        up_direct.wait()
        up_acc[...] = (up_acc[...].astype(F32) + up_mid[...].astype(F32)).astype(BF16)
        for copy in (relay, middle, down_relay, down_middle):
            copy.wait_send()

    @pl.when(is_end)
    def _():
        down_joined.wait_send()
        up_joined.wait_send()

    for copy in mixes + near:
        copy.wait()
    out_back.wait()
    for copy in passed + branch_core + [down_two, down_one]:
        copy.wait_send()


def second_part(
    normed, grad, far_grads, ups, down, middle, mixed_rows, out_full, gain, collective_id
):
    rows, width = normed.shape
    half = far_grads.shape[0] + 1
    wide = 2 * half
    wide_of_up, part_rows, mid_size = ups[0].shape
    down_rows = down.shape[0]
    size, unit, part = mid_size // 2, mid_size // 4, width // 4
    steps = 9 + 2 * wide + 4 * half + 8
    total = wide * rows
    shape = jax.ShapeDtypeStruct
    vmem = lambda *dims: pltpu.VMEM(dims, BF16)
    return pl.pallas_call(
        functools.partial(second_kernel, wide),
        out_shape=[
            shape((rows, width), F32), shape((8, width), F32), shape((4 * rows, part), BF16),
            shape((half, rows, width), BF16),
            shape((width, unit), BF16), shape((size, part), BF16),
            shape((width, unit), BF16), shape((size, part), BF16),
            shape((width, mid_size), BF16), shape((size, width), BF16),
            shape((width, width), BF16), shape((len(straight_steps(wide)), rows, width), BF16),
        ],
        in_specs=[ANY] * 10 + [VMEM],
        out_specs=[VMEM] * 8 + [ANY] * 4,
        scratch_shapes=[
            vmem(total, width), vmem(total, width), vmem(wide, 4, part_rows, mid_size),
            vmem(4, down_rows, width), vmem(total, size), vmem(total, mid_size), vmem(total, width),
            vmem(half, rows, width), vmem(half - 1, rows, width), vmem(half, rows, width),
            vmem(width, unit), vmem(width, unit), vmem(size, part), vmem(size, part),
            vmem(width, mid_size), vmem(size, width), vmem(rows, width), vmem(rows, width),
            DMA((steps,)), DMA((steps,)), DMA((14 + half,)),
        ],
        compiler_params=pltpu.CompilerParams(
            collective_id=collective_id, has_side_effects=True, vmem_limit_bytes=63 * 2**20
        ),
    )(
        normed, grad, far_grads, *ups, down, middle, mixed_rows, out_full,
        gain,
    )


def add_up(parts):
    total = parts[0].astype(F32)
    for part in parts[1:]:
        total = total + part.astype(F32)
    return total


def on_device(
    tokens, gain_one, in_weight, forget_bias, out_weight, gain_two, gate_up_weight, down_weight,
    segment_ids, cotangent,
):
    wide, narrow = lax.axis_size("wide"), lax.axis_size("narrow")
    w, z = lax.axis_index("wide"), lax.axis_index("narrow")
    rows, width = tokens.shape
    slot = rows * narrow
    heads = forget_bias.shape[0]
    head_size = width // heads
    own_heads = heads // narrow
    own_width = own_heads * head_size
    part_rows = in_weight.shape[0]
    hidden_all = down_weight.shape[0] * wide * narrow
    unit = hidden_all // (2 * wide)
    columns = 4 * own_width + LANES
    base = 4 * width

    small = in_weight[:, base:].reshape(part_rows, 3, narrow, own_heads)
    small = jnp.moveaxis(small, 2, 0).reshape(narrow, part_rows, 3 * own_heads)
    small = jnp.pad(small, ((0, 0), (0, 0), (0, LANES - 3 * own_heads)))
    aligned = unit % LANES == 0

    def split_weights(sources, targets):
        copies = [(sources[1], targets[0].at[:, :, pl.ds(4 * own_width, LANES)])]
        for n in range(narrow):
            for group in range(4):
                copies.append(
                    (
                        sources[0].at[:, pl.ds(group * width + n * own_width, own_width)],
                        targets[0].at[n, :, pl.ds(group * own_width, own_width)],
                    )
                )
        return copies

    shapes = [
        jax.ShapeDtypeStruct((narrow, part_rows, columns), BF16),
        jax.ShapeDtypeStruct((wide, part_rows, 4 * unit), BF16),
    ]
    copies = 4 * narrow + 1
    fused = aligned and part_rows % 16 == 0
    if not fused:
        in_parts = local_copies(split_weights, copies, [in_weight, small], shapes[:1], False)[0]
        up_parts = jnp.moveaxis(gate_up_weight.reshape(part_rows, 4, wide, unit), 2, 0)
        up_parts = up_parts.reshape(wide, part_rows, 4 * unit)

    segments = segment_ids[0]
    joined = (segments[1:] == segments[:-1]).astype(F32)
    cont = jnp.concatenate([jnp.zeros((1,), F32), joined])
    cont = jnp.broadcast_to(cont[:, None], (slot, LANES))
    own_bias = lax.dynamic_slice_in_dim(forget_bias, z * own_heads, own_heads)
    bias = jnp.broadcast_to(jnp.pad(own_bias, (0, LANES - own_heads))[None], (8, LANES))
    block = min(256, slot)
    def row_block(ref, n):
        return ref.at[pl.ds(pl.multiple_of(n * rows, rows), rows), :]

    def column_block(ref, n):
        return ref.at[:, pl.ds(pl.multiple_of(n * own_width, LANES), own_width)]

    straight, diagonal = straight_steps(wide), diagonal_steps(wide)
    inputs = tokens.astype(F32)
    half = wide // 2
    if fused:
        (
            normed_one, in_full, out_full, projected, attended, logs, mixed_rows, middle, normed_two,
            up_block, up_two, up_one, down_block, grad_got,
        ) = first_part(
            tokens, in_weight, small, out_weight, gate_up_weight, cotangent, down_weight, gain_one,
            gain_two, bias, cont, wide, own_heads, head_size, block, 0,
        )
    else:
        pairs = []
        for i in range(wide * narrow):
            to_wide = (i % (2 * wide)) // 2
            to_narrow = i % 2 + 2 * (i // (2 * wide))
            pairs.append((i, to_wide * narrow + to_narrow))
        down_block = lax.ppermute(down_weight, ("wide", "narrow"), pairs)

        slot_tokens, in_full, out_full, up_block, grad_far = gather_all(
            tokens, in_parts, out_weight, up_parts, cotangent
        )
        slot_tokens = slot_tokens.reshape(slot, width)
        in_full = in_full.reshape(width, columns)
        out_full = out_full.reshape(width, width)

        up_two = on_line(up_block, LINE_TWO)
        up_one = on_line(up_block, LINE_ONE)

        slot_floats = slot_tokens.astype(F32)
        normed_one = (slot_floats * rms_factor(slot_floats) * gain_one).astype(BF16)
        projected = dot_f32(normed_one, in_full)

        mixed, attended, logs = attention_forward(
            projected, bias, cont, own_heads, head_size, block
        )

        mixed_rows, *grad_near = exchange(
            mixed, row_block, column_block, (rows, width), straight, [cotangent] * len(straight), 1
        )
        grads = {0: cotangent}
        grads.update({k: grad_near[n] for n, k in enumerate(straight)})
        grads.update({k: grad_far[n] for n, k in enumerate(diagonal)})
        grads = [grads[k] for k in range(0, wide, 2)]
        down_block = follow(down_block, mixed_rows)
        down_two = on_line(down_block, LINE_TWO)
        down_one = on_line(down_block, LINE_ONE)
        middle = inputs + dot_f32(mixed_rows, out_full)
        normed_two = (middle * rms_factor(middle) * gain_two).astype(BF16)

    if fused:
        (
            grad_middle, grad_gain_two, slot_grad, branch_sum, up_src, down_src, up_acc, down_acc,
            up_one, down_one, out_part, branch_near,
        ) = second_part(
            normed_two, cotangent, grad_got, [up_block, up_two, up_one], down_block, middle,
            mixed_rows, out_full, gain_two, 2,
        )
        grad_gain_two = grad_gain_two[0]
    else:
        ups = [up_block] + [follow(piece, normed_two) for piece in (up_two, up_one)]
        plane_normed, plane_grad, up_full, down_full = gather_rows(
            normed_two, grads, ups, [down_block, down_two, down_one], 2
        )
        plane_normed = plane_normed.reshape(wide * rows, width)
        plane_grad = plane_grad.reshape(wide * rows, width)
        up_full = up_full.reshape(width, 4 * unit)
        down_full = down_full.reshape(2 * unit, width)
        hidden, gate_up_grad, norm_even, norm_odd, branch = feed_forward(
            plane_normed, plane_grad, up_full, down_full, rows
        )
        grad_up_full = dot_f32(plane_normed, gate_up_grad, ((0,), (0,))).astype(BF16)
        grad_down_full = dot_f32(hidden, plane_grad, ((0,), (0,))).astype(BF16)
        if unit % LANES:
            grouped = grad_up_full.reshape(width, 4, unit)
            grad_up_full = jnp.pad(grouped, ((0, 0), (0, 0), (0, LANES - unit))).reshape(width, -1)
        branch = branch.reshape(wide, rows, width)
        fits = wide <= 8
        norm_got = along_wide(norm_odd.reshape(half, rows, width), 1, wide)
        (
            grad_normed_two, branch_sum, up_src, down_src, up_one, down_one, up_acc, down_acc,
        ) = middle_sums(
            norm_even.reshape(half, rows, width), norm_got,
            branch if fits else branch[:2, :16], grad_up_full, grad_down_full, 6,
        )
        if not fits:
            received = along_wide(branch[half:], 1, wide)
            branch_sum = (branch[:half].astype(F32) + received.astype(F32)).astype(BF16)
        upstream = cotangent.astype(F32)
        grad_middle_norm, grad_gain_two = rms_back(middle, gain_two, grad_normed_two)
        grad_middle = upstream + grad_middle_norm
        branch_one_grad = grad_middle.astype(BF16)
        grad_mixed = dot_f32(branch_one_grad, out_full, ((1,), (1,))).astype(BF16)
        slot_grad, *branch_near = exchange(
            grad_mixed, column_block, row_block, (slot, own_width), straight,
            [branch_sum[k // 2] for k in straight], 3,
        )
        branch_near = jnp.stack(branch_near)
        out_part = dot_f32(mixed_rows, branch_one_grad, ((0,), (0,))).astype(BF16)
    wide_rows = width // wide
    (
        unused, bias_grad, norm_part, in_part, grad_out, up_two, down_two, up_one, down_one,
        branch_far,
    ) = attention_backward(
        projected, bias, cont, attended, logs, slot_grad, in_full, normed_one,
        [up_src, down_src, up_one, down_one], out_part.reshape(wide, wide_rows, width), branch_sum,
        own_heads, head_size, block, 7,
    )
    branches = [branch_sum, branch_near, branch_far]
    all_bias = lax.dynamic_update_slice(
        jnp.zeros((width,), F32), bias_grad[0, :own_heads], (z * own_heads,)
    )
    small = jnp.stack([jnp.zeros((width,), F32), grad_gain_two, all_bias])
    small = jnp.pad(small, ((0, 5), (0, 0)))
    low = lambda part: part.astype(BF16)
    output, grad_tokens, grad_in, grad_up, grad_down, totals = last_part(
        norm_part, in_part.reshape(wide, wide_rows, columns), [low(up_acc), up_one, up_two],
        [low(down_acc), down_one, down_two], branches, tokens, middle, grad_middle, gain_one, small,
        own_width, own_heads, (base + 3 * heads) // narrow, 4,
    )
    if not aligned:
        grad_up = grad_up.reshape(wide_rows, wide, LANES)[:, :, :unit]
        grad_up = grad_up.reshape(wide_rows, wide * unit)
    return (
        output,
        grad_tokens,
        totals[0],
        grad_in,
        totals[2, :heads],
        grad_out,
        totals[1],
        grad_up,
        grad_down,
    )


def solution(mesh):
    both = ("wide", "narrow")
    in_specs = (
        P(both, None), P(), P(both, None), P(), P(both, None), P(), P(both, None), P(both, None),
        P("wide", None), P(both, None),
    )
    out_specs = (
        P(both, None), P(both, None), P(), P("wide", "narrow"), P(), P("wide", "narrow"), P(),
        P("wide", "narrow"), P("wide", "narrow"),
    )
    return jax.shard_map(
        on_device, mesh=mesh, in_specs=in_specs, out_specs=out_specs, check_vma=False
    )
```

```python
import functools

import jax
import jax.numpy as jnp
from jax import lax
from jax.experimental import pallas as pl
from jax.experimental.pallas import tpu as pltpu
from jax.sharding import PartitionSpec as P

EPSILON = 1e-06
SEPARATE = 128.0
F32 = jnp.float32
BF16 = jnp.bfloat16
LANES = 128
EXACT = lax.Precision.HIGHEST
ANY = pl.BlockSpec(memory_space=pltpu.HBM)


def dot_f32(left, right, dims=((1,), (0,))):
    return lax.dot_general(left, right, (dims, ((), ())), preferred_element_type=F32)


def along_wide(block, flip, wide):
    return lax.ppermute(block, "wide", [(i, i ^ flip) for i in range(wide)])


def copy_kernel(plan, count, *refs):
    sources, targets, sems = refs[:count], refs[count:-1], refs[-1]
    copies = plan(sources, targets)

    def each(act):
        for n, (src, dst, *when) in enumerate(copies):
            copy = pltpu.make_async_copy(src, dst, sems.at[n])
            if when:
                pl.when(when[0])(functools.partial(act, copy))
            else:
                act(copy)

    each(lambda copy: copy.start())
    each(lambda copy: copy.wait())


def local_copies(plan, copies, sources, shapes, gather):
    moved = sum(s.size * s.dtype.itemsize for s in shapes)
    inside = pl.BlockSpec(memory_space=pltpu.VMEM)
    return pl.pallas_call(
        functools.partial(copy_kernel, plan, len(sources)),
        out_shape=shapes,
        in_specs=[ANY if gather else inside] * len(sources),
        out_specs=[inside if gather else ANY] * len(shapes),
        compiler_params=pltpu.CompilerParams(vmem_limit_bytes=16 * 2**20),
        scratch_shapes=[pltpu.SemaphoreType.DMA((copies,))],
        cost_estimate=pl.CostEstimate(flops=0, bytes_accessed=2 * moved, transcendentals=0),
    )(*sources)


def flipped(me, k):
    out = me
    bit = 1
    while bit <= k:
        if k & bit:
            out = out + bit - 2 * bit * lax.rem(lax.div(out, bit), 2)
        bit *= 2
    return out


LINE_TWO = [(0, 2), (2, 0), (1, 3), (3, 1)]
LINE_ONE = [(0, 1), (1, 0), (2, 3), (3, 2)]
LINE_MIDDLE = [(1, 2), (2, 1)]
LINE_OUT = [(2, 3), (1, 0)]
LINE_IN = [(0, 1), (3, 2)]


def on_line(block, pairs):
    return lax.ppermute(block, "narrow", pairs)


def follow(array, *earlier):
    return lax.optimization_barrier((array, *earlier))[0]


MESH = pl.DeviceIdType.MESH
VMEM = pl.BlockSpec(memory_space=pltpu.VMEM)
DMA = pltpu.SemaphoreType.DMA


def greet(devices):
    barrier = pltpu.get_barrier_semaphore()
    for device in devices:
        pl.semaphore_signal(barrier, inc=1, device_id=device, device_id_type=MESH)
    pl.semaphore_wait(barrier, len(devices))


class Sender:
    def __init__(self, send, recv):
        self.send, self.recv, self.used = send, recv, 0

    def plan(self, src, dst, device):
        n = self.used
        self.used += 1
        return pltpu.make_async_remote_copy(
            src_ref=src, dst_ref=dst, send_sem=self.send.at[n], recv_sem=self.recv.at[n],
            device_id=device, device_id_type=MESH,
        )


def narrow_device(n):
    return {"narrow": n}


def wide_device(n):
    return {"wide": n}


def wide_steps(wide):
    return [1] + list(range(2, wide, 2))


def straight_steps(wide):
    return [k for k in range(2, wide, 2) if k & (k - 1) == 0]


def diagonal_steps(wide):
    return [k for k in range(2, wide, 2) if k & (k - 1)]


def by_device(ref, w):
    return (lambda k: ref.at[flipped(w, k)]), (lambda k, to: ref.at[flipped(w, k)])


class WideGather:
    def __init__(self, sender, w, wide, part, target):
        self.far = list(range(2, wide, 2))
        self.first = {
            k: sender.plan(part(0), target(0, k), wide_device(flipped(w, k)))
            for k in wide_steps(wide)
        }
        sibling = wide_device(flipped(w, 1))
        self.second = {k: sender.plan(part(k), target(k, 1), sibling) for k in self.far}

    def start(self):
        for k in self.far + [1]:
            self.first[k].start()

    def pass_on(self):
        for k in self.far:
            self.first[k].wait_recv()
            self.second[k].start()

    def received(self):
        self.first[1].wait_recv()
        for k in self.far:
            self.second[k].wait_recv()

    def sent(self):
        for copy in list(self.first.values()) + list(self.second.values()):
            copy.wait_send()

    def finish(self):
        self.received()
        self.sent()


def gather_kernel(
    wide, x_ref, in_ref, out_ref, up_ref, grad_ref, slot_ref, in_full, out_full, up_block, grad_far,
    send, recv, local,
):
    w, z = lax.axis_index("wide"), lax.axis_index("narrow")
    line = [flipped(z, k) for k in range(4)]
    sender = Sender(send, recv)
    own = [
        pltpu.make_async_copy(in_ref.at[z], in_full.at[w, z], local.at[0]),
        pltpu.make_async_copy(out_ref, out_full.at[w, z], local.at[1]),
        pltpu.make_async_copy(x_ref, slot_ref.at[z], local.at[2]),
        pltpu.make_async_copy(up_ref.at[w], up_block.at[w], local.at[3]),
    ]
    for copy in own:
        copy.start()
    greet(
        [narrow_device(line[k]) for k in (1, 2, 3)]
        + [wide_device(flipped(w, k)) for k in range(1, wide)]
    )
    ups = [
        sender.plan(up_ref.at[flipped(w, k)], up_block.at[w], wide_device(flipped(w, k)))
        for k in range(1, wide)
    ]
    grads = [
        sender.plan(grad_ref, grad_far.at[n], wide_device(flipped(w, k)))
        for n, k in enumerate(diagonal_steps(wide))
    ]
    is_middle = (z == 1) | (z == 2)
    is_end = (z == 0) | (z == 3)
    ins = [
        sender.plan(in_ref.at[line[k]], in_full.at[w, z], narrow_device(line[k])) for k in (2, 3, 1)
    ]
    outs = [sender.plan(out_ref, out_full.at[w, z], narrow_device(line[k])) for k in (2, 3, 1)]
    two = sender.plan(x_ref, slot_ref.at[z], narrow_device(line[2]))
    one = sender.plan(x_ref, slot_ref.at[z], narrow_device(line[1]))
    middle = sender.plan(x_ref, slot_ref.at[z], narrow_device(line[3]))
    relay = sender.plan(slot_ref.at[line[2]], slot_ref.at[line[2]], narrow_device(line[1]))
    in_wide = WideGather(sender, w, wide, *by_device(in_full, w))
    out_wide = WideGather(sender, w, wide, *by_device(out_full, w))
    for copy in ins + outs + ups:
        copy.start()
    own[0].wait()
    for copy in ins:
        copy.wait_recv()
    in_wide.start()
    two.start()
    one.start()
    own[1].wait()
    for copy in outs:
        copy.wait_recv()
    out_wide.start()
    in_wide.pass_on()
    for copy in grads:
        copy.start()
    two.wait_recv()

    @pl.when(is_middle)
    def _():
        relay.start()
        middle.start()

    out_wide.pass_on()
    one.wait_recv()
    own[2].wait()
    own[3].wait()
    for copy in ups + grads:
        copy.wait()

    @pl.when(is_middle)
    def _():
        middle.wait_recv()
        middle.wait_send()
        relay.wait_send()

    @pl.when(is_end)
    def _():
        relay.wait_recv()

    for copy in ins + outs + [two, one]:
        copy.wait_send()
    in_wide.finish()
    out_wide.finish()


def gather_all(tokens, in_parts, out_weight, up_parts, cotangent):
    narrow, wide = in_parts.shape[0], up_parts.shape[0]
    steps = 10 + 4 * wide
    shapes = [
        (narrow,) + tokens.shape, (wide,) + in_parts.shape, (wide, narrow) + out_weight.shape,
        up_parts.shape, (len(diagonal_steps(wide)),) + cotangent.shape,
    ]
    return pl.pallas_call(
        functools.partial(gather_kernel, wide),
        out_shape=[jax.ShapeDtypeStruct(shape, BF16) for shape in shapes],
        in_specs=[ANY] * 5,
        out_specs=[VMEM] * 5,
        scratch_shapes=[DMA((steps,)), DMA((steps,)), DMA((4,))],
        compiler_params=pltpu.CompilerParams(
            collective_id=0, has_side_effects=True, vmem_limit_bytes=40 * 2**20
        ),
    )(tokens, in_parts, out_weight, up_parts, cotangent)


def exchange_kernel(source, target, steps, *refs):
    count = len(steps)
    src_ref, sides, dst_ref = refs[0], refs[1 : 1 + count], refs[1 + count]
    got = refs[2 + count : 2 + 2 * count]
    send, recv, local = refs[2 + 2 * count :]
    w, z = lax.axis_index("wide"), lax.axis_index("narrow")
    line = [flipped(z, k) for k in range(4)]
    sender = Sender(send, recv)
    own = pltpu.make_async_copy(source(src_ref, z), target(dst_ref, z), local.at[0])
    own.start()
    greet(
        [narrow_device(line[k]) for k in (1, 2, 3)] + [wide_device(flipped(w, k)) for k in steps]
    )
    copies = [
        sender.plan(source(src_ref, line[k]), target(dst_ref, z), narrow_device(line[k]))
        for k in (2, 3, 1)
    ]
    copies += [
        sender.plan(sides[n], got[n], wide_device(flipped(w, k))) for n, k in enumerate(steps)
    ]
    for copy in copies:
        copy.start()
    own.wait()
    for copy in copies:
        copy.wait()


def exchange(array, source, target, shape, steps, sides, collective_id):
    count = len(steps) + 4
    return pl.pallas_call(
        functools.partial(exchange_kernel, source, target, steps),
        out_shape=[jax.ShapeDtypeStruct(shape, array.dtype)]
        + [jax.ShapeDtypeStruct(side.shape, side.dtype) for side in sides],
        in_specs=[ANY] * (1 + len(sides)),
        out_specs=[VMEM] * (1 + len(sides)),
        scratch_shapes=[DMA((count,)), DMA((count,)), DMA((1,))],
        compiler_params=pltpu.CompilerParams(
            collective_id=collective_id, has_side_effects=True, vmem_limit_bytes=16 * 2**20
        ),
    )(array, *sides)


def place_of(k, wide):
    return k // 2 + (k % 2) * (wide // 2)


def rows_kernel(wide, *refs):
    half = wide // 2
    grads = refs[:half]
    (
        src_ref, up_ref, up_two, up_one, down_ref, down_two, down_one, dst_ref, grad_ref, up_full,
        down_full, send, recv, local,
    ) = refs[half:]
    w, z = lax.axis_index("wide"), lax.axis_index("narrow")
    line = [flipped(z, k) for k in range(4)]
    is_middle = (z == 1) | (z == 2)
    is_end = (z == 0) | (z == 3)
    sender = Sender(send, recv)
    up_at = lambda n: up_full.at[:, n]
    down_at = lambda n: down_full.at[n]
    moves = [
        (src_ref, dst_ref.at[0]),
        (down_ref, down_at(z)), (down_two, down_at(line[2])), (down_one, down_at(line[1])),
        (up_ref, up_at(z)), (up_two, up_at(line[2])), (up_one, up_at(line[1])),
    ] + [(grads[n], grad_ref.at[n]) for n in range(half)]
    own = [pltpu.make_async_copy(src, dst, local.at[n]) for n, (src, dst) in enumerate(moves)]
    for copy in own:
        copy.start()
    greet(
        [wide_device(flipped(w, k)) for k in wide_steps(wide)]
        + [narrow_device(line[k]) for k in (1, 3)]
    )
    gather = WideGather(
        sender, w, wide, lambda k: src_ref if k == 0 else dst_ref.at[place_of(k, wide)],
        lambda k, to: dst_ref.at[place_of(k ^ to, wide)],
    )
    middles = [
        sender.plan(up_ref, up_at(z), narrow_device(line[3])),
        sender.plan(down_ref, down_at(z), narrow_device(line[3])),
    ]
    relays = [
        sender.plan(up_two, up_at(line[2]), narrow_device(line[1])),
        sender.plan(down_two, down_at(line[2]), narrow_device(line[1])),
    ]
    gather.start()

    @pl.when(is_middle)
    def _():
        for copy in middles + relays:
            copy.start()

    sibling = wide_device(flipped(w, 1))
    copies = [sender.plan(grads[n], grad_ref.at[half + n], sibling) for n in range(half)]
    for copy in copies:
        copy.start()
    gather.pass_on()

    @pl.when(is_middle)
    def _():
        for copy in middles:
            copy.wait()
        for copy in relays:
            copy.wait_send()

    @pl.when(is_end)
    def _():
        for copy in relays:
            copy.wait_recv()

    for copy in own + copies:
        copy.wait()
    gather.finish()


def gather_rows(array, grads, ups, downs, collective_id):
    half = len(grads)
    wide = 2 * half
    whole = jax.ShapeDtypeStruct((wide,) + array.shape, array.dtype)
    up_shape = ups[0].shape
    full = jax.ShapeDtypeStruct((up_shape[0], 4) + up_shape[1:], BF16)
    return pl.pallas_call(
        functools.partial(rows_kernel, wide),
        out_shape=[whole, whole, full, jax.ShapeDtypeStruct((4,) + downs[0].shape, BF16)],
        in_specs=[ANY] * (half + 7),
        out_specs=[VMEM, ANY if wide > 8 else VMEM, VMEM, VMEM],
        scratch_shapes=[DMA((2 * wide + 4,)), DMA((2 * wide + 4,)), DMA((half + 7,))],
        compiler_params=pltpu.CompilerParams(
            collective_id=collective_id, has_side_effects=True, vmem_limit_bytes=48 * 2**20
        ),
    )(*grads, array, *ups, *downs)


def hidden_kernel(
    half, normed_ref, grad_ref, up_ref, down_ref, hidden_ref, mid_ref, even_ref, odd_ref, branch_ref
):
    size = down_ref.shape[0]
    gate_up = dot_f32(normed_ref[...], up_ref[...])
    grad_hidden = dot_f32(grad_ref[...], down_ref[...], ((1,), (1,)))
    gate, up = gate_up[:, :size], gate_up[:, size:]
    opened = jax.nn.sigmoid(gate)
    acted = gate * opened
    hidden_ref[...] = (acted * up).astype(BF16)
    mid_ref[:, :size] = (grad_hidden * up * (opened * (1.0 + gate * (1.0 - opened)))).astype(BF16)
    mid_ref[:, size:] = (grad_hidden * acted).astype(BF16)
    grad_normed = dot_f32(mid_ref[...], up_ref[...], ((1,), (1,))).astype(BF16)
    branch_ref[...] = dot_f32(hidden_ref[...], down_ref[...]).astype(BF16)
    step = pl.program_id(0)

    @pl.when(step < half)
    def _():
        even_ref[...] = grad_normed

    @pl.when(step >= half)
    def _():
        odd_ref[...] = grad_normed


def feed_forward(normed, grad, up_full, down_full, rows):
    total, width = normed.shape
    blocks = total // rows
    half = blocks // 2
    size = down_full.shape[0]
    row_block = lambda columns: pl.BlockSpec((rows, columns), lambda i: (i, 0))
    fixed = lambda array: pl.BlockSpec(array.shape, lambda i: (0, 0))
    return pl.pallas_call(
        functools.partial(hidden_kernel, half),
        grid=(blocks,),
        in_specs=[row_block(width), row_block(width), fixed(up_full), fixed(down_full)],
        out_specs=[
            row_block(size), row_block(2 * size),
            pl.BlockSpec((rows, width), lambda i: (jnp.minimum(i, half - 1), 0)),
            pl.BlockSpec((rows, width), lambda i: (jnp.maximum(i - half, 0), 0)),
            row_block(width),
        ],
        out_shape=[
            jax.ShapeDtypeStruct((total, size), BF16),
            jax.ShapeDtypeStruct((total, 2 * size), BF16),
            jax.ShapeDtypeStruct((total // 2, width), BF16),
            jax.ShapeDtypeStruct((total // 2, width), BF16),
            jax.ShapeDtypeStruct((total, width), BF16),
        ],
        compiler_params=pltpu.CompilerParams(vmem_limit_bytes=48 * 2**20),
    )(normed, grad, up_full, down_full)


def middle_kernel(
    wide, even_ref, got_ref, branch_ref, up_ref, down_ref, norm_sum, branch_sum, up_src, down_src,
    up_one, down_one, up_acc, down_acc, core_buf, own_buf, far_buf, branch_buf, up_join, up_mid,
    down_join, down_mid, up_own, down_own, send, recv, local,
):
    w, z = lax.axis_index("wide"), lax.axis_index("narrow")
    line = [flipped(z, k) for k in range(4)]
    half = wide // 2
    unit = up_src.shape[1]
    part = down_src.shape[1]
    sender = Sender(send, recv)
    is_middle = (z == 1) | (z == 2)
    is_end = (z == 0) | (z == 3)

    def up_share(n):
        return up_ref.at[:, pl.ds(pl.multiple_of(n * unit, unit), unit)]

    def down_share(n):
        return down_ref.at[:, pl.ds(pl.multiple_of(n * part, part), part)]

    moves = [
        (up_share(line[2]), up_src), (down_share(line[2]), down_src),
        (up_share(z), up_own), (down_share(z), down_own),
        (up_share(line[1]), up_one), (down_share(line[1]), down_one),
    ]
    moves += [(got_ref.at[n], core_buf.at[n]) for n in range(half)]
    moves += [(even_ref.at[n], own_buf.at[n]) for n in range(half)]
    pairs = branch_sum.shape[0]
    moves += [(branch_ref.at[n], branch_sum.at[n]) for n in range(pairs)]
    own = [pltpu.make_async_copy(src, dst, local.at[n]) for n, (src, dst) in enumerate(moves)]
    for copy in own:
        copy.start()
    greet(
        [wide_device(flipped(w, k)) for k in wide_steps(wide)]
        + [narrow_device(line[k]) for k in (1, 3)]
    )
    sibling = wide_device(flipped(w, 1))
    far = [
        sender.plan(own_buf.at[n], far_buf.at[n - 1], wide_device(flipped(w, 2 * n)))
        for n in range(1, half)
    ]
    branch_core = [
        sender.plan(branch_ref.at[pairs + n], branch_buf.at[n], sibling) for n in range(pairs)
    ]
    joins = [
        sender.plan(up_share(line[3]), up_join, narrow_device(line[1])),
        sender.plan(down_share(line[3]), down_join, narrow_device(line[1])),
    ]
    mids = [
        sender.plan(up_share(line[3]), up_mid, narrow_device(line[3])),
        sender.plan(down_share(line[3]), down_mid, narrow_device(line[3])),
    ]
    order = list(range(1, half)) + [0]

    @pl.when(is_end)
    def _():
        for copy in joins:
            copy.start()

    @pl.when(is_middle)
    def _():
        for copy in mids:
            copy.start()

    for n in order:
        own[6 + n].wait()
        own[6 + half + n].wait()
        total = own_buf[n].astype(F32) + core_buf[n].astype(F32)
        own_buf[n] = total.astype(BF16)
        if n > 0:
            far[n - 1].start()
    for copy in branch_core:
        copy.start()
    for n in range(pairs):
        branch_core[n].wait_recv()
        own[6 + 2 * half + n].wait()
        total = branch_sum[n].astype(F32) + branch_buf[n].astype(F32)
        branch_sum[n] = total.astype(BF16)
    for n in range(6):
        own[n].wait()

    @pl.when(is_middle)
    def _():
        for copy in joins:
            copy.wait_recv()
        up_src[...] = (up_src[...].astype(F32) + up_join[...].astype(F32)).astype(BF16)
        down_src[...] = (down_src[...].astype(F32) + down_join[...].astype(F32)).astype(BF16)

    total = own_buf[0].astype(F32)
    for n in range(1, half):
        far[n - 1].wait_recv()
        total = total + far_buf[n - 1].astype(F32)
    norm_sum[...] = total
    up_acc[...] = up_own[...].astype(F32)
    down_acc[...] = down_own[...].astype(F32)

    @pl.when(is_middle)
    def _():
        for copy in mids:
            copy.wait()
        up_acc[...] += up_mid[...].astype(F32)
        down_acc[...] += down_mid[...].astype(F32)

    @pl.when(is_end)
    def _():
        for copy in joins:
            copy.wait_send()

    for copy in far + branch_core:
        copy.wait_send()


def middle_sums(even, got, branch, grad_up, grad_down, collective_id):
    half, rows, width = even.shape
    wide = 2 * half
    unit, part = grad_up.shape[1] // 4, grad_down.shape[1] // 4
    up_shape, down_shape = (grad_up.shape[0], unit), (grad_down.shape[0], part)
    steps = 4 * half + 6
    rows_buf = pltpu.VMEM((half, rows, width), BF16)
    pairs = branch.shape[0] // 2
    return pl.pallas_call(
        functools.partial(middle_kernel, wide),
        out_shape=[
            jax.ShapeDtypeStruct((rows, width), F32),
            jax.ShapeDtypeStruct((pairs,) + branch.shape[1:], BF16),
            *[jax.ShapeDtypeStruct(up_shape, BF16), jax.ShapeDtypeStruct(down_shape, BF16)] * 2,
            jax.ShapeDtypeStruct(up_shape, F32),
            jax.ShapeDtypeStruct(down_shape, F32),
        ],
        in_specs=[ANY] * 5,
        out_specs=[VMEM] * 8,
        scratch_shapes=[
            rows_buf, rows_buf, pltpu.VMEM((half - 1, rows, width), BF16),
            pltpu.VMEM((pairs,) + branch.shape[1:], BF16),
            *[pltpu.VMEM(up_shape, BF16)] * 2, *[pltpu.VMEM(down_shape, BF16)] * 2,
            pltpu.VMEM(up_shape, BF16), pltpu.VMEM(down_shape, BF16),
            DMA((steps,)), DMA((steps,)), DMA((6 + 3 * half,)),
        ],
        compiler_params=pltpu.CompilerParams(
            collective_id=collective_id, has_side_effects=True, vmem_limit_bytes=58 * 2**20
        ),
    )(even, got, branch, grad_up, grad_down)


def last_kernel(
    wide, rows, own_width, own_heads, norm_ref, in_ref, up_parts, down_parts, branch_refs, token_ref,
    middle_ref, grad_ref, gain_ref, gain_two_ref, bias_ref, output, grad_tokens, grad_in, grad_up, grad_down, totals, join_buf, one_buf, mid_buf, two_buf, two_src, own_norm, norm_sum,
    in_core, in_own, in_far, in_sum, in_got, after_got, tail_buf, up_low, up_bufs, up_got, down_low,
    down_bufs, down_got, branch_bufs, narrow_buf, wide_buf, sum_buf, send, recv, down_send, down_recv,
    local,
):
    w, z = lax.axis_index("wide"), lax.axis_index("narrow")
    line = [flipped(z, k) for k in range(4)]
    half = wide // 2
    unit = up_low.shape[1]
    wide_rows, width = grad_in.shape[0], token_ref.shape[1]
    sender = Sender(send, recv)
    is_middle = (z == 1) | (z == 2)
    is_end = (z == 0) | (z == 3)

    def norm_block(n):
        return norm_ref.at[pl.ds(pl.multiple_of(n * rows, rows), rows), :]

    def up_rows(n):
        return up_low.at[pl.ds(pl.multiple_of(n * wide_rows, 16), wide_rows), :]

    def up_columns(n):
        return up_got.at[:, pl.ds(pl.multiple_of(n * unit, LANES), unit)]

    def section(n):
        return in_sum.at[:, pl.ds(pl.multiple_of(n * own_width, LANES), own_width)]

    def after_section(n):
        return in_sum.at[:, pl.ds(pl.multiple_of((n + 1) * own_width, LANES), LANES)]

    moves = [(norm_block(line[2]), two_src), (norm_block(z), own_norm)]
    moves += [(in_ref.at[flipped(w, 2 * n)], in_own.at[n]) for n in range(half)]
    ffn_at = len(moves)
    moves += [(ref, up_bufs.at[n]) for n, ref in enumerate(up_parts)]
    moves += [(ref, down_bufs.at[n]) for n, ref in enumerate(down_parts)]
    branch_at = len(moves)
    moves += [(ref, branch_bufs.at[n]) for n, ref in enumerate(branch_refs)]
    own = [pltpu.make_async_copy(src, dst, local.at[n]) for n, (src, dst) in enumerate(moves)]
    for copy in own:
        copy.start()
    greet(
        [narrow_device(line[k]) for k in (1, 2, 3)]
        + [wide_device(flipped(w, k)) for k in range(1, wide)]
    )
    sibling = wide_device(flipped(w, 1))
    joined = sender.plan(norm_block(line[3]), join_buf, narrow_device(line[1]))
    one = sender.plan(norm_block(line[1]), one_buf, narrow_device(line[1]))
    middle = sender.plan(norm_block(line[3]), mid_buf, narrow_device(line[3]))
    two = sender.plan(two_src, two_buf, narrow_device(line[2]))
    core = [
        sender.plan(in_ref.at[flipped(w, 2 * n + 1)], in_core.at[n], sibling) for n in range(half)
    ]
    far = [
        sender.plan(in_own.at[n], in_far.at[n - 1], wide_device(flipped(w, 2 * n)))
        for n in range(1, half)
    ]
    sections = [
        sender.plan(section(line[k]), in_got.at[z], narrow_device(line[k])) for k in (2, 3, 1)
    ]
    afters = [
        (
            (z == 0) | (line[k] == 3), (line[k] == 0) | (z == 3),
            sender.plan(after_section(line[k]), after_got.at[z], narrow_device(line[k])),
        )
        for k in (2, 3, 1)
    ]
    ups = [
        sender.plan(up_rows(flipped(w, k)), up_columns(w), wide_device(flipped(w, k)))
        for k in range(1, wide)
    ]
    first = [
        sender.plan(sum_buf, narrow_buf.at[z], narrow_device(line[k])) for k in (1, 2, 3)
    ]
    second = [
        sender.plan(sum_buf, wide_buf.at[w], wide_device(flipped(w, k))) for k in range(1, wide)
    ]
    parity, target = lax.rem(w, 2), lax.div(w, 2)
    depth = down_low.shape[0] // 2
    down_at = pl.ds(pl.multiple_of(parity * depth, 16), depth)
    downs = []
    for n in range(2):
        owner = target + n * half
        src, dst = down_low.at[pl.ds(n * depth, depth), :], down_got.at[down_at, :]
        push = pltpu.make_async_remote_copy(
            src_ref=src, dst_ref=dst, send_sem=down_send.at[n], recv_sem=down_recv.at[parity],
            device_id=wide_device(owner), device_id_type=MESH,
        )
        stay = pltpu.make_async_copy(src, dst, local.at[len(moves) + 1 + n])
        downs.append((owner == w, push, stay))

    order = list(range(1, half)) + [0]
    for n in order:
        core[n].start()

    @pl.when(is_end)
    def _():
        joined.start()

    @pl.when(is_middle)
    def _():
        middle.start()

    for n in order:
        core[n].wait_recv()
        own[2 + n].wait()
        total = in_own[n].astype(F32) + in_core[n].astype(F32)
        in_own[n] = total.astype(BF16)
        if n > 0:
            far[n - 1].start()
    own[0].wait()

    @pl.when(is_middle)
    def _():
        joined.wait_recv()
        two_src[...] = (two_src[...].astype(F32) + join_buf[...].astype(F32)).astype(BF16)

    two.start()
    one.start()
    for n in range(6):
        own[ffn_at + n].wait()
    up_low[...] = add_up([up_bufs[n] for n in range(3)]).astype(BF16)
    down_low[...] = add_up([down_bufs[n] for n in range(3)]).astype(BF16)
    for copy in ups:
        copy.start()
    for stays, push, stay in downs:
        pl.when(stays)(stay.start)
        pl.when(jnp.logical_not(stays))(push.start)
    up_got[:, pl.ds(pl.multiple_of(w * unit, LANES), unit)] = up_low[
        pl.ds(pl.multiple_of(w * wide_rows, 16), wide_rows), :
    ]
    total = middle_ref[...]
    for n in range(half):
        own[branch_at + n].wait()
        total = total + branch_bufs[n].astype(F32)
    output[...] = total.astype(BF16)

    total = in_own[0].astype(F32)
    for n in range(1, half):
        far[n - 1].wait_recv()
        total = total + in_far[n - 1].astype(F32)
    in_sum[...] = total.astype(BF16)
    mine = pltpu.make_async_copy(section(z), in_got.at[z], local.at[len(moves)])
    mine.start()
    own[1].wait()
    one.wait_recv()
    norm_sum[...] = own_norm[...].astype(F32) + one_buf[...].astype(F32)

    @pl.when(is_middle)
    def _():
        middle.wait()
        norm_sum[...] += mid_buf[...].astype(F32)

    two.wait_recv()
    for copy in sections:
        copy.start()
    for sends, gets, copy in afters:
        pl.when(sends)(copy.start)
    after_got[z] = after_section(z)[...]
    grads = norm_sum[...] + two_buf[...].astype(F32)
    values = token_ref[...].astype(F32)
    factor = rms_factor(values)
    normed = values * factor
    scaled = grads * gain_ref[...].reshape(1, width)
    inner = jnp.mean(scaled * normed, axis=-1, keepdims=True)
    grad_tokens[...] = grad_ref[...] + factor * (scaled - normed * inner)
    lane = iota((8, LANES), 1)
    bias = jnp.where(lane < own_heads, bias_ref[...], 0.0)
    narrow_buf[z] = jnp.zeros(sum_buf.shape, F32)
    narrow_buf[z, 1:2, :] = gain_two_ref[0:1, :]
    narrow_buf[z, 2:3, :LANES] = pltpu.roll(bias, z * own_heads, 1)[0:1, :]
    narrow_buf[z, 0:1, :] = jnp.sum(grads * normed, axis=0, keepdims=True)
    sum_buf[...] = narrow_buf[z]
    for copy in first:
        copy.start()

    for copy in ups:
        copy.wait_recv()
    grad_up[...] = up_got[...].astype(F32)
    for n, (stays, push, stay) in enumerate(downs):
        pl.when(stays)(stay.wait)
        pl.when(jnp.logical_not(stays))(push.wait_send)
    for n in range(2):
        source = lax.rem(2 * w + n, wide)
        arrived = pltpu.make_async_remote_copy(
            src_ref=down_low.at[pl.ds(0, depth), :], dst_ref=down_got.at[pl.ds(n * depth, depth), :],
            send_sem=down_send.at[n], recv_sem=down_recv.at[n], device_id=sibling,
            device_id_type=MESH,
        )
        pl.when(source != w)(arrived.wait_recv)
    grad_down[...] = down_got[...].astype(F32)

    for copy in first:
        copy.wait()
    sum_buf[...] = narrow_buf[0] + narrow_buf[1] + narrow_buf[2] + narrow_buf[3]
    for copy in second:
        copy.start()
    wide_buf[w] = sum_buf[...]

    for copy in sections:
        copy.wait_recv()
    mine.wait()
    for sends, gets, copy in afters:
        pl.when(gets)(copy.wait_recv)

    @pl.when(z == 3)
    def _():
        row, lane = iota((LANES, LANES), 0), iota((LANES, LANES), 1)
        last = jnp.zeros((wide_rows, LANES), F32)
        for n in range(4):
            group = lax.div(row, own_heads)
            place = group * (4 * own_heads) + n * own_heads + row - group * own_heads
            spot = ((lane == place) & (row < 3 * own_heads)).astype(BF16)
            last = last + dot_f32(after_got[n], spot)
        tail_buf[...] = last

    @pl.when(z != 3)
    def _():
        tail_buf[...] = after_got[0].astype(F32)

    whole = jnp.concatenate([in_got[n].astype(F32) for n in range(4)] + [tail_buf[...]], axis=1)
    move = whole.shape[1] - (grad_in.shape[1] - width) * z
    grad_in[...] = pltpu.roll(whole, lax.rem(move, whole.shape[1]), 1)[:, : grad_in.shape[1]]

    for copy in second:
        copy.wait()
    total = wide_buf[0]
    for n in range(1, wide):
        total = total + wide_buf[n]
    totals[...] = total

    @pl.when(is_end)
    def _():
        joined.wait_send()

    for sends, gets, copy in afters:
        pl.when(sends)(copy.wait_send)
    for copy in [one, two] + core + far + sections + ups:
        copy.wait_send()


def grouped_last_kernel(wide, rows, own_width, own_heads, *refs):
    own, near, far = refs[8:11]
    branches = [own.at[0]]
    branches += [near.at[n] for n in range(near.shape[0])] + [far.at[n] for n in range(far.shape[0])]
    last_kernel(
        wide, rows, own_width, own_heads, *refs[:2], refs[2:5], refs[5:8], branches, *refs[11:],
    )


def last_part(
    norm_part, in_part, ups, downs, branches, tokens, middle, grad_middle, gain, gain_two, bias, own_width,
    own_heads,
    shard, collective_id,
):
    wide, wide_rows, columns = in_part.shape
    half = wide // 2
    rows, width = tokens.shape
    unit = ups[0].shape[1]
    steps = 4 + 2 * half + 12 + 2 * wide
    shape = jax.ShapeDtypeStruct
    vmem = lambda *dims: pltpu.VMEM(dims, BF16)
    return pl.pallas_call(
        functools.partial(grouped_last_kernel, wide, rows, own_width, own_heads),
        out_shape=[
            shape((rows, width), BF16), shape((rows, width), F32), shape((wide_rows, shard), F32),
            shape((wide_rows, wide * unit), F32), shape(downs[0].shape, F32),
            shape(gain_two.shape, F32),
        ],
        in_specs=[ANY] * 11 + [VMEM] * 6,
        out_specs=[VMEM] * 6,
        scratch_shapes=[
            *[vmem(rows, width)] * 6, pltpu.VMEM((rows, width), F32),
            vmem(half, wide_rows, columns), vmem(half, wide_rows, columns),
            vmem(half - 1, wide_rows, columns), vmem(wide_rows, columns),
            vmem(4, wide_rows, own_width), vmem(4, wide_rows, LANES),
            pltpu.VMEM((wide_rows, LANES), F32), vmem(*ups[0].shape), vmem(3, *ups[0].shape),
            vmem(wide_rows, wide * unit), vmem(*downs[0].shape), vmem(3, *downs[0].shape),
            vmem(*downs[0].shape), vmem(half, rows, width),
            pltpu.VMEM((4,) + gain_two.shape, F32), pltpu.VMEM((wide,) + gain_two.shape, F32),
            pltpu.VMEM(gain_two.shape, F32),
            DMA((steps,)), DMA((steps,)), DMA((2,)), DMA((2,)), DMA((12 + 2 * half,)),
        ],
        compiler_params=pltpu.CompilerParams(
            collective_id=collective_id, has_side_effects=True, vmem_limit_bytes=60 * 2**20
        ),
    )(
        norm_part, in_part, *ups, *downs, *branches, tokens, middle, grad_middle,
        gain, gain_two, bias,
    )


def rms_factor(values):
    return lax.rsqrt(jnp.mean(values * values, axis=-1, keepdims=True) + EPSILON)


def rms_back(values, gain, grad):
    factor = rms_factor(values)
    normed = values * factor
    grad_gain = jnp.sum(grad * normed, axis=0)
    scaled = grad * gain
    inner = jnp.mean(scaled * normed, axis=-1, keepdims=True)
    return (factor * (scaled - normed * inner), grad_gain)


def log_sigmoid(v):
    return jnp.minimum(v, 0.0) - jnp.log1p(jnp.exp(-jnp.abs(v)))


def iota(shape, dim):
    return lax.broadcasted_iota(jnp.int32, shape, dim)


def running_sum(v, reverse):
    rows = v.shape[0]
    index = iota(v.shape, 0)
    step = 1
    while step < rows:
        if reverse:
            v = v + jnp.where(index < rows - step, pltpu.roll(v, rows - step, 0), 0.0)
        else:
            v = v + jnp.where(index >= step, pltpu.roll(v, step, 0), 0.0)
        step *= 2
    return v


def half_of(lane, head_size):
    return (lane >= head_size).astype(jnp.int32)


def spread(first, head_size):
    row, lane = iota((LANES, LANES), 0), iota((LANES, LANES), 1)
    return row == first + half_of(lane, head_size)


def collect(first, head_size):
    row, lane = iota((LANES, LANES), 0), iota((LANES, LANES), 1)
    return lane == first + half_of(row, head_size)


def same_head(head_size):
    row, lane = iota((LANES, LANES), 0), iota((LANES, LANES), 1)
    return (half_of(row, head_size) == half_of(lane, head_size)).astype(F32)


def exact_dot(left, right):
    return lax.dot_general(
        left, right, (((1,), (0,)), ((), ())), precision=EXACT, preferred_element_type=F32
    )


def head_mean(v, head_size):
    return exact_dot(v, same_head(head_size)) * (1.0 / head_size)


def prologue(pair, heads, head_size, q_ref, k_ref, v_ref, small_low, cont):
    spot = lambda group: spread(group * heads + 2 * pair, head_size).astype(BF16)
    key_mix = jax.nn.sigmoid(dot_f32(small_low, spot(1)))
    value_mix = jax.nn.sigmoid(dot_f32(small_low, spot(2)))
    queries = q_ref[...].astype(BF16).astype(F32)
    keys = k_ref[...].astype(BF16).astype(F32)
    values = v_ref[...].astype(BF16).astype(F32)
    key_step = pltpu.roll(keys, 1, 0) * cont - keys
    value_step = pltpu.roll(values, 1, 0) * cont - values
    shifted = keys + key_mix * key_step
    value_low = (values + value_mix * value_step).astype(BF16)
    query_factor = lax.rsqrt(head_mean(queries * queries, head_size) + EPSILON)
    key_factor = lax.rsqrt(head_mean(shifted * shifted, head_size) + EPSILON)
    return (
        queries * query_factor,
        shifted * key_factor,
        value_low,
        query_factor,
        key_factor,
        key_mix,
        value_mix,
        key_step,
        value_step,
    )


def small_columns(small_ref, bias_ref):
    return (small_ref[...] + bias_ref[0:1, :]).astype(BF16)


def decay_of(small_low, cont):
    return running_sum(log_sigmoid(small_low.astype(F32)) - SEPARATE * (1.0 - cont), False)


def forward_pair(
    pair, heads, head_size, block, q_ref, k_ref, v_ref, gate_ref, small_low, cont, decay_all,
    mixed_ref, att_ref, log_ref,
):
    query, key, value_low, *unused = prologue(
        pair, heads, head_size, q_ref, k_ref, v_ref, small_low, cont
    )
    rows = query.shape[0]
    query = query.astype(BF16) * BF16(head_size**-0.5)
    key = key.astype(BF16)
    decay = exact_dot(decay_all, spread(2 * pair, head_size).astype(F32))
    decay_rows = decay.T
    lane = iota((1, LANES), 1)
    ones = jnp.ones((rows, LANES), BF16)
    value_wide = jnp.concatenate([value_low, ones], axis=1)
    for i in range(rows // block):
        lo, hi = i * block, (i + 1) * block
        row_index = iota((block, hi), 0) + lo
        visible = iota((block, hi), 1) <= row_index
        outs, sums = [], []
        for head in range(2):
            mine = (lane >= head_size) if head else (lane < head_size)
            at = head * head_size
            left = jnp.where(mine, query[lo:hi], BF16(0.0))
            scores = dot_f32(left, key[:hi], ((1,), (1,)))
            scores = scores + decay[lo:hi, at : at + 1] - decay_rows[at : at + 1, :hi]
            weights = jnp.where(visible, jnp.exp(scores), 0.0).astype(BF16)
            both = dot_f32(weights, value_wide[:hi])
            outs.append(both[:, :LANES])
            sums.append(both[:, LANES:])
        first = lane < head_size
        total = jnp.where(first, sums[0], sums[1])
        attended = (jnp.where(first, outs[0], outs[1]) / total).astype(BF16)
        att_ref[lo:hi, :] = attended
        log_ref[lo:hi, :] = jnp.log(total)
        opened = jax.nn.sigmoid(gate_ref[lo:hi, :])
        mixed_ref[lo:hi, :] = (attended.astype(F32) * opened).astype(BF16)


def forward_kernel(
    heads, head_size, block, q_ref, k_ref, v_ref, gate_ref, small_ref, bias_ref, cont_ref,
    mixed_ref, att_ref, log_ref, decay_scr,
):
    pair = pl.program_id(0)
    cont = cont_ref[...]
    small_low = small_columns(small_ref, bias_ref)

    @pl.when(pair == 0)
    def _():
        decay_scr[...] = decay_of(small_low, cont)

    forward_pair(
        pair, heads, head_size, block, q_ref, k_ref, v_ref, gate_ref, small_low, cont,
        decay_scr[...], mixed_ref, att_ref, log_ref,
    )


def share_of(ref, like, n):
    size = like.shape[1]
    if ref.shape[1] == size:
        return ref
    return ref.at[:, pl.ds(pl.multiple_of(n * size, size), size)]


def backward_kernel(
    heads, head_size, block, wide, *refs
):
    q_ref, k_ref, v_ref, gate_ref, small_ref, bias_ref, cont_ref, att_ref, log_ref, grad_ref = refs[:10]
    in_ref, normed_ref, up_src, down_src, up_one, down_one, part_ref, branch_ref = refs[10:18]
    out_ref, bias_grad_ref, norm_ref, in_part_ref, grad_out = refs[18:23]
    up_two_got, down_two_got, up_one_got, down_one_got, branch_got = refs[23:28]
    decay_scr, small_scr, dq_scr, part_core, part_own, part_far, part_sum, part_got = refs[28:36]
    in_buf, send, recv, local = refs[36:]
    pair = pl.program_id(0)
    pairs = heads * head_size // LANES
    half = wide // 2
    row_steps = out_ref.shape[0] // norm_ref.shape[0]
    w, z = lax.axis_index("wide"), lax.axis_index("narrow")
    sender = Sender(send, recv)
    one, two = flipped(z, 1), flipped(z, 2)
    copies = [
        sender.plan(up_src, up_two_got, narrow_device(two)),
        sender.plan(down_src, down_two_got, narrow_device(two)),
        sender.plan(share_of(up_one, up_src, one), up_one_got, narrow_device(one)),
        sender.plan(share_of(down_one, down_src, one), down_one_got, narrow_device(one)),
    ]
    core = [
        sender.plan(part_ref.at[flipped(w, 2 * n + 1)], part_core.at[n], wide_device(flipped(w, 1)))
        for n in range(half)
    ]
    far = [
        sender.plan(part_own.at[n], part_far.at[n - 1], wide_device(flipped(w, 2 * n)))
        for n in range(1, half)
    ]
    branches = [
        sender.plan(branch_ref.at[k // 2], branch_got.at[n], wide_device(flipped(w, k)))
        for n, k in enumerate(diagonal_steps(wide))
    ]
    own = [
        pltpu.make_async_copy(part_ref.at[flipped(w, 2 * n)], part_own.at[n], local.at[n])
        for n in range(half)
    ]
    in_copy = pltpu.make_async_copy(in_ref, in_buf, local.at[half])
    own_width = heads * head_size

    def part_columns(n):
        return part_sum.at[:, pl.ds(pl.multiple_of(n * own_width, LANES), own_width)]

    outs = [
        sender.plan(part_columns(flipped(z, k)), part_got.at[k - 1], narrow_device(flipped(z, k)))
        for k in (1, 2, 3)
    ]

    @pl.when(pair == 0)
    def _():
        greet(
            [narrow_device(flipped(z, k)) for k in (1, 2, 3)]
            + [wide_device(flipped(w, k)) for k in wide_steps(wide)]
        )
        for copy in copies + core + own + [in_copy]:
            copy.start()

    @pl.when(pair == 1)
    def _():
        for n in range(half):
            core[n].wait_recv()
            own[n].wait()
            part_own[n] = (part_own[n].astype(F32) + part_core[n].astype(F32)).astype(BF16)
            if n > 0:
                far[n - 1].start()

    @pl.when(pair < pairs)
    def _():
        backward_pair(
            pair, pairs, heads, head_size, block, q_ref, k_ref, v_ref, gate_ref, small_ref,
            bias_ref, cont_ref, att_ref, log_ref, grad_ref, out_ref, bias_grad_ref, decay_scr,
            small_scr, dq_scr,
        )

    @pl.when(pair == pairs)
    def _():
        in_copy.wait()

    @pl.when((pair >= pairs) & (pair < pairs + row_steps))
    def _():
        size = norm_ref.shape[0]
        at = pl.ds(pl.multiple_of((pair - pairs) * size, size), size)
        norm_ref[...] = dot_f32(out_ref[at, :], in_buf[...], ((1,), (1,))).astype(BF16)

    @pl.when(pair == pairs + row_steps)
    def _():
        total = part_own[0].astype(F32)
        for n in range(1, half):
            far[n - 1].wait_recv()
            total = total + part_far[n - 1].astype(F32)
        part_sum[...] = total.astype(BF16)
        for copy in outs + branches:
            copy.start()

    @pl.when(pair >= pairs + row_steps)
    def _():
        in_part_ref[...] = dot_f32(normed_ref[...], out_ref[...], ((0,), (0,))).astype(BF16)

    @pl.when(pair == pl.num_programs(0) - 1)
    def _():
        for copy in outs + copies + branches:
            copy.wait()
        total = part_columns(z)[...].astype(F32)
        for n in range(3):
            total = total + part_got[n].astype(F32)
        grad_out[...] = total
        for copy in core + far:
            copy.wait_send()


def backward_pair(
    pair, pairs, heads, head_size, block, q_ref, k_ref, v_ref, gate_ref, small_ref, bias_ref, cont_ref,
    att_ref, log_ref, grad_ref, out_ref, bias_grad_ref, decay_scr, small_scr, dq_scr,
):
    cont = cont_ref[...]
    small_low = small_columns(small_ref, bias_ref)
    rows = cont.shape[0]
    width = heads * head_size

    @pl.when(pair == 0)
    def _():
        decay_scr[...] = decay_of(small_low, cont)
        small_scr[...] = jnp.zeros_like(small_scr)

    (
        query_norm, key_norm, value_low, query_factor, key_factor, key_mix, value_mix, key_step,
        value_step,
    ) = prologue(pair, heads, head_size, q_ref, k_ref, v_ref, small_low, cont)
    query = query_norm.astype(BF16) * BF16(head_size**-0.5)
    key = key_norm.astype(BF16)
    opened = jax.nn.sigmoid(gate_ref[...])
    attended = att_ref[...].astype(F32)
    grad_mixed = grad_ref[...].astype(F32)
    grad_low = (grad_mixed * opened).astype(BF16)
    grad_gate = grad_mixed * attended * opened * (1.0 - opened)

    def columns(group):
        at = group * width + pair * LANES
        return pl.ds(pl.multiple_of(at, LANES), LANES)

    out_ref[:, columns(3)] = grad_gate.astype(BF16)
    inner = exact_dot(grad_low.astype(F32) * attended, same_head(head_size))
    decay = exact_dot(decay_scr[...], spread(2 * pair, head_size).astype(F32))
    level_rows = (decay - log_ref[...]).T
    inner_rows = inner.T
    lane = iota((1, LANES), 1)
    ones = jnp.ones((rows, LANES), BF16)
    query_wide = jnp.concatenate([query, ones], axis=1)
    key_wide = jnp.concatenate([key, ones], axis=1)
    key_parts, value_parts, query_parts = [], [], []
    for head in range(2):
        mine = (lane >= head_size) if head else (lane < head_size)
        at = head * head_size
        keys_out, values_out = [], []
        for j in range(rows // block):
            lo, hi = j * block, (j + 1) * block
            span = rows - lo
            visible = iota((block, span), 0) <= iota((block, span), 1)
            scores = dot_f32(
                jnp.where(mine, key[lo:hi], BF16(0.0)), query[lo:], ((1,), (1,))
            )
            scores = scores + level_rows[at : at + 1, lo:] - decay[lo:hi, at : at + 1]
            probs = jnp.where(visible, jnp.exp(scores), 0.0)
            grad_probs = dot_f32(
                jnp.where(mine, value_low[lo:hi], BF16(0.0)), grad_low[lo:], ((1,), (1,))
            )
            grad_scores = (probs * (grad_probs - inner_rows[at : at + 1, lo:])).astype(BF16)
            values_out.append(dot_f32(probs.astype(BF16), grad_low[lo:]))
            keys_out.append(dot_f32(grad_scores, query_wide[lo:]))
            part = dot_f32(grad_scores, key_wide[lo:hi], ((0,), (0,)))
            if j == 0:
                dq_scr[...] = part
            else:
                dq_scr[lo:, :] += part
        key_parts.append(jnp.concatenate(keys_out, axis=0))
        value_parts.append(jnp.concatenate(values_out, axis=0))
        query_parts.append(dq_scr[...])
    first = lane < head_size

    def join(parts):
        return jnp.where(first, parts[0], parts[1])

    grad_query = join([p[:, :LANES] for p in query_parts]) * head_size**-0.5
    grad_key = join([p[:, :LANES] for p in key_parts])
    grad_value = join(value_parts)
    grad_decay = join([p[:, LANES:] for p in query_parts]) - join([p[:, LANES:] for p in key_parts])

    def norm_back(grad, normed, factor):
        return factor * (grad - normed * head_mean(grad * normed, head_size))

    def shift_back(grad, mix):
        return grad * (1.0 - mix) + pltpu.roll(grad * mix * cont, rows - 1, 0)

    grad_query = norm_back(grad_query, query_norm, query_factor)
    grad_shifted = norm_back(grad_key, key_norm, key_factor)
    out_ref[:, columns(0)] = grad_query.astype(BF16)
    out_ref[:, columns(1)] = shift_back(grad_shifted, key_mix).astype(BF16)
    out_ref[:, columns(2)] = shift_back(grad_value, value_mix).astype(BF16)
    key_logit = grad_shifted * key_step * key_mix * (1.0 - key_mix)
    value_logit = grad_value * value_step * value_mix * (1.0 - value_mix)
    single = (lax.rem(lane, head_size) == 0).astype(F32)
    small_scr[...] += (
        exact_dot(grad_decay * single, collect(2 * pair, head_size).astype(F32))
        + exact_dot(key_logit, collect(heads + 2 * pair, head_size).astype(F32))
        + exact_dot(value_logit, collect(2 * heads + 2 * pair, head_size).astype(F32))
    )

    @pl.when(pair == pairs - 1)
    def _():
        grads = small_scr[...]
        forget = running_sum(grads, True) * jax.nn.sigmoid(-small_low.astype(F32))
        result = jnp.where(lane < heads, forget, grads)
        out_ref[:, 4 * width :] = result.astype(BF16)
        bias_grad_ref[...] = jnp.broadcast_to(
            jnp.sum(result, axis=0, keepdims=True), bias_grad_ref.shape
        )


def attention_specs(rows, pairs):
    def block_at(group):
        return pl.BlockSpec((rows, LANES), lambda p: (0, group * pairs + jnp.minimum(p, pairs - 1)))

    def fixed(height, column=0):
        return pl.BlockSpec((height, LANES), lambda p: (0, column))

    base = [block_at(0), block_at(1), block_at(2), block_at(3), fixed(rows, 4 * pairs), fixed(8), fixed(rows)]
    return base, pl.BlockSpec((rows, LANES), lambda p: (0, jnp.minimum(p, pairs - 1)))


def attention_forward(projected, bias, cont, heads, head_size, block):
    rows = projected.shape[0]
    pairs = heads * head_size // LANES
    base, own = attention_specs(rows, pairs)
    wide = jax.ShapeDtypeStruct((rows, heads * head_size), BF16)
    return pl.pallas_call(
        functools.partial(forward_kernel, heads, head_size, block),
        grid=(pairs,),
        in_specs=base,
        out_specs=[own] * 3,
        out_shape=[wide, wide, jax.ShapeDtypeStruct(wide.shape, F32)],
        scratch_shapes=[pltpu.VMEM((rows, LANES), F32)],
        compiler_params=pltpu.CompilerParams(vmem_limit_bytes=48 * 2**20),
    )(*([projected] * 5), bias, cont)


def attention_backward(
    projected, bias, cont, attended, logs, grad, in_full, normed_one, shares, out_part, branches, heads,
    head_size, block, collective_id,
):
    rows = projected.shape[0]
    width = normed_one.shape[1]
    wide, wide_rows = out_part.shape[:2]
    half = wide // 2
    pairs = heads * head_size // LANES
    base, own = attention_specs(rows, pairs)
    columns = 4 * heads * head_size + LANES
    step = min(256, rows)
    row_steps, in_steps = rows // step, width // 256
    steps = 8 + 3 * wide
    part = lambda count: pltpu.VMEM((count, wide_rows, width), BF16)
    shape = jax.ShapeDtypeStruct

    def later(first, count):
        return lambda p: jnp.clip(p - first, 0, count - 1)

    row_at, in_at = later(pairs, row_steps), later(pairs + row_steps, in_steps)
    return pl.pallas_call(
        functools.partial(backward_kernel, heads, head_size, block, wide),
        grid=(pairs + row_steps + in_steps,),
        in_specs=base
        + [own] * 3
        + [
            ANY,
            pl.BlockSpec((rows, 256), lambda p: (0, in_at(p))),
        ]
        + [ANY] * 6,
        out_specs=[
            pl.BlockSpec((rows, columns), lambda p: (0, 0)),
            pl.BlockSpec((8, LANES), lambda p: (0, 0)),
            pl.BlockSpec((step, width), lambda p: (row_at(p), 0)),
            pl.BlockSpec((256, columns), lambda p: (in_at(p), 0)),
            pl.BlockSpec((wide_rows, heads * head_size), lambda p: (0, 0)),
        ]
        + [ANY] * 5,
        out_shape=[
            shape((rows, columns), BF16), shape((8, LANES), F32), shape((rows, width), BF16),
            shape((width, columns), BF16), shape((wide_rows, heads * head_size), F32),
            *[shape(share.shape, BF16) for share in shares[:2] * 2],
            shape((len(diagonal_steps(wide)),) + branches.shape[1:], BF16),
        ],
        scratch_shapes=[
            pltpu.VMEM((rows, LANES), F32), pltpu.VMEM((rows, LANES), F32),
            pltpu.VMEM((rows, 2 * LANES), F32), part(half), part(half), part(half - 1),
            pltpu.VMEM((wide_rows, width), BF16),
            pltpu.VMEM((3, wide_rows, heads * head_size), BF16),
            pltpu.VMEM(in_full.shape, BF16),
            DMA((steps,)), DMA((steps,)), DMA((half + 1,)),
        ],
        compiler_params=pltpu.CompilerParams(
            collective_id=collective_id, has_side_effects=True, vmem_limit_bytes=60 * 2**20
        ),
    )(
        *([projected] * 5), bias, cont, attended, logs, grad, in_full, normed_one, *shares, out_part,
        branches,
    )


def first_kernel(
    wide, heads, head_size, block, x_ref, in_ref, small_ref, out_ref, up_ref, grad_ref, down_ref, gain_one_ref,
    gain_two_ref, bias_ref, cont_ref, normed_out, in_out, out_out, proj_out, att_ref, log_ref,
    mixed_rows, middle_ref, normed_two_ref, up_out, up_two, up_one, down_got, grad_got, slot, in_buf,
    out_buf, up_buf, normed, proj, mixed, decay_scr, send, recv, local,
):
    w, z = lax.axis_index("wide"), lax.axis_index("narrow")
    line = [flipped(z, k) for k in range(4)]
    rows, width = x_ref.shape
    own_width = heads * head_size
    part_rows = out_ref.shape[0]
    is_middle = (z == 1) | (z == 2)
    is_end = (z == 0) | (z == 3)
    sender = Sender(send, recv)
    used = []

    def local_copy(src, dst):
        copy = pltpu.make_async_copy(src, dst, local.at[len(used)])
        used.append(copy)
        return copy

    def slot_rows(n):
        return slot.at[pl.ds(pl.multiple_of(n * rows, rows), rows), :]

    def weight_rows(ref, w_of, z_of):
        at = (w_of * 4 + z_of) * part_rows
        return ref.at[pl.ds(pl.multiple_of(at, 16), part_rows), :]

    def wide_rows(ref, w_of):
        at = w_of * 4 * part_rows
        return ref.at[pl.ds(pl.multiple_of(at, 16), 4 * part_rows), :]

    def by_rows(ref):
        return (
            (lambda k: wide_rows(ref, flipped(w, k))),
            (lambda k, to: wide_rows(ref, flipped(w, k))),
        )

    unit = up_buf.shape[2] // 4

    def in_pieces(n):
        target = lambda at, size: in_buf.at[
            pl.ds(pl.multiple_of((w * 4 + z) * part_rows, 16), part_rows), pl.ds(at, size)
        ]
        for group in range(4):
            at = pl.multiple_of(group * width + n * own_width, LANES)
            yield in_ref.at[:, pl.ds(at, own_width)], target(group * own_width, own_width)
        yield small_ref.at[n], target(4 * own_width, LANES)

    def up_pieces(n):
        for group in range(4):
            at = pl.multiple_of((group * wide + n) * unit, LANES)
            yield up_ref.at[:, pl.ds(at, unit)], up_buf.at[w, :, pl.ds(group * unit, unit)]

    own_in = [local_copy(*piece) for piece in in_pieces(z)]
    own_up = [local_copy(*piece) for piece in up_pieces(w)]
    own_out = local_copy(out_ref, weight_rows(out_buf, w, z))
    own_x = local_copy(x_ref, slot_rows(z))
    for copy in used:
        copy.start()

    index = w * 4 + z
    down_wide = lax.div(lax.rem(index, 2 * wide), 2)
    down_narrow = lax.rem(index, 2) + 2 * lax.div(index, 2 * wide)
    from_index = 2 * wide * lax.div(z, 2) + 2 * w + lax.rem(z, 2)
    from_wide_index, from_narrow_index = lax.div(from_index, 4), lax.rem(from_index, 4)
    moves = jnp.logical_not((down_wide == w) & (down_narrow == z))
    down_push = sender.plan(
        down_ref, down_got, {"wide": down_wide, "narrow": down_narrow}
    )
    down_stay = local_copy(down_ref, down_got)

    barrier = pltpu.get_barrier_semaphore()
    partners = [narrow_device(line[k]) for k in (1, 2, 3)]
    partners += [wide_device(flipped(w, k)) for k in range(1, wide)]
    for device in partners:
        pl.semaphore_signal(barrier, inc=1, device_id=device, device_id_type=MESH)

    @pl.when(moves)
    def _():
        for device in (
            {"wide": from_wide_index, "narrow": from_narrow_index},
            {"wide": down_wide, "narrow": down_narrow},
        ):
            pl.semaphore_signal(barrier, inc=1, device_id=device, device_id_type=MESH)
        pl.semaphore_wait(barrier, len(partners) + 2)

    @pl.when(jnp.logical_not(moves))
    def _():
        pl.semaphore_wait(barrier, len(partners))

    ins = [
        sender.plan(*piece, narrow_device(line[k])) for k in (2, 3, 1) for piece in in_pieces(line[k])
    ]
    outs = [
        sender.plan(out_ref, weight_rows(out_buf, w, z), narrow_device(line[k])) for k in (2, 1)
    ]
    out_middle = sender.plan(out_ref, weight_rows(out_buf, w, z), narrow_device(line[3]))
    out_relay = sender.plan(
        weight_rows(out_buf, w, line[2]), weight_rows(out_buf, w, line[2]), narrow_device(line[1])
    )
    ups = [
        sender.plan(*piece, wide_device(flipped(w, k)))
        for k in range(1, wide)
        for piece in up_pieces(flipped(w, k))
    ]
    grads = {
        k: sender.plan(grad_ref, grad_got.at[k // 2 - 1], wide_device(flipped(w, k)))
        for k in range(2, wide, 2)
    }
    two = sender.plan(x_ref, slot_rows(z), narrow_device(line[2]))
    one = sender.plan(x_ref, slot_rows(z), narrow_device(line[1]))
    middle = sender.plan(x_ref, slot_rows(z), narrow_device(line[3]))
    relay = sender.plan(slot_rows(line[2]), slot_rows(line[2]), narrow_device(line[1]))
    in_wide = WideGather(sender, w, wide, *by_rows(in_buf))
    out_wide = WideGather(sender, w, wide, *by_rows(out_buf))
    up_steps = [
        sender.plan(up_buf, up_two, narrow_device(line[2])),
        sender.plan(up_buf, up_one, narrow_device(line[1])),
    ]
    mixes = [
        sender.plan(
            mixed.at[pl.ds(pl.multiple_of(line[k] * rows, rows), rows), :],
            mixed_rows.at[:, pl.ds(pl.multiple_of(z * own_width, LANES), own_width)],
            narrow_device(line[k]),
        )
        for k in (2, 3, 1)
    ]

    for copy in ins + outs + ups + [two]:
        copy.start()
    for copy in own_in:
        copy.wait()
    for copy in ins:
        copy.wait_recv()
    in_wide.start()
    one.start()
    own_out.wait()
    outs[0].wait_recv()

    @pl.when(is_middle)
    def _():
        out_relay.start()
        out_middle.start()

    in_wide.pass_on()
    outs[1].wait_recv()

    @pl.when(is_middle)
    def _():
        out_middle.wait_recv()

    @pl.when(is_end)
    def _():
        out_relay.wait_recv()

    out_wide.start()
    for k in diagonal_steps(wide):
        grads[k].start()
    two.wait_recv()

    @pl.when(is_middle)
    def _():
        relay.start()
        middle.start()

    for copy in own_up:
        copy.wait()
    for copy in ups:
        copy.wait_recv()
    up_back = local_copy(up_buf, up_out)
    up_back.start()
    in_wide.received()
    in_back = local_copy(in_buf, in_out)
    in_back.start()
    own_x.wait()

    def project(t, carry):
        @pl.when(t == 2)
        def _():
            one.wait_recv()

        @pl.when((t == 3) & is_middle)
        def _():
            middle.wait_recv()

        @pl.when((t == 3) & is_end)
        def _():
            relay.wait_recv()

        @pl.when(t == 3)
        def _():
            for copy in up_steps:
                copy.start()
            for k in straight_steps(wide):
                grads[k].start()

        @pl.when((t == 3) & moves)
        def _():
            down_push.start()

        @pl.when((t == 3) & jnp.logical_not(moves))
        def _():
            down_stay.start()

        n = jnp.where(t == 0, z, jnp.where(t == 1, line[2], jnp.where(t == 2, line[1], line[3])))
        at = pl.ds(pl.multiple_of(n * rows, rows), rows)
        values = slot[at, :].astype(F32)
        low = (values * rms_factor(values) * gain_one_ref[...].reshape(1, width)).astype(BF16)
        normed[at, :] = low
        proj[at, :] = dot_f32(low, in_buf[...])
        return carry

    lax.fori_loop(0, 4, project, 0)
    normed_back = local_copy(normed, normed_out)
    proj_back = local_copy(proj, proj_out)
    normed_back.start()
    proj_back.start()

    cont = cont_ref[...]
    groups = own_width // LANES
    small_low = small_columns(proj.at[:, pl.ds(4 * own_width, LANES)], bias_ref)
    decay_scr[...] = decay_of(small_low, cont)

    def attend(pair, carry):
        def at(group):
            return pl.ds(pl.multiple_of((group * groups + pair) * LANES, LANES), LANES)

        forward_pair(
            pair, heads, head_size, block, proj.at[:, at(0)], proj.at[:, at(1)], proj.at[:, at(2)],
            proj.at[:, at(3)], small_low, cont, decay_scr[...], mixed.at[:, at(0)],
            att_ref.at[:, at(0)], log_ref.at[:, at(0)],
        )
        return carry

    lax.fori_loop(0, groups, attend, 0)
    for copy in mixes:
        copy.start()
    out_wide.pass_on()
    mixed_rows[:, pl.ds(pl.multiple_of(z * own_width, LANES), own_width)] = mixed[
        pl.ds(pl.multiple_of(z * rows, rows), rows), :
    ]
    out_wide.received()
    out_back = local_copy(out_buf, out_out)
    out_back.start()
    for copy in mixes:
        copy.wait_recv()
    inputs = slot[pl.ds(pl.multiple_of(z * rows, rows), rows), :].astype(F32)
    values = inputs + dot_f32(mixed_rows[...], out_buf[...])
    middle_ref[...] = values
    normed_two_ref[...] = (values * rms_factor(values) * gain_two_ref[...].reshape(1, width)).astype(BF16)

    for copy in up_steps:
        copy.wait()
    for copy in grads.values():
        copy.wait()

    @pl.when(moves)
    def _():
        down_push.wait()

    @pl.when(jnp.logical_not(moves))
    def _():
        down_stay.wait()

    @pl.when(is_middle)
    def _():
        relay.wait_send()
        middle.wait_send()
        out_relay.wait_send()
        out_middle.wait_send()

    for copy in ins + outs + ups + [two, one] + mixes:
        copy.wait_send()
    in_wide.sent()
    out_wide.sent()
    for copy in (up_back, in_back, normed_back, proj_back, out_back):
        copy.wait()


def first_part(
    tokens, in_weight, small, out_weight, gate_up_weight, cotangent, down_weight, gain_one, gain_two, bias,
    cont, wide, heads, head_size, block, collective_id,
):
    rows, width = tokens.shape
    slot, own_width = 4 * rows, heads * head_size
    columns = 4 * own_width + LANES
    steps = 8 * wide + 40
    up_shape = (wide, gate_up_weight.shape[0], gate_up_weight.shape[1] // wide)
    shape = jax.ShapeDtypeStruct
    return pl.pallas_call(
        functools.partial(first_kernel, wide, heads, head_size, block),
        out_shape=[
            shape((slot, width), BF16), shape((width, columns), BF16), shape((width, width), BF16),
            shape((slot, columns), F32), shape((slot, own_width), BF16),
            shape((slot, own_width), F32), shape((rows, width), BF16), shape((rows, width), F32),
            shape((rows, width), BF16), shape(up_shape, BF16), shape(up_shape, BF16),
            shape(up_shape, BF16), shape(down_weight.shape, BF16),
            shape((wide // 2 - 1, rows, width), BF16),
        ],
        in_specs=[ANY] * 7 + [VMEM] * 4,
        out_specs=[ANY] * 4 + [VMEM] * 5 + [ANY] * 5,
        scratch_shapes=[
            pltpu.VMEM((slot, width), BF16), pltpu.VMEM((width, columns), BF16),
            pltpu.VMEM((width, width), BF16), pltpu.VMEM(up_shape, BF16),
            pltpu.VMEM((slot, width), BF16), pltpu.VMEM((slot, columns), F32),
            pltpu.VMEM((slot, own_width), BF16), pltpu.VMEM((slot, LANES), F32),
            DMA((steps,)), DMA((steps,)), DMA((20,)),
        ],
        compiler_params=pltpu.CompilerParams(
            collective_id=collective_id, has_side_effects=True, vmem_limit_bytes=60 * 2**20
        ),
    )(
        tokens, in_weight, small, out_weight, gate_up_weight, cotangent, down_weight, gain_one,
        gain_two, bias, cont,
    )


def second_kernel(
    wide, src_ref, grad_ref, far_grads, up_ref, up_two, up_one, down_ref, middle_ref, mixed_ref, out_ref,
    gain_ref, grad_middle, gain_grad, slot_grad, branch_sum, up_src, down_src, up_acc, down_acc,
    up_grad_out, down_grad_out, out_part, branch_near, normed, grads, up_full, down_full, hidden, mid,
    rows_buf, core_buf, far_buf, branch_buf, up_join, up_mid, down_join, down_mid, up_grad, down_grad,
    grad_mixed, mixed_buf, send, recv, local,
):
    w, z = lax.axis_index("wide"), lax.axis_index("narrow")
    line = [flipped(z, k) for k in range(4)]
    rows, width = src_ref.shape
    half = wide // 2
    size = hidden.shape[1]
    unit, part = up_src.shape[1], down_src.shape[1]
    is_middle = (z == 1) | (z == 2)
    is_end = (z == 0) | (z == 3)
    sender = Sender(send, recv)
    sibling = wide_device(flipped(w, 1))

    def at_place(ref, place):
        return ref.at[pl.ds(pl.multiple_of(place * rows, rows), rows), :]

    up_at = lambda n: up_full.at[:, n]
    down_at = lambda n: down_full.at[n]
    moves = [
        (src_ref, at_place(normed, 0)), (up_ref, up_at(z)), (up_two, up_at(line[2])),
        (up_one, up_at(line[1])), (down_ref, down_at(z)), (grad_ref, at_place(grads, 0)),
    ] + [(far_grads.at[n - 1], at_place(grads, n)) for n in range(1, half)]
    own = [pltpu.make_async_copy(src, dst, local.at[n]) for n, (src, dst) in enumerate(moves)]
    for copy in own:
        copy.start()
    greet(
        [wide_device(flipped(w, k)) for k in wide_steps(wide)]
        + [narrow_device(line[k]) for k in (1, 2, 3)]
    )
    gather = WideGather(
        sender, w, wide, lambda k: src_ref if k == 0 else at_place(normed, place_of(k, wide)),
        lambda k, to: at_place(normed, place_of(k ^ to, wide)),
    )
    middle = sender.plan(up_ref, up_at(z), narrow_device(line[3]))
    relay = sender.plan(up_two, up_at(line[2]), narrow_device(line[1]))
    down_two = sender.plan(down_ref, down_at(z), narrow_device(line[2]))
    down_one = sender.plan(down_ref, down_at(z), narrow_device(line[1]))
    down_middle = sender.plan(down_ref, down_at(z), narrow_device(line[3]))
    down_relay = sender.plan(down_at(line[2]), down_at(line[2]), narrow_device(line[1]))
    passed = [
        sender.plan(
            grad_ref if n == 0 else far_grads.at[n - 1], at_place(grads, half + n), sibling
        )
        for n in range(half)
    ]
    core = [
        sender.plan(at_place(rows_buf, half + n), core_buf.at[n], sibling) for n in range(half)
    ]
    far = [
        sender.plan(at_place(rows_buf, n), far_buf.at[n - 1], wide_device(flipped(w, 2 * n)))
        for n in range(1, half)
    ]
    branch_core = [
        sender.plan(at_place(normed, half + n), branch_buf.at[n], sibling) for n in range(half)
    ]

    def up_share(n):
        return up_grad.at[:, pl.ds(pl.multiple_of(n * unit, unit), unit)]

    def down_share(n):
        return down_grad.at[:, pl.ds(pl.multiple_of(n * part, part), part)]

    down_joined = sender.plan(down_share(line[3]), down_join, narrow_device(line[1]))
    down_direct = sender.plan(down_share(line[3]), down_mid, narrow_device(line[3]))
    up_joined = sender.plan(up_share(line[3]), up_join, narrow_device(line[1]))
    up_direct = sender.plan(up_share(line[3]), up_mid, narrow_device(line[3]))
    own_width = width // 4
    mixes = [
        sender.plan(
            grad_mixed.at[:, pl.ds(pl.multiple_of(line[k] * own_width, LANES), own_width)],
            slot_grad.at[pl.ds(pl.multiple_of(z * rows, rows), rows), :], narrow_device(line[k]),
        )
        for k in (2, 3, 1)
    ]
    near = [
        sender.plan(branch_sum.at[k // 2], branch_near.at[n], wide_device(flipped(w, k)))
        for n, k in enumerate(straight_steps(wide))
    ]

    gather.start()

    @pl.when(is_middle)
    def _():
        relay.start()
        middle.start()

    down_two.start()
    down_two.wait_recv()

    @pl.when(is_middle)
    def _():
        down_relay.start()
        down_middle.start()

    down_one.start()
    for copy in passed:
        copy.start()
    for copy in own[:4]:
        copy.wait()

    @pl.when(is_middle)
    def _():
        middle.wait_recv()

    @pl.when(is_end)
    def _():
        relay.wait_recv()

    up_shape = (width, 4 * unit)
    down_shape = (size, width)

    def arriving(t, carry):
        @pl.when(t == 1)
        def _():
            gather.first[1].wait_recv()

        for n, k in enumerate(gather.far):

            @pl.when(t == 2 + n)
            def _():
                gather.first[k].wait_recv()
                gather.second[k].start()

            @pl.when(t == half + 1 + n)
            def _():
                gather.second[k].wait_recv()

        place = jnp.where(t < 2, t * half, jnp.where(t < half + 1, t - 1, t))
        at = pl.ds(pl.multiple_of(place * rows, rows), rows)
        mid[at, :] = dot_f32(normed[at, :], up_full[...].reshape(up_shape)).astype(BF16)
        return carry

    lax.fori_loop(0, wide, arriving, 0)
    for copy in own[4:]:
        copy.wait()
    for copy in passed + [down_one]:
        copy.wait_recv()

    @pl.when(is_middle)
    def _():
        down_middle.wait_recv()

    @pl.when(is_end)
    def _():
        down_relay.wait_recv()

    def block(t, carry):
        pick = half - 1 - lax.div(t, 2)
        place = jnp.where(lax.rem(t, 2) == 0, half + pick, pick)
        at = pl.ds(pl.multiple_of(place * rows, rows), rows)
        gate_up = mid[at, :].astype(F32)
        grad_hidden = dot_f32(grads[at, :], down_full[...].reshape(down_shape), ((1,), (1,)))
        gate, up = gate_up[:, :size], gate_up[:, size:]
        opened = jax.nn.sigmoid(gate)
        acted = gate * opened
        hidden[at, :] = (acted * up).astype(BF16)
        mid[at, :size] = (grad_hidden * up * (opened * (1.0 + gate * (1.0 - opened)))).astype(BF16)
        mid[at, size:] = (grad_hidden * acted).astype(BF16)
        rows_buf[at, :] = dot_f32(mid[at, :], up_full[...].reshape(up_shape), ((1,), (1,))).astype(
            BF16
        )
        for n in range(half):

            @pl.when(t == 2 * (half - 1 - n))
            def _():
                core[n].start()

        for n in range(half):

            @pl.when(t == 2 * (half - 1 - n) + 1)
            def _():
                core[n].wait_recv()
                total = rows_buf[n * rows : (n + 1) * rows, :].astype(F32) + core_buf[n].astype(F32)
                rows_buf[n * rows : (n + 1) * rows, :] = total.astype(BF16)
                if n > 0:
                    far[n - 1].start()

        return carry

    lax.fori_loop(0, wide, block, 0)

    step = min(256, size)
    for n in range(size // step):
        cut = slice(n * step, (n + 1) * step)
        down_grad[cut, :] = dot_f32(hidden[:, cut], grads[...], ((0,), (0,))).astype(BF16)

    @pl.when(is_end)
    def _():
        down_joined.start()

    @pl.when(is_middle)
    def _():
        down_direct.start()

    reloads = [
        pltpu.make_async_copy(out_ref, grads.at[pl.ds(0, width), :], local.at[9 + half]),
        pltpu.make_async_copy(grad_ref, grads.at[pl.ds(width, rows), :], local.at[10 + half]),
        pltpu.make_async_copy(mixed_ref, mixed_buf, local.at[11 + half]),
        pltpu.make_async_copy(middle_ref, grad_middle, local.at[12 + half]),
    ]
    for copy in reloads:
        copy.start()

    def up_rows(n, carry):
        at = pl.ds(pl.multiple_of(n * 256, 256), 256)
        up_grad[at, :] = dot_f32(normed[:, at], mid[...], ((0,), (0,))).astype(BF16)
        return carry

    lax.fori_loop(0, width // 256, up_rows, 0)

    @pl.when(is_end)
    def _():
        up_joined.start()

    @pl.when(is_middle)
    def _():
        up_direct.start()

    backs = [
        pltpu.make_async_copy(up_grad, up_grad_out, local.at[5 + half]),
        pltpu.make_async_copy(down_grad, down_grad_out, local.at[6 + half]),
        pltpu.make_async_copy(up_share(line[2]), up_src, local.at[7 + half]),
        pltpu.make_async_copy(down_share(line[2]), down_src, local.at[8 + half]),
    ]
    for copy in backs:
        copy.start()
    gather.sent()

    def branch(t, carry):
        place = lax.rem(t + half, wide)
        at = pl.ds(pl.multiple_of(place * rows, rows), rows)
        normed[at, :] = dot_f32(hidden[at, :], down_full[...].reshape(down_shape)).astype(BF16)
        for n in range(half):

            @pl.when(t == n)
            def _():
                branch_core[n].start()

        return carry

    lax.fori_loop(0, wide, branch, 0)
    for n in range(half):
        branch_core[n].wait_recv()
        total = normed[n * rows : (n + 1) * rows, :].astype(F32) + branch_buf[n].astype(F32)
        branch_sum[n] = total.astype(BF16)

    total = rows_buf[:rows, :].astype(F32)
    for n in range(1, half):
        far[n - 1].wait_recv()
        total = total + far_buf[n - 1].astype(F32)
    for copy in core + far:
        copy.wait_send()
    for copy in reloads:
        copy.wait()
    values = grad_middle[...]
    factor = rms_factor(values)
    values = values * factor
    gain_grad[...] = jnp.broadcast_to(
        jnp.sum(total * values, axis=0, keepdims=True), gain_grad.shape
    )
    total = total * gain_ref[...].reshape(1, width)
    inner = jnp.mean(total * values, axis=-1, keepdims=True)
    total = grads[width : width + rows, :].astype(F32) + factor * (total - values * inner)
    grad_middle[...] = total
    branch_grad = total.astype(BF16)
    grad_mixed[...] = dot_f32(branch_grad, grads[:width, :], ((1,), (1,))).astype(BF16)
    for copy in mixes + near:
        copy.start()
    slot_grad[pl.ds(pl.multiple_of(z * rows, rows), rows), :] = grad_mixed[
        :, pl.ds(pl.multiple_of(z * own_width, LANES), own_width)
    ]
    for n in range(width // 256):
        cut = slice(n * 256, (n + 1) * 256)
        rows_buf[cut, :] = dot_f32(mixed_buf[:, cut], branch_grad, ((0,), (0,))).astype(BF16)
    out_back = pltpu.make_async_copy(
        rows_buf.at[pl.ds(0, width), :], out_part, local.at[13 + half]
    )
    out_back.start()
    for copy in backs:
        copy.wait()
    up_acc[...] = up_grad[:, pl.ds(pl.multiple_of(z * unit, unit), unit)]
    down_acc[...] = down_grad[:, pl.ds(pl.multiple_of(z * part, part), part)]

    @pl.when(is_middle)
    def _():
        down_joined.wait_recv()
        down_src[...] = (down_src[...].astype(F32) + down_join[...].astype(F32)).astype(BF16)
        up_joined.wait_recv()
        up_src[...] = (up_src[...].astype(F32) + up_join[...].astype(F32)).astype(BF16)
        down_direct.wait()
        down_acc[...] = (down_acc[...].astype(F32) + down_mid[...].astype(F32)).astype(BF16)
        up_direct.wait()
        up_acc[...] = (up_acc[...].astype(F32) + up_mid[...].astype(F32)).astype(BF16)
        for copy in (relay, middle, down_relay, down_middle):
            copy.wait_send()

    @pl.when(is_end)
    def _():
        down_joined.wait_send()
        up_joined.wait_send()

    for copy in mixes + near:
        copy.wait()
    out_back.wait()
    for copy in passed + branch_core + [down_two, down_one]:
        copy.wait_send()


def second_part(
    normed, grad, far_grads, ups, down, middle, mixed_rows, out_full, gain, collective_id
):
    rows, width = normed.shape
    half = far_grads.shape[0] + 1
    wide = 2 * half
    wide_of_up, part_rows, mid_size = ups[0].shape
    down_rows = down.shape[0]
    size, unit, part = mid_size // 2, mid_size // 4, width // 4
    steps = 9 + 2 * wide + 4 * half + 8
    total = wide * rows
    shape = jax.ShapeDtypeStruct
    vmem = lambda *dims: pltpu.VMEM(dims, BF16)
    return pl.pallas_call(
        functools.partial(second_kernel, wide),
        out_shape=[
            shape((rows, width), F32), shape((8, width), F32), shape((4 * rows, part), BF16),
            shape((half, rows, width), BF16),
            shape((width, unit), BF16), shape((size, part), BF16),
            shape((width, unit), BF16), shape((size, part), BF16),
            shape((width, mid_size), BF16), shape((size, width), BF16),
            shape((width, width), BF16), shape((len(straight_steps(wide)), rows, width), BF16),
        ],
        in_specs=[ANY] * 10 + [VMEM],
        out_specs=[VMEM] * 8 + [ANY] * 4,
        scratch_shapes=[
            vmem(total, width), vmem(total, width), vmem(wide, 4, part_rows, mid_size),
            vmem(4, down_rows, width), vmem(total, size), vmem(total, mid_size), vmem(total, width),
            vmem(half, rows, width), vmem(half - 1, rows, width), vmem(half, rows, width),
            vmem(width, unit), vmem(width, unit), vmem(size, part), vmem(size, part),
            vmem(width, mid_size), vmem(size, width), vmem(rows, width), vmem(rows, width),
            DMA((steps,)), DMA((steps,)), DMA((14 + half,)),
        ],
        compiler_params=pltpu.CompilerParams(
            collective_id=collective_id, has_side_effects=True, vmem_limit_bytes=63 * 2**20
        ),
    )(
        normed, grad, far_grads, *ups, down, middle, mixed_rows, out_full,
        gain,
    )


def add_up(parts):
    total = parts[0].astype(F32)
    for part in parts[1:]:
        total = total + part.astype(F32)
    return total


def on_device(
    tokens, gain_one, in_weight, forget_bias, out_weight, gain_two, gate_up_weight, down_weight,
    segment_ids, cotangent,
):
    wide, narrow = lax.axis_size("wide"), lax.axis_size("narrow")
    w, z = lax.axis_index("wide"), lax.axis_index("narrow")
    rows, width = tokens.shape
    slot = rows * narrow
    heads = forget_bias.shape[0]
    head_size = width // heads
    own_heads = heads // narrow
    own_width = own_heads * head_size
    part_rows = in_weight.shape[0]
    hidden_all = down_weight.shape[0] * wide * narrow
    unit = hidden_all // (2 * wide)
    columns = 4 * own_width + LANES
    base = 4 * width

    small = in_weight[:, base:].reshape(part_rows, 3, narrow, own_heads)
    small = jnp.moveaxis(small, 2, 0).reshape(narrow, part_rows, 3 * own_heads)
    small = jnp.pad(small, ((0, 0), (0, 0), (0, LANES - 3 * own_heads)))
    aligned = unit % LANES == 0

    def split_weights(sources, targets):
        copies = [(sources[1], targets[0].at[:, :, pl.ds(4 * own_width, LANES)])]
        for n in range(narrow):
            for group in range(4):
                copies.append(
                    (
                        sources[0].at[:, pl.ds(group * width + n * own_width, own_width)],
                        targets[0].at[n, :, pl.ds(group * own_width, own_width)],
                    )
                )
        return copies

    shapes = [
        jax.ShapeDtypeStruct((narrow, part_rows, columns), BF16),
        jax.ShapeDtypeStruct((wide, part_rows, 4 * unit), BF16),
    ]
    copies = 4 * narrow + 1
    fused = aligned and part_rows % 16 == 0
    if not fused:
        in_parts = local_copies(split_weights, copies, [in_weight, small], shapes[:1], False)[0]
        up_parts = jnp.moveaxis(gate_up_weight.reshape(part_rows, 4, wide, unit), 2, 0)
        up_parts = up_parts.reshape(wide, part_rows, 4 * unit)

    segments = segment_ids[0]
    joined = (segments[1:] == segments[:-1]).astype(F32)
    cont = jnp.concatenate([jnp.zeros((1,), F32), joined])
    cont = jnp.broadcast_to(cont[:, None], (slot, LANES))
    own_bias = lax.dynamic_slice_in_dim(forget_bias, z * own_heads, own_heads)
    bias = jnp.broadcast_to(jnp.pad(own_bias, (0, LANES - own_heads))[None], (8, LANES))
    block = min(256, slot)
    def row_block(ref, n):
        return ref.at[pl.ds(pl.multiple_of(n * rows, rows), rows), :]

    def column_block(ref, n):
        return ref.at[:, pl.ds(pl.multiple_of(n * own_width, LANES), own_width)]

    straight, diagonal = straight_steps(wide), diagonal_steps(wide)
    inputs = tokens.astype(F32)
    half = wide // 2
    if fused:
        (
            normed_one, in_full, out_full, projected, attended, logs, mixed_rows, middle, normed_two,
            up_block, up_two, up_one, down_block, grad_got,
        ) = first_part(
            tokens, in_weight, small, out_weight, gate_up_weight, cotangent, down_weight, gain_one,
            gain_two, bias, cont, wide, own_heads, head_size, block, 0,
        )
    else:
        pairs = []
        for i in range(wide * narrow):
            to_wide = (i % (2 * wide)) // 2
            to_narrow = i % 2 + 2 * (i // (2 * wide))
            pairs.append((i, to_wide * narrow + to_narrow))
        down_block = lax.ppermute(down_weight, ("wide", "narrow"), pairs)

        slot_tokens, in_full, out_full, up_block, grad_far = gather_all(
            tokens, in_parts, out_weight, up_parts, cotangent
        )
        slot_tokens = slot_tokens.reshape(slot, width)
        in_full = in_full.reshape(width, columns)
        out_full = out_full.reshape(width, width)

        up_two = on_line(up_block, LINE_TWO)
        up_one = on_line(up_block, LINE_ONE)

        slot_floats = slot_tokens.astype(F32)
        normed_one = (slot_floats * rms_factor(slot_floats) * gain_one).astype(BF16)
        projected = dot_f32(normed_one, in_full)

        mixed, attended, logs = attention_forward(
            projected, bias, cont, own_heads, head_size, block
        )

        mixed_rows, *grad_near = exchange(
            mixed, row_block, column_block, (rows, width), straight, [cotangent] * len(straight), 1
        )
        grads = {0: cotangent}
        grads.update({k: grad_near[n] for n, k in enumerate(straight)})
        grads.update({k: grad_far[n] for n, k in enumerate(diagonal)})
        grads = [grads[k] for k in range(0, wide, 2)]
        down_block = follow(down_block, mixed_rows)
        down_two = on_line(down_block, LINE_TWO)
        down_one = on_line(down_block, LINE_ONE)
        middle = inputs + dot_f32(mixed_rows, out_full)
        normed_two = (middle * rms_factor(middle) * gain_two).astype(BF16)

    if fused:
        (
            grad_middle, grad_gain_two, slot_grad, branch_sum, up_src, down_src, up_acc, down_acc,
            up_one, down_one, out_part, branch_near,
        ) = second_part(
            normed_two, cotangent, grad_got, [up_block, up_two, up_one], down_block, middle,
            mixed_rows, out_full, gain_two, 2,
        )
    else:
        ups = [up_block] + [follow(piece, normed_two) for piece in (up_two, up_one)]
        plane_normed, plane_grad, up_full, down_full = gather_rows(
            normed_two, grads, ups, [down_block, down_two, down_one], 2
        )
        plane_normed = plane_normed.reshape(wide * rows, width)
        plane_grad = plane_grad.reshape(wide * rows, width)
        up_full = up_full.reshape(width, 4 * unit)
        down_full = down_full.reshape(2 * unit, width)
        hidden, gate_up_grad, norm_even, norm_odd, branch = feed_forward(
            plane_normed, plane_grad, up_full, down_full, rows
        )
        grad_up_full = dot_f32(plane_normed, gate_up_grad, ((0,), (0,))).astype(BF16)
        grad_down_full = dot_f32(hidden, plane_grad, ((0,), (0,))).astype(BF16)
        if unit % LANES:
            grouped = grad_up_full.reshape(width, 4, unit)
            grad_up_full = jnp.pad(grouped, ((0, 0), (0, 0), (0, LANES - unit))).reshape(width, -1)
        branch = branch.reshape(wide, rows, width)
        fits = wide <= 8
        norm_got = along_wide(norm_odd.reshape(half, rows, width), 1, wide)
        (
            grad_normed_two, branch_sum, up_src, down_src, up_one, down_one, up_acc, down_acc,
        ) = middle_sums(
            norm_even.reshape(half, rows, width), norm_got,
            branch if fits else branch[:2, :16], grad_up_full, grad_down_full, 6,
        )
        if not fits:
            received = along_wide(branch[half:], 1, wide)
            branch_sum = (branch[:half].astype(F32) + received.astype(F32)).astype(BF16)
        upstream = cotangent.astype(F32)
        grad_middle_norm, grad_gain_two = rms_back(middle, gain_two, grad_normed_two)
        grad_middle = upstream + grad_middle_norm
        branch_one_grad = grad_middle.astype(BF16)
        grad_mixed = dot_f32(branch_one_grad, out_full, ((1,), (1,))).astype(BF16)
        slot_grad, *branch_near = exchange(
            grad_mixed, column_block, row_block, (slot, own_width), straight,
            [branch_sum[k // 2] for k in straight], 3,
        )
        branch_near = jnp.stack(branch_near)
        out_part = dot_f32(mixed_rows, branch_one_grad, ((0,), (0,))).astype(BF16)
    wide_rows = width // wide
    (
        unused, bias_grad, norm_part, in_part, grad_out, up_two, down_two, up_one, down_one,
        branch_far,
    ) = attention_backward(
        projected, bias, cont, attended, logs, slot_grad, in_full, normed_one,
        [up_src, down_src, up_one, down_one], out_part.reshape(wide, wide_rows, width), branch_sum,
        own_heads, head_size, block, 7,
    )
    branches = [branch_sum, branch_near, branch_far]
    if not fused:
        grad_gain_two = jnp.broadcast_to(grad_gain_two[None], (8, width))
    low = lambda part: part.astype(BF16)
    output, grad_tokens, grad_in, grad_up, grad_down, totals = last_part(
        norm_part, in_part.reshape(wide, wide_rows, columns), [low(up_acc), up_one, up_two],
        [low(down_acc), down_one, down_two], branches, tokens, middle, grad_middle, gain_one, grad_gain_two,
        bias_grad,
        own_width, own_heads, (base + 3 * heads) // narrow, 4,
    )
    if not aligned:
        grad_up = grad_up.reshape(wide_rows, wide, LANES)[:, :, :unit]
        grad_up = grad_up.reshape(wide_rows, wide * unit)
    return (
        output,
        grad_tokens,
        totals[0],
        grad_in,
        totals[2, :heads],
        grad_out,
        totals[1],
        grad_up,
        grad_down,
    )


def solution(mesh):
    both = ("wide", "narrow")
    in_specs = (
        P(both, None), P(), P(both, None), P(), P(both, None), P(), P(both, None), P(both, None),
        P("wide", None), P(both, None),
    )
    out_specs = (
        P(both, None), P(both, None), P(), P("wide", "narrow"), P(), P("wide", "narrow"), P(),
        P("wide", "narrow"), P("wide", "narrow"),
    )
    return jax.shard_map(
        on_device, mesh=mesh, in_specs=in_specs, out_specs=out_specs, check_vma=False
    )
```
